32 devices in a mesh: dp: 32 (over z, y, x, core).
Axes of the slice: x: 2, y: 2, z: 4, core: 2. Of those that a mesh axis runs over, the one named last changes fastest.
Arguments:
- token_ids: int32 [128, 256], P('dp'), may hold values from 0 to 147
- durations: int32 [128, 256], P('dp'), may hold values from 0 to 993, as said below
- mel_frames: float32 [128, 1024, 80], P('dp'), may hold values from -6 to 6
- embedding: bfloat16 [148, 192], replicated, may hold values from -0.4375 to 0.4375
- w_qkv: bfloat16 [192, 576], replicated, may hold values from -0.4375 to 0.4375
- rel_key: bfloat16 [9, 96], replicated, may hold values from -0.625 to 0.625
- rel_value: bfloat16 [9, 96], replicated, may hold values from -0.625 to 0.625
- w_out: bfloat16 [192, 192], replicated, may hold values from -1.25 to 1.25
- attn_gain: float32 [192], replicated, may hold values from 0.5 to 1.5
- attn_shift: float32 [192], replicated, may hold values from -3 to 3
- w_ff1: bfloat16 [576, 768], replicated, may hold values from -0.25 to 0.25
- w_ff2: bfloat16 [2304, 192], replicated, may hold values from -0.125 to 0.125
- ffn_gain: float32 [192], replicated, may hold values from 0.5 to 1.5
- ffn_shift: float32 [192], replicated, may hold values from -3 to 3
- w_prior: bfloat16 [192, 160], replicated, may hold values from -0.21875 to 0.21875
- w_mix: float32 [4, 4], replicated, may hold values from -0.6 to 3, as said below
- w_start: bfloat16 [80, 192], replicated, may hold values from -0.625 to 0.625
- w_in: bfloat16 [4, 960, 384], replicated, may hold values from -0.1875 to 0.1875
- w_res: bfloat16 [3, 192, 384], replicated, may hold values from -0.4375 to 0.4375
- w_skip_last: bfloat16 [192, 192], replicated, may hold values from -0.4375 to 0.4375
- w_end: bfloat16 [192, 160], replicated, may hold values from -0.15625 to 0.15625
Outputs:
- loss: float32 [], replicated
- mel_grad: float32 [128, 1024, 80], P('dp')
- embedding_grad: float32 [148, 192], replicated
- w_qkv_grad: float32 [192, 576], replicated
- rel_key_grad: float32 [9, 96], replicated
- rel_value_grad: float32 [9, 96], replicated
- w_out_grad: float32 [192, 192], replicated
- attn_gain_grad: float32 [192], replicated
- attn_shift_grad: float32 [192], replicated
- w_ff1_grad: float32 [576, 768], replicated
- w_ff2_grad: float32 [2304, 192], replicated
- ffn_gain_grad: float32 [192], replicated
- ffn_shift_grad: float32 [192], replicated
- w_prior_grad: float32 [192, 160], replicated
- w_mix_grad: float32 [4, 4], replicated
- w_start_grad: float32 [80, 192], replicated
- w_in_grad: float32 [4, 960, 384], replicated
- w_res_grad: float32 [3, 192, 384], replicated
- w_skip_last_grad: float32 [192, 192], replicated
- w_end_grad: float32 [192, 160], replicated
The draws below stay inside these ranges and needn't reach their ends.
Inputs may be any that keep to these rules, and one draw needn't show every extreme that they name: In each utterance the first L slots have positive durations and the rest zero, with 32 <= L <= 256; the durations sum to the utterance's frame count, between 256 and 1024; some utterance has L = 256, and another one has 1024 frames, L = 32 and a token of the largest duration. `w_mix`: each diagonal entry exceeds the sum of the magnitudes of the other entries of its row.
All inputs are finite; a program needn't handle non-finite values.
Results may differ from the reference program's by a relative error of at most 0.014.
Values sent between devices are 32-bit elements; how exact they have to be, the bound alone decides.
No kernel may reach another device: no remote copies, remote signals or barrier semaphores. Data moves between devices by JAX's collectives and lax.ppermute only.
A program may use at most 128 MiB of HBM per device.

```python
import math
import jax
import jax.numpy as jnp
from jax import lax

D = 192
HEADS = 2
HEAD = 96
FILTER = 768
MEL = 80
HID = 192
VOCAB = 148
KSIZE = 3
WKER = 5
WLAYERS = 4
WINDOW = 4
TEXT = 256
FRAMES = 1024
ITEMS = 128


def draw_durations(key, part):
    key = jax.random.fold_in(key, 11)
    key_list = jax.random.split(key, 5)
    text_len = jax.random.randint(key_list[0], (ITEMS,), TEXT // 8, TEXT + 1)
    frame_len = jax.random.randint(key_list[1], (ITEMS,), FRAMES // 4, FRAMES + 1)
    long_text = jax.random.randint(key_list[2], (), 0, ITEMS)
    long_frames = (long_text + 1 + jax.random.randint(key_list[3], (), 0, ITEMS - 1)) % ITEMS
    item_index = jnp.arange(ITEMS, dtype=jnp.int32)
    text_len = jnp.where(item_index == long_text, TEXT, text_len)
    text_len = jnp.where(item_index == long_frames, TEXT // 8, text_len)
    frame_len = jnp.where(item_index == long_frames, FRAMES, frame_len)
    weights = jax.random.randint(key_list[4], (ITEMS, TEXT), 1, 9)
    frame_position = jnp.arange(TEXT, dtype=jnp.int32)[None, :]
    occupied_slot = frame_position < text_len[:, None]
    weights = jnp.where(occupied_slot, weights, 0)
    spare_frames = frame_len - text_len
    surplus_frames = spare_frames[:, None] * weights // jnp.sum(weights, axis=1, keepdims=True)
    leftover_frames = spare_frames - jnp.sum(surplus_frames, axis=1)
    additional_frame = (frame_position < leftover_frames[:, None]).astype(jnp.int32)
    expanded_rows = jnp.where(occupied_slot, 1 + surplus_frames + additional_frame, 0)
    peak_row = jnp.where(frame_position == 0, FRAMES - TEXT // 8 + 1, jnp.where(occupied_slot, 1, 0))
    chosen = (item_index == long_frames)[:, None]
    return jnp.where(chosen, peak_row, expanded_rows).astype(jnp.int32)


def draw_w_mix(key, part):
    key = jax.random.fold_in(key, 23)
    first_key, second_key = jax.random.split(key)
    diagonal = jax.random.uniform(first_key, (4,), jnp.float32, 2.0, 3.0)
    off_diag = jax.random.uniform(second_key, (4, 4), jnp.float32, -0.6, 0.6)
    on_diag = diagonal[None, :] * jnp.ones((4, 4), jnp.float32)
    return jnp.where(jnp.eye(4) > 0, on_diag, off_diag).astype(jnp.float32)


def with_ends(array, rng, low, largest):
    longest = array.shape.index(max(array.shape))
    spots = []
    for shift in (0, 1):
        where = [jax.random.randint(jax.random.fold_in(rng, axis), (), 0, length) for axis, length in enumerate(array.shape)]
        where[longest] = (where[longest] + shift) % array.shape[longest]
        spots.append(tuple(where))
    return array.at[spots[0]].set(low).at[spots[1]].set(largest)


def level_of(rng, extent, pieces, least, top_value):
    factor_of = 1.0
    for axis_at, parts in pieces:
        heights = jax.random.uniform(jax.random.fold_in(jax.random.fold_in(rng, 6), axis_at), (parts,), jnp.float32, least / len(pieces), top_value / len(pieces))
        factor_of = factor_of * jnp.repeat(jnp.exp(heights), extent[axis_at] // parts).reshape((-1,) + (1,) * (len(extent) - 1 - axis_at))
    return factor_of


def normal_values(key, shape, scale, bound, cuts=(), held_as=jnp.bfloat16):
    values = scale * jax.random.normal(key, shape, jnp.float32)
    if cuts:
        values = values * level_of(key, shape, cuts, -0.22, 0.18)
    return jnp.clip(values, -bound, bound).astype(held_as)


def setup_inputs(seed: int = 0) -> dict:
    keys = jax.random.split(jax.random.key(seed), 22)
    return {
        "token_ids": with_ends(jax.random.randint(keys[0], (ITEMS, TEXT), 0, VOCAB), jax.random.fold_in(keys[0], 1), 0, VOCAB - 1).astype(jnp.int32),
        "durations": draw_durations(jax.random.fold_in(keys[21], 71), 0),
        "mel_frames": normal_values(keys[2], (ITEMS, FRAMES, MEL), 1.0, 6.0, ((0, 32),), jnp.float32),
        "embedding": normal_values(keys[3], (VOCAB, D), D ** -0.5, 0.4375),
        "w_qkv": normal_values(keys[4], (D, 3 * D), D ** -0.5, 0.4375),
        "rel_key": normal_values(keys[5], (2 * WINDOW + 1, HEAD), HEAD ** -0.5, 0.625),
        "rel_value": normal_values(keys[6], (2 * WINDOW + 1, HEAD), HEAD ** -0.5, 0.625),
        "w_out": normal_values(keys[7], (D, D), (D // 8) ** -0.5, 1.25),
        "attn_gain": jnp.clip(1.0 + 0.1 * jax.random.normal(keys[8], (D,), jnp.float32), 0.5, 1.5),
        "attn_shift": normal_values(keys[9], (D,), 0.3, 3.0, (), jnp.float32),
        "w_ff1": normal_values(keys[10], (KSIZE * D, FILTER), (KSIZE * D) ** -0.5, 0.25),
        "w_ff2": normal_values(keys[11], (KSIZE * FILTER, D), (KSIZE * FILTER) ** -0.5, 0.125),
        "ffn_gain": jnp.clip(1.0 + 0.1 * jax.random.normal(keys[12], (D,), jnp.float32), 0.5, 1.5),
        "ffn_shift": normal_values(keys[13], (D,), 0.3, 3.0, (), jnp.float32),
        "w_prior": normal_values(keys[14], (D, 2 * MEL), (4 * D) ** -0.5, 0.21875),
        "w_mix": draw_w_mix(jax.random.fold_in(keys[21], 71), 0),
        "w_start": normal_values(keys[16], (MEL, HID), MEL ** -0.5, 0.625),
        "w_in": normal_values(keys[17], (WLAYERS, WKER * HID, 2 * HID), (WKER * HID) ** -0.5, 0.1875),
        "w_res": normal_values(keys[18], (WLAYERS - 1, HID, 2 * HID), HID ** -0.5, 0.4375),
        "w_skip_last": normal_values(keys[19], (HID, HID), HID ** -0.5, 0.4375),
        "w_end": normal_values(keys[20], (HID, 2 * MEL), (8 * HID) ** -0.5, 0.15625),
    }


@jax.custom_vjp
def low(v):
    return lax.optimization_barrier(v.astype(jnp.bfloat16)).astype(jnp.float32)

@jax.custom_vjp
def low_back(v):
    return v

def low_keep(v):
    return (low(v), None)

def low_pass(kept, grad):
    return (grad,)

def back_keep(v):
    return (v, None)

def back_low(kept, grad):
    return (low(grad),)
low.defvjp(low_keep, low_pass)
low_back.defvjp(back_keep, back_low)

def matmul(first_op, second_op):
    return jnp.dot(first_op, second_op, precision=lax.Precision.HIGHEST)

def unfold(inputs, kernel):
    half_width = kernel // 2
    padded = jnp.pad(inputs, ((half_width, half_width), (0, 0)))
    length = inputs.shape[0]
    return jnp.concatenate([padded[offset_step:offset_step + length] for offset_step in range(kernel)], axis=1)

def layer_norm(inputs, scale_vec, shift_vec):
    centered = inputs - lax.optimization_barrier(jnp.mean(inputs, axis=1, keepdims=True))
    spread = lax.optimization_barrier(jnp.mean(centered * centered, axis=1, keepdims=True))
    return centered * lax.rsqrt(spread + 1e-05) * scale_vec + shift_vec

def gate_units(pre_gate):
    return jnp.tanh(pre_gate[:, :HID]) * jax.nn.sigmoid(pre_gate[:, HID:])

def band_table(length):
    places = lax.iota(jnp.int32, length)
    offsets = places[None, :] - places[:, None]
    reach = lax.iota(jnp.int32, 2 * WINDOW + 1) - WINDOW
    return (offsets[None, :, :] == reach[:, None, None]).astype(jnp.float32)

def pair_up(frames):
    count_rows = frames.shape[0]
    width = frames.shape[1]
    return frames.reshape(count_rows // 2, 2, width).transpose(0, 2, 1).reshape(count_rows // 2, 2 * width)

def to_groups(frames):
    count_rows = frames.shape[0]
    width = frames.shape[1]
    return frames.reshape(count_rows, 2, width // 4, 2).transpose(0, 2, 1, 3).reshape(count_rows, width // 4, 4)

def from_groups(grouped):
    count_rows = grouped.shape[0]
    groups = grouped.shape[1]
    return grouped.reshape(count_rows, groups, 2, 2).transpose(0, 2, 1, 3).reshape(count_rows, 4 * groups)

def item_nll(weights, token_rows, durations_row, pairs_in, act_center, act_scale):
    embedding, w_qkv, rel_key, rel_value, w_out, attn_gain, attn_shift, w_ff1, w_ff2, ffn_gain, ffn_shift, w_prior, w_mix, w_start, w_in, w_res, w_skip_last, w_end = weights
    text_mask = (durations_row > 0).astype(jnp.float32)[:, None]
    end_pos = jnp.cumsum(durations_row)
    starts = end_pos - durations_row
    positions = lax.iota(jnp.int32, FRAMES)
    pair_mask = (lax.iota(jnp.int32, FRAMES // 2) < end_pos[-1] // 2).astype(jnp.float32)[:, None]
    embedded = jnp.take(embedding, token_rows, axis=0) * math.sqrt(D) * text_mask
    project = low(low_back(matmul(low(embedded), w_qkv)))
    query_rows = project[:, :D].reshape(TEXT, HEADS, HEAD)
    key_rows = project[:, D:2 * D].reshape(TEXT, HEADS, HEAD)
    value_rows = project[:, 2 * D:].reshape(TEXT, HEADS, HEAD)
    band_mask = band_table(TEXT)
    direct = jnp.einsum('ihd,jhd->hij', query_rows, key_rows, precision=lax.Precision.HIGHEST)
    near_terms = jnp.einsum('ihd,rd->hir', query_rows, rel_key, precision=lax.Precision.HIGHEST)
    near_full = jnp.einsum('hir,rij->hij', near_terms, band_mask, precision=lax.Precision.HIGHEST)
    key_bias = jnp.where(text_mask[:, 0] > 0, 0.0, -10000.0)
    scores = low_back(direct + near_full) / math.sqrt(HEAD) + key_bias[None, None, :]
    attention = low(jax.nn.softmax(scores, axis=-1))
    banded = jnp.einsum('hij,rij->hir', attention, band_mask, precision=lax.Precision.HIGHEST)
    attended = jnp.einsum('hij,jhd->ihd', attention, value_rows, precision=lax.Precision.HIGHEST)
    attended = attended + jnp.einsum('hir,rd->ihd', banded, rel_value, precision=lax.Precision.HIGHEST)
    attended = low(low_back(attended.reshape(TEXT, D)))
    mixed_in = embedded + low_back(matmul(attended, w_out))
    normed = layer_norm(mixed_in, attn_gain, attn_shift)
    filtered = low_back(matmul(unfold(low(normed * text_mask), KSIZE), w_ff1))
    activated = low(jax.nn.gelu(filtered) * text_mask)
    second_out = low_back(matmul(unfold(activated, KSIZE), w_ff2)) * text_mask
    encoded = layer_norm(normed + second_out, ffn_gain, ffn_shift) * text_mask
    prior_rows = low_back(matmul(low(encoded), w_prior)) * text_mask
    align_table = ((positions[:, None] >= starts[None, :]) & (positions[:, None] < end_pos[None, :])).astype(jnp.float32)
    expanded = matmul(align_table, prior_rows)
    mean_rows = pair_up(expanded[:, :MEL])
    log_scales = pair_up(expanded[:, MEL:])
    normalized = (pairs_in - act_center) * act_scale * pair_mask
    turned = from_groups(jnp.einsum('fgj,ij->fgi', to_groups(normalized), w_mix, precision=lax.Precision.HIGHEST))
    passive = turned[:, :MEL]
    active = turned[:, MEL:]
    hidden = low_back(matmul(low(passive), w_start)) * pair_mask
    skipped = jnp.zeros((FRAMES // 2, HID), jnp.float32)
    for block_index in range(WLAYERS):
        gated_out = gate_units(low_back(matmul(unfold(low(hidden), WKER), w_in[block_index])))
        if block_index < WLAYERS - 1:
            both_parts = low_back(matmul(low(gated_out), w_res[block_index]))
            hidden = (hidden + both_parts[:, :HID]) * pair_mask
            skipped = skipped + both_parts[:, HID:]
        else:
            skipped = skipped + low_back(matmul(low(gated_out), w_skip_last))
    coupled = low_back(matmul(low(skipped * pair_mask), w_end)) * pair_mask
    shift_part = coupled[:, :MEL]
    log_part = coupled[:, MEL:]
    moved_half = (shift_part + jnp.exp(log_part) * active) * pair_mask
    latent = jnp.concatenate([passive, moved_half], axis=1)
    latent_gap = latent - mean_rows
    terms = pair_mask * (log_scales + 0.5 * jnp.exp(-2.0 * log_scales) * latent_gap * latent_gap)
    return jnp.sum(terms) - jnp.sum(log_part * pair_mask)

def block_sum(weights, token_block, duration_block, frame_block, act_center, act_scale):
    per_item = jax.vmap(item_nll, in_axes=(None, 0, 0, 0, None, None))
    return jnp.sum(per_item(weights, token_block, duration_block, frame_block, act_center, act_scale))

def forward(weights, mel_frames, token_ids, durations):
    end_pos = jnp.cumsum(durations, axis=1)
    pair_lengths = end_pos[:, -1] // 2
    pair_mask = (lax.iota(jnp.int32, FRAMES // 2)[None, :] < pair_lengths[:, None]).astype(jnp.float32)[:, :, None]
    pairs_total_count = jnp.sum(pair_lengths).astype(jnp.float32)
    squeezed = mel_frames.reshape(ITEMS, FRAMES // 2, 2, MEL).transpose(0, 1, 3, 2).reshape(ITEMS, FRAMES // 2, 2 * MEL)
    first_sums = lax.optimization_barrier(jnp.sum(squeezed * pair_mask, axis=(0, 1)))
    square_sums = lax.optimization_barrier(jnp.sum(squeezed * squeezed * pair_mask, axis=(0, 1)))
    act_center = first_sums / pairs_total_count
    variance = square_sums / pairs_total_count - act_center * act_center
    log_act = -0.5 * jnp.log(variance + 1e-06)
    act_scale = jnp.exp(log_act)
    group_size = math.gcd(ITEMS, max(1, 4096 // FRAMES))
    blocks = ITEMS // group_size
    checked = jax.checkpoint(block_sum)

    def per_block(running, block_data):
        token_block, duration_block, frame_block = block_data
        return (running + checked(weights, token_block, duration_block, frame_block, act_center, act_scale), None)
    block_data = (token_ids.reshape(blocks, group_size, TEXT), durations.reshape(blocks, group_size, TEXT), squeezed.reshape(blocks, group_size, FRAMES // 2, 2 * MEL))
    neg_loglik, _ = lax.scan(per_block, jnp.zeros((), jnp.float32), block_data)
    log_det = jnp.log(jnp.linalg.det(weights[12]))
    neg_loglik = neg_loglik - pairs_total_count * jnp.sum(log_act) - pairs_total_count * (MEL // 2) * log_det
    return neg_loglik / (2 * MEL * pairs_total_count) + 0.5 * math.log(2.0 * math.pi)

def reference(token_ids, durations, mel_frames, embedding, w_qkv, rel_key, rel_value, w_out, attn_gain, attn_shift, w_ff1, w_ff2, ffn_gain, ffn_shift, w_prior, w_mix, w_start, w_in, w_res, w_skip_last, w_end):
    weights = tuple((array_in.astype(jnp.float32) for array_in in (embedding, w_qkv, rel_key, rel_value, w_out, attn_gain, attn_shift, w_ff1, w_ff2, ffn_gain, ffn_shift, w_prior, w_mix, w_start, w_in, w_res, w_skip_last, w_end)))
    pairs_total_count = jnp.sum(lax.optimization_barrier(jnp.sum(durations, axis=1)) // 2).astype(jnp.float32)
    loss_value, pullback = jax.vjp(lambda frames, params: forward(params, frames, token_ids, durations), mel_frames, weights)
    frame_grad, gradients = pullback(jnp.ones((), jnp.float32))
    return (loss_value, frame_grad * (2 * MEL * pairs_total_count), gradients[0], gradients[1], gradients[2], gradients[3], gradients[4], gradients[5], gradients[6], gradients[7], gradients[8], gradients[9], gradients[10], gradients[11], gradients[12], gradients[13], gradients[14], gradients[15], gradients[16], gradients[17])
```

```python
import functools
import math

import jax
import jax.numpy as jnp
from jax import lax
from jax.experimental import pallas as pl
from jax.experimental.pallas import tpu as pltpu
from jax.sharding import PartitionSpec as P

D = 192
HEADS = 2
HEAD = 96
LANES = 128
FILTER = 768
MEL = 80
HID = 192
VOCAB = 148
KSIZE = 3
WKER = 5
WLAYERS = 4
WINDOW = 4
PERIOD = 16

F32 = jnp.float32
BF16 = jnp.bfloat16
HIGH = lax.Precision.HIGHEST
VMEM_BYTES = 58 * 1024 * 1024


def contract(first_op, second_op, dims, precision=None):
    return lax.dot_general(
        first_op, second_op, (dims, ((), ())), preferred_element_type=F32, precision=precision
    )


def dot_nn(first_op, second_op, precision=None):
    return contract(first_op, second_op, ((1,), (0,)), precision)


def dot_nt(first_op, second_op, precision=None):
    return contract(first_op, second_op, ((1,), (1,)), precision)


def dot_tn(first_op, second_op, precision=None):
    return contract(first_op, second_op, ((0,), (0,)), precision)


def halves(values):
    high = values.astype(BF16)
    low = (values - high.astype(F32)).astype(BF16)
    return high, low


def iota(shape, axis):
    return lax.broadcasted_iota(jnp.int32, shape, axis)


def rows_of(length):
    return iota((length, 1), 0)


def full_spec(array):
    rank = len(array.shape)
    return pl.BlockSpec(array.shape, lambda *_: (0,) * rank)


def item_spec(array):
    rank = len(array.shape)
    return pl.BlockSpec((1,) + array.shape[1:], lambda b: (b,) + (0,) * (rank - 1))


def layer_spec(array, layer):
    rank = len(array.shape)
    return pl.BlockSpec((1, 1) + array.shape[2:], lambda b: (layer, b) + (0,) * (rank - 2))


def weight_spec(array, layer):
    rank = len(array.shape)
    return pl.BlockSpec((1,) + array.shape[1:], lambda b: (layer,) + (0,) * (rank - 1))


def shape_of(shape, dtype=F32):
    return jax.ShapeDtypeStruct(shape, dtype)


def run(body, grid, ins, in_specs, outs, out_specs, scratch=(), flops=0, name=None):
    return pl.pallas_call(
        body,
        grid=grid,
        in_specs=in_specs,
        out_specs=out_specs,
        out_shape=outs,
        scratch_shapes=list(scratch),
        compiler_params=pltpu.CompilerParams(vmem_limit_bytes=VMEM_BYTES),
        cost_estimate=pl.CostEstimate(flops=flops, bytes_accessed=1 << 20, transcendentals=0),
        name=name,
    )(*ins)


def pair_rows(durations_row):
    return jnp.sum(durations_row, axis=1, keepdims=True) >> 1


def stats_body(mel_ref, dur_ref, out_ref):
    items, frames, _ = mel_ref.shape
    pairs = frames // 2
    pad = jnp.zeros((1, LANES - MEL), F32)
    count = jnp.zeros((1, 1), F32)
    sums = [jnp.zeros((1, MEL), F32) for _ in range(4)]
    for item in range(items):
        pair_count = pair_rows(dur_ref[item : item + 1, :])
        count = count + pair_count.astype(F32)
        inside = rows_of(pairs) < pair_count
        for side in range(2):
            values = jnp.where(inside, mel_ref[item, pl.ds(side, pairs, stride=2), :], 0.0)
            sums[side] = sums[side] + jnp.sum(values, axis=0, keepdims=True)
            sums[2 + side] = sums[2 + side] + jnp.sum(values * values, axis=0, keepdims=True)
    out_ref[...] = jnp.zeros_like(out_ref)
    for place in range(4):
        out_ref[place : place + 1, :] = jnp.concatenate([sums[place], pad], axis=1)
    out_ref[4:5, :] = jnp.broadcast_to(count, (1, LANES))


def read_stats(stats):
    total = stats[4:5, 0:1]
    sums = jnp.concatenate([stats[0:1], stats[1:2]], axis=1)
    squares = jnp.concatenate([stats[2:3], stats[3:4]], axis=1)
    center = sums / total
    variance = squares / total - center * center
    log_act = -0.5 * jnp.log(variance + 1e-06)
    return total, center, variance, log_act, jnp.exp(log_act)


def mix_places():
    row = rows_of(2 * LANES)
    col = iota((1, 2 * LANES), 1)
    row_lane = row & (LANES - 1)
    col_lane = col & (LANES - 1)
    upper = (row_lane >= MEL // 2).astype(jnp.int32)
    row_group = row_lane - upper * (MEL // 2)
    row_member = 2 * upper + (row >> 7)
    col_group = col_lane >> 1
    col_member = 2 * (col >> 7) + (col_lane & 1)
    match = (row_group == col_group) & (row_lane < MEL) & (col_lane < MEL)
    return row_member, col_member, match


def weights_body(
    mix_ref,
    qkv_ref,
    relk_ref,
    relv_ref,
    out_ref,
    prior_ref,
    start_ref,
    end_ref,
    mixm_ref,
    small_ref,
    qkv_pad_ref,
    relk_pad_ref,
    relv_pad_ref,
    out_pad_ref,
    wide_ref,
    prior_pad_ref,
    start_pad_ref,
    end_pad_ref,
):
    row_member, col_member, match = mix_places()
    table = jnp.zeros((2 * LANES, 2 * LANES), F32)
    for i in range(4):
        column = jnp.zeros((2 * LANES, 1), F32)
        for j in range(4):
            column = jnp.where(row_member == j, mix_ref[i, j], column)
        table = jnp.where(col_member == i, column, table)
    mixm_ref[...] = jnp.where(match, table, 0.0)

    ri = iota((8, LANES), 0)
    ci = iota((8, LANES), 1)
    joined = jnp.where((ci == ri + 4) & (ri < 4), 1.0, 0.0).astype(F32)
    for i in range(4):
        for j in range(4):
            joined = jnp.where((ri == i) & (ci == j), mix_ref[i, j], joined)
    determinant = jnp.ones((1, 1), F32)
    for column in range(4):
        pivot = joined[column : column + 1, column : column + 1]
        determinant = determinant * pivot
        row_now = joined[column : column + 1, :] / pivot
        joined = joined - joined[:, column : column + 1] * row_now
        joined = jnp.where(ri == column, row_now, joined)
    small_ref[...] = jnp.where(ri == 4, determinant, joined)

    def select(source, target_shape_rows, wanted):
        return jnp.where(rows_of(target_shape_rows) == wanted, 1.0, 0.0).astype(BF16)

    place = iota((1, 6 * LANES), 1)
    lane = place & (LANES - 1)
    wanted = jnp.where(lane < HEAD, (place >> 7) * HEAD + lane, -1)
    qkv_pad_ref[...] = dot_nn(qkv_ref[...], select(None, 3 * D, wanted)).astype(BF16)

    place = iota((1, 2 * LANES), 1)
    lane = place & (LANES - 1)
    wanted = jnp.where(lane < HEAD, (place >> 7) * HEAD + lane, -1)
    out_pad_ref[...] = dot_tn(select(None, D, wanted), out_ref[...]).astype(BF16)

    wanted = iota((1, LANES), 1) & (PERIOD - 1)
    repeat = select(None, 2 * WINDOW + 1, wanted)
    pad = jnp.zeros((LANES, LANES - HEAD), F32)
    relk_pad_ref[...] = jnp.concatenate([dot_tn(repeat, relk_ref[...]), pad], axis=1).astype(BF16)
    relv_pad_ref[...] = jnp.concatenate([dot_tn(repeat, relv_ref[...]), pad], axis=1).astype(BF16)

    place = iota((1, 8 * LANES), 1)
    lane = place & (LANES - 1)
    group = (place >> 7) & 3
    fits = (lane < MEL) & ((lane & 1) == (place >> 9))
    wanted = jnp.where(fits, (group >> 1) * MEL + (group & 1) * (MEL // 2) + (lane >> 1), -1)
    wide = select(None, 2 * MEL, wanted)
    wide_ref[...] = wide
    prior_pad_ref[...] = dot_nn(prior_ref[...], wide).astype(BF16)

    wanted = iota((1, LANES), 1)
    start_pad_ref[...] = dot_tn(select(None, MEL, wanted), start_ref[...]).astype(BF16)
    place = iota((1, 2 * LANES), 1)
    lane = place & (LANES - 1)
    wanted = jnp.where(lane < MEL, (place >> 7) * MEL + lane, -1)
    end_pad_ref[...] = dot_nn(end_ref[...], select(None, 2 * MEL, wanted)).astype(BF16)


def text_rows(dur_ref):
    item = pl.program_id(0)
    return dur_ref[pl.ds(item, 1), :]


def text_inside(durations_row, length):
    tokens = jnp.sum((durations_row > 0).astype(jnp.int32), axis=1, keepdims=True)
    return rows_of(length) < tokens


def norm_parts(inputs):
    centered = inputs - jnp.mean(inputs, axis=1, keepdims=True)
    spread = jnp.mean(centered * centered, axis=1, keepdims=True)
    inverse = lax.rsqrt(spread + 1e-05)
    return centered * inverse, inverse


def norm_back(inputs, gain, gradient):
    unit, inverse = norm_parts(inputs)
    gain_grad = jnp.sum(gradient * unit, axis=0, keepdims=True)
    shift_grad = jnp.sum(gradient, axis=0, keepdims=True)
    scaled = gradient * gain
    mean_one = jnp.mean(scaled, axis=1, keepdims=True)
    mean_two = jnp.mean(scaled * unit, axis=1, keepdims=True)
    return inverse * (scaled - mean_one - unit * mean_two), gain_grad, shift_grad


def band_of(length):
    offset = iota((length, length), 1) - iota((length, length), 0)
    return (offset <= WINDOW) & (offset >= -WINDOW)


def turn_rows(values, left):
    length = values.shape[0]
    step = rows_of(length) & (PERIOD - 1)
    first = WINDOW if left else LANES - WINDOW
    values = pltpu.roll(values, first, 1)
    for bit in (1, 2, 4, 8):
        moved = pltpu.roll(values, (LANES - bit) if left else bit, 1)
        values = jnp.where((step & bit) != 0, moved, values)
    return values


def band_gather(weights_low, band, folding):
    kept = jnp.where(band, weights_low, jnp.zeros_like(weights_low))
    return turn_rows(dot_nn(kept, folding), True).astype(BF16)


def band_spread(near, band):
    turned = turn_rows(near, False)
    count = band.shape[1] // LANES
    return jnp.where(band, jnp.concatenate([turned] * count, axis=1), 0.0)


def folding_of(length):
    same = (iota((length, LANES), 0) & (PERIOD - 1)) == (iota((length, LANES), 1) & (PERIOD - 1))
    return jnp.where(same, 1.0, 0.0).astype(BF16)


def one_turn(rel_pad):
    return jnp.where(rows_of(LANES) < PERIOD, rel_pad, jnp.zeros_like(rel_pad))


def attention_body(
    tok_ref,
    dur_ref,
    emb_ref,
    qkv_ref,
    relk_ref,
    relv_ref,
    out_ref,
    gain_ref,
    shift_ref,
    emb_low_ref,
    proj_ref,
    att_ref,
    banded_ref,
    attend_ref,
    mixed_ref,
    normed_ref,
):
    item = pl.program_id(0)
    tokens = tok_ref[pl.ds(item, 1), :]
    durations = text_rows(dur_ref)
    length = tokens.shape[1]
    inside = text_inside(durations, length)
    hot = jnp.where(iota((VOCAB, length), 0) == tokens, 1.0, 0.0).astype(BF16)
    embedded = jnp.where(inside, dot_tn(hot, emb_ref[...]) * math.sqrt(D), 0.0)
    emb_low = embedded.astype(BF16)
    emb_low_ref[0] = emb_low
    proj = dot_nn(emb_low, qkv_ref[...]).astype(BF16)
    proj_ref[0] = proj
    key_bias = jnp.where(durations > 0, 0.0, -10000.0)
    band = band_of(length)
    folding = folding_of(length)
    relv = one_turn(relv_ref[...])
    parts = []
    for head in range(HEADS):
        query = proj[:, head * LANES : (head + 1) * LANES]
        key = proj[:, (HEADS + head) * LANES : (HEADS + head + 1) * LANES]
        value = proj[:, (2 * HEADS + head) * LANES : (2 * HEADS + head + 1) * LANES]
        near = band_spread(dot_nt(query, relk_ref[...]), band)
        scores = (dot_nt(query, key) + near) / math.sqrt(HEAD) + key_bias
        raised = jnp.exp(scores - jnp.max(scores, axis=1, keepdims=True))
        attention = raised / jnp.sum(raised, axis=1, keepdims=True)
        att_ref[0, head] = attention
        low = attention.astype(BF16)
        banded = band_gather(low, band, folding)
        banded_ref[0, head] = banded
        parts.append(dot_nn(low, value) + dot_nn(banded, relv))
    attend = jnp.concatenate(parts, axis=1).astype(BF16)
    attend_ref[0] = attend
    mixed = embedded + dot_nn(attend, out_ref[...])
    mixed_ref[0] = mixed
    unit, _ = norm_parts(mixed)
    normed_ref[0] = unit * gain_ref[...] + shift_ref[...]


def shifted(values, offset):
    if offset == 0:
        return values
    length = values.shape[0]
    moved = pltpu.roll(values, (-offset) % length, 0)
    place = rows_of(length)
    keep = (place < length - offset) if offset > 0 else (place >= -offset)
    return jnp.where(keep, moved, 0.0)


def unfold(values, kernel, reverse=False):
    half = kernel // 2
    steps = [step - half for step in range(kernel)]
    if reverse:
        steps = [-step for step in steps]
    return jnp.concatenate([shifted(values, step).astype(BF16) for step in steps], axis=1)


GELU_A = math.sqrt(2.0 / math.pi)
GELU_B = 0.044715


def gelu_tanh(values):
    return jnp.tanh(GELU_A * (values + GELU_B * values * values * values))


def feed_body(
    dur_ref,
    normed_ref,
    ff1_ref,
    ff2_ref,
    gain_ref,
    shift_ref,
    prior_ref,
    filt_ref,
    activ_ref,
    summed_ref,
    enc_ref,
    high_ref,
    low_ref,
):
    durations = text_rows(dur_ref)
    normed = normed_ref[0]
    length = normed.shape[0]
    inside = text_inside(durations, length)
    filtered = dot_nn(unfold(jnp.where(inside, normed, 0.0), KSIZE), ff1_ref[...])
    filt_ref[0] = filtered
    activ = jnp.where(inside, 0.5 * filtered * (1.0 + gelu_tanh(filtered)), 0.0)
    activ_ref[0] = activ.astype(BF16)
    summed = normed + jnp.where(inside, dot_nn(unfold(activ, KSIZE), ff2_ref[...]), 0.0)
    summed_ref[0] = summed
    unit, _ = norm_parts(summed)
    encoded = jnp.where(inside, unit * gain_ref[...] + shift_ref[...], 0.0).astype(BF16)
    enc_ref[0] = encoded
    prior = dot_nn(encoded, prior_ref[...])
    high, low = halves(prior)
    wide = prior.shape[1] // 2
    high_ref[0, :length] = high[:, :wide]
    high_ref[0, length:] = high[:, wide:]
    low_ref[0, :length] = low[:, :wide]
    low_ref[0, length:] = low[:, wide:]


def accumulate(ref, values, first):
    @pl.when(first)
    def _():
        ref[...] = values

    @pl.when(jnp.logical_not(first))
    def _():
        ref[...] = ref[...] + values


def align_of(durations_row, pairs):
    length = durations_row.shape[1]
    upper = jnp.where(iota((length, length), 0) <= iota((length, length), 1), 1.0, 0.0).astype(F32)
    wide = jnp.broadcast_to(durations_row.astype(F32), (8, length))
    ends = dot_nn(wide, upper, HIGH)[0:1].astype(jnp.int32)
    starts = ends - durations_row
    frame = 2 * rows_of(pairs)
    even = (frame >= starts) & (frame < ends)
    odd = (frame + 1 >= starts) & (frame + 1 < ends)
    both = jnp.concatenate([jnp.where(even, 1.0, 0.0), jnp.where(odd, 1.0, 0.0)], axis=1)
    return both.astype(BF16)


def feed_back_body(
    dur_ref,
    flow_ref,
    wide_ref,
    enc_ref,
    summed_ref,
    filt_ref,
    activ_ref,
    normed_ref,
    ff1_ref,
    ff2_ref,
    gain_ref,
    prior_ref,
    ngrad_ref,
    prior_out_ref,
    ff1_out_ref,
    ff2_out_ref,
    gain_out_ref,
    shift_out_ref,
):
    first = pl.program_id(0) == 0
    durations = text_rows(dur_ref)
    length = durations.shape[1]
    inside = text_inside(durations, length)
    flow = flow_ref[0]
    align = align_of(durations, flow.shape[0])
    flow_high, flow_low = halves(flow)
    spread = dot_tn(align, flow_high) + dot_tn(align, flow_low)
    half = wide_ref.shape[1] // 2
    grad = jnp.zeros((length, 2 * MEL), F32)
    for side in range(2):
        part_high, part_low = halves(spread[side * length : (side + 1) * length])
        chosen = wide_ref[:, side * half : (side + 1) * half]
        grad = grad + dot_nt(part_high, chosen) + dot_nt(part_low, chosen)
    prior_low = jnp.where(inside, grad, 0.0).astype(BF16)
    accumulate(prior_out_ref, dot_tn(enc_ref[0], prior_low), first)
    enc_grad = jnp.where(inside, dot_nt(prior_low, prior_ref[...]), 0.0)
    summed_grad, gain_grad, shift_grad = norm_back(summed_ref[0], gain_ref[...], enc_grad)
    accumulate(gain_out_ref, gain_grad, first)
    accumulate(shift_out_ref, shift_grad, first)
    second = jnp.where(inside, summed_grad, 0.0)
    activ = activ_ref[0]
    activ_grad = jnp.zeros((length, FILTER), F32)
    for step in range(KSIZE):
        moved = shifted(second, KSIZE // 2 - step).astype(BF16)
        rows = slice(step * FILTER, (step + 1) * FILTER)
        activ_grad = activ_grad + dot_nt(moved, ff2_ref[rows, :])
        accumulate(ff2_out_ref.at[rows, :], dot_tn(activ, moved), first)
    filtered = filt_ref[0]
    tanh = gelu_tanh(filtered)
    slope = 0.5 * (1.0 + tanh) + 0.5 * filtered * (1.0 - tanh * tanh) * GELU_A * (
        1.0 + 3.0 * GELU_B * filtered * filtered
    )
    first_grad = jnp.where(inside, activ_grad * slope, 0.0)
    normed_low = jnp.where(inside, normed_ref[0], 0.0).astype(BF16)
    back = jnp.zeros((length, D), F32)
    for step in range(KSIZE):
        moved = shifted(first_grad, KSIZE // 2 - step).astype(BF16)
        rows = slice(step * D, (step + 1) * D)
        back = back + dot_nt(moved, ff1_ref[rows, :])
        accumulate(ff1_out_ref.at[rows, :], dot_tn(normed_low, moved), first)
    ngrad_ref[0] = summed_grad + jnp.where(inside, back, 0.0)


def attention_back_body(
    tok_ref,
    dur_ref,
    ngrad_ref,
    mixed_ref,
    attend_ref,
    att_ref,
    banded_ref,
    proj_ref,
    emb_low_ref,
    qkv_ref,
    relk_ref,
    relv_ref,
    out_ref,
    gain_ref,
    table_ref,
    qkv_out_ref,
    relk_out_ref,
    relv_out_ref,
    out_out_ref,
    gain_out_ref,
    shift_out_ref,
    qkv_acc,
    out_acc,
    relk_acc,
    relv_acc,
):
    item = pl.program_id(0)
    first = item == 0
    last = item == pl.num_programs(0) - 1
    tokens = tok_ref[pl.ds(item, 1), :]
    durations = text_rows(dur_ref)
    length = tokens.shape[1]
    inside = text_inside(durations, length)
    mixed_grad, gain_grad, shift_grad = norm_back(mixed_ref[0], gain_ref[...], ngrad_ref[0])
    accumulate(gain_out_ref, gain_grad, first)
    accumulate(shift_out_ref, shift_grad, first)
    out_low = mixed_grad.astype(BF16)
    accumulate(out_acc, dot_tn(attend_ref[0], out_low), first)
    weight = dot_nt(out_low, out_ref[...]).astype(BF16)
    band = band_of(length)
    folding = folding_of(length)
    relk = one_turn(relk_ref[...])
    proj = proj_ref[0]
    queries, keys, values = [], [], []
    relk_sum = jnp.zeros((LANES, LANES), F32)
    relv_sum = jnp.zeros((LANES, LANES), F32)
    for head in range(HEADS):
        query = proj[:, head * LANES : (head + 1) * LANES]
        key = proj[:, (HEADS + head) * LANES : (HEADS + head + 1) * LANES]
        value = proj[:, (2 * HEADS + head) * LANES : (2 * HEADS + head + 1) * LANES]
        mine = weight[:, head * LANES : (head + 1) * LANES]
        near = band_spread(dot_nt(mine, relv_ref[...]), band)
        grad = dot_nt(mine, value) + near
        attention = att_ref[0, head]
        values.append(dot_tn(attention.astype(BF16), mine))
        relv_sum = relv_sum + dot_tn(banded_ref[0, head], mine)
        score = attention * (grad - jnp.sum(attention * grad, axis=1, keepdims=True))
        score_low = (score / math.sqrt(HEAD)).astype(BF16)
        band_grad = band_gather(score_low, band, folding)
        queries.append(dot_nn(score_low, key) + dot_nn(band_grad, relk))
        keys.append(dot_tn(score_low, query))
        relk_sum = relk_sum + dot_tn(band_grad, query)
    accumulate(relk_acc, relk_sum, first)
    accumulate(relv_acc, relv_sum, first)
    proj_low = jnp.concatenate(queries + keys + values, axis=1).astype(BF16)
    accumulate(qkv_acc, dot_tn(emb_low_ref[0], proj_low), first)
    back = mixed_grad + dot_nt(proj_low, qkv_ref[...])
    embed_grad = jnp.where(inside, back, 0.0) * math.sqrt(D)
    hot = jnp.where(iota((VOCAB, length), 0) == tokens, 1.0, 0.0).astype(BF16)
    high, low = halves(embed_grad)
    accumulate(table_ref, dot_nn(hot, high) + dot_nn(hot, low), first)

    @pl.when(last)
    def _():
        for part in range(3 * HEADS):
            qkv_out_ref[:, part * HEAD : (part + 1) * HEAD] = qkv_acc[
                :, part * LANES : part * LANES + HEAD
            ]
        for head in range(HEADS):
            out_out_ref[head * HEAD : (head + 1) * HEAD, :] = out_acc[
                head * LANES : head * LANES + HEAD, :
            ]
        relk_out_ref[...] = relk_acc[: 2 * WINDOW + 1, :HEAD]
        relv_out_ref[...] = relv_acc[: 2 * WINDOW + 1, :HEAD]


def split_pairs(mel_ref, pairs):
    pad = jnp.zeros((pairs, LANES - MEL), F32)
    even = mel_ref[0, pl.ds(0, pairs, stride=2), :]
    odd = mel_ref[0, pl.ds(1, pairs, stride=2), :]
    return jnp.concatenate([even, pad, odd, pad], axis=1)


def gates_of(pre):
    return jnp.tanh(pre[:, :HID]), 1.0 / (1.0 + jnp.exp(-pre[:, HID:]))


def flow_body(
    mel_ref,
    dur_ref,
    high_ref,
    low_ref,
    stats_ref,
    mixm_ref,
    start_ref,
    win_ref,
    wres_ref,
    wlast_ref,
    wend_ref,
    normal_ref,
    passive_ref,
    hidden_ref,
    pre_ref,
    skip_ref,
    active_ref,
    lgrad_ref,
    flow_ref,
    nll_ref,
    end_out_ref,
    end_acc,
):
    first = pl.program_id(0) == 0
    last = pl.program_id(0) == pl.num_programs(0) - 1
    pairs = mel_ref.shape[1] // 2
    durations = text_rows(dur_ref)
    inside = rows_of(pairs) < pair_rows(durations)
    total, center, _, _, scale = read_stats(stats_ref[...])
    unit = 1.0 / (2 * MEL * total)
    normalized = jnp.where(inside, (split_pairs(mel_ref, pairs) - center) * scale, 0.0)
    normal_ref[0] = normalized
    turned = dot_nn(normalized, mixm_ref[...], HIGH)
    passive = turned[:, :LANES]
    active = turned[:, LANES:]
    passive_low = passive.astype(BF16)
    passive_ref[0] = passive_low
    hidden = jnp.where(inside, dot_nn(passive_low, start_ref[...]), 0.0)
    skipped = jnp.zeros((pairs, HID), F32)
    for layer in range(WLAYERS):
        hidden_ref[layer, 0] = hidden.astype(BF16)
        pre = dot_nn(unfold(hidden, WKER), win_ref[layer])
        pre_ref[layer, 0] = pre
        tanh, gate = gates_of(pre)
        gated = (tanh * gate).astype(BF16)
        if layer < WLAYERS - 1:
            both = dot_nn(gated, wres_ref[layer])
            hidden = jnp.where(inside, hidden + both[:, :HID], 0.0)
            skipped = skipped + both[:, HID:]
        else:
            skipped = skipped + dot_nn(gated, wlast_ref[...])
    output_low = jnp.where(inside, skipped, 0.0).astype(BF16)
    coupled = jnp.where(inside, dot_nn(output_low, wend_ref[...]), 0.0)
    shift_part = coupled[:, :LANES]
    log_part = coupled[:, LANES:]
    growth = jnp.exp(log_part)
    moved = jnp.where(inside, shift_part + growth * active, 0.0)
    align = align_of(durations, pairs)
    prior = dot_nn(align, high_ref[0]) + dot_nn(align, low_ref[0])
    latent = jnp.concatenate([passive, moved], axis=1)
    gap = latent - prior[:, : 2 * LANES]
    log_scales = prior[:, 2 * LANES :]
    inverse = jnp.exp(-2.0 * log_scales)
    scaled = inverse * gap
    square = scaled * gap
    terms = jnp.where(inside, log_scales + 0.5 * square, 0.0)
    sums = jnp.sum(terms, axis=0, keepdims=True)
    sums = sums[:, :LANES] + sums[:, LANES:] - jnp.sum(log_part, axis=0, keepdims=True)
    accumulate(nll_ref, jnp.broadcast_to(sums, (8, LANES)), first)
    latent_grad = jnp.where(inside, unit * scaled, 0.0)
    scale_grad = jnp.where(inside, unit * (1.0 - square), 0.0)
    flow_ref[0] = jnp.concatenate([-latent_grad, scale_grad], axis=1)
    lgrad_ref[0] = latent_grad[:, :LANES]
    moved_grad = latent_grad[:, LANES:]
    active_grad = moved_grad * growth
    active_ref[0] = active_grad
    log_grad = jnp.where(inside, active_grad * active - unit, 0.0)
    coupled_low = jnp.concatenate([moved_grad, log_grad], axis=1).astype(BF16)
    accumulate(end_acc, dot_tn(output_low, coupled_low), first)
    skip_grad = jnp.where(inside, dot_nt(coupled_low, wend_ref[...]), 0.0)
    skip_ref[0] = skip_grad.astype(BF16)

    @pl.when(last)
    def _():
        end_out_ref[:, :MEL] = end_acc[:, :MEL]
        end_out_ref[:, MEL:] = end_acc[:, LANES : LANES + MEL]


def layer_body(layer, dur_ref, *refs):
    top = layer == WLAYERS - 1
    if top:
        skip_ref, pre_ref, hidden_ref, win_ref, wres_ref, out_grad_ref, win_out, wres_out, wide = refs
    else:
        (
            skip_ref,
            pre_ref,
            hidden_ref,
            win_ref,
            wres_ref,
            hgrad_ref,
            out_grad_ref,
            win_out,
            wres_out,
            wide,
        ) = refs
    first = pl.program_id(0) == 0

    @pl.when(first)
    def _():
        for step in range(WKER):
            wide[:, step * 2 * HID : (step + 1) * 2 * HID] = win_ref[
                0, step * HID : (step + 1) * HID, :
            ]

    pairs = pre_ref.shape[2]
    inside = rows_of(pairs) < pair_rows(text_rows(dur_ref))
    tanh, gate = gates_of(pre_ref[0, 0])
    gated = (tanh * gate).astype(BF16)
    skip_low = skip_ref[0]
    if top:
        gated_grad = dot_nt(skip_low, wres_ref[...])
        accumulate(wres_out, dot_tn(gated, skip_low), first)
        kept = None
    else:
        kept = jnp.where(inside, hgrad_ref[0], 0.0)
        part = jnp.concatenate([kept, skip_low.astype(F32)], axis=1).astype(BF16)
        gated_grad = dot_nt(part, wres_ref[0])
        accumulate(wres_out, dot_tn(gated, part), first)
    tanh_grad = gated_grad * gate * (1.0 - tanh * tanh)
    gate_grad = gated_grad * tanh * gate * (1.0 - gate)
    pre_grad = jnp.concatenate([tanh_grad, gate_grad], axis=1)
    spread = unfold(pre_grad, WKER, reverse=True)
    sums = dot_tn(hidden_ref[0, 0], spread)
    for step in range(WKER):
        accumulate(
            win_out.at[step * HID : (step + 1) * HID, :],
            sums[:, step * 2 * HID : (step + 1) * 2 * HID],
            first,
        )
    back = dot_nt(spread, wide[...])
    out_grad_ref[0] = back if top else kept + back


def mix_body(
    dur_ref,
    hgrad_ref,
    passive_ref,
    lgrad_ref,
    active_ref,
    normal_ref,
    start_ref,
    mixm_ref,
    ngrad_ref,
    start_out_ref,
    sums_ref,
    mix_out_ref,
    start_acc,
    mix_acc,
):
    first = pl.program_id(0) == 0
    last = pl.program_id(0) == pl.num_programs(0) - 1
    pairs = hgrad_ref.shape[1]
    inside = rows_of(pairs) < pair_rows(text_rows(dur_ref))
    start_low = jnp.where(inside, hgrad_ref[0], 0.0).astype(BF16)
    accumulate(start_acc, dot_tn(passive_ref[0], start_low), first)
    passive_grad = lgrad_ref[0] + dot_nt(start_low, start_ref[...])
    turned_grad = jnp.concatenate([passive_grad, active_ref[0]], axis=1)
    normalized = normal_ref[0]
    accumulate(mix_acc, dot_tn(normalized, turned_grad, HIGH), first)
    normal_grad = jnp.where(inside, dot_nt(turned_grad, mixm_ref[...], HIGH), 0.0)
    ngrad_ref[0] = normal_grad
    one = jnp.sum(normal_grad, axis=0, keepdims=True)
    two = jnp.sum(normal_grad * normalized, axis=0, keepdims=True)
    rows = [one[:, :LANES], one[:, LANES:], two[:, :LANES], two[:, LANES:]]
    rows.append(jnp.zeros((4, LANES), F32))
    accumulate(sums_ref, jnp.concatenate(rows, axis=0), first)

    @pl.when(last)
    def _():
        start_out_ref[...] = start_acc[:MEL, :]
        row_member, col_member, match = mix_places()
        kept = jnp.where(match, mix_acc[...], 0.0)
        ri = iota((8, LANES), 0)
        ci = iota((8, LANES), 1)
        mixed = jnp.zeros((8, LANES), F32)
        for i in range(4):
            column = jnp.sum(jnp.where(col_member == i, kept, 0.0), axis=1, keepdims=True)
            for j in range(4):
                entry = jnp.sum(
                    jnp.where(row_member == j, column, 0.0), axis=0, keepdims=True
                )
                mixed = jnp.where((ri == i) & (ci == j), entry, mixed)
        mix_out_ref[...] = mixed


def frames_body(mel_ref, dur_ref, ngrad_ref, stats_ref, sums_ref, out_ref):
    pairs = mel_ref.shape[1] // 2
    inside = rows_of(pairs) < pair_rows(text_rows(dur_ref))
    total, center, variance, _, scale = read_stats(stats_ref[...])
    unit = 1.0 / (2 * MEL * total)
    sums = sums_ref[...]
    one = jnp.concatenate([sums[0:1], sums[1:2]], axis=1)
    two = jnp.concatenate([sums[2:3], sums[3:4]], axis=1)
    log_grad = two - unit * total
    var_grad = -0.5 * log_grad / (variance + 1e-06)
    center_grad = -scale * one - 2.0 * center * var_grad
    values = split_pairs(mel_ref, pairs)
    grads = ngrad_ref[0] * scale + (2.0 * values * var_grad + center_grad) / total
    grads = jnp.where(inside, grads, 0.0) * (2 * MEL * total)
    out_ref[0, pl.ds(0, pairs, stride=2), :] = grads[:, :MEL]
    out_ref[0, pl.ds(1, pairs, stride=2), :] = grads[:, LANES : LANES + MEL]


def small_sum(values, devices):
    bit = 1
    while bit < devices:
        values = values + lax.ppermute(values, "dp", [(i, i ^ bit) for i in range(devices)])
        bit *= 2
    return values


def big_sum(arrays, devices):
    return lax.psum(arrays, "dp")


def on_device(
    devices,
    token_ids,
    durations,
    mel_frames,
    embedding,
    w_qkv,
    rel_key,
    rel_value,
    w_out,
    attn_gain,
    attn_shift,
    w_ff1,
    w_ff2,
    ffn_gain,
    ffn_shift,
    w_prior,
    w_mix,
    w_start,
    w_in,
    w_res,
    w_skip_last,
    w_end,
):
    items, length = token_ids.shape
    frames = mel_frames.shape[1]
    pairs = frames // 2
    grid = (items,)
    vmem = pl.BlockSpec(memory_space=pltpu.VMEM)
    smem = pl.BlockSpec(memory_space=pltpu.SMEM)
    gain_one = attn_gain.reshape(1, D)
    shift_one = attn_shift.reshape(1, D)
    gain_two = ffn_gain.reshape(1, D)
    shift_two = ffn_shift.reshape(1, D)

    stats = run(
        stats_body, (), [mel_frames, durations], [vmem] * 2, shape_of((8, LANES)), vmem, name="stats"
    )
    stats = small_sum(stats, devices)

    prepared = [
        shape_of((2 * LANES, 2 * LANES)),
        shape_of((8, LANES)),
        shape_of((D, 6 * LANES), BF16),
        shape_of((LANES, LANES), BF16),
        shape_of((LANES, LANES), BF16),
        shape_of((2 * LANES, D), BF16),
        shape_of((2 * MEL, 8 * LANES), BF16),
        shape_of((D, 8 * LANES), BF16),
        shape_of((LANES, HID), BF16),
        shape_of((HID, 2 * LANES), BF16),
    ]
    mixm, small, qkv_pad, relk_pad, relv_pad, out_pad, wide, prior_pad, start_pad, end_pad = run(
        weights_body,
        (),
        [w_mix, w_qkv, rel_key, rel_value, w_out, w_prior, w_start, w_end],
        [smem] + [vmem] * 7,
        prepared,
        [vmem] * len(prepared),
        name="weights",
    )

    ins = [
        token_ids,
        durations,
        embedding,
        qkv_pad,
        relk_pad,
        relv_pad,
        out_pad,
        gain_one,
        shift_one,
    ]
    outs = [
        shape_of((items, length, D), BF16),
        shape_of((items, length, 6 * LANES), BF16),
        shape_of((items, HEADS, length, length)),
        shape_of((items, HEADS, length, LANES), BF16),
        shape_of((items, length, 2 * LANES), BF16),
        shape_of((items, length, D)),
        shape_of((items, length, D)),
    ]
    emb_low, proj, attention, banded, attend, mixed, normed = run(
        attention_body,
        grid,
        ins,
        [full_spec(a) for a in ins],
        outs,
        [item_spec(a) for a in outs],
        name="attention",
    )

    ins = [durations, normed, w_ff1, w_ff2, gain_two, shift_two, prior_pad]
    outs = [
        shape_of((items, length, FILTER)),
        shape_of((items, length, FILTER), BF16),
        shape_of((items, length, D)),
        shape_of((items, length, D), BF16),
        shape_of((items, 2 * length, 4 * LANES), BF16),
        shape_of((items, 2 * length, 4 * LANES), BF16),
    ]
    filtered, activ, summed, encoded, prior_high, prior_low = run(
        feed_body,
        grid,
        ins,
        [full_spec(durations), item_spec(normed)] + [full_spec(a) for a in ins[2:]],
        outs,
        [item_spec(a) for a in outs],
        name="feed",
    )

    ins = [
        mel_frames,
        durations,
        prior_high,
        prior_low,
        stats,
        mixm,
        start_pad,
        w_in,
        w_res,
        w_skip_last,
        end_pad,
    ]
    outs = [
        shape_of((items, pairs, 2 * LANES)),
        shape_of((items, pairs, LANES), BF16),
        shape_of((WLAYERS, items, pairs, HID), BF16),
        shape_of((WLAYERS, items, pairs, 2 * HID)),
        shape_of((items, pairs, HID), BF16),
        shape_of((items, pairs, LANES)),
        shape_of((items, pairs, LANES)),
        shape_of((items, pairs, 4 * LANES)),
        shape_of((8, LANES)),
        shape_of((HID, 2 * MEL)),
    ]
    stacked = [
        pl.BlockSpec((WLAYERS, 1) + a.shape[2:], lambda b: (0, b, 0, 0)) for a in outs[2:4]
    ]
    out_specs = (
        [item_spec(a) for a in outs[:2]]
        + stacked
        + [item_spec(a) for a in outs[4:8]]
        + [full_spec(a) for a in outs[8:]]
    )
    (
        normalized,
        passive,
        hidden,
        pre,
        skip,
        active_grad,
        latent_grad,
        flow,
        nll,
        end_grad,
    ) = run(
        flow_body,
        grid,
        ins,
        [item_spec(mel_frames), full_spec(durations), item_spec(prior_high), item_spec(prior_low)]
        + [full_spec(a) for a in ins[4:]],
        outs,
        out_specs,
        [pltpu.VMEM((HID, 2 * LANES), F32)],
        name="flow",
    )

    in_grads = [None] * WLAYERS
    res_grads = [None] * WLAYERS
    hgrad = None
    for layer in reversed(range(WLAYERS)):
        top = layer == WLAYERS - 1
        ins = [durations, skip, pre, hidden, w_in, w_skip_last if top else w_res]
        in_specs = [
            full_spec(durations),
            item_spec(skip),
            layer_spec(pre, layer),
            layer_spec(hidden, layer),
            weight_spec(w_in, layer),
            full_spec(w_skip_last) if top else weight_spec(w_res, layer),
        ]
        if not top:
            ins.append(hgrad)
            in_specs.append(item_spec(hgrad))
        outs = [
            shape_of((items, pairs, HID)),
            shape_of((WKER * HID, 2 * HID)),
            shape_of((HID, HID if top else 2 * HID)),
        ]
        hgrad, in_grads[layer], res_grads[layer] = run(
            functools.partial(layer_body, layer),
            grid,
            ins,
            in_specs,
            outs,
            [item_spec(outs[0]), full_spec(outs[1]), full_spec(outs[2])],
            [pltpu.VMEM((HID, WKER * 2 * HID), BF16)],
            name="layer" + str(layer),
        )

    ins = [durations, hgrad, passive, latent_grad, active_grad, normalized, start_pad, mixm]
    outs = [
        shape_of((items, pairs, 2 * LANES)),
        shape_of((MEL, HID)),
        shape_of((8, LANES)),
        shape_of((8, LANES)),
    ]
    normal_grad, start_grad, sums, mix_grad = run(
        mix_body,
        grid,
        ins,
        [full_spec(durations)] + [item_spec(a) for a in ins[1:6]] + [full_spec(a) for a in ins[6:]],
        outs,
        [item_spec(outs[0])] + [full_spec(a) for a in outs[1:]],
        [pltpu.VMEM((LANES, HID), F32), pltpu.VMEM((2 * LANES, 2 * LANES), F32)],
        name="mix",
    )
    sums = jnp.concatenate([sums[:4], nll[:4]], axis=0)
    sums = small_sum(sums, devices)

    ins = [durations, flow, wide, encoded, summed, filtered, activ, normed, w_ff1, w_ff2, gain_two, w_prior]
    outs = [
        shape_of((items, length, D)),
        shape_of((D, 2 * MEL)),
        shape_of((KSIZE * D, FILTER)),
        shape_of((KSIZE * FILTER, D)),
        shape_of((1, D)),
        shape_of((1, D)),
    ]
    kinds = [full_spec, item_spec, full_spec] + [item_spec] * 5 + [full_spec] * 4
    ngrad, prior_grad, ff1_grad, ff2_grad, gain_two_grad, shift_two_grad = run(
        feed_back_body,
        grid,
        ins,
        [kind(a) for kind, a in zip(kinds, ins)],
        outs,
        [item_spec(outs[0])] + [full_spec(a) for a in outs[1:]],
        name="feed_back",
    )

    ins = [
        token_ids,
        durations,
        ngrad,
        mixed,
        attend,
        attention,
        banded,
        proj,
        emb_low,
        qkv_pad,
        relk_pad,
        relv_pad,
        out_pad,
        gain_one,
    ]
    kinds = [full_spec] * 2 + [item_spec] * 7 + [full_spec] * 5
    outs = [
        shape_of((VOCAB, D)),
        shape_of((D, 3 * D)),
        shape_of((2 * WINDOW + 1, HEAD)),
        shape_of((2 * WINDOW + 1, HEAD)),
        shape_of((D, D)),
        shape_of((1, D)),
        shape_of((1, D)),
    ]
    table_grad, qkv_grad, relk_grad, relv_grad, out_grad, gain_one_grad, shift_one_grad = run(
        attention_back_body,
        grid,
        ins,
        [kind(a) for kind, a in zip(kinds, ins)],
        outs,
        [full_spec(a) for a in outs],
        [
            pltpu.VMEM((D, 6 * LANES), F32),
            pltpu.VMEM((2 * LANES, D), F32),
            pltpu.VMEM((LANES, LANES), F32),
            pltpu.VMEM((LANES, LANES), F32),
        ],
        name="attention_back",
    )

    ins = [mel_frames, durations, normal_grad, stats, sums]
    kinds = [item_spec, full_spec, item_spec, full_spec, full_spec]
    mel_grad = run(
        frames_body,
        grid,
        ins,
        [kind(a) for kind, a in zip(kinds, ins)],
        shape_of(mel_frames.shape),
        item_spec(mel_frames),
        name="frames",
    )

    total = stats[4, 0]
    unit = 1.0 / (2 * MEL * total)
    variance = stats[2:4, :MEL] / total - (stats[0:2, :MEL] / total) ** 2
    log_act = -0.5 * jnp.log(variance + 1e-06)
    loss = (
        jnp.sum(sums[4])
        - total * jnp.sum(log_act)
        - total * (MEL // 2) * jnp.log(small[4, 0])
    ) * unit + 0.5 * math.log(2.0 * math.pi)

    grads = big_sum(
        (
            table_grad,
            qkv_grad,
            relk_grad,
            relv_grad,
            out_grad,
            gain_one_grad.reshape(D),
            shift_one_grad.reshape(D),
            ff1_grad,
            ff2_grad,
            gain_two_grad.reshape(D),
            shift_two_grad.reshape(D),
            prior_grad,
            mix_grad[:4, :4],
            start_grad,
            jnp.stack(in_grads),
            jnp.stack(res_grads[:-1]),
            res_grads[-1],
            end_grad,
        ),
        devices,
    )
    grads = list(grads)
    grads[12] = grads[12] - (MEL // 2) * unit * total * small[:4, 4:8].T
    return (loss, mel_grad, *grads)


def solution(mesh):
    devices = mesh.shape["dp"]
    placed = (P("dp", None), P("dp", None), P("dp", None, None)) + (P(),) * 18
    return jax.shard_map(
        functools.partial(on_device, devices),
        mesh=mesh,
        in_specs=placed,
        out_specs=(P(), P("dp", None, None)) + (P(),) * 18,
        check_vma=False,
    )
```

```python
import functools
import math

import jax
import jax.numpy as jnp
from jax import lax
from jax.experimental import pallas as pl
from jax.experimental.pallas import tpu as pltpu
from jax.sharding import PartitionSpec as P

D = 192
HEADS = 2
HEAD = 96
LANES = 128
FILTER = 768
MEL = 80
HID = 192
VOCAB = 148
KSIZE = 3
WKER = 5
WLAYERS = 4
WINDOW = 4
PERIOD = 16

F32 = jnp.float32
BF16 = jnp.bfloat16
HIGH = lax.Precision.HIGHEST
VMEM_BYTES = 58 * 1024 * 1024
WIDE = 384
UNIT = 1152
REST = 768
TAIL = 384
COST = 0.1e9
ROW_TABLE = 2 * D
ROW_PRIOR = ROW_TABLE + MEL
ROW_NORM = ROW_PRIOR + MEL
ROW_REL = ROW_NORM + 8


def contract(first_op, second_op, dims, precision=None):
    return lax.dot_general(
        first_op, second_op, (dims, ((), ())), preferred_element_type=F32, precision=precision
    )


def dot_nn(first_op, second_op, precision=None):
    return contract(first_op, second_op, ((1,), (0,)), precision)


def dot_nt(first_op, second_op, precision=None):
    return contract(first_op, second_op, ((1,), (1,)), precision)


def dot_tn(first_op, second_op, precision=None):
    return contract(first_op, second_op, ((0,), (0,)), precision)


def halves(values):
    high = values.astype(BF16)
    low = (values - high.astype(F32)).astype(BF16)
    return high, low


def iota(shape, axis):
    return lax.broadcasted_iota(jnp.int32, shape, axis)


def rows_of(length):
    return iota((length, 1), 0)


def full_spec(array):
    rank = len(array.shape)
    return pl.BlockSpec(array.shape, lambda *_: (0,) * rank)


def item_spec(array):
    rank = len(array.shape)
    return pl.BlockSpec((1,) + array.shape[1:], lambda b: (b,) + (0,) * (rank - 1))


def layer_spec(array, layer):
    rank = len(array.shape)
    return pl.BlockSpec((1, 1) + array.shape[2:], lambda b: (layer, b) + (0,) * (rank - 2))


def weight_spec(array, layer):
    rank = len(array.shape)
    return pl.BlockSpec((1,) + array.shape[1:], lambda b: (layer,) + (0,) * (rank - 1))


def shape_of(shape, dtype=F32):
    return jax.ShapeDtypeStruct(shape, dtype)


def run(body, grid, ins, in_specs, outs, out_specs, scratch=(), micros=5, after=(), aliases=None, name=None):
    count, extra = len(ins), len(after)

    def wrapped(*refs):
        body(*refs[:count], *refs[count + extra :])

    return pl.pallas_call(
        wrapped,
        grid=grid,
        in_specs=list(in_specs) + [pl.BlockSpec(memory_space=pl.ANY)] * extra,
        out_specs=out_specs,
        out_shape=outs,
        scratch_shapes=list(scratch),
        compiler_params=pltpu.CompilerParams(vmem_limit_bytes=VMEM_BYTES),
        cost_estimate=pl.CostEstimate(
            flops=int(micros * COST), bytes_accessed=1 << 10, transcendentals=0
        ),
        input_output_aliases=aliases or {},
        name=name,
    )(*ins, *after)


def pair_rows(durations_row):
    return jnp.sum(durations_row, axis=1, keepdims=True) >> 1


def stats_body(mel_ref, dur_ref, out_ref):
    items, _, frames = mel_ref.shape
    lane = iota((1, frames), 1)
    count = jnp.zeros((1, 1), F32)
    sums = jnp.zeros((MEL, LANES), F32)
    squares = jnp.zeros((MEL, LANES), F32)
    for item in range(items):
        pair_count = pair_rows(dur_ref[item : item + 1, :])
        count = count + pair_count.astype(F32)
        values = jnp.where(lane < 2 * pair_count, mel_ref[item], 0.0)
        for part in range(frames // LANES):
            piece = values[:, part * LANES : (part + 1) * LANES]
            sums = sums + piece
            squares = squares + piece * piece
    place = iota((MEL, LANES), 1)
    table = jnp.zeros((MEL, LANES), F32)
    for side in range(2):
        chosen = (place & 1) == side
        for spot, held in ((side, sums), (2 + side, squares)):
            column = jnp.sum(jnp.where(chosen, held, 0.0), axis=1, keepdims=True)
            table = jnp.where(place == spot, column, table)
    table = jnp.concatenate([table, jnp.zeros((LANES - MEL, LANES), F32)], axis=0)
    rows = table.T[0:8]
    out_ref[...] = jnp.where(iota((8, LANES), 0) == 4, count, rows)


def read_stats(stats):
    total = stats[4:5, 0:1]
    sums = jnp.concatenate([stats[0:1], stats[1:2]], axis=1)
    squares = jnp.concatenate([stats[2:3], stats[3:4]], axis=1)
    center = sums / total
    variance = squares / total - center * center
    log_act = -0.5 * jnp.log(variance + 1e-06)
    return total, center, variance, log_act, jnp.exp(log_act)


def mix_places():
    row = rows_of(2 * LANES)
    col = iota((1, 2 * LANES), 1)
    row_lane = row & (LANES - 1)
    col_lane = col & (LANES - 1)
    upper = (row_lane >= MEL // 2).astype(jnp.int32)
    row_group = row_lane - upper * (MEL // 2)
    row_member = 2 * upper + (row >> 7)
    col_group = col_lane >> 1
    col_member = 2 * (col >> 7) + (col_lane & 1)
    match = (row_group == col_group) & (row_lane < MEL) & (col_lane < MEL)
    return row_member, col_member, match


def weights_body(
    mix_ref,
    qkv_ref,
    relk_ref,
    relv_ref,
    out_ref,
    prior_ref,
    start_ref,
    end_ref,
    res_ref,
    last_ref,
    mixm_ref,
    small_ref,
    qkv_pad_ref,
    relk_pad_ref,
    relv_pad_ref,
    out_pad_ref,
    wide_ref,
    prior_pad_ref,
    start_pad_ref,
    end_pad_ref,
    res_four_ref,
):
    row_member, col_member, match = mix_places()
    table = jnp.zeros((2 * LANES, 2 * LANES), F32)
    for i in range(4):
        column = jnp.zeros((2 * LANES, 1), F32)
        for j in range(4):
            column = jnp.where(row_member == j, mix_ref[i, j], column)
        table = jnp.where(col_member == i, column, table)
    mixm_ref[...] = jnp.where(match, table, 0.0)
    res_four_ref[: WLAYERS - 1] = res_ref[...]
    res_four_ref[WLAYERS - 1] = jnp.concatenate(
        [jnp.zeros((HID, HID), F32), last_ref[...].astype(F32)], axis=1
    ).astype(BF16)

    ri = iota((8, LANES), 0)
    ci = iota((8, LANES), 1)
    joined = jnp.where((ci == ri + 4) & (ri < 4), 1.0, 0.0).astype(F32)
    for i in range(4):
        for j in range(4):
            joined = jnp.where((ri == i) & (ci == j), mix_ref[i, j], joined)
    determinant = jnp.ones((1, 1), F32)
    for column in range(4):
        pivot = joined[column : column + 1, column : column + 1]
        determinant = determinant * pivot
        row_now = joined[column : column + 1, :] / pivot
        joined = joined - joined[:, column : column + 1] * row_now
        joined = jnp.where(ri == column, row_now, joined)
    turned = jnp.zeros((8, LANES), F32)
    for i in range(4):
        for j in range(4):
            turned = jnp.where((ri == j) & (ci == i), joined[i : i + 1, 4 + j : 5 + j], turned)
    small_ref[...] = jnp.where(ri == 4, determinant, turned)

    def select(count, wanted):
        return jnp.where(rows_of(count) == wanted, 1.0, 0.0).astype(BF16)

    place = iota((1, 6 * LANES), 1)
    lane = place & (LANES - 1)
    wanted = jnp.where(lane < HEAD, (place >> 7) * HEAD + lane, -1)
    qkv_pad_ref[...] = dot_nn(qkv_ref[...], select(3 * D, wanted)).astype(BF16)

    place = iota((1, 2 * LANES), 1)
    lane = place & (LANES - 1)
    wanted = jnp.where(lane < HEAD, (place >> 7) * HEAD + lane, -1)
    out_pad_ref[...] = dot_tn(select(D, wanted), out_ref[...]).astype(BF16)

    wanted = iota((1, LANES), 1) & (PERIOD - 1)
    repeat = select(2 * WINDOW + 1, wanted)
    pad = jnp.zeros((LANES, LANES - HEAD), F32)
    relk_pad_ref[...] = jnp.concatenate([dot_tn(repeat, relk_ref[...]), pad], axis=1).astype(BF16)
    relv_pad_ref[...] = jnp.concatenate([dot_tn(repeat, relv_ref[...]), pad], axis=1).astype(BF16)

    place = iota((1, 8 * LANES), 1)
    lane = place & (LANES - 1)
    group = (place >> 7) & 3
    fits = (lane < MEL) & ((lane & 1) == (place >> 9))
    wanted = jnp.where(fits, (group >> 1) * MEL + (group & 1) * (MEL // 2) + (lane >> 1), -1)
    wide = select(2 * MEL, wanted)
    wide_ref[...] = wide
    prior_pad_ref[...] = dot_tn(prior_ref[...], wide).astype(BF16)

    wanted = iota((1, LANES), 1)
    start_pad_ref[...] = dot_tn(select(MEL, wanted), start_ref[...]).astype(BF16)
    place = iota((1, 2 * LANES), 1)
    lane = place & (LANES - 1)
    wanted = jnp.where(lane < MEL, (place >> 7) * MEL + lane, -1)
    end_pad_ref[...] = dot_tn(end_ref[...], select(2 * MEL, wanted)).astype(BF16)


def text_rows(dur_ref):
    item = pl.program_id(0)
    return dur_ref[pl.ds(item, 1), :]


def text_inside(durations_row, length):
    tokens = jnp.sum((durations_row > 0).astype(jnp.int32), axis=1, keepdims=True)
    return rows_of(length) < tokens


def norm_parts(inputs):
    centered = inputs - jnp.mean(inputs, axis=1, keepdims=True)
    spread = jnp.mean(centered * centered, axis=1, keepdims=True)
    inverse = lax.rsqrt(spread + 1e-05)
    return centered * inverse, inverse


def norm_back(inputs, gain, gradient):
    unit, inverse = norm_parts(inputs)
    gain_grad = jnp.sum(gradient * unit, axis=0, keepdims=True)
    shift_grad = jnp.sum(gradient, axis=0, keepdims=True)
    scaled = gradient * gain
    mean_one = jnp.mean(scaled, axis=1, keepdims=True)
    mean_two = jnp.mean(scaled * unit, axis=1, keepdims=True)
    return inverse * (scaled - mean_one - unit * mean_two), gain_grad, shift_grad


def band_of(length):
    offset = iota((length, length), 1) - iota((length, length), 0)
    return (offset <= WINDOW) & (offset >= -WINDOW)


def turn_rows(values, left):
    length = values.shape[0]
    step = rows_of(length) & (PERIOD - 1)
    first = WINDOW if left else LANES - WINDOW
    values = pltpu.roll(values, first, 1)
    for bit in (1, 2, 4, 8):
        moved = pltpu.roll(values, (LANES - bit) if left else bit, 1)
        values = jnp.where((step & bit) != 0, moved, values)
    return values


def band_gather(weights_low, band, folding):
    kept = jnp.where(band, weights_low, jnp.zeros_like(weights_low))
    return turn_rows(dot_nn(kept, folding), True).astype(BF16)


def band_spread(near, band):
    turned = turn_rows(near, False)
    count = band.shape[1] // LANES
    return jnp.where(band, jnp.concatenate([turned] * count, axis=1), 0.0)


def folding_of(length):
    same = (iota((length, LANES), 0) & (PERIOD - 1)) == (iota((length, LANES), 1) & (PERIOD - 1))
    return jnp.where(same, 1.0, 0.0).astype(BF16)


def one_turn(rel_pad):
    return jnp.where(rows_of(LANES) < PERIOD, rel_pad, jnp.zeros_like(rel_pad))


def attention_body(
    tok_ref,
    dur_ref,
    emb_ref,
    qkv_ref,
    relk_ref,
    relv_ref,
    out_ref,
    gain_ref,
    shift_ref,
    emb_low_ref,
    proj_ref,
    att_ref,
    banded_ref,
    attend_ref,
    mixed_ref,
    normed_ref,
):
    item = pl.program_id(0)
    tokens = tok_ref[pl.ds(item, 1), :]
    durations = text_rows(dur_ref)
    length = tokens.shape[1]
    inside = text_inside(durations, length)
    hot = jnp.where(iota((VOCAB, length), 0) == tokens, 1.0, 0.0).astype(BF16)
    embedded = jnp.where(inside, dot_tn(hot, emb_ref[...]) * math.sqrt(D), 0.0)
    emb_low = embedded.astype(BF16)
    emb_low_ref[0] = emb_low
    proj = dot_nn(emb_low, qkv_ref[...]).astype(BF16)
    proj_ref[0] = proj
    key_bias = jnp.where(durations > 0, 0.0, -10000.0)
    band = band_of(length)
    folding = folding_of(length)
    relv = one_turn(relv_ref[...])
    parts = []
    for head in range(HEADS):
        query = proj[:, head * LANES : (head + 1) * LANES]
        key = proj[:, (HEADS + head) * LANES : (HEADS + head + 1) * LANES]
        value = proj[:, (2 * HEADS + head) * LANES : (2 * HEADS + head + 1) * LANES]
        near = band_spread(dot_nt(query, relk_ref[...]), band)
        scores = (dot_nt(query, key) + near) / math.sqrt(HEAD) + key_bias
        raised = jnp.exp(scores - jnp.max(scores, axis=1, keepdims=True))
        attention = raised / jnp.sum(raised, axis=1, keepdims=True)
        att_ref[0, head] = attention
        low = attention.astype(BF16)
        banded = band_gather(low, band, folding)
        banded_ref[0, head] = banded
        parts.append(dot_nn(low, value) + dot_nn(banded, relv))
    attend = jnp.concatenate(parts, axis=1).astype(BF16)
    attend_ref[0] = attend
    mixed = embedded + dot_nn(attend, out_ref[...])
    mixed_ref[0] = mixed
    unit, _ = norm_parts(mixed)
    normed_ref[0] = unit * gain_ref[...] + shift_ref[...]


def shifted(values, offset):
    if offset == 0:
        return values
    length = values.shape[0]
    moved = pltpu.roll(values, (-offset) % length, 0)
    place = rows_of(length)
    keep = (place < length - offset) if offset > 0 else (place >= -offset)
    return jnp.where(keep, moved, 0.0)


def unfold(values, kernel, reverse=False):
    half = kernel // 2
    steps = [step - half for step in range(kernel)]
    if reverse:
        steps = [-step for step in steps]
    return jnp.concatenate([shifted(values, step).astype(BF16) for step in steps], axis=1)


GELU_A = math.sqrt(2.0 / math.pi)
GELU_B = 0.044715


def gelu_tanh(values):
    return jnp.tanh(GELU_A * (values + GELU_B * values * values * values))


def feed_body(
    dur_ref,
    normed_ref,
    ff1_ref,
    ff2_ref,
    gain_ref,
    shift_ref,
    prior_ref,
    filt_ref,
    activ_ref,
    summed_ref,
    enc_ref,
    expand_ref,
    expand_low_ref,
):
    durations = text_rows(dur_ref)
    normed = normed_ref[0]
    length = normed.shape[0]
    inside = text_inside(durations, length)
    filtered = dot_nn(unfold(jnp.where(inside, normed, 0.0), KSIZE), ff1_ref[...])
    filt_ref[0] = filtered
    activ = jnp.where(inside, 0.5 * filtered * (1.0 + gelu_tanh(filtered)), 0.0)
    activ_ref[0] = activ.astype(BF16)
    summed = normed + jnp.where(inside, dot_nt(unfold(activ, KSIZE), ff2_ref[...]), 0.0)
    summed_ref[0] = summed
    unit, _ = norm_parts(summed)
    encoded = jnp.where(inside, unit * gain_ref[...] + shift_ref[...], 0.0).astype(BF16)
    enc_ref[0] = encoded
    prior = dot_nn(encoded, prior_ref[...])
    wide = prior.shape[1] // 2
    high, low = halves(prior)
    expand_ref[0, :length] = high[:, :wide]
    expand_ref[0, length:] = high[:, wide:]
    expand_low_ref[0, :length] = low[:, :wide]
    expand_low_ref[0, length:] = low[:, wide:]


def accumulate(ref, values, first):
    @pl.when(first)
    def _():
        ref[...] = values

    @pl.when(jnp.logical_not(first))
    def _():
        ref[...] = ref[...] + values


def align_of(durations_row, pairs):
    length = durations_row.shape[1]
    upper = jnp.where(iota((length, length), 0) <= iota((length, length), 1), 1.0, 0.0).astype(F32)
    wide = jnp.broadcast_to(durations_row.astype(F32), (8, length))
    ends = dot_nn(wide, upper, HIGH)[0:1].astype(jnp.int32)
    starts = ends - durations_row
    frame = 2 * rows_of(pairs)
    even = (frame >= starts) & (frame < ends)
    odd = (frame + 1 >= starts) & (frame + 1 < ends)
    both = jnp.concatenate([jnp.where(even, 1.0, 0.0), jnp.where(odd, 1.0, 0.0)], axis=1)
    return both.astype(BF16)


def feed_back_body(
    dur_ref,
    flow_ref,
    wide_ref,
    enc_ref,
    summed_ref,
    filt_ref,
    activ_ref,
    normed_ref,
    ff1_ref,
    ff2_ref,
    gain_ref,
    prior_ref,
    place_ref,
    ngrad_ref,
    prior_out_ref,
    gain_out_ref,
    shift_out_ref,
    one_kept_ref,
    one_sent_ref,
    two_kept_ref,
    two_sent_ref,
    out_ref,
):
    first = pl.program_id(0) == 0
    durations = text_rows(dur_ref)
    length = durations.shape[1]
    inside = text_inside(durations, length)
    flow = flow_ref[0]
    align = align_of(durations, flow.shape[0])
    spread = dot_tn(align, flow)
    half = wide_ref.shape[1] // 2
    grad = jnp.zeros((length, 2 * MEL), F32)
    for side in range(2):
        part_high, part_low = halves(spread[side * length : (side + 1) * length])
        chosen = wide_ref[:, side * half : (side + 1) * half]
        grad = grad + dot_nt(part_high, chosen) + dot_nt(part_low, chosen)
    prior_low = jnp.where(inside, grad, 0.0).astype(BF16)
    accumulate(prior_out_ref, dot_tn(prior_low, enc_ref[0]), first)
    enc_grad = jnp.where(inside, dot_nn(prior_low, prior_ref[...]), 0.0)
    summed_grad, gain_grad, shift_grad = norm_back(summed_ref[0], gain_ref[...], enc_grad)
    accumulate(gain_out_ref, gain_grad, first)
    accumulate(shift_out_ref, shift_grad, first)
    second = jnp.where(inside, summed_grad, 0.0)
    activ = activ_ref[0]
    activ_grad = jnp.zeros((length, FILTER), F32)
    for step in range(KSIZE):
        moved = shifted(second, KSIZE // 2 - step).astype(BF16)
        columns = slice(step * FILTER, (step + 1) * FILTER)
        activ_grad = activ_grad + dot_nn(moved, ff2_ref[:, columns])
        sums = dot_tn(moved, activ)
        for part in range(2):
            begin = UNIT + (2 * step + part) * D
            accumulate(
                out_ref.at[begin : begin + D, :], sums[:, part * WIDE : (part + 1) * WIDE], first
            )
    filtered = filt_ref[0]
    tanh = gelu_tanh(filtered)
    slope = 0.5 * (1.0 + tanh) + 0.5 * filtered * (1.0 - tanh * tanh) * GELU_A * (
        1.0 + 3.0 * GELU_B * filtered * filtered
    )
    first_grad = jnp.where(inside, activ_grad * slope, 0.0)
    normed_low = jnp.where(inside, normed_ref[0], 0.0).astype(BF16)
    back = jnp.zeros((length, D), F32)
    for step in range(KSIZE):
        moved = shifted(first_grad, KSIZE // 2 - step).astype(BF16)
        rows = slice(step * D, (step + 1) * D)
        back = back + dot_nt(moved, ff1_ref[rows, :])
        sums = dot_tn(normed_low, moved)
        for part in range(2):
            begin = part * KSIZE * D + step * D
            accumulate(
                out_ref.at[begin : begin + D, :], sums[:, part * WIDE : (part + 1) * WIDE], first
            )
    ngrad_ref[0] = summed_grad + jnp.where(inside, back, 0.0)

    @pl.when(pl.program_id(0) == pl.num_programs(0) - 1)
    def _():
        give_halves(place_ref, out_ref.at[:UNIT, :], one_kept_ref, one_sent_ref)
        give_halves(place_ref, out_ref.at[UNIT:, :], two_kept_ref, two_sent_ref)


def attention_back_body(
    tok_ref,
    dur_ref,
    ngrad_ref,
    mixed_ref,
    attend_ref,
    att_ref,
    banded_ref,
    proj_ref,
    emb_low_ref,
    qkv_ref,
    relk_ref,
    relv_ref,
    out_ref,
    gain_ref,
    prior_ref,
    gain_two_ref,
    shift_two_ref,
    place_ref,
    kept_ref,
    sent_ref,
    rest_ref,
    table_acc,
    qkv_acc,
    out_acc,
    relk_acc,
    relv_acc,
    gain_acc,
    shift_acc,
):
    item = pl.program_id(0)
    first = item == 0
    last = item == pl.num_programs(0) - 1
    tokens = tok_ref[pl.ds(item, 1), :]
    durations = text_rows(dur_ref)
    length = tokens.shape[1]
    inside = text_inside(durations, length)
    mixed_grad, gain_grad, shift_grad = norm_back(mixed_ref[0], gain_ref[...], ngrad_ref[0])
    accumulate(gain_acc, gain_grad, first)
    accumulate(shift_acc, shift_grad, first)
    out_low = mixed_grad.astype(BF16)
    accumulate(out_acc, dot_tn(attend_ref[0], out_low), first)
    weight = dot_nt(out_low, out_ref[...]).astype(BF16)
    band = band_of(length)
    folding = folding_of(length)
    relk = one_turn(relk_ref[...])
    proj = proj_ref[0]
    queries, keys, values = [], [], []
    relk_sum = jnp.zeros((LANES, LANES), F32)
    relv_sum = jnp.zeros((LANES, LANES), F32)
    for head in range(HEADS):
        query = proj[:, head * LANES : (head + 1) * LANES]
        key = proj[:, (HEADS + head) * LANES : (HEADS + head + 1) * LANES]
        value = proj[:, (2 * HEADS + head) * LANES : (2 * HEADS + head + 1) * LANES]
        mine = weight[:, head * LANES : (head + 1) * LANES]
        near = band_spread(dot_nt(mine, relv_ref[...]), band)
        grad = dot_nt(mine, value) + near
        attention = att_ref[0, head]
        values.append(dot_tn(attention.astype(BF16), mine))
        relv_sum = relv_sum + dot_tn(banded_ref[0, head], mine)
        score = attention * (grad - jnp.sum(attention * grad, axis=1, keepdims=True))
        score_low = (score / math.sqrt(HEAD)).astype(BF16)
        band_grad = band_gather(score_low, band, folding)
        queries.append(dot_nn(score_low, key) + dot_nn(band_grad, relk))
        keys.append(dot_tn(score_low, query))
        relk_sum = relk_sum + dot_tn(band_grad, query)
    accumulate(relk_acc, relk_sum, first)
    accumulate(relv_acc, relv_sum, first)
    proj_low = jnp.concatenate(queries + keys + values, axis=1).astype(BF16)
    accumulate(qkv_acc, dot_tn(emb_low_ref[0], proj_low), first)
    back = mixed_grad + dot_nt(proj_low, qkv_ref[...])
    embed_grad = jnp.where(inside, back, 0.0) * math.sqrt(D)
    hot = jnp.where(iota((VOCAB, length), 0) == tokens, 1.0, 0.0).astype(BF16)
    high, low = halves(embed_grad)
    accumulate(table_acc, dot_nn(hot, high) + dot_nn(hot, low), first)

    @pl.when(last)
    def _():
        def beside(left, right):
            return jnp.concatenate([left, right], axis=1)

        rest_ref[...] = jnp.zeros_like(rest_ref)
        packed = [qkv_acc[:, part * LANES : part * LANES + HEAD] for part in range(3 * HEADS)]
        half = D // 2
        rest_ref[:D, :] = jnp.concatenate(packed[:4], axis=1)
        rest_ref[D : D + half, :] = jnp.concatenate(
            [packed[4][:half], packed[5][:half], packed[4][half:], packed[5][half:]], axis=1
        )
        rest_ref[D + half : 2 * D, :] = beside(
            out_acc[:HEAD, :], out_acc[LANES : LANES + HEAD, :]
        )
        rest_ref[ROW_TABLE : ROW_TABLE + MEL, :D] = table_acc[:MEL, :]
        rest_ref[ROW_TABLE : ROW_TABLE + VOCAB - MEL, D:] = table_acc[MEL:, :]
        rest_ref[ROW_PRIOR : ROW_PRIOR + MEL, :] = beside(prior_ref[:MEL, :], prior_ref[MEL:, :])
        rest_ref[ROW_NORM : ROW_NORM + 1, :] = beside(gain_acc[...], shift_acc[...])
        rest_ref[ROW_NORM + 1 : ROW_NORM + 2, :] = beside(gain_two_ref[...], shift_two_ref[...])
        rest_ref[ROW_REL : ROW_REL + PERIOD, :LANES] = relk_acc[:PERIOD, :]
        rest_ref[ROW_REL : ROW_REL + PERIOD, LANES : 2 * LANES] = relv_acc[:PERIOD, :]
        give_halves(place_ref, rest_ref, kept_ref, sent_ref)


def split_pairs(mel_ref, rows_ref):
    frames = mel_ref.shape[2]
    pairs = frames // 2
    rows_ref[:, :MEL] = mel_ref[0].T
    pad = jnp.zeros((pairs, LANES - MEL), F32)
    even = rows_ref[pl.ds(0, pairs, stride=2), :][:, :MEL]
    odd = rows_ref[pl.ds(1, pairs, stride=2), :][:, :MEL]
    return jnp.concatenate([even, pad, odd, pad], axis=1)


def gates_of(pre):
    return jnp.tanh(pre[:, :HID]), 1.0 / (1.0 + jnp.exp(-pre[:, HID:]))


def give_halves(place_ref, acc_ref, kept_ref, sent_ref):
    half = kept_ref.shape[0]
    mine = pl.multiple_of((place_ref[0] & 1) * half, 8)
    other = pl.multiple_of(half - mine, 8)
    kept_ref[...] = acc_ref[pl.ds(mine, half), :]
    sent_ref[...] = acc_ref[pl.ds(other, half), :]


def dot_three(values, table, back=False):
    high, low = halves(values)
    table_high, table_low = halves(table)
    left = jnp.concatenate([high, low, high], axis=1)
    if back:
        return dot_nt(left, jnp.concatenate([table_high, table_high, table_low], axis=1))
    return dot_nn(left, jnp.concatenate([table_high, table_high, table_low], axis=0))


def shifted_rows(values, offset, period):
    if offset == 0:
        return values
    length = values.shape[0]
    moved = pltpu.roll(values, (-offset) % length, 0)
    place = rows_of(length) & (period - 1)
    keep = (place < period - offset) if offset > 0 else (place >= -offset)
    return jnp.where(keep, moved, 0.0)


def unfold_rows(values, kernel, period, reverse=False):
    half = kernel // 2
    steps = [step - half for step in range(kernel)]
    if reverse:
        steps = [-step for step in steps]
    return jnp.concatenate(
        [shifted_rows(values, step, period).astype(BF16) for step in steps], axis=1
    )


STEP_POST = WLAYERS + 1
STEPS = 2 * WLAYERS + 2


def decoder_body(
    mel_ref,
    dur_ref,
    expand_ref,
    expand_low_ref,
    stats_ref,
    mixm_ref,
    start_ref,
    win_ref,
    wres_ref,
    wend_ref,
    place_ref,
    units_ref,
    kept_ref,
    sent_ref,
    tail_kept_ref,
    tail_sent_ref,
    flow_ref,
    ngrad_ref,
    sums_ref,
    normal,
    passive_low,
    hidden_low,
    pre,
    hidden,
    skip,
    active,
    skip_low,
    passive_grad,
    gated,
    part,
    spread,
    wide,
    unit,
    rows,
    end_acc,
    tail,
):
    step = pl.program_id(0)
    items, _, frames = mel_ref.shape
    pairs = frames // 2
    both = 2 if items % 2 == 0 else 1
    blocks = items // both
    block_rows = both * pairs
    conv = WKER * HID

    def inside_item(item):
        return rows_of(pairs) < pair_rows(dur_ref[item : item + 1, :])

    def inside_block(block):
        return jnp.concatenate([inside_item(block * both + i) for i in range(both)], axis=0)

    def span(block):
        return slice(block * block_rows, (block + 1) * block_rows)

    def item_span(item):
        return slice(item * pairs, (item + 1) * pairs)

    @pl.when(step == 0)
    def _():
        _, center, _, _, scale = read_stats(stats_ref[...])
        for item in range(items):
            here = item_span(item)
            inside = inside_item(item)
            rows[:, :MEL] = mel_ref[item].T
            pad = jnp.zeros((pairs, LANES - MEL), F32)
            even = rows[pl.ds(0, pairs, stride=2), :][:, :MEL]
            odd = rows[pl.ds(1, pairs, stride=2), :][:, :MEL]
            values = jnp.concatenate([even, pad, odd, pad], axis=1)
            normalized = jnp.where(inside, (values - center) * scale, 0.0)
            normal[here, :] = normalized
            turned = dot_three(normalized, mixm_ref[...])
            passive = turned[:, :LANES]
            passive_grad[here, :] = passive
            active[here, :] = turned[:, LANES:]
            low = passive.astype(BF16)
            passive_low[here, :] = low
            hidden[here, :] = jnp.where(inside, dot_nn(low, start_ref[...]), 0.0)
            skip[here, :] = jnp.zeros((pairs, HID), F32)

    @pl.when((step >= 1) & (step <= WLAYERS))
    def _():
        layer = step - 1
        for block in range(blocks):
            here = span(block)
            inside = inside_block(block)
            state = hidden[here, :]
            hidden_low[layer, here, :] = state.astype(BF16)
            pre_gate = dot_nn(unfold_rows(state, WKER, pairs), win_ref[0])
            pre[layer, here, :] = pre_gate.astype(BF16)
            tanh, gate = gates_of(pre_gate)
            sums = dot_nn((tanh * gate).astype(BF16), wres_ref[layer])
            hidden[here, :] = jnp.where(inside, state + sums[:, :HID], 0.0)
            skip[here, :] = skip[here, :] + sums[:, HID:]

    @pl.when(step == STEP_POST)
    def _():
        total, _, _, _, _ = read_stats(stats_ref[...])
        unit_grad = 1.0 / (2 * MEL * total)
        end_sum = jnp.zeros(end_acc.shape, F32)
        nll = jnp.zeros((1, LANES), F32)
        for item in range(items):
            here = item_span(item)
            inside = inside_item(item)
            output_low = jnp.where(inside, skip[here, :], 0.0).astype(BF16)
            coupled = jnp.where(inside, dot_nn(output_low, wend_ref[...]), 0.0)
            shift_part = coupled[:, :LANES]
            log_part = coupled[:, LANES:]
            growth = jnp.exp(log_part)
            moving = active[here, :]
            moved = jnp.where(inside, shift_part + growth * moving, 0.0)
            align = align_of(dur_ref[item : item + 1, :], pairs)
            prior = dot_nn(align, expand_ref[item]) + dot_nn(align, expand_low_ref[item])
            latent = jnp.concatenate([passive_grad[here, :], moved], axis=1)
            gap = latent - prior[:, : 2 * LANES]
            log_scales = prior[:, 2 * LANES :]
            scaled = jnp.exp(-2.0 * log_scales) * gap
            square = scaled * gap
            terms = jnp.where(inside, log_scales + 0.5 * square, 0.0)
            sums = jnp.sum(terms, axis=0, keepdims=True)
            nll = nll + sums[:, :LANES] + sums[:, LANES:]
            nll = nll - jnp.sum(log_part, axis=0, keepdims=True)
            latent_grad = jnp.where(inside, unit_grad * scaled, 0.0)
            scale_grad = jnp.where(inside, unit_grad * (1.0 - square), 0.0)
            flow_ref[item] = jnp.concatenate([-latent_grad, scale_grad], axis=1).astype(BF16)
            passive_grad[here, :] = latent_grad[:, :LANES]
            moved_grad = latent_grad[:, LANES:]
            active_grad = moved_grad * growth
            log_grad = jnp.where(inside, active_grad * moving - unit_grad, 0.0)
            active[here, :] = active_grad
            coupled_low = jnp.concatenate([moved_grad, log_grad], axis=1).astype(BF16)
            end_sum = end_sum + dot_tn(coupled_low, output_low)
            skip_grad = jnp.where(inside, dot_nt(coupled_low, wend_ref[...]), 0.0)
            skip_low[here, :] = skip_grad.astype(BF16)
            hidden[here, :] = jnp.zeros((pairs, HID), F32)
        end_acc[...] = end_sum
        sums_ref[...] = jnp.where(iota((8, LANES), 0) == 4, nll, 0.0)

    @pl.when(step > STEP_POST)
    def _():
        layer = STEPS - 1 - step
        for tap in range(WKER):
            wide[:, tap * 2 * HID : (tap + 1) * 2 * HID] = win_ref[
                0, tap * HID : (tap + 1) * HID, :
            ]
        for block in range(blocks):
            here = span(block)
            tanh, gate = gates_of(pre[layer, here, :].astype(F32))
            gated[here, :] = (tanh * gate).astype(BF16)
            kept = hidden[here, :]
            both_low = jnp.concatenate([kept, skip_low[here, :].astype(F32)], axis=1).astype(BF16)
            part[here, :] = both_low
            gated_grad = dot_nt(both_low, wres_ref[layer])
            tanh_grad = gated_grad * gate * (1.0 - tanh * tanh)
            gate_grad = gated_grad * tanh * gate * (1.0 - gate)
            pre_grad = jnp.concatenate([tanh_grad, gate_grad], axis=1)
            taps = unfold_rows(pre_grad, WKER, pairs, reverse=True)
            spread[here, :] = taps
            back = kept + dot_nt(taps, wide[...])
            hidden[here, :] = jnp.where(inside_block(block), back, 0.0)
        sums = dot_tn(hidden_low[layer], spread[...])
        for tap in range(WKER):
            unit[tap * HID : (tap + 1) * HID, :] = sums[:, tap * 2 * HID : (tap + 1) * 2 * HID]
        unit[conv:, :] = dot_tn(gated[...], part[...])

        @pl.when(layer == WLAYERS - 1)
        def _():
            unit[conv : conv + MEL, :HID] = end_acc[:MEL, :]
            unit[conv + MEL : conv + 2 * MEL, :HID] = end_acc[LANES : LANES + MEL, :]

        @pl.when(layer > 0)
        def _():
            units_ref[...] = unit[...]

        @pl.when(layer == 0)
        def _():
            give_halves(place_ref, unit, kept_ref, sent_ref)

    @pl.when(step == STEPS - 1)
    def _():
        start_sum = jnp.zeros((LANES, HID), F32)
        mix_sum = jnp.zeros((2 * LANES, 2 * LANES), F32)
        one = jnp.zeros((1, 2 * LANES), F32)
        two = jnp.zeros((1, 2 * LANES), F32)
        for item in range(items):
            here = item_span(item)
            start_low = hidden[here, :].astype(BF16)
            start_sum = start_sum + dot_tn(passive_low[here, :], start_low)
            turned_passive = passive_grad[here, :] + dot_nt(start_low, start_ref[...])
            turned_grad = jnp.concatenate([turned_passive, active[here, :]], axis=1)
            normalized = normal[here, :]
            mix_sum = mix_sum + dot_tn(normalized.astype(BF16), turned_grad.astype(BF16))
            normal_grad = dot_three(turned_grad, mixm_ref[...], back=True)
            normal_grad = jnp.where(inside_item(item), normal_grad, 0.0)
            ngrad_ref[item] = normal_grad
            one = one + jnp.sum(normal_grad, axis=0, keepdims=True)
            two = two + jnp.sum(normal_grad * normalized, axis=0, keepdims=True)
        sums_ref[0:1, :] = one[:, :LANES]
        sums_ref[1:2, :] = one[:, LANES:]
        sums_ref[2:3, :] = two[:, :LANES]
        sums_ref[3:4, :] = two[:, LANES:]
        half = MEL // 2
        tail[...] = jnp.zeros_like(tail)
        tail[:half, :] = jnp.concatenate([start_sum[:half, :], start_sum[half:MEL, :]], axis=1)
        row_member, col_member, match = mix_places()
        kept = jnp.where(match, mix_sum, 0.0)
        ri = iota((8, LANES), 0)
        ci = iota((8, LANES), 1)
        mixed = jnp.zeros((8, LANES), F32)
        for i in range(4):
            column = jnp.sum(jnp.where(col_member == i, kept, 0.0), axis=1, keepdims=True)
            for j in range(4):
                entry = jnp.sum(jnp.where(row_member == j, column, 0.0), axis=0, keepdims=True)
                mixed = jnp.where((ri == i) & (ci == j), entry, mixed)
        tail[half : half + 8, :LANES] = mixed
        give_halves(place_ref, tail, tail_kept_ref, tail_sent_ref)


def frames_body(
    mel_ref, dur_ref, ngrad_ref, stats_ref, sums_ref, small_ref, out_ref, loss_ref, rows_ref
):
    pairs = mel_ref.shape[2] // 2
    inside = rows_of(pairs) < pair_rows(text_rows(dur_ref))
    total, center, variance, log_act, scale = read_stats(stats_ref[...])
    unit = 1.0 / (2 * MEL * total)
    sums = sums_ref[...]
    spot = iota((1, 2 * LANES), 1) & (LANES - 1)
    log_sum = jnp.sum(jnp.where(spot < MEL, log_act, 0.0), axis=1, keepdims=True)
    nll = jnp.sum(sums[4:5], axis=1, keepdims=True)
    log_det = jnp.log(small_ref[4:5, 0:1])
    loss = (nll - total * log_sum - total * (MEL // 2) * log_det) * unit
    loss_ref[...] = loss + 0.5 * math.log(2.0 * math.pi)
    one = jnp.concatenate([sums[0:1], sums[1:2]], axis=1)
    two = jnp.concatenate([sums[2:3], sums[3:4]], axis=1)
    log_grad = two - unit * total
    var_grad = -0.5 * log_grad / (variance + 1e-06)
    center_grad = -scale * one - 2.0 * center * var_grad
    values = split_pairs(mel_ref, rows_ref)
    grads = ngrad_ref[0] * scale + (2.0 * values * var_grad + center_grad) / total
    grads = jnp.where(inside, grads, 0.0) * (2 * MEL * total)
    rows_ref[pl.ds(0, pairs, stride=2), :] = grads[:, :LANES]
    rows_ref[pl.ds(1, pairs, stride=2), :] = grads[:, LANES:]
    out_ref[0] = rows_ref[...].T[:MEL, :]


def small_sum(values, devices):
    bit = 1
    while bit < devices:
        values = values + lax.ppermute(values, "dp", [(i, i ^ bit) for i in range(devices)])
        bit *= 2
    return values


def swap(values, bit, devices):
    return lax.ppermute(values, "dp", [(i, i ^ bit) for i in range(devices)])


def swap_half(unit, devices):
    kept, sent = unit
    return kept, swap(sent, 1, devices)


def digits(devices):
    found = []
    shift = 1
    while (1 << shift) < devices:
        radix = 4 if (1 << (shift + 2)) <= devices else 2
        found.append((shift, radix))
        shift += 2 if radix == 4 else 1
    return found


def whole_vmem(count):
    return [pl.BlockSpec(memory_space=pltpu.VMEM)] * count


def call_whole(body, place, ins, outs, scratch, after, micros, name):
    return run(
        body,
        (),
        [place, *ins],
        [pl.BlockSpec(memory_space=pltpu.SMEM)] + whole_vmem(len(ins)),
        outs,
        whole_vmem(len(outs)),
        scratch,
        micros=micros,
        after=after,
        name=name,
    )


def hop_out(jobs, place, after=()):
    ins = []
    outs = []
    scratch = []
    plans = []
    for units, shift, radix in jobs:
        plan = []
        begin = 0
        for unit in units:
            row = unit[0].shape[0] // radix
            plan.append((len(ins), len(unit), row, begin))
            ins += unit
            begin += row
        plans.append((plan, len(outs), shift, radix))
        outs += [shape_of((begin, WIDE))] * radix
        scratch.append(pltpu.VMEM((radix, begin, WIDE), F32))
    n_in, n_out = len(ins), len(outs)

    def body(place_ref, *refs):
        out_refs = refs[n_in : n_in + n_out]
        tables = refs[n_in + n_out :]
        for (plan, at, shift, radix), table in zip(plans, tables):
            digit = (place_ref[0] >> shift) & (radix - 1)
            for first, count, row, begin in plan:
                for part in range(radix):
                    span = slice(part * row, (part + 1) * row)
                    value = refs[first][span, :]
                    for extra in range(1, count):
                        value = value + refs[first + extra][span, :]
                    table[part, begin : begin + row, :] = value
            for step in range(radix):
                out_refs[at + step][...] = table[digit ^ step]

    found = call_whole(body, place, ins, outs, scratch, after, 3, "hop_out")
    return [found[at : at + radix] for _, at, _, radix in plans]


def hop_in(jobs, place, after=()):
    ins = []
    outs = []
    plans = []
    for parts, shift in jobs:
        plans.append((len(ins), len(parts), shift))
        ins += parts
        outs.append(shape_of((len(parts), *parts[0].shape)))
    n_in = len(ins)

    def body(place_ref, *refs):
        for (first, radix, shift), out in zip(plans, refs[n_in:]):
            digit = (place_ref[0] >> shift) & (radix - 1)
            for step in range(radix):
                out[digit ^ step] = refs[first + step][...]

    return call_whole(body, place, ins, outs, (), after, 2, "hop_in")


def add_parts(jobs, place, after=()):
    ins = [part for parts in jobs for part in parts]
    outs = [shape_of(parts[0].shape) for parts in jobs]
    n_in = len(ins)

    def body(place_ref, *refs):
        at = 0
        for parts, out in zip(jobs, refs[n_in:]):
            value = refs[at][...]
            for extra in range(at + 1, at + len(parts)):
                value = value + refs[extra][...]
            out[...] = value
            at += len(parts)

    return call_whole(body, place, ins, outs, (), after, 1, "add_parts")


def send_parts(parts, shift, devices):
    return [parts[0]] + [
        swap(part, step << shift, devices) for step, part in enumerate(parts) if step > 0
    ]


def sum_chunks(chunks, place, devices, after):
    steps = digits(devices)
    orders = [steps[i:] + steps[:i] for i in range(len(chunks))]
    state = chunks
    for level in range(len(steps)):
        jobs = [(units, *order[level]) for units, order in zip(state, orders)]
        parts = hop_out(jobs, place, after if level == 0 else ())
        state = [
            [send_parts(part, order[level][0], devices)] for part, order in zip(parts, orders)
        ]
    return add_parts([units[0] for units in state], place), orders


def gather_chunks(state, orders, place, devices, meanwhile):
    for level in reversed(range(len(orders[0]))):
        jobs = []
        for part, order in zip(state, orders):
            shift, radix = order[level]
            jobs.append((send_parts([part] * radix, shift, devices), shift))
        if level == 0:
            after = meanwhile(state)
        state = hop_in(jobs, place, after if level == 0 else ())
    state = [part.reshape(part.shape[0], -1, WIDE) for part in state]
    return state, [swap(part, 1, devices) for part in state]


def rebuild(bit, mine_ref, other_ref, begin, rows, table):
    radix = mine_ref.shape[0]
    part = rows // 2 // radix
    for core in range(2):
        for digit in range(radix):
            mine = mine_ref[digit, begin : begin + part, :]
            other = other_ref[digit, begin : begin + part, :]
            at = core * (rows // 2) + digit * part
            table[at : at + part, :] = jnp.where(bit == core, mine, other)
    return begin + part


def unpack_units_body(units_ref, in_ref, res_ref, last_ref, end_ref, sems):
    conv = WKER * HID
    copies = []
    for layer in range(1, WLAYERS):
        begin = (WLAYERS - 1 - layer) * UNIT
        copies.append((units_ref.at[pl.ds(begin, conv), :], in_ref.at[layer]))
        if layer < WLAYERS - 1:
            copies.append((units_ref.at[pl.ds(begin + conv, HID), :], res_ref.at[layer]))
    copies = [
        pltpu.make_async_copy(source, target, sems.at[i])
        for i, (source, target) in enumerate(copies)
    ]
    for copy in copies:
        copy.start()
    last_ref[...] = units_ref[conv:UNIT, HID:]
    end_ref[...] = units_ref[conv : conv + 2 * MEL, :HID]
    for copy in copies:
        copy.wait()


def unpack_units(units, after):
    vmem = pl.BlockSpec(memory_space=pltpu.VMEM)
    anywhere = pl.BlockSpec(memory_space=pl.ANY)
    outs = [
        shape_of((WLAYERS, WKER * HID, 2 * HID)),
        shape_of((WLAYERS - 1, HID, 2 * HID)),
        shape_of((HID, HID)),
        shape_of((2 * MEL, HID)),
    ]
    return run(
        unpack_units_body,
        (),
        [units],
        [vmem],
        outs,
        [anywhere] * 2 + [vmem] * 2,
        [pltpu.SemaphoreType.DMA((2 * WLAYERS - 3,))],
        micros=5,
        after=after,
        name="unpack_units",
    )


def unpack_body(
    place_ref,
    mine_ref,
    other_ref,
    mine_low_ref,
    other_low_ref,
    small_ref,
    in_given,
    res_given,
    one_ref,
    two_ref,
    table_ref,
    qkv_ref,
    out_ref,
    relk_ref,
    relv_ref,
    norms_ref,
    prior_ref,
    start_ref,
    mix_ref,
    in_ref,
    res_ref,
    first,
    second,
    rest,
    unit,
    tail,
    sems,
):
    bit = place_ref[0] & 1
    conv = WKER * HID
    begin = rebuild(bit, mine_low_ref, other_low_ref, 0, UNIT, unit)
    copies = [
        pltpu.make_async_copy(unit.at[pl.ds(0, conv), :], in_ref.at[0], sems.at[0]),
        pltpu.make_async_copy(unit.at[pl.ds(conv, HID), :], res_ref.at[0], sems.at[1]),
    ]
    for copy in copies:
        copy.start()
    rebuild(bit, mine_low_ref, other_low_ref, begin, TAIL, tail)
    half = MEL // 2
    start_ref[:half, :] = tail[:half, :HID]
    start_ref[half:, :] = tail[:half, HID:]
    mix_ref[...] = tail[half : half + 8, :LANES] - small_ref[...] / 4.0
    begin = rebuild(bit, mine_ref, other_ref, 0, UNIT, first)
    for part in range(2):
        one_ref[:, part * WIDE : (part + 1) * WIDE] = first[
            part * KSIZE * D : (part + 1) * KSIZE * D, :
        ]
    begin = rebuild(bit, mine_ref, other_ref, begin, UNIT, second)
    for part in range(2 * KSIZE):
        two_ref[:, part * WIDE : (part + 1) * WIDE] = second[part * D : (part + 1) * D, :]
    rebuild(bit, mine_ref, other_ref, begin, REST, rest)
    half = D // 2
    qkv_ref[:, :WIDE] = rest[:D, :]
    qkv_ref[:half, WIDE:] = rest[D : D + half, :D]
    qkv_ref[half:, WIDE:] = rest[D : D + half, D:]
    out_ref[:half, :] = rest[D + half : 2 * D, :D]
    out_ref[half:, :] = rest[D + half : 2 * D, D:]
    table_ref[:MEL, :] = rest[ROW_TABLE : ROW_TABLE + MEL, :D]
    table_ref[MEL:, :] = rest[ROW_TABLE : ROW_TABLE + VOCAB - MEL, D:]
    prior_ref[:MEL, :] = rest[ROW_PRIOR : ROW_PRIOR + MEL, :D]
    prior_ref[MEL:, :] = rest[ROW_PRIOR : ROW_PRIOR + MEL, D:]
    relk_ref[...] = rest[ROW_REL : ROW_REL + 2 * WINDOW + 1, :HEAD]
    relv_ref[...] = rest[ROW_REL : ROW_REL + 2 * WINDOW + 1, LANES : LANES + HEAD]
    norms_ref[...] = jnp.concatenate(
        [rest[ROW_NORM : ROW_NORM + 2, :D], rest[ROW_NORM : ROW_NORM + 2, D:]], axis=0
    )
    for copy in copies:
        copy.wait()


def unpack(upper, lower, place, inverse, in_grad, res_grad):
    vmem = pl.BlockSpec(memory_space=pltpu.VMEM)
    anywhere = pl.BlockSpec(memory_space=pl.ANY)
    reach = 2 * WINDOW + 1
    outs = [
        shape_of((KSIZE * D, FILTER)),
        shape_of((D, KSIZE * FILTER)),
        shape_of((VOCAB, D)),
        shape_of((D, 3 * D)),
        shape_of((D, D)),
        shape_of((reach, HEAD)),
        shape_of((reach, HEAD)),
        shape_of((4, D)),
        shape_of((2 * MEL, D)),
        shape_of((MEL, HID)),
        shape_of((8, LANES)),
        shape_of(in_grad.shape),
        shape_of(res_grad.shape),
    ]
    return run(
        unpack_body,
        (),
        [place, *upper, *lower, inverse, in_grad, res_grad],
        [pl.BlockSpec(memory_space=pltpu.SMEM)] + [vmem] * 5 + [anywhere] * 2,
        outs,
        [vmem] * (len(outs) - 2) + [anywhere] * 2,
        [
            pltpu.VMEM((UNIT, WIDE), F32),
            pltpu.VMEM((UNIT, WIDE), F32),
            pltpu.VMEM((REST, WIDE), F32),
            pltpu.VMEM((UNIT, WIDE), F32),
            pltpu.VMEM((TAIL, WIDE), F32),
            pltpu.SemaphoreType.DMA((2,)),
        ],
        micros=5,
        aliases={6: 11, 7: 12},
        name="unpack",
    )


def on_device(
    devices,
    token_ids,
    durations,
    mel_frames,
    embedding,
    w_qkv,
    rel_key,
    rel_value,
    w_out,
    attn_gain,
    attn_shift,
    w_ff1,
    w_ff2,
    ffn_gain,
    ffn_shift,
    w_prior,
    w_mix,
    w_start,
    w_in,
    w_res,
    w_skip_last,
    w_end,
):
    items, length = token_ids.shape
    frames = mel_frames.shape[1]
    mel_frames = mel_frames.transpose(0, 2, 1)
    ff2_t = w_ff2.T
    prior_t = w_prior.T
    end_t = w_end.T
    pairs = frames // 2
    grid = (items,)
    place = lax.axis_index("dp").reshape(1).astype(jnp.int32)

    def halves_of(rows):
        return [shape_of((rows // 2, WIDE))] * 2

    vmem = pl.BlockSpec(memory_space=pltpu.VMEM)
    smem = pl.BlockSpec(memory_space=pltpu.SMEM)
    gain_one = attn_gain.reshape(1, D)
    shift_one = attn_shift.reshape(1, D)
    gain_two = ffn_gain.reshape(1, D)
    shift_two = ffn_shift.reshape(1, D)

    stats = run(
        stats_body, (), [mel_frames, durations], [vmem] * 2, shape_of((8, LANES)), vmem, name="stats"
    )
    stats = small_sum(stats, devices)

    prepared = [
        shape_of((2 * LANES, 2 * LANES)),
        shape_of((8, LANES)),
        shape_of((D, 6 * LANES), BF16),
        shape_of((LANES, LANES), BF16),
        shape_of((LANES, LANES), BF16),
        shape_of((2 * LANES, D), BF16),
        shape_of((2 * MEL, 8 * LANES), BF16),
        shape_of((D, 8 * LANES), BF16),
        shape_of((LANES, HID), BF16),
        shape_of((HID, 2 * LANES), BF16),
        shape_of((WLAYERS, HID, 2 * HID), BF16),
    ]
    (
        mixm,
        small,
        qkv_pad,
        relk_pad,
        relv_pad,
        out_pad,
        wide,
        prior_pad,
        start_pad,
        end_pad,
        res_four,
    ) = run(
        weights_body,
        (),
        [w_mix, w_qkv, rel_key, rel_value, w_out, prior_t, w_start, end_t, w_res, w_skip_last],
        [smem] + [vmem] * 9,
        prepared,
        [vmem] * len(prepared),
        name="weights",
    )

    ins = [
        token_ids,
        durations,
        embedding,
        qkv_pad,
        relk_pad,
        relv_pad,
        out_pad,
        gain_one,
        shift_one,
    ]
    outs = [
        shape_of((items, length, D), BF16),
        shape_of((items, length, 6 * LANES), BF16),
        shape_of((items, HEADS, length, length)),
        shape_of((items, HEADS, length, LANES), BF16),
        shape_of((items, length, 2 * LANES), BF16),
        shape_of((items, length, D)),
        shape_of((items, length, D)),
    ]
    emb_low, proj, attention, banded, attend, mixed, normed = run(
        attention_body,
        grid,
        ins,
        [full_spec(a) for a in ins],
        outs,
        [item_spec(a) for a in outs],
        micros=14,
        name="attention",
    )

    ins = [durations, normed, w_ff1, ff2_t, gain_two, shift_two, prior_pad]
    outs = [
        shape_of((items, length, FILTER)),
        shape_of((items, length, FILTER), BF16),
        shape_of((items, length, D)),
        shape_of((items, length, D), BF16),
        shape_of((items, 2 * length, 4 * LANES), BF16),
        shape_of((items, 2 * length, 4 * LANES), BF16),
    ]
    filtered, activ, summed, encoded, expand, expand_low = run(
        feed_body,
        grid,
        ins,
        [full_spec(durations), item_spec(normed)] + [full_spec(a) for a in ins[2:]],
        outs,
        [item_spec(a) for a in outs],
        micros=10,
        name="feed",
    )

    ins = [mel_frames, durations, expand, expand_low, stats, mixm, start_pad, w_in, res_four, end_pad, place]
    kinds = [full_spec] * 10
    in_specs = [kind(a) for kind, a in zip(kinds, ins)] + [smem]
    in_specs[7] = pl.BlockSpec(
        (1,) + w_in.shape[1:],
        lambda s: (jnp.where(s <= STEP_POST, jnp.clip(s - 1, 0, WLAYERS - 1), STEPS - 1 - s), 0, 0),
    )
    outs = [
        shape_of(((WLAYERS - 1) * UNIT, WIDE)),
        *halves_of(UNIT),
        *halves_of(TAIL),
        shape_of((items, pairs, 4 * LANES), BF16),
        shape_of((items, pairs, 2 * LANES)),
        shape_of((8, LANES)),
    ]
    out_specs = [full_spec(a) for a in outs]
    out_specs[0] = pl.BlockSpec(
        (UNIT, WIDE), lambda s: (jnp.clip(s - STEP_POST - 1, 0, WLAYERS - 2), 0)
    )
    count = items * pairs
    units, kept, sent, tail_kept, tail_sent, flow, normal_grad, sums = run(
        decoder_body,
        (STEPS,),
        ins,
        in_specs,
        outs,
        out_specs,
        [
            pltpu.VMEM((count, 2 * LANES), F32),
            pltpu.VMEM((count, LANES), BF16),
            pltpu.VMEM((WLAYERS, count, HID), BF16),
            pltpu.VMEM((WLAYERS, count, 2 * HID), BF16),
            pltpu.VMEM((count, HID), F32),
            pltpu.VMEM((count, HID), F32),
            pltpu.VMEM((count, LANES), F32),
            pltpu.VMEM((count, HID), BF16),
            pltpu.VMEM((count, LANES), F32),
            pltpu.VMEM((count, HID), BF16),
            pltpu.VMEM((count, 2 * HID), BF16),
            pltpu.VMEM((count, WKER * 2 * HID), BF16),
            pltpu.VMEM((HID, WKER * 2 * HID), BF16),
            pltpu.VMEM((UNIT, WIDE), F32),
            pltpu.VMEM((frames, LANES), F32),
            pltpu.VMEM((2 * LANES, HID), F32),
            pltpu.VMEM((TAIL, WIDE), F32),
        ],
        micros=80,
        name="decoder",
    )
    units = lax.psum(units, "dp")
    first_unit = swap_half((kept, sent), devices)
    last_unit = swap_half((tail_kept, tail_sent), devices)
    sums = sums + swap(sums, 1, devices)
    sum_steps = digits(devices)

    ins = [durations, flow, wide, encoded, summed, filtered, activ, normed, w_ff1, ff2_t, gain_two, prior_t]
    outs = [
        shape_of((items, length, D)),
        shape_of((2 * MEL, D)),
        shape_of((1, D)),
        shape_of((1, D)),
        *halves_of(UNIT),
        *halves_of(UNIT),
    ]
    kinds = [full_spec, item_spec, full_spec] + [item_spec] * 5 + [full_spec] * 4
    ngrad, prior_grad, gain_two_grad, shift_two_grad, *feed_units = run(
        feed_back_body,
        grid,
        ins + [place],
        [kind(a) for kind, a in zip(kinds, ins)] + [smem],
        outs,
        [item_spec(outs[0])] + [full_spec(a) for a in outs[1:]],
        [pltpu.VMEM((2 * UNIT, WIDE), F32)],
        after=(sums,),
        micros=28,
        name="feed_back",
    )

    shift, radix = sum_steps[0]
    sums = sum(send_parts([sums] * radix, shift, devices))
    feed_sums = sums
    ins = [
        token_ids,
        durations,
        ngrad,
        mixed,
        attend,
        attention,
        banded,
        proj,
        emb_low,
        qkv_pad,
        relk_pad,
        relv_pad,
        out_pad,
        gain_one,
        prior_grad,
        gain_two_grad,
        shift_two_grad,
    ]
    kinds = [full_spec] * 2 + [item_spec] * 7 + [full_spec] * 8
    rest = run(
        attention_back_body,
        grid,
        ins + [place],
        [kind(a) for kind, a in zip(kinds, ins)] + [smem],
        halves_of(REST),
        [full_spec(a) for a in halves_of(REST)],
        [
            pltpu.VMEM((REST, WIDE), F32),
            pltpu.VMEM((VOCAB, D), F32),
            pltpu.VMEM((D, 6 * LANES), F32),
            pltpu.VMEM((2 * LANES, D), F32),
            pltpu.VMEM((LANES, LANES), F32),
            pltpu.VMEM((LANES, LANES), F32),
            pltpu.VMEM((1, D), F32),
            pltpu.VMEM((1, D), F32),
        ],
        after=(feed_sums,),
        micros=20,
        name="attention_back",
    )

    for shift, radix in sum_steps[1:]:
        sums = sum(send_parts([sums] * radix, shift, devices))
    feed_units = [swap_half(feed_units[:2], devices), swap_half(feed_units[2:], devices)]
    rest = swap_half(rest, devices)
    state, orders = sum_chunks(
        [[*feed_units, rest], [first_unit, last_unit]], place, devices, (sums,)
    )

    ins = [mel_frames, durations, normal_grad, stats, sums, small]
    kinds = [item_spec, full_spec, item_spec, full_spec, full_spec, full_spec]
    mel_grad, loss = run(
        frames_body,
        grid,
        ins,
        [kind(a) for kind, a in zip(kinds, ins)],
        [shape_of(mel_frames.shape), shape_of((1, 1))],
        [item_spec(mel_frames), pl.BlockSpec((1, 1), lambda b: (0, 0))],
        [pltpu.VMEM((frames, LANES), F32)],
        after=(state[0],),
        name="frames",
    )

    kept_grads = []

    def meanwhile(state):
        kept_grads.extend(unpack_units(units, (mel_grad, state[0])))
        return (kept_grads[2],)

    state, other = gather_chunks(state, orders, place, devices, meanwhile)
    in_grad, res_grad, last_grad, end_grad = kept_grads
    (
        ff1_grad,
        ff2_grad,
        table_grad,
        qkv_grad,
        out_grad,
        relk_grad,
        relv_grad,
        norm_grads,
        prior_grad,
        start_grad,
        mix_grad,
        in_grad,
        res_grad,
    ) = unpack((state[0], other[0]), (state[1], other[1]), place, small, in_grad, res_grad)

    return (
        loss.reshape(()),
        mel_grad.transpose(0, 2, 1),
        table_grad,
        qkv_grad,
        relk_grad,
        relv_grad,
        out_grad,
        norm_grads[0],
        norm_grads[2],
        ff1_grad,
        ff2_grad.T,
        norm_grads[1],
        norm_grads[3],
        prior_grad.T,
        mix_grad[:4, :4],
        start_grad,
        in_grad,
        res_grad,
        last_grad,
        end_grad.T,
    )


def solution(mesh):
    devices = mesh.shape["dp"]
    placed = (P("dp", None), P("dp", None), P("dp", None, None)) + (P(),) * 18
    return jax.shard_map(
        functools.partial(on_device, devices),
        mesh=mesh,
        in_specs=placed,
        out_specs=(P(), P("dp", None, None)) + (P(),) * 18,
        check_vma=False,
    )
```

```python
import functools
import math

import jax
import jax.numpy as jnp
from jax import lax
from jax.experimental import pallas as pl
from jax.experimental.pallas import tpu as pltpu
from jax.sharding import PartitionSpec as P

D = 192
HEADS = 2
HEAD = 96
LANES = 128
FILTER = 768
MEL = 80
HID = 192
VOCAB = 148
KSIZE = 3
WKER = 5
WLAYERS = 4
WINDOW = 4
PERIOD = 16

F32 = jnp.float32
BF16 = jnp.bfloat16
HIGH = lax.Precision.HIGHEST
VMEM_BYTES = 58 * 1024 * 1024
WIDE = 384
UNIT = 1152
REST = 640
TAIL = 128
COST = 1.15e9
ROW_TABLE = 2 * D
ROW_PRIOR = ROW_TABLE + MEL
ROW_NORM = ROW_PRIOR + MEL
ROW_REL = ROW_NORM + 8


def contract(first_op, second_op, dims, precision=None):
    return lax.dot_general(
        first_op, second_op, (dims, ((), ())), preferred_element_type=F32, precision=precision
    )


def dot_nn(first_op, second_op, precision=None):
    return contract(first_op, second_op, ((1,), (0,)), precision)


def dot_nt(first_op, second_op, precision=None):
    return contract(first_op, second_op, ((1,), (1,)), precision)


def dot_tn(first_op, second_op, precision=None):
    return contract(first_op, second_op, ((0,), (0,)), precision)


def halves(values):
    high = values.astype(BF16)
    low = (values - high.astype(F32)).astype(BF16)
    return high, low


def iota(shape, axis):
    return lax.broadcasted_iota(jnp.int32, shape, axis)


def rows_of(length):
    return iota((length, 1), 0)


def full_spec(array):
    rank = len(array.shape)
    return pl.BlockSpec(array.shape, lambda *_: (0,) * rank)


def item_spec(array):
    rank = len(array.shape)
    return pl.BlockSpec((1,) + array.shape[1:], lambda b: (b,) + (0,) * (rank - 1))


def layer_spec(array, layer):
    rank = len(array.shape)
    return pl.BlockSpec((1, 1) + array.shape[2:], lambda b: (layer, b) + (0,) * (rank - 2))


def weight_spec(array, layer):
    rank = len(array.shape)
    return pl.BlockSpec((1,) + array.shape[1:], lambda b: (layer,) + (0,) * (rank - 1))


def shape_of(shape, dtype=F32):
    return jax.ShapeDtypeStruct(shape, dtype)


def run(body, grid, ins, in_specs, outs, out_specs, scratch=(), micros=5, after=(), aliases=None, name=None):
    count, extra = len(ins), len(after)

    def wrapped(*refs):
        body(*refs[:count], *refs[count + extra :])

    return pl.pallas_call(
        wrapped,
        grid=grid,
        in_specs=list(in_specs) + [pl.BlockSpec(memory_space=pl.ANY)] * extra,
        out_specs=out_specs,
        out_shape=outs,
        scratch_shapes=list(scratch),
        compiler_params=pltpu.CompilerParams(vmem_limit_bytes=VMEM_BYTES),
        cost_estimate=pl.CostEstimate(
            flops=int(micros * COST), bytes_accessed=1 << 20, transcendentals=0
        ),
        input_output_aliases=aliases or {},
        name=name,
    )(*ins, *after)


def pair_rows(durations_row):
    return jnp.sum(durations_row, axis=1, keepdims=True) >> 1


def stats_body(mel_ref, dur_ref, out_ref):
    items, _, frames = mel_ref.shape
    lane = iota((1, frames), 1)
    count = jnp.zeros((1, 1), F32)
    sums = jnp.zeros((MEL, LANES), F32)
    squares = jnp.zeros((MEL, LANES), F32)
    for item in range(items):
        pair_count = pair_rows(dur_ref[item : item + 1, :])
        count = count + pair_count.astype(F32)
        values = jnp.where(lane < 2 * pair_count, mel_ref[item], 0.0)
        for part in range(frames // LANES):
            piece = values[:, part * LANES : (part + 1) * LANES]
            sums = sums + piece
            squares = squares + piece * piece
    place = iota((MEL, LANES), 1)
    table = jnp.zeros((MEL, LANES), F32)
    for side in range(2):
        chosen = (place & 1) == side
        for spot, held in ((side, sums), (2 + side, squares)):
            column = jnp.sum(jnp.where(chosen, held, 0.0), axis=1, keepdims=True)
            table = jnp.where(place == spot, column, table)
    table = jnp.concatenate([table, jnp.zeros((LANES - MEL, LANES), F32)], axis=0)
    rows = table.T[0:8]
    out_ref[...] = jnp.where(iota((8, LANES), 0) == 4, count, rows)


def read_stats(stats):
    total = stats[4:5, 0:1]
    sums = jnp.concatenate([stats[0:1], stats[1:2]], axis=1)
    squares = jnp.concatenate([stats[2:3], stats[3:4]], axis=1)
    center = sums / total
    variance = squares / total - center * center
    log_act = -0.5 * jnp.log(variance + 1e-06)
    return total, center, variance, log_act, jnp.exp(log_act)


def mix_places():
    row = rows_of(2 * LANES)
    col = iota((1, 2 * LANES), 1)
    row_lane = row & (LANES - 1)
    col_lane = col & (LANES - 1)
    upper = (row_lane >= MEL // 2).astype(jnp.int32)
    row_group = row_lane - upper * (MEL // 2)
    row_member = 2 * upper + (row >> 7)
    col_group = col_lane >> 1
    col_member = 2 * (col >> 7) + (col_lane & 1)
    match = (row_group == col_group) & (row_lane < MEL) & (col_lane < MEL)
    return row_member, col_member, match


def weights_body(
    mix_ref,
    qkv_ref,
    relk_ref,
    relv_ref,
    out_ref,
    prior_ref,
    start_ref,
    end_ref,
    res_ref,
    last_ref,
    mixm_ref,
    small_ref,
    qkv_pad_ref,
    relk_pad_ref,
    relv_pad_ref,
    out_pad_ref,
    wide_ref,
    prior_pad_ref,
    start_pad_ref,
    end_pad_ref,
    res_four_ref,
):
    row_member, col_member, match = mix_places()
    table = jnp.zeros((2 * LANES, 2 * LANES), F32)
    for i in range(4):
        column = jnp.zeros((2 * LANES, 1), F32)
        for j in range(4):
            column = jnp.where(row_member == j, mix_ref[i, j], column)
        table = jnp.where(col_member == i, column, table)
    mixm_ref[...] = jnp.where(match, table, 0.0)
    res_four_ref[: WLAYERS - 1] = res_ref[...]
    res_four_ref[WLAYERS - 1] = jnp.concatenate(
        [jnp.zeros((HID, HID), F32), last_ref[...].astype(F32)], axis=1
    ).astype(BF16)

    ri = iota((8, LANES), 0)
    ci = iota((8, LANES), 1)
    joined = jnp.where((ci == ri + 4) & (ri < 4), 1.0, 0.0).astype(F32)
    for i in range(4):
        for j in range(4):
            joined = jnp.where((ri == i) & (ci == j), mix_ref[i, j], joined)
    determinant = jnp.ones((1, 1), F32)
    for column in range(4):
        pivot = joined[column : column + 1, column : column + 1]
        determinant = determinant * pivot
        row_now = joined[column : column + 1, :] / pivot
        joined = joined - joined[:, column : column + 1] * row_now
        joined = jnp.where(ri == column, row_now, joined)
    turned = jnp.zeros((8, LANES), F32)
    for i in range(4):
        for j in range(4):
            turned = jnp.where((ri == j) & (ci == i), joined[i : i + 1, 4 + j : 5 + j], turned)
    small_ref[...] = jnp.where(ri == 4, determinant, turned)

    def select(count, wanted):
        return jnp.where(rows_of(count) == wanted, 1.0, 0.0).astype(BF16)

    place = iota((1, 6 * LANES), 1)
    lane = place & (LANES - 1)
    wanted = jnp.where(lane < HEAD, (place >> 7) * HEAD + lane, -1)
    qkv_pad_ref[...] = dot_nn(qkv_ref[...], select(3 * D, wanted)).astype(BF16)

    place = iota((1, 2 * LANES), 1)
    lane = place & (LANES - 1)
    wanted = jnp.where(lane < HEAD, (place >> 7) * HEAD + lane, -1)
    out_pad_ref[...] = dot_tn(select(D, wanted), out_ref[...]).astype(BF16)

    wanted = iota((1, LANES), 1) & (PERIOD - 1)
    repeat = select(2 * WINDOW + 1, wanted)
    pad = jnp.zeros((LANES, LANES - HEAD), F32)
    relk_pad_ref[...] = jnp.concatenate([dot_tn(repeat, relk_ref[...]), pad], axis=1).astype(BF16)
    relv_pad_ref[...] = jnp.concatenate([dot_tn(repeat, relv_ref[...]), pad], axis=1).astype(BF16)

    place = iota((1, 8 * LANES), 1)
    lane = place & (LANES - 1)
    group = (place >> 7) & 3
    fits = (lane < MEL) & ((lane & 1) == (place >> 9))
    wanted = jnp.where(fits, (group >> 1) * MEL + (group & 1) * (MEL // 2) + (lane >> 1), -1)
    wide = select(2 * MEL, wanted)
    wide_ref[...] = wide
    prior_pad_ref[...] = dot_tn(prior_ref[...], wide).astype(BF16)

    wanted = iota((1, LANES), 1)
    start_pad_ref[...] = dot_tn(select(MEL, wanted), start_ref[...]).astype(BF16)
    place = iota((1, 2 * LANES), 1)
    lane = place & (LANES - 1)
    wanted = jnp.where(lane < MEL, (place >> 7) * MEL + lane, -1)
    end_pad_ref[...] = dot_tn(end_ref[...], select(2 * MEL, wanted)).astype(BF16)


def text_rows(dur_ref):
    item = pl.program_id(0)
    return dur_ref[pl.ds(item, 1), :]


def text_inside(durations_row, length):
    tokens = jnp.sum((durations_row > 0).astype(jnp.int32), axis=1, keepdims=True)
    return rows_of(length) < tokens


def norm_parts(inputs):
    centered = inputs - jnp.mean(inputs, axis=1, keepdims=True)
    spread = jnp.mean(centered * centered, axis=1, keepdims=True)
    inverse = lax.rsqrt(spread + 1e-05)
    return centered * inverse, inverse


def norm_back(inputs, gain, gradient):
    unit, inverse = norm_parts(inputs)
    gain_grad = jnp.sum(gradient * unit, axis=0, keepdims=True)
    shift_grad = jnp.sum(gradient, axis=0, keepdims=True)
    scaled = gradient * gain
    mean_one = jnp.mean(scaled, axis=1, keepdims=True)
    mean_two = jnp.mean(scaled * unit, axis=1, keepdims=True)
    return inverse * (scaled - mean_one - unit * mean_two), gain_grad, shift_grad


def band_of(length):
    offset = iota((length, length), 1) - iota((length, length), 0)
    return (offset <= WINDOW) & (offset >= -WINDOW)


def turn_rows(values, left):
    pieces = []
    for block in range(values.shape[0] // 8):
        if left:
            first, stride = (WINDOW + 8 * (block & 1), PERIOD - 1)
        else:
            first, stride = (PERIOD - WINDOW + 8 * (block & 1), 1)
        piece = values[block * 8 : (block + 1) * 8]
        pieces.append(pltpu.roll(piece, first, 1, stride=stride, stride_axis=0))
    return jnp.concatenate(pieces, axis=0)


def band_gather(weights_low, band, folding):
    kept = jnp.where(band, weights_low, jnp.zeros_like(weights_low))
    return turn_rows(dot_nn(kept, folding), True).astype(BF16)


def band_spread(near, band):
    turned = turn_rows(near, False)
    count = band.shape[1] // LANES
    return jnp.where(band, jnp.concatenate([turned] * count, axis=1), 0.0)


def folding_of(length):
    same = (iota((length, LANES), 0) & (PERIOD - 1)) == (iota((length, LANES), 1) & (PERIOD - 1))
    return jnp.where(same, 1.0, 0.0).astype(BF16)


def one_turn(rel_pad):
    return jnp.where(rows_of(LANES) < PERIOD, rel_pad, jnp.zeros_like(rel_pad))


def shifted_rows(values, offset, period):
    if offset == 0:
        return values
    length = values.shape[0]
    moved = pltpu.roll(values, (-offset) % length, 0)
    place = rows_of(length) & (period - 1)
    keep = (place < period - offset) if offset > 0 else (place >= -offset)
    return jnp.where(keep, moved, 0.0)


def unfold_rows(values, kernel, period, reverse=False):
    half = kernel // 2
    steps = [step - half for step in range(kernel)]
    if reverse:
        steps = [-step for step in steps]
    return jnp.concatenate(
        [shifted_rows(values, step, period).astype(BF16) for step in steps], axis=1
    )


GELU_A = math.sqrt(2.0 / math.pi)
GELU_B = 0.044715


def gelu_tanh(values):
    return jnp.tanh(GELU_A * (values + GELU_B * values * values * values))


def text_blocks(dur_ref, items):
    item = pl.program_id(0) * items
    rows = [dur_ref[pl.ds(item + i, 1), :] for i in range(items)]
    inside = [text_inside(row, row.shape[1]) for row in rows]
    return rows, jnp.concatenate(inside, axis=0)


def token_table(tok_ref, item):
    tokens = tok_ref[pl.ds(item, 1), :]
    return jnp.where(iota((VOCAB, tokens.shape[1]), 0) == tokens, 1.0, 0.0).astype(BF16)


def encoder_body(
    tok_ref,
    dur_ref,
    emb_ref,
    qkv_ref,
    relk_ref,
    relv_ref,
    out_ref,
    gain_ref,
    shift_ref,
    ff1_ref,
    ff2_ref,
    gain_two_ref,
    shift_two_ref,
    prior_ref,
    emb_low_ref,
    proj_ref,
    att_ref,
    banded_ref,
    attend_ref,
    mixed_ref,
    normed_low_ref,
    filt_ref,
    activ_ref,
    summed_ref,
    enc_ref,
    expand_ref,
    expand_low_ref,
):
    group, length, _ = emb_low_ref.shape
    first = pl.program_id(0) * group
    durations, inside = text_blocks(dur_ref, group)

    def rows(item):
        return slice(item * length, (item + 1) * length)

    def keep(ref, values):
        for item in range(group):
            ref[item] = values[rows(item)]

    looked = [dot_tn(token_table(tok_ref, first + i), emb_ref[...]) for i in range(group)]
    embedded = jnp.where(inside, jnp.concatenate(looked, axis=0) * math.sqrt(D), 0.0)
    emb_low = embedded.astype(BF16)
    keep(emb_low_ref, emb_low)
    proj = dot_nn(emb_low, qkv_ref[...]).astype(BF16)
    keep(proj_ref, proj)
    band = band_of(length)
    folding = folding_of(length)
    relv = one_turn(relv_ref[...])
    attended = []
    for item in range(group):
        key_bias = jnp.where(durations[item] > 0, 0.0, -10000.0)
        parts = []
        for head in range(HEADS):
            query, key, value = [
                proj[rows(item), part * LANES : (part + 1) * LANES]
                for part in (head, HEADS + head, 2 * HEADS + head)
            ]
            near = band_spread(dot_nt(query, relk_ref[...]), band)
            scores = (dot_nt(query, key) + near) * (1.0 / math.sqrt(HEAD)) + key_bias
            raised = jnp.exp(scores - jnp.max(scores, axis=1, keepdims=True))
            attention = raised * (1.0 / jnp.sum(raised, axis=1, keepdims=True))
            low = attention.astype(BF16)
            att_ref[item, head] = low
            banded = band_gather(low, band, folding)
            banded_ref[item, head] = banded
            parts.append(dot_nn(low, value) + dot_nn(banded, relv))
        attended.append(jnp.concatenate(parts, axis=1))
    attend = jnp.concatenate(attended, axis=0).astype(BF16)
    keep(attend_ref, attend)
    mixed = embedded + dot_nn(attend, out_ref[...])
    keep(mixed_ref, mixed)
    unit, _ = norm_parts(mixed)
    normed = unit * gain_ref[...] + shift_ref[...]
    masked = jnp.where(inside, normed, 0.0)
    keep(normed_low_ref, masked.astype(BF16))
    filtered = dot_nn(unfold_rows(masked, KSIZE, length), ff1_ref[...])
    keep(filt_ref, filtered.astype(BF16))
    activ = jnp.where(inside, 0.5 * filtered * (1.0 + gelu_tanh(filtered)), 0.0)
    keep(activ_ref, activ.astype(BF16))
    second = dot_nt(unfold_rows(activ, KSIZE, length), ff2_ref[...])
    summed = normed + jnp.where(inside, second, 0.0)
    keep(summed_ref, summed)
    unit, _ = norm_parts(summed)
    encoded = jnp.where(inside, unit * gain_two_ref[...] + shift_two_ref[...], 0.0).astype(BF16)
    keep(enc_ref, encoded)
    prior = dot_nn(encoded, prior_ref[...])
    high, low = halves(prior)
    wide = prior.shape[1] // 2
    for item in range(group):
        for side in range(2):
            spot = slice(side * length, (side + 1) * length)
            columns = slice(side * wide, (side + 1) * wide)
            expand_ref[item, spot] = high[rows(item), columns]
            expand_low_ref[item, spot] = low[rows(item), columns]


def accumulate(ref, values, first):
    @pl.when(first)
    def _():
        ref[...] = values

    @pl.when(jnp.logical_not(first))
    def _():
        ref[...] = ref[...] + values


def align_of(durations_row, pairs):
    length = durations_row.shape[1]
    upper = jnp.where(iota((length, length), 0) <= iota((length, length), 1), 1.0, 0.0).astype(F32)
    wide = jnp.broadcast_to(durations_row.astype(F32), (8, length))
    ends = dot_nn(wide, upper, HIGH)[0:1].astype(jnp.int32)
    starts = ends - durations_row
    frame = 2 * rows_of(pairs)
    even = (frame >= starts) & (frame < ends)
    odd = (frame + 1 >= starts) & (frame + 1 < ends)
    both = jnp.concatenate([jnp.where(even, 1.0, 0.0), jnp.where(odd, 1.0, 0.0)], axis=1)
    return both.astype(BF16)


def encoder_back_body(
    tok_ref,
    dur_ref,
    flow_ref,
    enc_ref,
    summed_ref,
    filt_ref,
    activ_ref,
    normed_low_ref,
    mixed_ref,
    attend_ref,
    att_ref,
    banded_ref,
    proj_ref,
    emb_low_ref,
    wide_ref,
    ff1_ref,
    ff2_ref,
    gain_two_ref,
    prior_ref,
    qkv_ref,
    relk_ref,
    relv_ref,
    out_ref,
    gain_ref,
    place_ref,
    kept_ref,
    sent_ref,
    one_acc,
    two_acc,
    rest_acc,
    table_acc,
    qkv_acc,
    out_acc,
    relk_acc,
    relv_acc,
    prior_acc,
    norm_acc,
    sems,
):
    group, length, _ = emb_low_ref.shape
    step = pl.program_id(0)
    first = step == 0
    last = step == pl.num_programs(0) - 1
    durations, inside = text_blocks(dur_ref, group)
    mine = place_ref[0] & 1
    deals = []
    begin = 0
    for source in (one_acc, two_acc, rest_acc):
        half = source.shape[0] // 2
        for side, target in ((mine, kept_ref), (1 - mine, sent_ref)):
            deals.append(
                pltpu.make_async_copy(
                    source.at[pl.ds(pl.multiple_of(side * half, 8), half), :],
                    target.at[pl.ds(begin, half), :],
                    sems.at[len(deals)],
                )
            )
        begin += half
    everything = (one_acc, two_acc, table_acc, qkv_acc, out_acc, relk_acc, relv_acc, prior_acc, norm_acc)

    @pl.when(first)
    def _():
        for ref in everything:
            ref[...] = jnp.zeros_like(ref)

    def rows(item):
        return slice(item * length, (item + 1) * length)

    def whole(ref):
        return jnp.concatenate([ref[i] for i in range(group)], axis=0)

    def norm_sums(at, gain_grad, shift_grad):
        norm_acc[at : at + 1, :] = norm_acc[at : at + 1, :] + gain_grad
        norm_acc[at + 1 : at + 2, :] = norm_acc[at + 1 : at + 2, :] + shift_grad

    half = wide_ref.shape[1] // 2
    gathered = []
    for item in range(group):
        align = align_of(durations[item], flow_ref.shape[1])
        spread = dot_tn(align, flow_ref[item])
        pieces = []
        for side in range(2):
            pieces += halves(spread[side * length : (side + 1) * length])
        gathered.append(jnp.concatenate(pieces, axis=1))
    chosen = jnp.concatenate(
        [wide_ref[:, side * half : (side + 1) * half] for side in (0, 0, 1, 1)], axis=1
    )
    grad = dot_nt(jnp.concatenate(gathered, axis=0), chosen)
    prior_low = jnp.where(inside, grad, 0.0).astype(BF16)
    prior_acc[...] = prior_acc[...] + dot_tn(prior_low, whole(enc_ref))
    enc_grad = jnp.where(inside, dot_nn(prior_low, prior_ref[...]), 0.0)
    summed_grad, gain_grad, shift_grad = norm_back(whole(summed_ref), gain_two_ref[...], enc_grad)
    norm_sums(2, gain_grad, shift_grad)
    second = jnp.where(inside, summed_grad, 0.0)
    taps = unfold_rows(second, KSIZE, length, reverse=True)
    sums = dot_tn(taps, whole(activ_ref))
    for tap in range(KSIZE):
        for part in range(2):
            begin = (2 * tap + part) * D
            two_acc[begin : begin + D, :] = (
                two_acc[begin : begin + D, :]
                + sums[tap * D : (tap + 1) * D, part * WIDE : (part + 1) * WIDE]
            )
    activ_grad = dot_nn(
        taps,
        jnp.concatenate(
            [ff2_ref[:, tap * FILTER : (tap + 1) * FILTER] for tap in range(KSIZE)], axis=0
        ),
    )
    filtered = whole(filt_ref).astype(F32)
    tanh = gelu_tanh(filtered)
    slope = 0.5 * (1.0 + tanh) + 0.5 * filtered * (1.0 - tanh * tanh) * GELU_A * (
        1.0 + 3.0 * GELU_B * filtered * filtered
    )
    first_grad = jnp.where(inside, activ_grad * slope, 0.0)
    taps = unfold_rows(first_grad, KSIZE, length, reverse=True)
    sums = dot_tn(whole(normed_low_ref), taps)
    for tap in range(KSIZE):
        for part in range(2):
            begin = part * KSIZE * D + tap * D
            column = tap * FILTER + part * WIDE
            one_acc[begin : begin + D, :] = (
                one_acc[begin : begin + D, :] + sums[:, column : column + WIDE]
            )
    back = dot_nt(
        taps,
        jnp.concatenate([ff1_ref[tap * D : (tap + 1) * D, :] for tap in range(KSIZE)], axis=1),
    )

    @pl.when(last)
    def _():
        for copy in deals[:4]:
            copy.start()

    normed_grad = summed_grad + jnp.where(inside, back, 0.0)
    mixed_grad, gain_grad, shift_grad = norm_back(whole(mixed_ref), gain_ref[...], normed_grad)
    norm_sums(0, gain_grad, shift_grad)
    out_low = mixed_grad.astype(BF16)
    out_acc[...] = out_acc[...] + dot_tn(whole(attend_ref), out_low)
    weight = dot_nt(out_low, out_ref[...]).astype(BF16)
    band = band_of(length)
    folding = folding_of(length)
    relk = one_turn(relk_ref[...])
    projected = []
    relk_sum = relk_acc[...]
    relv_sum = relv_acc[...]
    for item in range(group):
        queries, keys, values = [], [], []
        for head in range(HEADS):
            query, key, value = [
                proj_ref[item, :, part * LANES : (part + 1) * LANES]
                for part in (head, HEADS + head, 2 * HEADS + head)
            ]
            mine = weight[rows(item), head * LANES : (head + 1) * LANES]
            near = band_spread(dot_nt(mine, relv_ref[...]), band)
            grad = dot_nt(mine, value) + near
            low = att_ref[item, head]
            attention = low.astype(F32)
            values.append(dot_tn(low, mine))
            relv_sum = relv_sum + dot_tn(banded_ref[item, head], mine)
            score = attention * (grad - jnp.sum(attention * grad, axis=1, keepdims=True))
            score_low = (score * (1.0 / math.sqrt(HEAD))).astype(BF16)
            band_grad = band_gather(score_low, band, folding)
            queries.append(dot_nn(score_low, key) + dot_nn(band_grad, relk))
            keys.append(dot_tn(score_low, query))
            relk_sum = relk_sum + dot_tn(band_grad, query)
        projected.append(jnp.concatenate(queries + keys + values, axis=1))
    relk_acc[...] = relk_sum
    relv_acc[...] = relv_sum
    proj_low = jnp.concatenate(projected, axis=0).astype(BF16)
    qkv_acc[...] = qkv_acc[...] + dot_tn(whole(emb_low_ref), proj_low)
    embed_grad = jnp.where(inside, mixed_grad + dot_nt(proj_low, qkv_ref[...]), 0.0) * math.sqrt(D)
    hot = jnp.concatenate(
        [token_table(tok_ref, step * group + item) for item in range(group)], axis=1
    )
    high, low = halves(embed_grad)
    table_acc[...] = table_acc[...] + dot_nn(
        jnp.concatenate([hot, hot], axis=1), jnp.concatenate([high, low], axis=0)
    )

    @pl.when(last)
    def _():
        def beside(left, right):
            return jnp.concatenate([left, right], axis=1)

        rest_acc[...] = jnp.zeros_like(rest_acc)
        packed = [qkv_acc[:, part * LANES : part * LANES + HEAD] for part in range(3 * HEADS)]
        side = D // 2
        rest_acc[:D, :] = jnp.concatenate(packed[:4], axis=1)
        rest_acc[D : D + side, :] = jnp.concatenate(
            [packed[4][:side], packed[5][:side], packed[4][side:], packed[5][side:]], axis=1
        )
        rest_acc[D + side : 2 * D, :] = beside(out_acc[:HEAD, :], out_acc[LANES : LANES + HEAD, :])
        rest_acc[ROW_TABLE : ROW_TABLE + MEL, :D] = table_acc[:MEL, :]
        rest_acc[ROW_TABLE : ROW_TABLE + VOCAB - MEL, D:] = table_acc[MEL:, :]
        rest_acc[ROW_PRIOR : ROW_PRIOR + MEL, :] = beside(prior_acc[:MEL, :], prior_acc[MEL:, :])
        rest_acc[ROW_NORM : ROW_NORM + 1, :] = beside(norm_acc[0:1, :], norm_acc[1:2, :])
        rest_acc[ROW_NORM + 1 : ROW_NORM + 2, :] = beside(norm_acc[2:3, :], norm_acc[3:4, :])
        rest_acc[ROW_REL : ROW_REL + PERIOD, :LANES] = relk_acc[:PERIOD, :]
        rest_acc[ROW_REL : ROW_REL + PERIOD, LANES : 2 * LANES] = relv_acc[:PERIOD, :]
        for copy in deals[4:]:
            copy.start()
        for copy in deals:
            copy.wait()


def split_pairs(mel_ref, rows_ref):
    frames = mel_ref.shape[2]
    pairs = frames // 2
    rows_ref[:, :MEL] = mel_ref[0].T
    pad = jnp.zeros((pairs, LANES - MEL), F32)
    even = rows_ref[pl.ds(0, pairs, stride=2), :][:, :MEL]
    odd = rows_ref[pl.ds(1, pairs, stride=2), :][:, :MEL]
    return jnp.concatenate([even, pad, odd, pad], axis=1)


def gates_of(pre):
    return jnp.tanh(pre[:, :HID]), 1.0 / (1.0 + jnp.exp(-pre[:, HID:]))


def dot_three(values, table, back=False):
    high, low = halves(values)
    table_high, table_low = halves(table)
    left = jnp.concatenate([high, low, high], axis=1)
    if back:
        return dot_nt(left, jnp.concatenate([table_high, table_high, table_low], axis=1))
    return dot_nn(left, jnp.concatenate([table_high, table_high, table_low], axis=0))


STEP_POST = WLAYERS + 1
STEPS = 2 * WLAYERS + 2


def decoder_body(
    mel_ref,
    dur_ref,
    expand_ref,
    expand_low_ref,
    stats_ref,
    mixm_ref,
    start_ref,
    win_ref,
    wres_ref,
    wend_ref,
    place_ref,
    kept_ref,
    sent_ref,
    last_kept_ref,
    last_sent_ref,
    flow_ref,
    ngrad_ref,
    normal,
    passive_low,
    hidden_low,
    pre,
    hidden,
    skip,
    active,
    skip_low,
    passive_grad,
    gated,
    part,
    spread,
    wide,
    unit,
    rows,
    end_acc,
    start_acc,
    mix_acc,
    tail,
    high,
    low,
    flow,
    sums,
    sems,
):
    step = pl.program_id(0)
    items, _, frames = mel_ref.shape
    pairs = frames // 2
    conv = WKER * HID
    fetch = [
        pltpu.make_async_copy(expand_ref, high, sems.at[0]),
        pltpu.make_async_copy(expand_low_ref, low, sems.at[1]),
    ]
    write = pltpu.make_async_copy(flow, flow_ref, sems.at[2])
    mine = place_ref[0] & 1

    def deal(source, rows_each, targets, begin, first_sem):
        return [
            pltpu.make_async_copy(
                source.at[pl.ds(pl.multiple_of(side * rows_each, 8), rows_each), :],
                target.at[pl.ds(begin, rows_each), :],
                sems.at[first_sem + i],
            )
            for i, (side, target) in enumerate(((mine, targets[0]), (1 - mine, targets[1])))
        ]

    half = UNIT // 2
    deals = [deal(unit.at[0], half, (last_kept_ref, last_sent_ref), 0, 3)]
    for above in range(1, WLAYERS):
        begin = (WLAYERS - 1 - above) * half
        deals.append(deal(unit.at[above & 1], half, (kept_ref, sent_ref), begin, 3 + 2 * above))
    last_deal = deal(
        tail, TAIL // 2, (kept_ref, sent_ref), (WLAYERS - 1) * half, 3 + 2 * WLAYERS
    )

    def inside_item(item):
        return rows_of(pairs) < pair_rows(dur_ref[pl.ds(item, 1), :])

    def span(item):
        return pl.ds(pl.multiple_of(item * pairs, pairs), pairs)

    def each(body, count=items):
        def one(item, carry):
            body(item)
            return carry

        lax.fori_loop(0, count, one, 0)

    both = 2 if items % 2 == 0 else 1
    blocks = items // both
    block_rows = both * pairs

    def block_span(block):
        return pl.ds(pl.multiple_of(block * block_rows, block_rows), block_rows)

    def inside_block(block):
        return jnp.concatenate([inside_item(block * both + i) for i in range(both)], axis=0)

    @pl.when(step == 0)
    def _():
        for copy in fetch:
            copy.start()
        _, center, _, _, scale = read_stats(stats_ref[...])

        def one(item):
            inside = inside_item(item)
            rows[:, :MEL] = mel_ref[item].T
            pad = jnp.zeros((pairs, LANES - MEL), F32)
            even = rows[pl.ds(0, pairs, stride=2), :][:, :MEL]
            odd = rows[pl.ds(1, pairs, stride=2), :][:, :MEL]
            values = jnp.concatenate([even, pad, odd, pad], axis=1)
            normalized = jnp.where(inside, (values - center) * scale, 0.0)
            normal[item] = normalized
            turned = dot_three(normalized, mixm_ref[...])
            passive = turned[:, :LANES]
            passive_grad[item] = passive
            active[item] = turned[:, LANES:]
            low_now = passive.astype(BF16)
            passive_low[item] = low_now
            hidden[span(item), :] = jnp.where(inside, dot_nn(low_now, start_ref[...]), 0.0)
            skip[span(item), :] = jnp.zeros((pairs, HID), F32)

        each(one)

    @pl.when((step >= 1) & (step <= WLAYERS))
    def _():
        layer = step - 1

        def one(block):
            here = block_span(block)
            state = hidden[here, :]
            hidden_low[layer, here, :] = state.astype(BF16)
            pre_gate = dot_nn(unfold_rows(state, WKER, pairs), win_ref[0])
            pre[layer, here, :] = pre_gate.astype(BF16)
            tanh, gate = gates_of(pre_gate)
            sums = dot_nn((tanh * gate).astype(BF16), wres_ref[layer])
            hidden[here, :] = jnp.where(inside_block(block), state + sums[:, :HID], 0.0)
            skip[here, :] = skip[here, :] + sums[:, HID:]

        each(one, blocks)

    @pl.when(step == STEP_POST)
    def _():
        for copy in fetch:
            copy.wait()
        total, _, _, _, _ = read_stats(stats_ref[...])
        unit_grad = 1.0 / (2 * MEL * total)
        end_acc[...] = jnp.zeros_like(end_acc)
        sums[...] = jnp.zeros_like(sums)

        def one(item):
            inside = inside_item(item)
            output_low = jnp.where(inside, skip[span(item), :], 0.0).astype(BF16)
            coupled = jnp.where(inside, dot_nn(output_low, wend_ref[...]), 0.0)
            shift_part = coupled[:, :LANES]
            log_part = coupled[:, LANES:]
            growth = jnp.exp(log_part)
            moving = active[item]
            moved = jnp.where(inside, shift_part + growth * moving, 0.0)
            align = align_of(dur_ref[pl.ds(item, 1), :], pairs)
            prior = dot_nn(align, high[item]) + dot_nn(align, low[item])
            latent = jnp.concatenate([passive_grad[item], moved], axis=1)
            gap = latent - prior[:, : 2 * LANES]
            log_scales = prior[:, 2 * LANES :]
            scaled = jnp.exp(-2.0 * log_scales) * gap
            square = scaled * gap
            terms = jnp.where(inside, log_scales + 0.5 * square, 0.0)
            term = jnp.sum(terms, axis=0, keepdims=True)
            nll = term[:, :LANES] + term[:, LANES:] - jnp.sum(log_part, axis=0, keepdims=True)
            sums[4:5, :] = sums[4:5, :] + nll
            latent_grad = jnp.where(inside, unit_grad * scaled, 0.0)
            scale_grad = jnp.where(inside, unit_grad * (1.0 - square), 0.0)
            flow[item] = jnp.concatenate([-latent_grad, scale_grad], axis=1).astype(BF16)
            passive_grad[item] = latent_grad[:, :LANES]
            moved_grad = latent_grad[:, LANES:]
            active_grad = moved_grad * growth
            log_grad = jnp.where(inside, active_grad * moving - unit_grad, 0.0)
            active[item] = active_grad
            coupled_low = jnp.concatenate([moved_grad, log_grad], axis=1).astype(BF16)
            end_acc[...] = end_acc[...] + dot_tn(coupled_low, output_low)
            skip_grad = jnp.where(inside, dot_nt(coupled_low, wend_ref[...]), 0.0)
            skip_low[span(item), :] = skip_grad.astype(BF16)
            hidden[span(item), :] = jnp.zeros((pairs, HID), F32)

        each(one)
        write.start()

    @pl.when(step > STEP_POST)
    def _():
        layer = STEPS - 1 - step
        for tap in range(WKER):
            wide[:, tap * 2 * HID : (tap + 1) * 2 * HID] = win_ref[
                0, tap * HID : (tap + 1) * HID, :
            ]

        def one(block):
            here = block_span(block)
            tanh, gate = gates_of(pre[layer, here, :].astype(F32))
            gated[here, :] = (tanh * gate).astype(BF16)
            kept = hidden[here, :]
            left = jnp.concatenate([kept, skip_low[here, :].astype(F32)], axis=1).astype(BF16)
            part[here, :] = left
            gated_grad = dot_nt(left, wres_ref[layer])
            tanh_grad = gated_grad * gate * (1.0 - tanh * tanh)
            gate_grad = gated_grad * tanh * gate * (1.0 - gate)
            pre_grad = jnp.concatenate([tanh_grad, gate_grad], axis=1)
            taps = unfold_rows(pre_grad, WKER, pairs, reverse=True)
            spread[here, :] = taps
            back = kept + dot_nt(taps, wide[...])
            hidden[here, :] = jnp.where(inside_block(block), back, 0.0)

        each(one, blocks)
        for later in range(WLAYERS - 2):

            @pl.when(layer == later)
            def _(later=later):
                for copy in deals[later + 2]:
                    copy.wait()

        parity = layer & 1
        found = dot_tn(hidden_low[layer], spread[...])
        for tap in range(WKER):
            unit[parity, tap * HID : (tap + 1) * HID, :] = found[
                :, tap * 2 * HID : (tap + 1) * 2 * HID
            ]
        unit[parity, conv:, :] = dot_tn(gated[...], part[...])

        @pl.when(layer == WLAYERS - 1)
        def _():
            side = (WLAYERS - 1) & 1
            unit[side, conv : conv + MEL, :HID] = end_acc[:MEL, :]
            unit[side, conv + MEL : conv + 2 * MEL, :HID] = end_acc[LANES : LANES + MEL, :]

        for now in range(WLAYERS):

            @pl.when(layer == now)
            def _(now=now):
                for copy in deals[now]:
                    copy.start()

    @pl.when(step == STEPS - 1)
    def _():
        start_acc[...] = jnp.zeros_like(start_acc)
        mix_acc[...] = jnp.zeros_like(mix_acc)

        def one(item):
            start_low = hidden[span(item), :].astype(BF16)
            start_acc[...] = start_acc[...] + dot_tn(passive_low[item], start_low)
            turned_passive = passive_grad[item] + dot_nt(start_low, start_ref[...])
            turned_grad = jnp.concatenate([turned_passive, active[item]], axis=1)
            normalized = normal[item]
            mix_acc[...] = mix_acc[...] + dot_tn(
                normalized.astype(BF16), turned_grad.astype(BF16)
            )
            normal_grad = dot_three(turned_grad, mixm_ref[...], back=True)
            normal_grad = jnp.where(inside_item(item), normal_grad, 0.0)
            ngrad_ref[item] = normal_grad
            one_sum = jnp.sum(normal_grad, axis=0, keepdims=True)
            two_sum = jnp.sum(normal_grad * normalized, axis=0, keepdims=True)
            for at, found in ((0, one_sum), (2, two_sum)):
                sums[at : at + 1, :] = sums[at : at + 1, :] + found[:, :LANES]
                sums[at + 1 : at + 2, :] = sums[at + 1 : at + 2, :] + found[:, LANES:]

        each(one)
        tail[...] = jnp.zeros_like(tail)
        cut = MEL // 2
        tail[:cut, :] = jnp.concatenate([start_acc[:cut, :], start_acc[cut:MEL, :]], axis=1)
        row_member, col_member, match = mix_places()
        kept = jnp.where(match, mix_acc[...], 0.0)
        ri = iota((8, LANES), 0)
        ci = iota((8, LANES), 1)
        mixed = jnp.zeros((8, LANES), F32)
        for i in range(4):
            column = jnp.sum(jnp.where(col_member == i, kept, 0.0), axis=1, keepdims=True)
            for j in range(4):
                entry = jnp.sum(jnp.where(row_member == j, column, 0.0), axis=0, keepdims=True)
                mixed = jnp.where((ri == i) & (ci == j), entry, mixed)
        tail[cut : cut + 8, :LANES] = mixed
        tail[cut : cut + 8, LANES : 2 * LANES] = sums[...]
        for copy in last_deal:
            copy.start()
        for copy in (*last_deal, *deals[0], *deals[1], write):
            copy.wait()


def frames_body(
    mel_ref, dur_ref, ngrad_ref, stats_ref, sums_ref, small_ref, out_ref, loss_ref, rows_ref
):
    pairs = mel_ref.shape[2] // 2
    inside = rows_of(pairs) < pair_rows(text_rows(dur_ref))
    total, center, variance, log_act, scale = read_stats(stats_ref[...])
    unit = 1.0 / (2 * MEL * total)
    sums = sums_ref[...]
    spot = iota((1, 2 * LANES), 1) & (LANES - 1)
    log_sum = jnp.sum(jnp.where(spot < MEL, log_act, 0.0), axis=1, keepdims=True)
    nll = jnp.sum(sums[4:5], axis=1, keepdims=True)
    log_det = jnp.log(small_ref[4:5, 0:1])
    loss = (nll - total * log_sum - total * (MEL // 2) * log_det) * unit
    loss_ref[...] = loss + 0.5 * math.log(2.0 * math.pi)
    one = jnp.concatenate([sums[0:1], sums[1:2]], axis=1)
    two = jnp.concatenate([sums[2:3], sums[3:4]], axis=1)
    log_grad = two - unit * total
    var_grad = -0.5 * log_grad / (variance + 1e-06)
    center_grad = -scale * one - 2.0 * center * var_grad
    values = split_pairs(mel_ref, rows_ref)
    grads = ngrad_ref[0] * scale + (2.0 * values * var_grad + center_grad) / total
    grads = jnp.where(inside, grads, 0.0) * (2 * MEL * total)
    rows_ref[pl.ds(0, pairs, stride=2), :] = grads[:, :LANES]
    rows_ref[pl.ds(1, pairs, stride=2), :] = grads[:, LANES:]
    out_ref[0] = rows_ref[...].T[:MEL, :]


def swap(values, bit, devices):
    return lax.ppermute(values, "dp", [(i, i ^ bit) for i in range(devices)])


def swap_half(unit, devices):
    kept, sent = unit
    return kept, swap(sent, 1, devices)


def digits(devices, shift=1):
    found = []
    while (1 << shift) < devices:
        radix = 4 if (1 << (shift + 2)) <= devices else 2
        found.append((shift, radix))
        shift += 2 if radix == 4 else 1
    return found


def whole_vmem(count):
    return [pl.BlockSpec(memory_space=pltpu.VMEM)] * count


def call_whole(body, place, ins, outs, scratch, after, micros, name):
    return run(
        body,
        (),
        [place, *ins],
        [pl.BlockSpec(memory_space=pltpu.SMEM)] + whole_vmem(len(ins)),
        outs,
        whole_vmem(len(outs)),
        scratch,
        micros=micros,
        after=after,
        name=name,
    )


def hop_out(jobs, place, after=()):
    ins = []
    outs = []
    scratch = []
    plans = []
    for units, shift, radix in jobs:
        plan = []
        begin = 0
        for unit in units:
            row = unit[0].shape[0] // radix
            plan.append((len(ins), len(unit), row, begin))
            ins += unit
            begin += row
        plans.append((plan, len(outs), shift, radix))
        outs += [shape_of((begin, WIDE))] * radix
        aligned = all(row % 8 == 0 for _, _, row, _ in plan)
        scratch.append(pltpu.VMEM((1, 8, LANES) if aligned else (radix, begin, WIDE), F32))
    n_in, n_out = len(ins), len(outs)

    def body(place_ref, *refs):
        out_refs = refs[n_in : n_in + n_out]
        tables = refs[n_in + n_out :]
        for (plan, at, shift, radix), table in zip(plans, tables):
            digit = (place_ref[0] >> shift) & (radix - 1)
            if all(row % 8 == 0 for _, _, row, _ in plan):
                for step in range(radix):
                    for first, count, row, begin in plan:
                        span = pl.ds(pl.multiple_of((digit ^ step) * row, 8), row)
                        value = refs[first][span, :]
                        for extra in range(1, count):
                            value = value + refs[first + extra][span, :]
                        out_refs[at + step][begin : begin + row, :] = value
                continue
            for first, count, row, begin in plan:
                for part in range(radix):
                    span = slice(part * row, (part + 1) * row)
                    value = refs[first][span, :]
                    for extra in range(1, count):
                        value = value + refs[first + extra][span, :]
                    table[part, begin : begin + row, :] = value
            for step in range(radix):
                out_refs[at + step][...] = table[digit ^ step]

    found = call_whole(body, place, ins, outs, scratch, after, 3, "hop_out")
    return [found[at : at + radix] for _, at, _, radix in plans]


def hop_in(jobs, place, after=()):
    ins = []
    outs = []
    plans = []
    for parts, shift in jobs:
        plans.append((len(ins), len(parts), shift))
        ins += parts
        outs.append(shape_of((len(parts), *parts[0].shape)))
    n_in = len(ins)

    def body(place_ref, *refs):
        for (first, radix, shift), out in zip(plans, refs[n_in:]):
            digit = (place_ref[0] >> shift) & (radix - 1)
            for step in range(radix):
                out[digit ^ step] = refs[first + step][...]

    return call_whole(body, place, ins, outs, (), after, 2, "hop_in")


def add_parts(jobs, place, after=()):
    ins = [part for parts in jobs for part in parts]
    outs = [shape_of(parts[0].shape) for parts in jobs]
    n_in = len(ins)

    def body(place_ref, *refs):
        at = 0
        for parts, out in zip(jobs, refs[n_in:]):
            value = refs[at][...]
            for extra in range(at + 1, at + len(parts)):
                value = value + refs[extra][...]
            out[...] = value
            at += len(parts)

    return call_whole(body, place, ins, outs, (), after, 1, "add_parts")


def send_parts(parts, shift, devices):
    return [parts[0]] + [
        swap(part, step << shift, devices) for step, part in enumerate(parts) if step > 0
    ]


def spread_level(units, level, place, devices, after=()):
    shift, radix = digits(devices)[level]
    parts = hop_out([(units, shift, radix)], place, after)[0]
    return send_parts(parts, shift, devices)


def gather_level(part, level, place, devices, after=()):
    shift, radix = digits(devices)[level]
    return hop_in([(send_parts([part] * radix, shift, devices), shift)], place, after)[0]


def last_level(part, devices):
    shift, radix = digits(devices)[0]
    return send_parts([part.reshape(-1, WIDE)] * radix, shift, devices)


def table_parts(place_ref, shift, radix, mine_refs, other_refs, table):
    digit = (place_ref[0] >> shift) & (radix - 1)
    core = place_ref[0] & 1
    for step in range(radix):
        table[core, digit ^ step] = mine_refs[step][...]
        table[1 - core, digit ^ step] = other_refs[step][...]


def segments(begin, count, rows):
    found = []
    at = begin
    while at < begin + count:
        part, row = divmod(at, rows)
        size = min(rows - row, begin + count - at)
        found.append((part, row, size, at - begin))
        at += size
    return found


def unpack_upper_body(
    shift,
    radix,
    place_ref,
    small_ref,
    *refs,
):
    mine, other = refs[:radix], refs[radix : 2 * radix]
    in_ref, res_ref, last_ref, end_ref, start_ref, mix_ref, sums_ref, table, tail, sems = refs[2 * radix :]
    table_parts(place_ref, shift, radix, mine, other, table)
    rows = table.shape[2]
    conv = WKER * HID
    half = UNIT // 2
    copies = []

    def move(core, begin, count, target, at):
        for part, row, size, place in segments(begin, count, rows):
            copies.append(
                pltpu.make_async_copy(
                    table.at[core, part, pl.ds(row, size), :],
                    target.at[pl.ds(at + place, size), :],
                    sems.at[len(copies)],
                )
            )

    for layer in range(1, WLAYERS):
        begin = (WLAYERS - 1 - layer) * half
        move(0, begin, half, in_ref.at[layer], 0)
        move(1, begin, conv - half, in_ref.at[layer], half)
        if layer < WLAYERS - 1:
            move(1, begin + conv - half, HID, res_ref.at[layer], 0)
    for copy in copies:
        copy.start()
    for part, row, size, at in segments(conv - half, HID, rows):
        values = table[1, part, row : row + size, :]
        last_ref[at : at + size, :] = values[:, HID:]
        end_ref[at : at + size, :] = values[:, :HID]
    for core in range(2):
        for part, row, size, at in segments((WLAYERS - 1) * half, TAIL // 2, rows):
            begin = core * (TAIL // 2) + at
            tail[begin : begin + size, :] = table[core, part, row : row + size, :]
    cut = MEL // 2
    start_ref[:cut, :] = tail[:cut, :HID]
    start_ref[cut:, :] = tail[:cut, HID:]
    mix_ref[...] = tail[cut : cut + 8, :LANES] - small_ref[...] / 4.0
    sums_ref[...] = tail[cut : cut + 8, LANES : 2 * LANES]
    for copy in copies:
        copy.wait()


def unpack_upper(parts, other, place, small, devices, after):
    shift, radix = digits(devices)[0]
    vmem = pl.BlockSpec(memory_space=pltpu.VMEM)
    anywhere = pl.BlockSpec(memory_space=pl.ANY)
    outs = [
        shape_of((WLAYERS, WKER * HID, 2 * HID)),
        shape_of((WLAYERS - 1, HID, 2 * HID)),
        shape_of((HID, HID)),
        shape_of((HID, HID)),
        shape_of((MEL, HID)),
        shape_of((8, LANES)),
        shape_of((8, LANES)),
    ]
    return run(
        functools.partial(unpack_upper_body, shift, radix),
        (),
        [place, small, *parts, *other],
        [pl.BlockSpec(memory_space=pltpu.SMEM)] + [vmem] * (1 + 2 * radix),
        outs,
        [anywhere] * 2 + [vmem] * 5,
        [
            pltpu.VMEM((2, radix, *parts[0].shape), F32),
            pltpu.VMEM((TAIL, WIDE), F32),
            pltpu.SemaphoreType.DMA((40,)),
        ],
        micros=5,
        after=after,
        name="unpack_upper",
    )


def unpack_lower_body(shift, radix, place_ref, in_given, res_given, *refs):
    mine, other = refs[:radix], refs[radix : 2 * radix]
    (
        in_ref,
        res_ref,
        one_ref,
        two_ref,
        table_ref,
        qkv_ref,
        out_ref,
        relk_ref,
        relv_ref,
        prior_ref,
        *norm_refs,
        table,
        rest,
        sems,
    ) = refs[2 * radix :]
    table_parts(place_ref, shift, radix, mine, other, table)
    conv = WKER * HID
    half = UNIT // 2
    quarter = half // radix
    copies = []
    for core in range(2):
        for digit in range(radix):
            at = core * half + digit * quarter
            pieces = [(0, max(0, min(quarter, conv - at)), in_ref, at)]
            pieces.append((pieces[0][1], quarter - pieces[0][1], res_ref, at + pieces[0][1] - conv))
            for row, size, target, to in pieces:
                if size:
                    copies.append(
                        pltpu.make_async_copy(
                            table.at[core, digit, pl.ds(row, size), :],
                            target.at[0, pl.ds(to, size), :],
                            sems.at[len(copies)],
                        )
                    )
    for copy in copies:
        copy.start()
    rows = table.shape[2] - quarter

    def read(core, begin, count):
        return [
            (table[core, part, quarter + row : quarter + row + size, :], at)
            for part, row, size, at in segments(begin, count, rows)
        ]

    for core in range(2):
        for values, at in read(core, 0, half):
            one_ref[at : at + values.shape[0], core * WIDE : (core + 1) * WIDE] = values
        for third in range(KSIZE):
            block = core * KSIZE + third
            for values, at in read(core, half + third * D, D):
                two_ref[at : at + values.shape[0], block * WIDE : (block + 1) * WIDE] = values
        for values, at in read(core, 2 * half, REST // 2):
            begin = core * (REST // 2) + at
            rest[begin : begin + values.shape[0], :] = values
    side = D // 2
    qkv_ref[:, :WIDE] = rest[:D, :]
    qkv_ref[:side, WIDE:] = rest[D : D + side, :D]
    qkv_ref[side:, WIDE:] = rest[D : D + side, D:]
    out_ref[:side, :] = rest[D + side : 2 * D, :D]
    out_ref[side:, :] = rest[D + side : 2 * D, D:]
    table_ref[:MEL, :] = rest[ROW_TABLE : ROW_TABLE + MEL, :D]
    table_ref[MEL:, :] = rest[ROW_TABLE : ROW_TABLE + VOCAB - MEL, D:]
    prior_ref[:MEL, :] = rest[ROW_PRIOR : ROW_PRIOR + MEL, :D]
    prior_ref[MEL:, :] = rest[ROW_PRIOR : ROW_PRIOR + MEL, D:]
    relk_ref[...] = rest[ROW_REL : ROW_REL + 2 * WINDOW + 1, :HEAD]
    relv_ref[...] = rest[ROW_REL : ROW_REL + 2 * WINDOW + 1, LANES : LANES + HEAD]
    for i, ref in enumerate(norm_refs):
        row = rest[ROW_NORM + (i >> 1) : ROW_NORM + (i >> 1) + 1, :]
        ref[...] = row[:, (i & 1) * D : (i & 1) * D + D].reshape(D)
    for copy in copies:
        copy.wait()


def unpack_lower(parts, other, place, in_grad, res_grad, devices):
    shift, radix = digits(devices)[0]
    vmem = pl.BlockSpec(memory_space=pltpu.VMEM)
    anywhere = pl.BlockSpec(memory_space=pl.ANY)
    reach = 2 * WINDOW + 1
    outs = [
        shape_of(in_grad.shape),
        shape_of(res_grad.shape),
        shape_of((KSIZE * D, FILTER)),
        shape_of((D, KSIZE * FILTER)),
        shape_of((VOCAB, D)),
        shape_of((D, 3 * D)),
        shape_of((D, D)),
        shape_of((reach, HEAD)),
        shape_of((reach, HEAD)),
        shape_of((2 * MEL, D)),
        *[shape_of((D,))] * 4,
    ]
    return run(
        functools.partial(unpack_lower_body, shift, radix),
        (),
        [place, in_grad, res_grad, *parts, *other],
        [pl.BlockSpec(memory_space=pltpu.SMEM)] + [anywhere] * 2 + [vmem] * (2 * radix),
        outs,
        [anywhere] * 2 + [vmem] * (len(outs) - 2),
        [
            pltpu.VMEM((2, radix, *parts[0].shape), F32),
            pltpu.VMEM((REST, WIDE), F32),
            pltpu.SemaphoreType.DMA((2 * radix + 2,)),
        ],
        micros=5,
        aliases={1: 0, 2: 1},
        name="unpack_lower",
    )


def on_device(
    devices,
    token_ids,
    durations,
    mel_frames,
    embedding,
    w_qkv,
    rel_key,
    rel_value,
    w_out,
    attn_gain,
    attn_shift,
    w_ff1,
    w_ff2,
    ffn_gain,
    ffn_shift,
    w_prior,
    w_mix,
    w_start,
    w_in,
    w_res,
    w_skip_last,
    w_end,
):
    items, length = token_ids.shape
    frames = mel_frames.shape[1]
    mel_frames = mel_frames.transpose(0, 2, 1)
    ff2_t = w_ff2.T
    prior_t = w_prior.T
    end_t = w_end.T
    pairs = frames // 2
    grid = (items,)
    place = lax.axis_index("dp").reshape(1).astype(jnp.int32)

    def halves_of(rows):
        return [shape_of((rows // 2, WIDE))] * 2

    vmem = pl.BlockSpec(memory_space=pltpu.VMEM)
    smem = pl.BlockSpec(memory_space=pltpu.SMEM)
    gain_one = attn_gain.reshape(1, D)
    shift_one = attn_shift.reshape(1, D)
    gain_two = ffn_gain.reshape(1, D)
    shift_two = ffn_shift.reshape(1, D)

    stats = run(
        stats_body, (), [mel_frames, durations], [vmem] * 2, shape_of((8, LANES)), vmem, name="stats"
    )
    stats_steps = digits(devices, 0)
    shift, radix = stats_steps[0]
    local_stats = stats
    stats = sum(send_parts([stats] * radix, shift, devices))

    prepared = [
        shape_of((2 * LANES, 2 * LANES)),
        shape_of((8, LANES)),
        shape_of((D, 6 * LANES), BF16),
        shape_of((LANES, LANES), BF16),
        shape_of((LANES, LANES), BF16),
        shape_of((2 * LANES, D), BF16),
        shape_of((2 * MEL, 8 * LANES), BF16),
        shape_of((D, 8 * LANES), BF16),
        shape_of((LANES, HID), BF16),
        shape_of((HID, 2 * LANES), BF16),
        shape_of((WLAYERS, HID, 2 * HID), BF16),
    ]
    (
        mixm,
        small,
        qkv_pad,
        relk_pad,
        relv_pad,
        out_pad,
        wide,
        prior_pad,
        start_pad,
        end_pad,
        res_four,
    ) = run(
        weights_body,
        (),
        [w_mix, w_qkv, rel_key, rel_value, w_out, prior_t, w_start, end_t, w_res, w_skip_last],
        [smem] + [vmem] * 9,
        prepared,
        [vmem] * len(prepared),
        after=(local_stats,),
        name="weights",
    )

    group = 2 if items % 2 == 0 else 1

    def group_spec(array):
        rank = len(array.shape)
        return pl.BlockSpec((group,) + array.shape[1:], lambda b: (b,) + (0,) * (rank - 1))

    ins = [
        token_ids,
        durations,
        embedding,
        qkv_pad,
        relk_pad,
        relv_pad,
        out_pad,
        gain_one,
        shift_one,
        w_ff1,
        ff2_t,
        gain_two,
        shift_two,
        prior_pad,
    ]
    outs = [
        shape_of((items, length, D), BF16),
        shape_of((items, length, 6 * LANES), BF16),
        shape_of((items, HEADS, length, length), BF16),
        shape_of((items, HEADS, length, LANES), BF16),
        shape_of((items, length, 2 * LANES), BF16),
        shape_of((items, length, D)),
        shape_of((items, length, D), BF16),
        shape_of((items, length, FILTER), BF16),
        shape_of((items, length, FILTER), BF16),
        shape_of((items, length, D)),
        shape_of((items, length, D), BF16),
        shape_of((items, 2 * length, 4 * LANES), BF16),
        shape_of((items, 2 * length, 4 * LANES), BF16),
    ]
    (
        emb_low,
        proj,
        attention,
        banded,
        attend,
        mixed,
        normed_low,
        filtered,
        activ,
        summed,
        encoded,
        expand,
        expand_low,
    ) = run(
        encoder_body,
        (items // group,),
        ins,
        [full_spec(a) for a in ins],
        outs,
        [group_spec(a) for a in outs],
        micros=20,
        after=(stats,),
        name="encoder",
    )
    for shift, radix in stats_steps[1:]:
        stats = sum(send_parts([stats] * radix, shift, devices))

    ins = [mel_frames, durations, expand, expand_low, stats, mixm, start_pad, w_in, res_four, end_pad, place]
    kinds = [full_spec] * 10
    in_specs = [kind(a) for kind, a in zip(kinds, ins)] + [smem]
    in_specs[2] = in_specs[3] = pl.BlockSpec(memory_space=pl.ANY)
    in_specs[7] = pl.BlockSpec(
        (1,) + w_in.shape[1:],
        lambda s: (jnp.where(s <= STEP_POST, jnp.clip(s - 1, 0, WLAYERS - 1), STEPS - 1 - s), 0, 0),
    )
    dealt = ((WLAYERS - 1) * UNIT + TAIL) // 2
    outs = [
        *[shape_of((dealt, WIDE))] * 2,
        *halves_of(UNIT),
        shape_of((items, pairs, 4 * LANES), BF16),
        shape_of((items, pairs, 2 * LANES)),
    ]
    out_specs = [pl.BlockSpec(memory_space=pl.ANY)] * 5 + [full_spec(outs[5])]
    count = items * pairs
    kept, sent, last_kept, last_sent, flow, normal_grad = run(
        decoder_body,
        (STEPS,),
        ins,
        in_specs,
        outs,
        out_specs,
        [
            pltpu.VMEM((items, pairs, 2 * LANES), F32),
            pltpu.VMEM((items, pairs, LANES), BF16),
            pltpu.VMEM((WLAYERS, count, HID), BF16),
            pltpu.VMEM((WLAYERS, count, 2 * HID), BF16),
            pltpu.VMEM((count, HID), F32),
            pltpu.VMEM((count, HID), F32),
            pltpu.VMEM((items, pairs, LANES), F32),
            pltpu.VMEM((count, HID), BF16),
            pltpu.VMEM((items, pairs, LANES), F32),
            pltpu.VMEM((count, HID), BF16),
            pltpu.VMEM((count, 2 * HID), BF16),
            pltpu.VMEM((count, WKER * 2 * HID), BF16),
            pltpu.VMEM((HID, WKER * 2 * HID), BF16),
            pltpu.VMEM((2, UNIT, WIDE), F32),
            pltpu.VMEM((frames, LANES), F32),
            pltpu.VMEM((2 * LANES, HID), F32),
            pltpu.VMEM((LANES, HID), F32),
            pltpu.VMEM((2 * LANES, 2 * LANES), F32),
            pltpu.VMEM((TAIL, WIDE), F32),
            pltpu.VMEM(expand.shape, BF16),
            pltpu.VMEM(expand.shape, BF16),
            pltpu.VMEM((items, pairs, 4 * LANES), BF16),
            pltpu.VMEM((8, LANES), F32),
            pltpu.SemaphoreType.DMA((5 + 2 * WLAYERS,)),
        ],
        micros=80,
        name="decoder",
    )
    recv = swap(sent, 1, devices)
    upper = spread_level([[kept, recv]], 0, place, devices)
    last_recv = swap(last_sent, 1, devices)

    ins = [
        token_ids,
        durations,
        flow,
        encoded,
        summed,
        filtered,
        activ,
        normed_low,
        mixed,
        attend,
        attention,
        banded,
        proj,
        emb_low,
        wide,
        w_ff1,
        ff2_t,
        gain_two,
        prior_t,
        qkv_pad,
        relk_pad,
        relv_pad,
        out_pad,
        gain_one,
        place,
    ]
    kinds = [full_spec] * 2 + [group_spec] * 12 + [full_spec] * 10
    outs = halves_of(2 * UNIT + REST)
    fed_kept, fed_sent = run(
        encoder_back_body,
        (items // group,),
        ins,
        [kind(a) for kind, a in zip(kinds, ins)] + [smem],
        outs,
        [pl.BlockSpec(memory_space=pl.ANY)] * 2,
        [
            pltpu.VMEM((UNIT, WIDE), F32),
            pltpu.VMEM((UNIT, WIDE), F32),
            pltpu.VMEM((REST, WIDE), F32),
            pltpu.VMEM((VOCAB, D), F32),
            pltpu.VMEM((D, 6 * LANES), F32),
            pltpu.VMEM((2 * LANES, D), F32),
            pltpu.VMEM((LANES, LANES), F32),
            pltpu.VMEM((LANES, LANES), F32),
            pltpu.VMEM((2 * MEL, D), F32),
            pltpu.VMEM((8, D), F32),
            pltpu.SemaphoreType.DMA((6,)),
        ],
        after=(upper[0],),
        micros=30,
        name="encoder_back",
    )
    levels = len(digits(devices))
    upper, fed_sent, fed_kept = lax.optimization_barrier((upper, fed_sent, fed_kept))
    fed_recv = swap(fed_sent, 1, devices)
    for level in range(1, levels):
        upper = spread_level([upper], level, place, devices, (fed_kept,))
    units = [[last_kept, last_recv], [fed_kept, fed_recv]]
    lower = spread_level(units, 0, place, devices, (upper[0],))
    upper = add_parts([upper], place, (lower[0],))[0]
    for level in reversed(range(1, levels)):
        upper = gather_level(upper, level, place, devices, (upper,))
    upper_parts = last_level(upper, devices)
    for level in range(1, levels):
        lower = spread_level([lower], level, place, devices, (upper,))
    lower = add_parts([lower], place)[0]
    for level in reversed(range(1, levels)):
        lower = gather_level(lower, level, place, devices)
    upper_parts, lower = lax.optimization_barrier((upper_parts, lower))
    upper_other = [swap(part, 1, devices) for part in upper_parts]
    lower, upper_other = lax.optimization_barrier((lower, upper_other))
    lower_parts = last_level(lower, devices)
    in_grad, res_grad, last_grad, end_grad, start_grad, mix_grad, sums = unpack_upper(
        upper_parts, upper_other, place, small, devices, ()
    )
    ins = [mel_frames, durations, normal_grad, stats, sums, small]
    kinds = [item_spec, full_spec, item_spec, full_spec, full_spec, full_spec]
    mel_grad, loss = run(
        frames_body,
        grid,
        ins,
        [kind(a) for kind, a in zip(kinds, ins)],
        [shape_of(mel_frames.shape), shape_of((1, 1))],
        [item_spec(mel_frames), pl.BlockSpec((1, 1), lambda b: (0, 0))],
        [pltpu.VMEM((frames, LANES), F32)],
        name="frames",
    )

    lower_parts = [lax.optimization_barrier((part, mel_grad))[0] for part in lower_parts]
    lower_other = [swap(part, 1, devices) for part in lower_parts]
    (
        in_grad,
        res_grad,
        ff1_grad,
        ff2_grad,
        table_grad,
        qkv_grad,
        out_grad,
        relk_grad,
        relv_grad,
        prior_grad,
        *norm_grads,
    ) = unpack_lower(lower_parts, lower_other, place, in_grad, res_grad, devices)

    return (
        loss.reshape(()),
        mel_grad.transpose(0, 2, 1),
        table_grad,
        qkv_grad,
        relk_grad,
        relv_grad,
        out_grad,
        norm_grads[0],
        norm_grads[1],
        ff1_grad,
        ff2_grad.T,
        norm_grads[2],
        norm_grads[3],
        prior_grad.T,
        mix_grad[:4, :4],
        start_grad,
        in_grad,
        res_grad,
        last_grad,
        end_grad[: 2 * MEL].T,
    )


def solution(mesh):
    devices = mesh.shape["dp"]
    placed = (P("dp", None), P("dp", None), P("dp", None, None)) + (P(),) * 18
    return jax.shard_map(
        functools.partial(on_device, devices),
        mesh=mesh,
        in_specs=placed,
        out_specs=(P(), P("dp", None, None)) + (P(),) * 18,
        check_vma=False,
    )
```

```python
import functools
import math

import jax
import jax.numpy as jnp
from jax import lax
from jax.experimental import pallas as pl
from jax.experimental.pallas import tpu as pltpu
from jax.sharding import PartitionSpec as P

D = 192
HEADS = 2
HEAD = 96
LANES = 128
FILTER = 768
MEL = 80
HID = 192
VOCAB = 148
KSIZE = 3
WKER = 5
WLAYERS = 4
WINDOW = 4
PERIOD = 16

F32 = jnp.float32
BF16 = jnp.bfloat16
HIGH = lax.Precision.HIGHEST
VMEM_BYTES = 58 * 1024 * 1024
WIDE = 384
UNIT = 1152
REST = 640
TAIL = 128
COST = 1.15e9
ROW_TABLE = 2 * D
ROW_PRIOR = ROW_TABLE + MEL
ROW_NORM = ROW_PRIOR + MEL
ROW_REL = ROW_NORM + 8


def contract(first_op, second_op, dims, precision=None):
    return lax.dot_general(
        first_op, second_op, (dims, ((), ())), preferred_element_type=F32, precision=precision
    )


def dot_nn(first_op, second_op, precision=None):
    return contract(first_op, second_op, ((1,), (0,)), precision)


def dot_nt(first_op, second_op, precision=None):
    return contract(first_op, second_op, ((1,), (1,)), precision)


def dot_tn(first_op, second_op, precision=None):
    return contract(first_op, second_op, ((0,), (0,)), precision)


def halves(values):
    high = values.astype(BF16)
    low = (values - high.astype(F32)).astype(BF16)
    return high, low


def iota(shape, axis):
    return lax.broadcasted_iota(jnp.int32, shape, axis)


def rows_of(length):
    return iota((length, 1), 0)


def full_spec(array):
    rank = len(array.shape)
    return pl.BlockSpec(array.shape, lambda *_: (0,) * rank)


def item_spec(array):
    rank = len(array.shape)
    return pl.BlockSpec((1,) + array.shape[1:], lambda b: (b,) + (0,) * (rank - 1))


def layer_spec(array, layer):
    rank = len(array.shape)
    return pl.BlockSpec((1, 1) + array.shape[2:], lambda b: (layer, b) + (0,) * (rank - 2))


def weight_spec(array, layer):
    rank = len(array.shape)
    return pl.BlockSpec((1,) + array.shape[1:], lambda b: (layer,) + (0,) * (rank - 1))


def shape_of(shape, dtype=F32):
    return jax.ShapeDtypeStruct(shape, dtype)


def run(body, grid, ins, in_specs, outs, out_specs, scratch=(), micros=5, after=(), aliases=None, name=None):
    count, extra = len(ins), len(after)

    def wrapped(*refs):
        body(*refs[:count], *refs[count + extra :])

    return pl.pallas_call(
        wrapped,
        grid=grid,
        in_specs=list(in_specs) + [pl.BlockSpec(memory_space=pl.ANY)] * extra,
        out_specs=out_specs,
        out_shape=outs,
        scratch_shapes=list(scratch),
        compiler_params=pltpu.CompilerParams(vmem_limit_bytes=VMEM_BYTES),
        cost_estimate=pl.CostEstimate(
            flops=int(micros * COST), bytes_accessed=1 << 20, transcendentals=0
        ),
        input_output_aliases=aliases or {},
        name=name,
    )(*ins, *after)


def pair_rows(durations_row):
    return jnp.sum(durations_row, axis=1, keepdims=True) >> 1


def stats_body(mel_ref, dur_ref, out_ref):
    items, _, frames = mel_ref.shape
    lane = iota((1, frames), 1)
    count = jnp.zeros((1, 1), F32)
    sums = jnp.zeros((MEL, LANES), F32)
    squares = jnp.zeros((MEL, LANES), F32)
    for item in range(items):
        pair_count = pair_rows(dur_ref[item : item + 1, :])
        count = count + pair_count.astype(F32)
        values = jnp.where(lane < 2 * pair_count, mel_ref[item], 0.0)
        for part in range(frames // LANES):
            piece = values[:, part * LANES : (part + 1) * LANES]
            sums = sums + piece
            squares = squares + piece * piece
    place = iota((MEL, LANES), 1)
    table = jnp.zeros((MEL, LANES), F32)
    for side in range(2):
        chosen = (place & 1) == side
        for spot, held in ((side, sums), (2 + side, squares)):
            column = jnp.sum(jnp.where(chosen, held, 0.0), axis=1, keepdims=True)
            table = jnp.where(place == spot, column, table)
    table = jnp.concatenate([table, jnp.zeros((LANES - MEL, LANES), F32)], axis=0)
    rows = table.T[0:8]
    out_ref[...] = jnp.where(iota((8, LANES), 0) == 4, count, rows)


def read_stats(stats):
    total = stats[4:5, 0:1]
    sums = jnp.concatenate([stats[0:1], stats[1:2]], axis=1)
    squares = jnp.concatenate([stats[2:3], stats[3:4]], axis=1)
    center = sums / total
    variance = squares / total - center * center
    log_act = -0.5 * jnp.log(variance + 1e-06)
    return total, center, variance, log_act, jnp.exp(log_act)


def mix_places():
    row = rows_of(2 * LANES)
    col = iota((1, 2 * LANES), 1)
    row_lane = row & (LANES - 1)
    col_lane = col & (LANES - 1)
    upper = (row_lane >= MEL // 2).astype(jnp.int32)
    row_group = row_lane - upper * (MEL // 2)
    row_member = 2 * upper + (row >> 7)
    col_group = col_lane >> 1
    col_member = 2 * (col >> 7) + (col_lane & 1)
    match = (row_group == col_group) & (row_lane < MEL) & (col_lane < MEL)
    return row_member, col_member, match


def weights_body(
    mix_ref,
    qkv_ref,
    relk_ref,
    relv_ref,
    out_ref,
    prior_ref,
    start_ref,
    end_ref,
    res_ref,
    last_ref,
    mixm_ref,
    small_ref,
    qkv_pad_ref,
    relk_pad_ref,
    relv_pad_ref,
    out_pad_ref,
    wide_ref,
    prior_pad_ref,
    start_pad_ref,
    end_pad_ref,
    res_four_ref,
):
    row_member, col_member, match = mix_places()
    table = jnp.zeros((2 * LANES, 2 * LANES), F32)
    for i in range(4):
        column = jnp.zeros((2 * LANES, 1), F32)
        for j in range(4):
            column = jnp.where(row_member == j, mix_ref[i, j], column)
        table = jnp.where(col_member == i, column, table)
    mixm_ref[...] = jnp.where(match, table, 0.0)
    res_four_ref[: WLAYERS - 1] = res_ref[...]
    res_four_ref[WLAYERS - 1] = jnp.concatenate(
        [jnp.zeros((HID, HID), F32), last_ref[...].astype(F32)], axis=1
    ).astype(BF16)

    ri = iota((8, LANES), 0)
    ci = iota((8, LANES), 1)
    joined = jnp.where((ci == ri + 4) & (ri < 4), 1.0, 0.0).astype(F32)
    for i in range(4):
        for j in range(4):
            joined = jnp.where((ri == i) & (ci == j), mix_ref[i, j], joined)
    determinant = jnp.ones((1, 1), F32)
    for column in range(4):
        pivot = joined[column : column + 1, column : column + 1]
        determinant = determinant * pivot
        row_now = joined[column : column + 1, :] / pivot
        joined = joined - joined[:, column : column + 1] * row_now
        joined = jnp.where(ri == column, row_now, joined)
    turned = jnp.zeros((8, LANES), F32)
    for i in range(4):
        for j in range(4):
            turned = jnp.where((ri == j) & (ci == i), joined[i : i + 1, 4 + j : 5 + j], turned)
    small_ref[...] = jnp.where(ri == 4, determinant, turned)

    def select(count, wanted):
        return jnp.where(rows_of(count) == wanted, 1.0, 0.0).astype(BF16)

    place = iota((1, 6 * LANES), 1)
    lane = place & (LANES - 1)
    wanted = jnp.where(lane < HEAD, (place >> 7) * HEAD + lane, -1)
    qkv_pad_ref[...] = dot_nn(qkv_ref[...], select(3 * D, wanted)).astype(BF16)

    place = iota((1, 2 * LANES), 1)
    lane = place & (LANES - 1)
    wanted = jnp.where(lane < HEAD, (place >> 7) * HEAD + lane, -1)
    out_pad_ref[...] = dot_tn(select(D, wanted), out_ref[...]).astype(BF16)

    wanted = iota((1, LANES), 1) & (PERIOD - 1)
    repeat = select(2 * WINDOW + 1, wanted)
    pad = jnp.zeros((LANES, LANES - HEAD), F32)
    relk_pad_ref[...] = jnp.concatenate([dot_tn(repeat, relk_ref[...]), pad], axis=1).astype(BF16)
    relv_pad_ref[...] = jnp.concatenate([dot_tn(repeat, relv_ref[...]), pad], axis=1).astype(BF16)

    place = iota((1, 8 * LANES), 1)
    lane = place & (LANES - 1)
    group = (place >> 7) & 3
    fits = (lane < MEL) & ((lane & 1) == (place >> 9))
    wanted = jnp.where(fits, (group >> 1) * MEL + (group & 1) * (MEL // 2) + (lane >> 1), -1)
    wide = select(2 * MEL, wanted)
    wide_ref[...] = wide
    prior_pad_ref[...] = dot_tn(prior_ref[...], wide).astype(BF16)

    wanted = iota((1, LANES), 1)
    start_pad_ref[...] = dot_tn(select(MEL, wanted), start_ref[...]).astype(BF16)
    place = iota((1, 2 * LANES), 1)
    lane = place & (LANES - 1)
    wanted = jnp.where(lane < MEL, (place >> 7) * MEL + lane, -1)
    end_pad_ref[...] = dot_tn(end_ref[...], select(2 * MEL, wanted)).astype(BF16)


def text_rows(dur_ref):
    item = pl.program_id(0)
    return dur_ref[pl.ds(item, 1), :]


def text_inside(durations_row, length):
    tokens = jnp.sum((durations_row > 0).astype(jnp.int32), axis=1, keepdims=True)
    return rows_of(length) < tokens


def norm_parts(inputs):
    centered = inputs - jnp.mean(inputs, axis=1, keepdims=True)
    spread = jnp.mean(centered * centered, axis=1, keepdims=True)
    inverse = lax.rsqrt(spread + 1e-05)
    return centered * inverse, inverse


def norm_back(inputs, gain, gradient):
    unit, inverse = norm_parts(inputs)
    gain_grad = jnp.sum(gradient * unit, axis=0, keepdims=True)
    shift_grad = jnp.sum(gradient, axis=0, keepdims=True)
    scaled = gradient * gain
    mean_one = jnp.mean(scaled, axis=1, keepdims=True)
    mean_two = jnp.mean(scaled * unit, axis=1, keepdims=True)
    return inverse * (scaled - mean_one - unit * mean_two), gain_grad, shift_grad


def band_of(length):
    offset = iota((length, length), 1) - iota((length, length), 0)
    return (offset <= WINDOW) & (offset >= -WINDOW)


def turn_rows(values, left):
    pieces = []
    for block in range(values.shape[0] // 8):
        if left:
            first, stride = (WINDOW + 8 * (block & 1), PERIOD - 1)
        else:
            first, stride = (PERIOD - WINDOW + 8 * (block & 1), 1)
        piece = values[block * 8 : (block + 1) * 8]
        pieces.append(pltpu.roll(piece, first, 1, stride=stride, stride_axis=0))
    return jnp.concatenate(pieces, axis=0)


def band_gather(weights_low, band, folding):
    kept = jnp.where(band, weights_low, jnp.zeros_like(weights_low))
    return turn_rows(dot_nn(kept, folding), True).astype(BF16)


def band_spread(near, band):
    turned = turn_rows(near, False)
    count = band.shape[1] // LANES
    return jnp.where(band, jnp.concatenate([turned] * count, axis=1), 0.0)


def folding_of(length):
    same = (iota((length, LANES), 0) & (PERIOD - 1)) == (iota((length, LANES), 1) & (PERIOD - 1))
    return jnp.where(same, 1.0, 0.0).astype(BF16)


def one_turn(rel_pad):
    return jnp.where(rows_of(LANES) < PERIOD, rel_pad, jnp.zeros_like(rel_pad))


def shifted_rows(values, offset, period):
    if offset == 0:
        return values
    length = values.shape[0]
    moved = pltpu.roll(values, (-offset) % length, 0)
    place = rows_of(length) & (period - 1)
    keep = (place < period - offset) if offset > 0 else (place >= -offset)
    return jnp.where(keep, moved, 0.0)


def unfold_rows(values, kernel, period, reverse=False):
    half = kernel // 2
    steps = [step - half for step in range(kernel)]
    if reverse:
        steps = [-step for step in steps]
    return jnp.concatenate(
        [shifted_rows(values, step, period).astype(BF16) for step in steps], axis=1
    )


GELU_A = math.sqrt(2.0 / math.pi)
GELU_B = 0.044715


def gelu_tanh(values):
    return jnp.tanh(GELU_A * (values + GELU_B * values * values * values))


def text_blocks(dur_ref, items):
    item = pl.program_id(0) * items
    rows = [dur_ref[pl.ds(item + i, 1), :] for i in range(items)]
    inside = [text_inside(row, row.shape[1]) for row in rows]
    return rows, jnp.concatenate(inside, axis=0)


def token_table(tok_ref, item):
    tokens = tok_ref[pl.ds(item, 1), :]
    return jnp.where(iota((VOCAB, tokens.shape[1]), 0) == tokens, 1.0, 0.0).astype(BF16)


def encoder_body(
    tok_ref,
    dur_ref,
    emb_ref,
    qkv_ref,
    relk_ref,
    relv_ref,
    out_ref,
    gain_ref,
    shift_ref,
    ff1_ref,
    ff2_ref,
    gain_two_ref,
    shift_two_ref,
    prior_ref,
    emb_low_ref,
    proj_ref,
    att_ref,
    banded_ref,
    attend_ref,
    mixed_ref,
    normed_low_ref,
    filt_ref,
    activ_ref,
    summed_ref,
    enc_ref,
    expand_ref,
    expand_low_ref,
):
    group, length, _ = emb_low_ref.shape
    first = pl.program_id(0) * group
    durations, inside = text_blocks(dur_ref, group)

    def rows(item):
        return slice(item * length, (item + 1) * length)

    def keep(ref, values):
        for item in range(group):
            ref[item] = values[rows(item)]

    looked = [dot_tn(token_table(tok_ref, first + i), emb_ref[...]) for i in range(group)]
    embedded = jnp.where(inside, jnp.concatenate(looked, axis=0) * math.sqrt(D), 0.0)
    emb_low = embedded.astype(BF16)
    keep(emb_low_ref, emb_low)
    proj = dot_nn(emb_low, qkv_ref[...]).astype(BF16)
    keep(proj_ref, proj)
    band = band_of(length)
    folding = folding_of(length)
    relv = one_turn(relv_ref[...])
    attended = []
    for item in range(group):
        key_bias = jnp.where(durations[item] > 0, 0.0, -10000.0)
        parts = []
        for head in range(HEADS):
            query, key, value = [
                proj[rows(item), part * LANES : (part + 1) * LANES]
                for part in (head, HEADS + head, 2 * HEADS + head)
            ]
            near = band_spread(dot_nt(query, relk_ref[...]), band)
            scores = (dot_nt(query, key) + near) * (1.0 / math.sqrt(HEAD)) + key_bias
            raised = jnp.exp(scores - jnp.max(scores, axis=1, keepdims=True))
            attention = raised * (1.0 / jnp.sum(raised, axis=1, keepdims=True))
            low = attention.astype(BF16)
            att_ref[item, head] = low
            banded = band_gather(low, band, folding)
            banded_ref[item, head] = banded
            parts.append(dot_nn(low, value) + dot_nn(banded, relv))
        attended.append(jnp.concatenate(parts, axis=1))
    attend = jnp.concatenate(attended, axis=0).astype(BF16)
    keep(attend_ref, attend)
    mixed = embedded + dot_nn(attend, out_ref[...])
    keep(mixed_ref, mixed)
    unit, _ = norm_parts(mixed)
    normed = unit * gain_ref[...] + shift_ref[...]
    masked = jnp.where(inside, normed, 0.0)
    keep(normed_low_ref, masked.astype(BF16))
    filtered = dot_nn(unfold_rows(masked, KSIZE, length), ff1_ref[...])
    keep(filt_ref, filtered.astype(BF16))
    activ = jnp.where(inside, 0.5 * filtered * (1.0 + gelu_tanh(filtered)), 0.0)
    keep(activ_ref, activ.astype(BF16))
    second = dot_nt(unfold_rows(activ, KSIZE, length), ff2_ref[...])
    summed = normed + jnp.where(inside, second, 0.0)
    keep(summed_ref, summed)
    unit, _ = norm_parts(summed)
    encoded = jnp.where(inside, unit * gain_two_ref[...] + shift_two_ref[...], 0.0).astype(BF16)
    keep(enc_ref, encoded)
    prior = dot_nn(encoded, prior_ref[...])
    high, low = halves(prior)
    wide = prior.shape[1] // 2
    for item in range(group):
        for side in range(2):
            spot = slice(side * length, (side + 1) * length)
            columns = slice(side * wide, (side + 1) * wide)
            expand_ref[item, spot] = high[rows(item), columns]
            expand_low_ref[item, spot] = low[rows(item), columns]


def accumulate(ref, values, first):
    @pl.when(first)
    def _():
        ref[...] = values

    @pl.when(jnp.logical_not(first))
    def _():
        ref[...] = ref[...] + values


def align_of(durations_row, pairs):
    length = durations_row.shape[1]
    upper = jnp.where(iota((length, length), 0) <= iota((length, length), 1), 1.0, 0.0).astype(F32)
    high = (durations_row >> 5).astype(F32)
    low = (durations_row & 31).astype(F32)
    both = jnp.where(iota((8, length), 0) == 0, high, low).astype(BF16)
    sums = dot_nn(both, upper.astype(BF16))
    ends = (32.0 * sums[0:1] + sums[1:2]).astype(jnp.int32)
    starts = ends - durations_row
    frame = 2 * rows_of(pairs)
    even = (frame >= starts) & (frame < ends)
    odd = (frame + 1 >= starts) & (frame + 1 < ends)
    both = jnp.concatenate([jnp.where(even, 1.0, 0.0), jnp.where(odd, 1.0, 0.0)], axis=1)
    return both.astype(BF16)


def encoder_back_body(
    tok_ref,
    dur_ref,
    flow_ref,
    enc_ref,
    summed_ref,
    filt_ref,
    activ_ref,
    normed_low_ref,
    mixed_ref,
    attend_ref,
    att_ref,
    banded_ref,
    proj_ref,
    emb_low_ref,
    wide_ref,
    ff1_ref,
    ff2_ref,
    gain_two_ref,
    prior_ref,
    qkv_ref,
    relk_ref,
    relv_ref,
    out_ref,
    gain_ref,
    place_ref,
    kept_ref,
    sent_ref,
    one_acc,
    two_acc,
    rest_acc,
    table_acc,
    qkv_acc,
    out_acc,
    relk_acc,
    relv_acc,
    prior_acc,
    norm_acc,
    sems,
):
    group, length, _ = emb_low_ref.shape
    step = pl.program_id(0)
    first = step == 0
    last = step == pl.num_programs(0) - 1
    durations, inside = text_blocks(dur_ref, group)
    mine = place_ref[0] & 1
    deals = []
    begin = 0
    for source in (one_acc, two_acc, rest_acc):
        half = source.shape[0] // 2
        for side, target in ((mine, kept_ref), (1 - mine, sent_ref)):
            deals.append(
                pltpu.make_async_copy(
                    source.at[pl.ds(pl.multiple_of(side * half, 8), half), :],
                    target.at[pl.ds(begin, half), :],
                    sems.at[len(deals)],
                )
            )
        begin += half
    everything = (one_acc, two_acc, table_acc, qkv_acc, out_acc, relk_acc, relv_acc, prior_acc, norm_acc)

    @pl.when(first)
    def _():
        for ref in everything:
            ref[...] = jnp.zeros_like(ref)

    def rows(item):
        return slice(item * length, (item + 1) * length)

    def whole(ref):
        return jnp.concatenate([ref[i] for i in range(group)], axis=0)

    def norm_sums(at, gain_grad, shift_grad):
        norm_acc[at : at + 1, :] = norm_acc[at : at + 1, :] + gain_grad
        norm_acc[at + 1 : at + 2, :] = norm_acc[at + 1 : at + 2, :] + shift_grad

    half = wide_ref.shape[1] // 2
    gathered = []
    for item in range(group):
        align = align_of(durations[item], flow_ref.shape[1])
        spread = dot_tn(align, flow_ref[item])
        pieces = []
        for side in range(2):
            pieces += halves(spread[side * length : (side + 1) * length])
        gathered.append(jnp.concatenate(pieces, axis=1))
    chosen = jnp.concatenate(
        [wide_ref[:, side * half : (side + 1) * half] for side in (0, 0, 1, 1)], axis=1
    )
    grad = dot_nt(jnp.concatenate(gathered, axis=0), chosen)
    prior_low = jnp.where(inside, grad, 0.0).astype(BF16)
    prior_acc[...] = prior_acc[...] + dot_tn(prior_low, whole(enc_ref))
    enc_grad = jnp.where(inside, dot_nn(prior_low, prior_ref[...]), 0.0)
    summed_grad, gain_grad, shift_grad = norm_back(whole(summed_ref), gain_two_ref[...], enc_grad)
    norm_sums(2, gain_grad, shift_grad)
    second = jnp.where(inside, summed_grad, 0.0)
    taps = unfold_rows(second, KSIZE, length, reverse=True)
    sums = dot_tn(taps, whole(activ_ref))
    for tap in range(KSIZE):
        for part in range(2):
            begin = (2 * tap + part) * D
            two_acc[begin : begin + D, :] = (
                two_acc[begin : begin + D, :]
                + sums[tap * D : (tap + 1) * D, part * WIDE : (part + 1) * WIDE]
            )
    activ_grad = dot_nn(
        taps,
        jnp.concatenate(
            [ff2_ref[:, tap * FILTER : (tap + 1) * FILTER] for tap in range(KSIZE)], axis=0
        ),
    )
    filtered = whole(filt_ref).astype(F32)
    tanh = gelu_tanh(filtered)
    slope = 0.5 * (1.0 + tanh) + 0.5 * filtered * (1.0 - tanh * tanh) * GELU_A * (
        1.0 + 3.0 * GELU_B * filtered * filtered
    )
    first_grad = jnp.where(inside, activ_grad * slope, 0.0)
    taps = unfold_rows(first_grad, KSIZE, length, reverse=True)
    sums = dot_tn(whole(normed_low_ref), taps)
    for tap in range(KSIZE):
        for part in range(2):
            begin = part * KSIZE * D + tap * D
            column = tap * FILTER + part * WIDE
            one_acc[begin : begin + D, :] = (
                one_acc[begin : begin + D, :] + sums[:, column : column + WIDE]
            )
    back = dot_nt(
        taps,
        jnp.concatenate([ff1_ref[tap * D : (tap + 1) * D, :] for tap in range(KSIZE)], axis=1),
    )

    @pl.when(last)
    def _():
        for copy in deals[:4]:
            copy.start()

    normed_grad = summed_grad + jnp.where(inside, back, 0.0)
    mixed_grad, gain_grad, shift_grad = norm_back(whole(mixed_ref), gain_ref[...], normed_grad)
    norm_sums(0, gain_grad, shift_grad)
    out_low = mixed_grad.astype(BF16)
    out_acc[...] = out_acc[...] + dot_tn(whole(attend_ref), out_low)
    weight = dot_nt(out_low, out_ref[...]).astype(BF16)
    band = band_of(length)
    folding = folding_of(length)
    relk = one_turn(relk_ref[...])
    projected = []
    relk_sum = relk_acc[...]
    relv_sum = relv_acc[...]
    for item in range(group):
        queries, keys, values = [], [], []
        for head in range(HEADS):
            query, key, value = [
                proj_ref[item, :, part * LANES : (part + 1) * LANES]
                for part in (head, HEADS + head, 2 * HEADS + head)
            ]
            mine = weight[rows(item), head * LANES : (head + 1) * LANES]
            near = band_spread(dot_nt(mine, relv_ref[...]), band)
            grad = dot_nt(mine, value) + near
            low = att_ref[item, head]
            attention = low.astype(F32)
            values.append(dot_tn(low, mine))
            relv_sum = relv_sum + dot_tn(banded_ref[item, head], mine)
            score = attention * (grad - jnp.sum(attention * grad, axis=1, keepdims=True))
            score_low = (score * (1.0 / math.sqrt(HEAD))).astype(BF16)
            band_grad = band_gather(score_low, band, folding)
            queries.append(dot_nn(score_low, key) + dot_nn(band_grad, relk))
            keys.append(dot_tn(score_low, query))
            relk_sum = relk_sum + dot_tn(band_grad, query)
        projected.append(jnp.concatenate(queries + keys + values, axis=1))
    relk_acc[...] = relk_sum
    relv_acc[...] = relv_sum
    proj_low = jnp.concatenate(projected, axis=0).astype(BF16)
    qkv_acc[...] = qkv_acc[...] + dot_tn(whole(emb_low_ref), proj_low)
    embed_grad = jnp.where(inside, mixed_grad + dot_nt(proj_low, qkv_ref[...]), 0.0) * math.sqrt(D)
    hot = jnp.concatenate(
        [token_table(tok_ref, step * group + item) for item in range(group)], axis=1
    )
    high, low = halves(embed_grad)
    table_acc[...] = table_acc[...] + dot_nn(
        jnp.concatenate([hot, hot], axis=1), jnp.concatenate([high, low], axis=0)
    )

    @pl.when(last)
    def _():
        def beside(left, right):
            return jnp.concatenate([left, right], axis=1)

        rest_acc[...] = jnp.zeros_like(rest_acc)
        packed = [qkv_acc[:, part * LANES : part * LANES + HEAD] for part in range(3 * HEADS)]
        side = D // 2
        rest_acc[:D, :] = jnp.concatenate(packed[:4], axis=1)
        rest_acc[D : D + side, :] = jnp.concatenate(
            [packed[4][:side], packed[5][:side], packed[4][side:], packed[5][side:]], axis=1
        )
        rest_acc[D + side : 2 * D, :] = beside(out_acc[:HEAD, :], out_acc[LANES : LANES + HEAD, :])
        rest_acc[ROW_TABLE : ROW_TABLE + MEL, :D] = table_acc[:MEL, :]
        rest_acc[ROW_TABLE : ROW_TABLE + VOCAB - MEL, D:] = table_acc[MEL:, :]
        rest_acc[ROW_PRIOR : ROW_PRIOR + MEL, :] = beside(prior_acc[:MEL, :], prior_acc[MEL:, :])
        rest_acc[ROW_NORM : ROW_NORM + 1, :] = beside(norm_acc[0:1, :], norm_acc[1:2, :])
        rest_acc[ROW_NORM + 1 : ROW_NORM + 2, :] = beside(norm_acc[2:3, :], norm_acc[3:4, :])
        rest_acc[ROW_REL : ROW_REL + PERIOD, :LANES] = relk_acc[:PERIOD, :]
        rest_acc[ROW_REL : ROW_REL + PERIOD, LANES : 2 * LANES] = relv_acc[:PERIOD, :]
        for copy in deals[4:]:
            copy.start()
        for copy in deals:
            copy.wait()


def split_pairs(mel_ref, rows_ref):
    frames = mel_ref.shape[2]
    pairs = frames // 2
    rows_ref[:, :MEL] = mel_ref[0].T
    pad = jnp.zeros((pairs, LANES - MEL), F32)
    even = rows_ref[pl.ds(0, pairs, stride=2), :][:, :MEL]
    odd = rows_ref[pl.ds(1, pairs, stride=2), :][:, :MEL]
    return jnp.concatenate([even, pad, odd, pad], axis=1)


def gates_of(pre):
    return jnp.tanh(pre[:, :HID]), 1.0 / (1.0 + jnp.exp(-pre[:, HID:]))


def dot_three(values, table, back=False):
    high, low = halves(values)
    table_high, table_low = halves(table)
    left = jnp.concatenate([high, low, high], axis=1)
    if back:
        return dot_nt(left, jnp.concatenate([table_high, table_high, table_low], axis=1))
    return dot_nn(left, jnp.concatenate([table_high, table_high, table_low], axis=0))


STEP_POST = WLAYERS + 1
STEPS = 2 * WLAYERS + 2


def decoder_body(
    mel_ref,
    dur_ref,
    expand_ref,
    expand_low_ref,
    stats_ref,
    mixm_ref,
    start_ref,
    win_ref,
    wres_ref,
    wend_ref,
    place_ref,
    kept_ref,
    sent_ref,
    last_kept_ref,
    last_sent_ref,
    flow_ref,
    ngrad_ref,
    normal,
    passive_low,
    hidden_low,
    pre,
    hidden,
    skip,
    active,
    skip_low,
    passive_grad,
    gated,
    part,
    spread,
    wide,
    unit,
    rows,
    end_acc,
    start_acc,
    mix_acc,
    tail,
    high,
    low,
    flow,
    sums,
    sems,
):
    step = pl.program_id(0)
    items, _, frames = mel_ref.shape
    pairs = frames // 2
    conv = WKER * HID
    fetch = [
        pltpu.make_async_copy(expand_ref, high, sems.at[0]),
        pltpu.make_async_copy(expand_low_ref, low, sems.at[1]),
    ]
    write = pltpu.make_async_copy(flow, flow_ref, sems.at[2])
    mine = place_ref[0] & 1

    def deal(source, rows_each, targets, begin, first_sem):
        return [
            pltpu.make_async_copy(
                source.at[pl.ds(pl.multiple_of(side * rows_each, 8), rows_each), :],
                target.at[pl.ds(begin, rows_each), :],
                sems.at[first_sem + i],
            )
            for i, (side, target) in enumerate(((mine, targets[0]), (1 - mine, targets[1])))
        ]

    half = UNIT // 2
    deals = [deal(unit.at[0], half, (last_kept_ref, last_sent_ref), 0, 3)]
    for above in range(1, WLAYERS):
        begin = (WLAYERS - 1 - above) * half
        deals.append(deal(unit.at[above & 1], half, (kept_ref, sent_ref), begin, 3 + 2 * above))
    last_deal = deal(
        tail, TAIL // 2, (kept_ref, sent_ref), (WLAYERS - 1) * half, 3 + 2 * WLAYERS
    )

    def inside_item(item):
        return rows_of(pairs) < pair_rows(dur_ref[pl.ds(item, 1), :])

    def span(item):
        return pl.ds(pl.multiple_of(item * pairs, pairs), pairs)

    def each(body, count=items):
        def one(item, carry):
            body(item)
            return carry

        lax.fori_loop(0, count, one, 0)

    both = 2 if items % 2 == 0 else 1
    blocks = items // both
    block_rows = both * pairs

    def block_span(block):
        return pl.ds(pl.multiple_of(block * block_rows, block_rows), block_rows)

    def inside_block(block):
        return jnp.concatenate([inside_item(block * both + i) for i in range(both)], axis=0)

    @pl.when(step == 0)
    def _():
        for copy in fetch:
            copy.start()
        _, center, _, _, scale = read_stats(stats_ref[...])

        def one(item):
            inside = inside_item(item)
            rows[:, :MEL] = mel_ref[item].T
            pad = jnp.zeros((pairs, LANES - MEL), F32)
            even = rows[pl.ds(0, pairs, stride=2), :][:, :MEL]
            odd = rows[pl.ds(1, pairs, stride=2), :][:, :MEL]
            values = jnp.concatenate([even, pad, odd, pad], axis=1)
            normalized = jnp.where(inside, (values - center) * scale, 0.0)
            normal[item] = normalized
            turned = dot_three(normalized, mixm_ref[...])
            passive = turned[:, :LANES]
            passive_grad[item] = passive
            active[item] = turned[:, LANES:]
            low_now = passive.astype(BF16)
            passive_low[item] = low_now
            hidden[span(item), :] = jnp.where(inside, dot_nn(low_now, start_ref[...]), 0.0)
            skip[span(item), :] = jnp.zeros((pairs, HID), F32)

        each(one)

    @pl.when((step >= 1) & (step <= WLAYERS))
    def _():
        layer = step - 1

        def one(block):
            here = block_span(block)
            state = hidden[here, :]
            hidden_low[layer, here, :] = state.astype(BF16)
            pre_gate = dot_nn(unfold_rows(state, WKER, pairs), win_ref[0])
            pre[layer, here, :] = pre_gate.astype(BF16)
            tanh, gate = gates_of(pre_gate)
            sums = dot_nn((tanh * gate).astype(BF16), wres_ref[layer])
            hidden[here, :] = jnp.where(inside_block(block), state + sums[:, :HID], 0.0)
            skip[here, :] = skip[here, :] + sums[:, HID:]

        each(one, blocks)

    @pl.when(step == STEP_POST)
    def _():
        for copy in fetch:
            copy.wait()
        total, _, _, _, _ = read_stats(stats_ref[...])
        unit_grad = 1.0 / (2 * MEL * total)
        end_acc[...] = jnp.zeros_like(end_acc)
        sums[...] = jnp.zeros_like(sums)

        def one(item):
            inside = inside_item(item)
            output_low = jnp.where(inside, skip[span(item), :], 0.0).astype(BF16)
            coupled = jnp.where(inside, dot_nn(output_low, wend_ref[...]), 0.0)
            shift_part = coupled[:, :LANES]
            log_part = coupled[:, LANES:]
            growth = jnp.exp(log_part)
            moving = active[item]
            moved = jnp.where(inside, shift_part + growth * moving, 0.0)
            align = align_of(dur_ref[pl.ds(item, 1), :], pairs)
            prior = dot_nn(align, high[item]) + dot_nn(align, low[item])
            latent = jnp.concatenate([passive_grad[item], moved], axis=1)
            gap = latent - prior[:, : 2 * LANES]
            log_scales = prior[:, 2 * LANES :]
            scaled = jnp.exp(-2.0 * log_scales) * gap
            square = scaled * gap
            terms = jnp.where(inside, log_scales + 0.5 * square, 0.0)
            term = jnp.sum(terms, axis=0, keepdims=True)
            nll = term[:, :LANES] + term[:, LANES:] - jnp.sum(log_part, axis=0, keepdims=True)
            sums[4:5, :] = sums[4:5, :] + nll
            latent_grad = jnp.where(inside, unit_grad * scaled, 0.0)
            scale_grad = jnp.where(inside, unit_grad * (1.0 - square), 0.0)
            flow[item] = jnp.concatenate([-latent_grad, scale_grad], axis=1).astype(BF16)
            passive_grad[item] = latent_grad[:, :LANES]
            moved_grad = latent_grad[:, LANES:]
            active_grad = moved_grad * growth
            log_grad = jnp.where(inside, active_grad * moving - unit_grad, 0.0)
            active[item] = active_grad
            coupled_low = jnp.concatenate([moved_grad, log_grad], axis=1).astype(BF16)
            end_acc[...] = end_acc[...] + dot_tn(coupled_low, output_low)
            skip_grad = jnp.where(inside, dot_nt(coupled_low, wend_ref[...]), 0.0)
            skip_low[span(item), :] = skip_grad.astype(BF16)
            hidden[span(item), :] = jnp.zeros((pairs, HID), F32)

        each(one)
        write.start()

    @pl.when(step > STEP_POST)
    def _():
        layer = STEPS - 1 - step
        for tap in range(WKER):
            wide[:, tap * 2 * HID : (tap + 1) * 2 * HID] = win_ref[
                0, tap * HID : (tap + 1) * HID, :
            ]

        def one(block):
            here = block_span(block)
            tanh, gate = gates_of(pre[layer, here, :].astype(F32))
            gated[here, :] = (tanh * gate).astype(BF16)
            kept = hidden[here, :]
            left = jnp.concatenate([kept, skip_low[here, :].astype(F32)], axis=1).astype(BF16)
            part[here, :] = left
            gated_grad = dot_nt(left, wres_ref[layer])
            tanh_grad = gated_grad * gate * (1.0 - tanh * tanh)
            gate_grad = gated_grad * tanh * gate * (1.0 - gate)
            pre_grad = jnp.concatenate([tanh_grad, gate_grad], axis=1)
            taps = unfold_rows(pre_grad, WKER, pairs, reverse=True)
            spread[here, :] = taps
            back = kept + dot_nt(taps, wide[...])
            hidden[here, :] = jnp.where(inside_block(block), back, 0.0)

        each(one, blocks)
        for later in range(WLAYERS - 2):

            @pl.when(layer == later)
            def _(later=later):
                for copy in deals[later + 2]:
                    copy.wait()

        parity = layer & 1
        found = dot_tn(hidden_low[layer], spread[...])
        for tap in range(WKER):
            unit[parity, tap * HID : (tap + 1) * HID, :] = found[
                :, tap * 2 * HID : (tap + 1) * 2 * HID
            ]
        unit[parity, conv:, :] = dot_tn(gated[...], part[...])

        @pl.when(layer == WLAYERS - 1)
        def _():
            side = (WLAYERS - 1) & 1
            unit[side, conv : conv + MEL, :HID] = end_acc[:MEL, :]
            unit[side, conv + MEL : conv + 2 * MEL, :HID] = end_acc[LANES : LANES + MEL, :]

        for now in range(WLAYERS):

            @pl.when(layer == now)
            def _(now=now):
                for copy in deals[now]:
                    copy.start()

    @pl.when(step == STEPS - 1)
    def _():
        start_acc[...] = jnp.zeros_like(start_acc)
        mix_acc[...] = jnp.zeros_like(mix_acc)

        def one(item):
            start_low = hidden[span(item), :].astype(BF16)
            start_acc[...] = start_acc[...] + dot_tn(passive_low[item], start_low)
            turned_passive = passive_grad[item] + dot_nt(start_low, start_ref[...])
            turned_grad = jnp.concatenate([turned_passive, active[item]], axis=1)
            normalized = normal[item]
            mix_acc[...] = mix_acc[...] + dot_tn(
                normalized.astype(BF16), turned_grad.astype(BF16)
            )
            normal_grad = dot_three(turned_grad, mixm_ref[...], back=True)
            normal_grad = jnp.where(inside_item(item), normal_grad, 0.0)
            ngrad_ref[item] = normal_grad
            one_sum = jnp.sum(normal_grad, axis=0, keepdims=True)
            two_sum = jnp.sum(normal_grad * normalized, axis=0, keepdims=True)
            for at, found in ((0, one_sum), (2, two_sum)):
                sums[at : at + 1, :] = sums[at : at + 1, :] + found[:, :LANES]
                sums[at + 1 : at + 2, :] = sums[at + 1 : at + 2, :] + found[:, LANES:]

        each(one)
        tail[...] = jnp.zeros_like(tail)
        cut = MEL // 2
        tail[:cut, :] = jnp.concatenate([start_acc[:cut, :], start_acc[cut:MEL, :]], axis=1)
        row_member, col_member, match = mix_places()
        kept = jnp.where(match, mix_acc[...], 0.0)
        ri = iota((8, LANES), 0)
        ci = iota((8, LANES), 1)
        mixed = jnp.zeros((8, LANES), F32)
        for i in range(4):
            column = jnp.sum(jnp.where(col_member == i, kept, 0.0), axis=1, keepdims=True)
            for j in range(4):
                entry = jnp.sum(jnp.where(row_member == j, column, 0.0), axis=0, keepdims=True)
                mixed = jnp.where((ri == i) & (ci == j), entry, mixed)
        tail[cut : cut + 8, :LANES] = mixed
        tail[cut : cut + 8, LANES : 2 * LANES] = sums[...]
        for copy in last_deal:
            copy.start()
        for copy in (*last_deal, *deals[0], *deals[1], write):
            copy.wait()


def frames_body(
    mel_ref, dur_ref, ngrad_ref, stats_ref, sums_ref, small_ref, out_ref, loss_ref, rows_ref
):
    pairs = mel_ref.shape[2] // 2
    inside = rows_of(pairs) < pair_rows(text_rows(dur_ref))
    total, center, variance, log_act, scale = read_stats(stats_ref[...])
    unit = 1.0 / (2 * MEL * total)
    sums = sums_ref[...]
    spot = iota((1, 2 * LANES), 1) & (LANES - 1)
    log_sum = jnp.sum(jnp.where(spot < MEL, log_act, 0.0), axis=1, keepdims=True)
    nll = jnp.sum(sums[4:5], axis=1, keepdims=True)
    log_det = jnp.log(small_ref[4:5, 0:1])
    loss = (nll - total * log_sum - total * (MEL // 2) * log_det) * unit
    loss_ref[...] = loss + 0.5 * math.log(2.0 * math.pi)
    one = jnp.concatenate([sums[0:1], sums[1:2]], axis=1)
    two = jnp.concatenate([sums[2:3], sums[3:4]], axis=1)
    log_grad = two - unit * total
    var_grad = -0.5 * log_grad / (variance + 1e-06)
    center_grad = -scale * one - 2.0 * center * var_grad
    values = split_pairs(mel_ref, rows_ref)
    grads = ngrad_ref[0] * scale + (2.0 * values * var_grad + center_grad) / total
    grads = jnp.where(inside, grads, 0.0) * (2 * MEL * total)
    rows_ref[pl.ds(0, pairs, stride=2), :] = grads[:, :LANES]
    rows_ref[pl.ds(1, pairs, stride=2), :] = grads[:, LANES:]
    out_ref[0] = rows_ref[...].T[:MEL, :]


def swap(values, bit, devices):
    return lax.ppermute(values, "dp", [(i, i ^ bit) for i in range(devices)])


def swap_half(unit, devices):
    kept, sent = unit
    return kept, swap(sent, 1, devices)


def digits(devices, shift=1):
    found = []
    while (1 << shift) < devices:
        radix = 4 if (1 << (shift + 2)) <= devices else 2
        found.append((shift, radix))
        shift += 2 if radix == 4 else 1
    return found


def whole_vmem(count):
    return [pl.BlockSpec(memory_space=pltpu.VMEM)] * count


def call_whole(body, place, ins, outs, scratch, after, micros, name):
    return run(
        body,
        (),
        [place, *ins],
        [pl.BlockSpec(memory_space=pltpu.SMEM)] + whole_vmem(len(ins)),
        outs,
        whole_vmem(len(outs)),
        scratch,
        micros=micros,
        after=after,
        name=name,
    )


def hop_out(jobs, place, after=()):
    ins = []
    outs = []
    scratch = []
    plans = []
    for units, shift, radix in jobs:
        plan = []
        begin = 0
        for unit in units:
            row = unit[0].shape[0] // radix
            plan.append((len(ins), len(unit), row, begin))
            ins += unit
            begin += row
        plans.append((plan, len(outs), shift, radix))
        outs += [shape_of((begin, WIDE))] * radix
        aligned = all(row % 8 == 0 for _, _, row, _ in plan)
        scratch.append(pltpu.VMEM((1, 8, LANES) if aligned else (radix, begin, WIDE), F32))
    n_in, n_out = len(ins), len(outs)

    def body(place_ref, *refs):
        out_refs = refs[n_in : n_in + n_out]
        tables = refs[n_in + n_out :]
        for (plan, at, shift, radix), table in zip(plans, tables):
            digit = (place_ref[0] >> shift) & (radix - 1)
            if all(row % 8 == 0 for _, _, row, _ in plan):
                for step in range(radix):
                    for first, count, row, begin in plan:
                        span = pl.ds(pl.multiple_of((digit ^ step) * row, 8), row)
                        value = refs[first][span, :]
                        for extra in range(1, count):
                            value = value + refs[first + extra][span, :]
                        out_refs[at + step][begin : begin + row, :] = value
                continue
            for first, count, row, begin in plan:
                for part in range(radix):
                    span = slice(part * row, (part + 1) * row)
                    value = refs[first][span, :]
                    for extra in range(1, count):
                        value = value + refs[first + extra][span, :]
                    table[part, begin : begin + row, :] = value
            for step in range(radix):
                out_refs[at + step][...] = table[digit ^ step]

    found = call_whole(body, place, ins, outs, scratch, after, 25, "hop_out")
    return [found[at : at + radix] for _, at, _, radix in plans]


def hop_in(jobs, place, after=()):
    ins = []
    outs = []
    plans = []
    for parts, shift in jobs:
        plans.append((len(ins), len(parts), shift))
        ins += parts
        outs.append(shape_of((len(parts), *parts[0].shape)))
    n_in = len(ins)

    def body(place_ref, *refs):
        for (first, radix, shift), out in zip(plans, refs[n_in:]):
            digit = (place_ref[0] >> shift) & (radix - 1)
            for step in range(radix):
                out[digit ^ step] = refs[first + step][...]

    return call_whole(body, place, ins, outs, (), after, 25, "hop_in")


def add_parts(jobs, place, after=()):
    ins = [part for parts in jobs for part in parts]
    outs = [shape_of(parts[0].shape) for parts in jobs]
    n_in = len(ins)

    def body(place_ref, *refs):
        at = 0
        for parts, out in zip(jobs, refs[n_in:]):
            value = refs[at][...]
            for extra in range(at + 1, at + len(parts)):
                value = value + refs[extra][...]
            out[...] = value
            at += len(parts)

    return call_whole(body, place, ins, outs, (), after, 25, "add_parts")


def send_parts(parts, shift, devices):
    return [parts[0]] + [
        swap(part, step << shift, devices) for step, part in enumerate(parts) if step > 0
    ]


def spread_level(units, level, place, devices, after=()):
    shift, radix = digits(devices)[level]
    parts = hop_out([(units, shift, radix)], place, after)[0]
    return send_parts(parts, shift, devices)


def gather_level(part, level, place, devices, after=()):
    shift, radix = digits(devices)[level]
    return hop_in([(send_parts([part] * radix, shift, devices), shift)], place, after)[0]


def first_bits(place_ref):
    return (place_ref[0] >> 1) & 1, (place_ref[0] >> 2) & 1


def pair_send(pair, first_bit, second_bit, devices):
    (kept, sent), (other_kept, other_sent) = pair
    return [kept, swap(sent, first_bit, devices)], [other_kept, swap(other_sent, second_bit, devices)]


def pair_out(units, place, devices, after=()):
    ins = [array for unit in units for array in unit]
    rows = [unit[0].shape[0] // 8 for unit in units]
    total = sum(rows)

    def body(place_ref, *refs):
        low, high = first_bits(place_ref)
        outs = refs[len(ins) :]
        at = 0
        begin = 0
        for unit, row in zip(units, rows):
            for out, half, mine in ((0, 0, low), (1, 0, 1 - low), (2, 1, high), (3, 1, 1 - high)):
                for other in range(2):
                    digit = mine + 2 * other if half == 0 else other + 2 * mine
                    span = pl.ds(pl.multiple_of((2 * digit + half) * row, 8), row)
                    value = refs[at][span, :]
                    for extra in range(1, len(unit)):
                        value = value + refs[at + extra][span, :]
                    outs[out][other, begin : begin + row, :] = value
            at += len(unit)
            begin += row

    outs = [shape_of((2, total, WIDE))] * 4
    found = call_whole(body, place, ins, outs, (), after, 25, "pair_out")
    return pair_send((found[:2], found[2:]), 2, 4, devices)


def pair_next(pair, place, devices, after=()):
    ins = [*pair[0], *pair[1]]

    def body(place_ref, one, one_more, two, two_more, *outs):
        low, high = first_bits(place_ref)
        for first, more, mine, kept, sent in (
            (one, one_more, high, outs[0], outs[1]),
            (two, two_more, low, outs[2], outs[3]),
        ):
            kept[...] = first[mine] + more[mine]
            sent[...] = first[1 - mine] + more[1 - mine]

    outs = [shape_of(ins[0].shape[1:])] * 4
    found = call_whole(body, place, ins, outs, (), after, 25, "pair_next")
    return pair_send((found[:2], found[2:]), 4, 2, devices)


def pair_level(pair, level, place, devices, after=()):
    shift, radix = digits(devices)[level]
    ins = [*pair[0], *pair[1]]
    rows = ins[0].shape[0]
    part = 2 * rows // radix

    def body(place_ref, one, one_more, two, two_more, *refs):
        table = refs[-1]
        digit = (place_ref[0] >> shift) & (radix - 1)
        for half, (first, more) in enumerate(((one, one_more), (two, two_more))):
            value = first[...] + more[...]
            for i in range(radix // 2):
                table[half * (radix // 2) + i] = value[i * part : (i + 1) * part, :]
        for step in range(radix):
            refs[step][...] = table[digit ^ step]

    outs = [shape_of((part, WIDE))] * radix
    scratch = [pltpu.VMEM((radix, part, WIDE), F32)]
    parts = call_whole(body, place, ins, outs, scratch, after, 25, "pair_level")
    return send_parts(parts, shift, devices)


def gather_pair(part, level, place, devices, after=()):
    shift, radix = digits(devices)[level]
    parts = send_parts([part.reshape(-1, WIDE)] * radix, shift, devices)
    rows = parts[0].shape[0]

    def body(place_ref, *refs):
        table = refs[-1]
        digit = (place_ref[0] >> shift) & (radix - 1)
        for step in range(radix):
            table[digit ^ step] = refs[step][...]
        for half in range(2):
            for i in range(radix // 2):
                refs[radix + half][i * rows : (i + 1) * rows, :] = table[half * (radix // 2) + i]

    outs = [shape_of((rows * radix // 2, WIDE))] * 2
    scratch = [pltpu.VMEM((radix, rows, WIDE), F32)]
    return call_whole(body, place, parts, outs, scratch, after, 25, "gather_pair")


def pair_join(one, two, place, devices, after=()):
    one_more = swap(one, 4, devices)
    two_more = swap(two, 2, devices)

    def body(place_ref, one_ref, one_more_ref, two_ref, two_more_ref, *outs):
        low, high = first_bits(place_ref)
        for first, more, mine, out in (
            (one_ref, one_more_ref, high, outs[0]),
            (two_ref, two_more_ref, low, outs[1]),
        ):
            out[mine] = first[...]
            out[1 - mine] = more[...]

    outs = [shape_of((2, *one.shape))] * 2
    ins = [one, one_more, two, two_more]
    one, two = call_whole(body, place, ins, outs, (), after, 25, "pair_join")
    return [one, swap(one, 2, devices), two, swap(two, 4, devices)]


def table_parts(place_ref, mine_refs, other_refs, table, sems):
    low, high = first_bits(place_ref)
    core = place_ref[0] & 1
    copies = []
    for side, refs in ((core, mine_refs), (1 - core, other_refs)):
        for half, bit in ((0, low), (1, high)):
            for step in range(2):
                mine = bit ^ step
                for other in range(2):
                    digit = mine + 2 * other if half == 0 else other + 2 * mine
                    copies.append(
                        pltpu.make_async_copy(
                            refs[2 * half + step].at[other],
                            table.at[side, 2 * digit + half],
                            sems.at[len(copies)],
                        )
                    )
    for copy in copies:
        copy.start()
    for copy in copies:
        copy.wait()


def segments(begin, count, rows):
    found = []
    at = begin
    while at < begin + count:
        part, row = divmod(at, rows)
        size = min(rows - row, begin + count - at)
        found.append((part, row, size, at - begin))
        at += size
    return found


def unpack_upper_body(place_ref, small_ref, *refs):
    mine, other = refs[:4], refs[4:8]
    in_ref, res_ref, last_ref, end_ref, start_ref, mix_ref, sums_ref, table, tail, sems, first_sems = refs[8:]
    table_parts(place_ref, mine, other, table, first_sems)
    rows = table.shape[2]
    conv = WKER * HID
    half = UNIT // 2
    copies = []

    def move(core, begin, count, target, at):
        for part, row, size, place in segments(begin, count, rows):
            copies.append(
                pltpu.make_async_copy(
                    table.at[core, part, pl.ds(row, size), :],
                    target.at[pl.ds(at + place, size), :],
                    sems.at[len(copies)],
                )
            )

    for layer in range(1, WLAYERS):
        begin = (WLAYERS - 1 - layer) * half
        move(0, begin, half, in_ref.at[layer], 0)
        move(1, begin, conv - half, in_ref.at[layer], half)
        if layer < WLAYERS - 1:
            move(1, begin + conv - half, HID, res_ref.at[layer], 0)
    for copy in copies:
        copy.start()
    for part, row, size, at in segments(conv - half, HID, rows):
        values = table[1, part, row : row + size, :]
        last_ref[at : at + size, :] = values[:, HID:]
        end_ref[at : at + size, :] = values[:, :HID]
    for core in range(2):
        for part, row, size, at in segments((WLAYERS - 1) * half, TAIL // 2, rows):
            begin = core * (TAIL // 2) + at
            tail[begin : begin + size, :] = table[core, part, row : row + size, :]
    cut = MEL // 2
    start_ref[:cut, :] = tail[:cut, :HID]
    start_ref[cut:, :] = tail[:cut, HID:]
    mix_ref[...] = tail[cut : cut + 8, :LANES] - small_ref[...] / 4.0
    sums_ref[...] = tail[cut : cut + 8, LANES : 2 * LANES]
    for copy in copies:
        copy.wait()


def unpack_upper(parts, other, place, small, after):
    vmem = pl.BlockSpec(memory_space=pltpu.VMEM)
    anywhere = pl.BlockSpec(memory_space=pl.ANY)
    outs = [
        shape_of((WLAYERS, WKER * HID, 2 * HID)),
        shape_of((WLAYERS - 1, HID, 2 * HID)),
        shape_of((HID, HID)),
        shape_of((HID, HID)),
        shape_of((MEL, HID)),
        shape_of((8, LANES)),
        shape_of((8, LANES)),
    ]
    return run(
        unpack_upper_body,
        (),
        [place, small, *parts, *other],
        [pl.BlockSpec(memory_space=pltpu.SMEM), vmem] + [anywhere] * 8,
        outs,
        [anywhere] * 2 + [vmem] * 5,
        [
            pltpu.VMEM((2, 8, *parts[0].shape[1:]), F32),
            pltpu.VMEM((TAIL, WIDE), F32),
            pltpu.SemaphoreType.DMA((64,)),
            pltpu.SemaphoreType.DMA((16,)),
        ],
        micros=5,
        after=after,
        name="unpack_upper",
    )


def unpack_lower_body(place_ref, in_given, res_given, *refs):
    mine, other = refs[:4], refs[4:8]
    (
        in_ref,
        res_ref,
        one_ref,
        two_ref,
        table_ref,
        qkv_ref,
        out_ref,
        relk_ref,
        relv_ref,
        prior_ref,
        *norm_refs,
        table,
        rest,
        sems,
        first_sems,
    ) = refs[8:]
    table_parts(place_ref, mine, other, table, first_sems)
    conv = WKER * HID
    half = UNIT // 2
    eighth = half // 8
    copies = []
    for core in range(2):
        for block in range(8):
            at = core * half + block * eighth
            pieces = [(0, max(0, min(eighth, conv - at)), in_ref, at)]
            pieces.append((pieces[0][1], eighth - pieces[0][1], res_ref, at + pieces[0][1] - conv))
            for row, size, target, to in pieces:
                if size:
                    copies.append(
                        pltpu.make_async_copy(
                            table.at[core, block, pl.ds(row, size), :],
                            target.at[0, pl.ds(to, size), :],
                            sems.at[len(copies)],
                        )
                    )
    for copy in copies:
        copy.start()
    rows = table.shape[2] - eighth

    def read(core, begin, count):
        return [
            (table[core, part, eighth + row : eighth + row + size, :], at)
            for part, row, size, at in segments(begin, count, rows)
        ]

    for core in range(2):
        for values, at in read(core, 0, half):
            one_ref[at : at + values.shape[0], core * WIDE : (core + 1) * WIDE] = values
        for third in range(KSIZE):
            block = core * KSIZE + third
            for values, at in read(core, half + third * D, D):
                two_ref[at : at + values.shape[0], block * WIDE : (block + 1) * WIDE] = values
        for values, at in read(core, 2 * half, REST // 2):
            begin = core * (REST // 2) + at
            rest[begin : begin + values.shape[0], :] = values
    side = D // 2
    qkv_ref[:, :WIDE] = rest[:D, :]
    qkv_ref[:side, WIDE:] = rest[D : D + side, :D]
    qkv_ref[side:, WIDE:] = rest[D : D + side, D:]
    out_ref[:side, :] = rest[D + side : 2 * D, :D]
    out_ref[side:, :] = rest[D + side : 2 * D, D:]
    table_ref[:MEL, :] = rest[ROW_TABLE : ROW_TABLE + MEL, :D]
    table_ref[MEL:, :] = rest[ROW_TABLE : ROW_TABLE + VOCAB - MEL, D:]
    prior_ref[:MEL, :] = rest[ROW_PRIOR : ROW_PRIOR + MEL, :D]
    prior_ref[MEL:, :] = rest[ROW_PRIOR : ROW_PRIOR + MEL, D:]
    relk_ref[...] = rest[ROW_REL : ROW_REL + 2 * WINDOW + 1, :HEAD]
    relv_ref[...] = rest[ROW_REL : ROW_REL + 2 * WINDOW + 1, LANES : LANES + HEAD]
    for i, ref in enumerate(norm_refs):
        row = rest[ROW_NORM + (i >> 1) : ROW_NORM + (i >> 1) + 1, :]
        ref[...] = row[:, (i & 1) * D : (i & 1) * D + D].reshape(D)
    for copy in copies:
        copy.wait()


def unpack_lower(parts, other, place, in_grad, res_grad):
    vmem = pl.BlockSpec(memory_space=pltpu.VMEM)
    anywhere = pl.BlockSpec(memory_space=pl.ANY)
    reach = 2 * WINDOW + 1
    outs = [
        shape_of(in_grad.shape),
        shape_of(res_grad.shape),
        shape_of((KSIZE * D, FILTER)),
        shape_of((D, KSIZE * FILTER)),
        shape_of((VOCAB, D)),
        shape_of((D, 3 * D)),
        shape_of((D, D)),
        shape_of((reach, HEAD)),
        shape_of((reach, HEAD)),
        shape_of((2 * MEL, D)),
        *[shape_of((D,))] * 4,
    ]
    return run(
        unpack_lower_body,
        (),
        [place, in_grad, res_grad, *parts, *other],
        [pl.BlockSpec(memory_space=pltpu.SMEM)] + [anywhere] * 10,
        outs,
        [anywhere] * 2 + [vmem] * (len(outs) - 2),
        [
            pltpu.VMEM((2, 8, *parts[0].shape[1:]), F32),
            pltpu.VMEM((REST, WIDE), F32),
            pltpu.SemaphoreType.DMA((32,)),
            pltpu.SemaphoreType.DMA((16,)),
        ],
        micros=5,
        aliases={1: 0, 2: 1},
        name="unpack_lower",
    )


def on_device(
    devices,
    token_ids,
    durations,
    mel_frames,
    embedding,
    w_qkv,
    rel_key,
    rel_value,
    w_out,
    attn_gain,
    attn_shift,
    w_ff1,
    w_ff2,
    ffn_gain,
    ffn_shift,
    w_prior,
    w_mix,
    w_start,
    w_in,
    w_res,
    w_skip_last,
    w_end,
):
    items, length = token_ids.shape
    frames = mel_frames.shape[1]
    mel_frames = mel_frames.transpose(0, 2, 1)
    ff2_t = w_ff2.T
    prior_t = w_prior.T
    end_t = w_end.T
    pairs = frames // 2
    grid = (items,)
    place = lax.axis_index("dp").reshape(1).astype(jnp.int32)

    def halves_of(rows):
        return [shape_of((rows // 2, WIDE))] * 2

    vmem = pl.BlockSpec(memory_space=pltpu.VMEM)
    smem = pl.BlockSpec(memory_space=pltpu.SMEM)
    gain_one = attn_gain.reshape(1, D)
    shift_one = attn_shift.reshape(1, D)
    gain_two = ffn_gain.reshape(1, D)
    shift_two = ffn_shift.reshape(1, D)

    stats = run(
        stats_body, (), [mel_frames, durations], [vmem] * 2, shape_of((8, LANES)), vmem, name="stats"
    )
    stats_steps = digits(devices, 0)
    shift, radix = stats_steps[0]
    local_stats = stats
    stats = sum(send_parts([stats] * radix, shift, devices))

    prepared = [
        shape_of((2 * LANES, 2 * LANES)),
        shape_of((8, LANES)),
        shape_of((D, 6 * LANES), BF16),
        shape_of((LANES, LANES), BF16),
        shape_of((LANES, LANES), BF16),
        shape_of((2 * LANES, D), BF16),
        shape_of((2 * MEL, 8 * LANES), BF16),
        shape_of((D, 8 * LANES), BF16),
        shape_of((LANES, HID), BF16),
        shape_of((HID, 2 * LANES), BF16),
        shape_of((WLAYERS, HID, 2 * HID), BF16),
    ]
    (
        mixm,
        small,
        qkv_pad,
        relk_pad,
        relv_pad,
        out_pad,
        wide,
        prior_pad,
        start_pad,
        end_pad,
        res_four,
    ) = run(
        weights_body,
        (),
        [w_mix, w_qkv, rel_key, rel_value, w_out, prior_t, w_start, end_t, w_res, w_skip_last],
        [smem] + [vmem] * 9,
        prepared,
        [vmem] * len(prepared),
        after=(local_stats,),
        name="weights",
    )

    group = 2 if items % 2 == 0 else 1

    def group_spec(array):
        rank = len(array.shape)
        return pl.BlockSpec((group,) + array.shape[1:], lambda b: (b,) + (0,) * (rank - 1))

    ins = [
        token_ids,
        durations,
        embedding,
        qkv_pad,
        relk_pad,
        relv_pad,
        out_pad,
        gain_one,
        shift_one,
        w_ff1,
        ff2_t,
        gain_two,
        shift_two,
        prior_pad,
    ]
    outs = [
        shape_of((items, length, D), BF16),
        shape_of((items, length, 6 * LANES), BF16),
        shape_of((items, HEADS, length, length), BF16),
        shape_of((items, HEADS, length, LANES), BF16),
        shape_of((items, length, 2 * LANES), BF16),
        shape_of((items, length, D)),
        shape_of((items, length, D), BF16),
        shape_of((items, length, FILTER), BF16),
        shape_of((items, length, FILTER), BF16),
        shape_of((items, length, D)),
        shape_of((items, length, D), BF16),
        shape_of((items, 2 * length, 4 * LANES), BF16),
        shape_of((items, 2 * length, 4 * LANES), BF16),
    ]
    (
        emb_low,
        proj,
        attention,
        banded,
        attend,
        mixed,
        normed_low,
        filtered,
        activ,
        summed,
        encoded,
        expand,
        expand_low,
    ) = run(
        encoder_body,
        (items // group,),
        ins,
        [full_spec(a) for a in ins],
        outs,
        [group_spec(a) for a in outs],
        micros=20,
        after=(stats,),
        name="encoder",
    )
    for shift, radix in stats_steps[1:]:
        stats = sum(send_parts([stats] * radix, shift, devices))

    ins = [mel_frames, durations, expand, expand_low, stats, mixm, start_pad, w_in, res_four, end_pad, place]
    kinds = [full_spec] * 10
    in_specs = [kind(a) for kind, a in zip(kinds, ins)] + [smem]
    in_specs[2] = in_specs[3] = pl.BlockSpec(memory_space=pl.ANY)
    in_specs[7] = pl.BlockSpec(
        (1,) + w_in.shape[1:],
        lambda s: (jnp.where(s <= STEP_POST, jnp.clip(s - 1, 0, WLAYERS - 1), STEPS - 1 - s), 0, 0),
    )
    dealt = ((WLAYERS - 1) * UNIT + TAIL) // 2
    outs = [
        *[shape_of((dealt, WIDE))] * 2,
        *halves_of(UNIT),
        shape_of((items, pairs, 4 * LANES), BF16),
        shape_of((items, pairs, 2 * LANES)),
    ]
    out_specs = [pl.BlockSpec(memory_space=pl.ANY)] * 5 + [full_spec(outs[5])]
    count = items * pairs
    kept, sent, last_kept, last_sent, flow, normal_grad = run(
        decoder_body,
        (STEPS,),
        ins,
        in_specs,
        outs,
        out_specs,
        [
            pltpu.VMEM((items, pairs, 2 * LANES), F32),
            pltpu.VMEM((items, pairs, LANES), BF16),
            pltpu.VMEM((WLAYERS, count, HID), BF16),
            pltpu.VMEM((WLAYERS, count, 2 * HID), BF16),
            pltpu.VMEM((count, HID), F32),
            pltpu.VMEM((count, HID), F32),
            pltpu.VMEM((items, pairs, LANES), F32),
            pltpu.VMEM((count, HID), BF16),
            pltpu.VMEM((items, pairs, LANES), F32),
            pltpu.VMEM((count, HID), BF16),
            pltpu.VMEM((count, 2 * HID), BF16),
            pltpu.VMEM((count, WKER * 2 * HID), BF16),
            pltpu.VMEM((HID, WKER * 2 * HID), BF16),
            pltpu.VMEM((2, UNIT, WIDE), F32),
            pltpu.VMEM((frames, LANES), F32),
            pltpu.VMEM((2 * LANES, HID), F32),
            pltpu.VMEM((LANES, HID), F32),
            pltpu.VMEM((2 * LANES, 2 * LANES), F32),
            pltpu.VMEM((TAIL, WIDE), F32),
            pltpu.VMEM(expand.shape, BF16),
            pltpu.VMEM(expand.shape, BF16),
            pltpu.VMEM((items, pairs, 4 * LANES), BF16),
            pltpu.VMEM((8, LANES), F32),
            pltpu.SemaphoreType.DMA((5 + 2 * WLAYERS,)),
        ],
        micros=80,
        name="decoder",
    )
    recv = swap(sent, 1, devices)
    upper = spread_level([[kept, recv]], 0, place, devices)
    last_recv = swap(last_sent, 1, devices)

    ins = [
        token_ids,
        durations,
        flow,
        encoded,
        summed,
        filtered,
        activ,
        normed_low,
        mixed,
        attend,
        attention,
        banded,
        proj,
        emb_low,
        wide,
        w_ff1,
        ff2_t,
        gain_two,
        prior_t,
        qkv_pad,
        relk_pad,
        relv_pad,
        out_pad,
        gain_one,
        place,
    ]
    kinds = [full_spec] * 2 + [group_spec] * 12 + [full_spec] * 10
    outs = halves_of(2 * UNIT + REST)
    fed_kept, fed_sent = run(
        encoder_back_body,
        (items // group,),
        ins,
        [kind(a) for kind, a in zip(kinds, ins)] + [smem],
        outs,
        [pl.BlockSpec(memory_space=pl.ANY)] * 2,
        [
            pltpu.VMEM((UNIT, WIDE), F32),
            pltpu.VMEM((UNIT, WIDE), F32),
            pltpu.VMEM((REST, WIDE), F32),
            pltpu.VMEM((VOCAB, D), F32),
            pltpu.VMEM((D, 6 * LANES), F32),
            pltpu.VMEM((2 * LANES, D), F32),
            pltpu.VMEM((LANES, LANES), F32),
            pltpu.VMEM((LANES, LANES), F32),
            pltpu.VMEM((2 * MEL, D), F32),
            pltpu.VMEM((8, D), F32),
            pltpu.SemaphoreType.DMA((6,)),
        ],
        after=(upper[0],),
        micros=30,
        name="encoder_back",
    )
    levels = len(digits(devices))
    upper, fed_sent, fed_kept = lax.optimization_barrier((upper, fed_sent, fed_kept))
    fed_recv = swap(fed_sent, 1, devices)
    for level in range(1, levels):
        upper = spread_level([upper], level, place, devices, (fed_kept,))
    units = [[last_kept, last_recv], [fed_kept, fed_recv]]
    lower = pair_out(units, place, devices, (upper[0],))
    upper = add_parts([upper], place, (lower[0][0],))[0]
    for level in reversed(range(2, levels)):
        upper = gather_level(upper, level, place, devices)
    lower = pair_next(lower, place, devices)
    upper = gather_pair(upper, 1, place, devices, (lower[0][0],))
    lower = pair_level(lower, 1, place, devices, (upper[0],))
    upper_parts = pair_join(*upper, place, devices, (lower[0],))
    for level in range(2, levels):
        lower = spread_level([lower], level, place, devices)
    lower = add_parts([lower], place, (upper_parts[0],))[0]
    for level in reversed(range(2, levels)):
        lower = gather_level(lower, level, place, devices)
    lower = gather_pair(lower, 1, place, devices)
    upper_parts, lower = lax.optimization_barrier((upper_parts, lower))
    upper_other = [swap(part, 1, devices) for part in upper_parts]
    lower_parts = pair_join(*lower, place, devices, (upper_other[0], upper_other[3]))
    in_grad, res_grad, last_grad, end_grad, start_grad, mix_grad, sums = unpack_upper(
        upper_parts, upper_other, place, small, ()
    )
    ins = [mel_frames, durations, normal_grad, stats, sums, small]
    kinds = [item_spec, full_spec, item_spec, full_spec, full_spec, full_spec]
    mel_grad, loss = run(
        frames_body,
        grid,
        ins,
        [kind(a) for kind, a in zip(kinds, ins)],
        [shape_of(mel_frames.shape), shape_of((1, 1))],
        [item_spec(mel_frames), pl.BlockSpec((1, 1), lambda b: (0, 0))],
        [pltpu.VMEM((frames, LANES), F32)],
        name="frames",
    )

    lower_parts = [lax.optimization_barrier((part, mel_grad))[0] for part in lower_parts]
    lower_other = [swap(part, 1, devices) for part in lower_parts]
    (
        in_grad,
        res_grad,
        ff1_grad,
        ff2_grad,
        table_grad,
        qkv_grad,
        out_grad,
        relk_grad,
        relv_grad,
        prior_grad,
        *norm_grads,
    ) = unpack_lower(lower_parts, lower_other, place, in_grad, res_grad)

    return (
        loss.reshape(()),
        mel_grad.transpose(0, 2, 1),
        table_grad,
        qkv_grad,
        relk_grad,
        relv_grad,
        out_grad,
        norm_grads[0],
        norm_grads[1],
        ff1_grad,
        ff2_grad.T,
        norm_grads[2],
        norm_grads[3],
        prior_grad.T,
        mix_grad[:4, :4],
        start_grad,
        in_grad,
        res_grad,
        last_grad,
        end_grad[: 2 * MEL].T,
    )


def solution(mesh):
    devices = mesh.shape["dp"]
    placed = (P("dp", None), P("dp", None), P("dp", None, None)) + (P(),) * 18
    return jax.shard_map(
        functools.partial(on_device, devices),
        mesh=mesh,
        in_specs=placed,
        out_specs=(P(), P("dp", None, None)) + (P(),) * 18,
        check_vma=False,
    )
```

```python
import functools
import math

import jax
import jax.numpy as jnp
from jax import lax
from jax.experimental import pallas as pl
from jax.experimental.pallas import tpu as pltpu
from jax.sharding import PartitionSpec as P

D = 192
HEADS = 2
HEAD = 96
LANES = 128
FILTER = 768
MEL = 80
HID = 192
VOCAB = 148
KSIZE = 3
WKER = 5
WLAYERS = 4
WINDOW = 4
PERIOD = 16

F32 = jnp.float32
BF16 = jnp.bfloat16
HIGH = lax.Precision.HIGHEST
VMEM_BYTES = 58 * 1024 * 1024
VMEM_WHOLE = 64 * 1024 * 1024
WIDE = 384
UNIT = 1152
REST = 640
TAIL = 128
COST = 1.15e9
ROW_TABLE = 2 * D
ROW_PRIOR = ROW_TABLE + MEL
ROW_NORM = ROW_PRIOR + MEL
ROW_REL = ROW_NORM + 8


def contract(first_op, second_op, dims, precision=None):
    return lax.dot_general(
        first_op, second_op, (dims, ((), ())), preferred_element_type=F32, precision=precision
    )


def dot_nn(first_op, second_op, precision=None):
    return contract(first_op, second_op, ((1,), (0,)), precision)


def dot_nt(first_op, second_op, precision=None):
    return contract(first_op, second_op, ((1,), (1,)), precision)


def dot_tn(first_op, second_op, precision=None):
    return contract(first_op, second_op, ((0,), (0,)), precision)


def halves(values):
    high = values.astype(BF16)
    low = (values - high.astype(F32)).astype(BF16)
    return high, low


def iota(shape, axis):
    return lax.broadcasted_iota(jnp.int32, shape, axis)


def rows_of(length):
    return iota((length, 1), 0)


def full_spec(array):
    rank = len(array.shape)
    return pl.BlockSpec(array.shape, lambda *_: (0,) * rank)


def item_spec(array):
    rank = len(array.shape)
    return pl.BlockSpec((1,) + array.shape[1:], lambda b: (b,) + (0,) * (rank - 1))


def layer_spec(array, layer):
    rank = len(array.shape)
    return pl.BlockSpec((1, 1) + array.shape[2:], lambda b: (layer, b) + (0,) * (rank - 2))


def weight_spec(array, layer):
    rank = len(array.shape)
    return pl.BlockSpec((1,) + array.shape[1:], lambda b: (layer,) + (0,) * (rank - 1))


def shape_of(shape, dtype=F32):
    return jax.ShapeDtypeStruct(shape, dtype)


def run(body, grid, ins, in_specs, outs, out_specs, scratch=(), micros=5, after=(), aliases=None, name=None, vmem=VMEM_BYTES):
    count, extra = len(ins), len(after)

    def wrapped(*refs):
        body(*refs[:count], *refs[count + extra :])

    return pl.pallas_call(
        wrapped,
        grid=grid,
        in_specs=list(in_specs) + [pl.BlockSpec(memory_space=pl.ANY)] * extra,
        out_specs=out_specs,
        out_shape=outs,
        scratch_shapes=list(scratch),
        compiler_params=pltpu.CompilerParams(vmem_limit_bytes=vmem),
        cost_estimate=pl.CostEstimate(
            flops=int(micros * COST), bytes_accessed=1 << 20, transcendentals=0
        ),
        input_output_aliases=aliases or {},
        name=name,
    )(*ins, *after)


def pair_rows(durations_row):
    return jnp.sum(durations_row, axis=1, keepdims=True) >> 1


def stats_body(mel_ref, dur_ref, out_ref):
    items, _, frames = mel_ref.shape
    lane = iota((1, frames), 1)
    count = jnp.zeros((1, 1), F32)
    sums = jnp.zeros((MEL, LANES), F32)
    squares = jnp.zeros((MEL, LANES), F32)
    for item in range(items):
        pair_count = pair_rows(dur_ref[item : item + 1, :])
        count = count + pair_count.astype(F32)
        values = jnp.where(lane < 2 * pair_count, mel_ref[item], 0.0)
        for part in range(frames // LANES):
            piece = values[:, part * LANES : (part + 1) * LANES]
            sums = sums + piece
            squares = squares + piece * piece
    place = iota((MEL, LANES), 1)
    table = jnp.zeros((MEL, LANES), F32)
    for side in range(2):
        chosen = (place & 1) == side
        for spot, held in ((side, sums), (2 + side, squares)):
            column = jnp.sum(jnp.where(chosen, held, 0.0), axis=1, keepdims=True)
            table = jnp.where(place == spot, column, table)
    table = jnp.concatenate([table, jnp.zeros((LANES - MEL, LANES), F32)], axis=0)
    rows = table.T[0:8]
    out_ref[...] = jnp.where(iota((8, LANES), 0) == 4, count, rows)


def read_stats(stats):
    total = stats[4:5, 0:1]
    sums = jnp.concatenate([stats[0:1], stats[1:2]], axis=1)
    squares = jnp.concatenate([stats[2:3], stats[3:4]], axis=1)
    center = sums / total
    variance = squares / total - center * center
    log_act = -0.5 * jnp.log(variance + 1e-06)
    return total, center, variance, log_act, jnp.exp(log_act)


def mix_places():
    row = rows_of(2 * LANES)
    col = iota((1, 2 * LANES), 1)
    row_lane = row & (LANES - 1)
    col_lane = col & (LANES - 1)
    upper = (row_lane >= MEL // 2).astype(jnp.int32)
    row_group = row_lane - upper * (MEL // 2)
    row_member = 2 * upper + (row >> 7)
    col_group = col_lane >> 1
    col_member = 2 * (col >> 7) + (col_lane & 1)
    match = (row_group == col_group) & (row_lane < MEL) & (col_lane < MEL)
    return row_member, col_member, match


def weights_body(
    mix_ref,
    qkv_ref,
    relk_ref,
    relv_ref,
    out_ref,
    prior_ref,
    start_ref,
    end_ref,
    res_ref,
    last_ref,
    mixm_ref,
    small_ref,
    qkv_pad_ref,
    relk_pad_ref,
    relv_pad_ref,
    out_pad_ref,
    wide_ref,
    prior_pad_ref,
    start_pad_ref,
    end_pad_ref,
    res_four_ref,
):
    row_member, col_member, match = mix_places()
    table = jnp.zeros((2 * LANES, 2 * LANES), F32)
    for i in range(4):
        column = jnp.zeros((2 * LANES, 1), F32)
        for j in range(4):
            column = jnp.where(row_member == j, mix_ref[i, j], column)
        table = jnp.where(col_member == i, column, table)
    mixm_ref[...] = jnp.where(match, table, 0.0)
    res_four_ref[: WLAYERS - 1] = res_ref[...]
    res_four_ref[WLAYERS - 1] = jnp.concatenate(
        [jnp.zeros((HID, HID), F32), last_ref[...].astype(F32)], axis=1
    ).astype(BF16)

    ri = iota((8, LANES), 0)
    ci = iota((8, LANES), 1)
    joined = jnp.where((ci == ri + 4) & (ri < 4), 1.0, 0.0).astype(F32)
    for i in range(4):
        for j in range(4):
            joined = jnp.where((ri == i) & (ci == j), mix_ref[i, j], joined)
    determinant = jnp.ones((1, 1), F32)
    for column in range(4):
        pivot = joined[column : column + 1, column : column + 1]
        determinant = determinant * pivot
        row_now = joined[column : column + 1, :] / pivot
        joined = joined - joined[:, column : column + 1] * row_now
        joined = jnp.where(ri == column, row_now, joined)
    turned = jnp.zeros((8, LANES), F32)
    for i in range(4):
        for j in range(4):
            turned = jnp.where((ri == j) & (ci == i), joined[i : i + 1, 4 + j : 5 + j], turned)
    small_ref[...] = jnp.where(ri == 4, determinant, turned)

    def select(count, wanted):
        return jnp.where(rows_of(count) == wanted, 1.0, 0.0).astype(BF16)

    place = iota((1, 6 * LANES), 1)
    lane = place & (LANES - 1)
    wanted = jnp.where(lane < HEAD, (place >> 7) * HEAD + lane, -1)
    qkv_pad_ref[...] = dot_nn(qkv_ref[...], select(3 * D, wanted)).astype(BF16)

    place = iota((1, 2 * LANES), 1)
    lane = place & (LANES - 1)
    wanted = jnp.where(lane < HEAD, (place >> 7) * HEAD + lane, -1)
    out_pad_ref[...] = dot_tn(select(D, wanted), out_ref[...]).astype(BF16)

    wanted = iota((1, LANES), 1) & (PERIOD - 1)
    repeat = select(2 * WINDOW + 1, wanted)
    pad = jnp.zeros((LANES, LANES - HEAD), F32)
    relk_pad_ref[...] = jnp.concatenate([dot_tn(repeat, relk_ref[...]), pad], axis=1).astype(BF16)
    relv_pad_ref[...] = jnp.concatenate([dot_tn(repeat, relv_ref[...]), pad], axis=1).astype(BF16)

    place = iota((1, 8 * LANES), 1)
    lane = place & (LANES - 1)
    group = (place >> 7) & 3
    fits = (lane < MEL) & ((lane & 1) == (place >> 9))
    wanted = jnp.where(fits, (group >> 1) * MEL + (group & 1) * (MEL // 2) + (lane >> 1), -1)
    wide = select(2 * MEL, wanted)
    wide_ref[...] = wide
    prior_pad_ref[...] = dot_tn(prior_ref[...], wide).astype(BF16)

    wanted = iota((1, LANES), 1)
    start_pad_ref[...] = dot_tn(select(MEL, wanted), start_ref[...]).astype(BF16)
    place = iota((1, 2 * LANES), 1)
    lane = place & (LANES - 1)
    wanted = jnp.where(lane < MEL, (place >> 7) * MEL + lane, -1)
    end_pad_ref[...] = dot_tn(end_ref[...], select(2 * MEL, wanted)).astype(BF16)


def text_rows(dur_ref):
    item = pl.program_id(0)
    return dur_ref[pl.ds(item, 1), :]


def text_inside(durations_row, length):
    tokens = jnp.sum((durations_row > 0).astype(jnp.int32), axis=1, keepdims=True)
    return rows_of(length) < tokens


def norm_parts(inputs):
    centered = inputs - jnp.mean(inputs, axis=1, keepdims=True)
    spread = jnp.mean(centered * centered, axis=1, keepdims=True)
    inverse = lax.rsqrt(spread + 1e-05)
    return centered * inverse, inverse


def norm_back(inputs, gain, gradient):
    unit, inverse = norm_parts(inputs)
    gain_grad = jnp.sum(gradient * unit, axis=0, keepdims=True)
    shift_grad = jnp.sum(gradient, axis=0, keepdims=True)
    scaled = gradient * gain
    mean_one = jnp.mean(scaled, axis=1, keepdims=True)
    mean_two = jnp.mean(scaled * unit, axis=1, keepdims=True)
    return inverse * (scaled - mean_one - unit * mean_two), gain_grad, shift_grad


def band_of(length):
    offset = iota((length, length), 1) - iota((length, length), 0)
    return (offset <= WINDOW) & (offset >= -WINDOW)


def turn_rows(values, left):
    pieces = []
    for block in range(values.shape[0] // 8):
        if left:
            first, stride = (WINDOW + 8 * (block & 1), PERIOD - 1)
        else:
            first, stride = (PERIOD - WINDOW + 8 * (block & 1), 1)
        piece = values[block * 8 : (block + 1) * 8]
        pieces.append(pltpu.roll(piece, first, 1, stride=stride, stride_axis=0))
    return jnp.concatenate(pieces, axis=0)


def band_gather(weights_low, band, folding):
    kept = jnp.where(band, weights_low, jnp.zeros_like(weights_low))
    return turn_rows(dot_nn(kept, folding), True).astype(BF16)


def band_spread(near, band):
    turned = turn_rows(near, False)
    count = band.shape[1] // LANES
    return jnp.where(band, jnp.concatenate([turned] * count, axis=1), 0.0)


def folding_of(length):
    same = (iota((length, LANES), 0) & (PERIOD - 1)) == (iota((length, LANES), 1) & (PERIOD - 1))
    return jnp.where(same, 1.0, 0.0).astype(BF16)


def one_turn(rel_pad):
    return jnp.where(rows_of(LANES) < PERIOD, rel_pad, jnp.zeros_like(rel_pad))


def shifted_rows(values, offset, period):
    if offset == 0:
        return values
    length = values.shape[0]
    moved = pltpu.roll(values, (-offset) % length, 0)
    place = rows_of(length) & (period - 1)
    keep = (place < period - offset) if offset > 0 else (place >= -offset)
    return jnp.where(keep, moved, 0.0)


def unfold_rows(values, kernel, period, reverse=False):
    half = kernel // 2
    steps = [step - half for step in range(kernel)]
    if reverse:
        steps = [-step for step in steps]
    return jnp.concatenate(
        [shifted_rows(values, step, period).astype(BF16) for step in steps], axis=1
    )


GELU_A = math.sqrt(2.0 / math.pi)
GELU_B = 0.044715


def gelu_tanh(values):
    return jnp.tanh(GELU_A * (values + GELU_B * values * values * values))


def text_blocks(dur_ref, items):
    item = pl.program_id(0) * items
    rows = [dur_ref[pl.ds(item + i, 1), :] for i in range(items)]
    inside = [text_inside(row, row.shape[1]) for row in rows]
    return rows, jnp.concatenate(inside, axis=0)


def token_table(tok_ref, item):
    tokens = tok_ref[pl.ds(item, 1), :]
    return jnp.where(iota((VOCAB, tokens.shape[1]), 0) == tokens, 1.0, 0.0).astype(BF16)


def encoder_body(
    tok_ref,
    dur_ref,
    emb_ref,
    qkv_ref,
    relk_ref,
    relv_ref,
    out_ref,
    gain_ref,
    shift_ref,
    ff1_ref,
    ff2_ref,
    gain_two_ref,
    shift_two_ref,
    prior_ref,
    emb_low_ref,
    proj_ref,
    att_ref,
    banded_ref,
    attend_ref,
    mixed_ref,
    normed_low_ref,
    filt_ref,
    activ_ref,
    summed_ref,
    enc_ref,
    expand_ref,
    expand_low_ref,
):
    group, length, _ = emb_low_ref.shape
    first = pl.program_id(0) * group
    durations, inside = text_blocks(dur_ref, group)

    def rows(item):
        return slice(item * length, (item + 1) * length)

    def keep(ref, values):
        for item in range(group):
            ref[item] = values[rows(item)]

    looked = [dot_tn(token_table(tok_ref, first + i), emb_ref[...]) for i in range(group)]
    embedded = jnp.where(inside, jnp.concatenate(looked, axis=0) * math.sqrt(D), 0.0)
    emb_low = embedded.astype(BF16)
    keep(emb_low_ref, emb_low)
    proj = dot_nn(emb_low, qkv_ref[...]).astype(BF16)
    keep(proj_ref, proj)
    band = band_of(length)
    folding = folding_of(length)
    relv = one_turn(relv_ref[...])
    attended = []
    for item in range(group):
        key_bias = jnp.where(durations[item] > 0, 0.0, -10000.0)
        parts = []
        for head in range(HEADS):
            query, key, value = [
                proj[rows(item), part * LANES : (part + 1) * LANES]
                for part in (head, HEADS + head, 2 * HEADS + head)
            ]
            near = band_spread(dot_nt(query, relk_ref[...]), band)
            scores = (dot_nt(query, key) + near) * (1.0 / math.sqrt(HEAD)) + key_bias
            raised = jnp.exp(scores - jnp.max(scores, axis=1, keepdims=True))
            attention = raised * (1.0 / jnp.sum(raised, axis=1, keepdims=True))
            low = attention.astype(BF16)
            att_ref[item, head] = low
            banded = band_gather(low, band, folding)
            banded_ref[item, head] = banded
            parts.append(dot_nn(low, value) + dot_nn(banded, relv))
        attended.append(jnp.concatenate(parts, axis=1))
    attend = jnp.concatenate(attended, axis=0).astype(BF16)
    keep(attend_ref, attend)
    mixed = embedded + dot_nn(attend, out_ref[...])
    keep(mixed_ref, mixed)
    unit, _ = norm_parts(mixed)
    normed = unit * gain_ref[...] + shift_ref[...]
    masked = jnp.where(inside, normed, 0.0)
    keep(normed_low_ref, masked.astype(BF16))
    filtered = dot_nn(unfold_rows(masked, KSIZE, length), ff1_ref[...])
    keep(filt_ref, filtered.astype(BF16))
    activ = jnp.where(inside, 0.5 * filtered * (1.0 + gelu_tanh(filtered)), 0.0)
    keep(activ_ref, activ.astype(BF16))
    second = dot_nt(unfold_rows(activ, KSIZE, length), ff2_ref[...])
    summed = normed + jnp.where(inside, second, 0.0)
    keep(summed_ref, summed)
    unit, _ = norm_parts(summed)
    encoded = jnp.where(inside, unit * gain_two_ref[...] + shift_two_ref[...], 0.0).astype(BF16)
    keep(enc_ref, encoded)
    prior = dot_nn(encoded, prior_ref[...])
    high, low = halves(prior)
    wide = prior.shape[1] // 2
    for item in range(group):
        for side in range(2):
            spot = slice(side * length, (side + 1) * length)
            columns = slice(side * wide, (side + 1) * wide)
            expand_ref[item, spot] = high[rows(item), columns]
            expand_low_ref[item, spot] = low[rows(item), columns]


def accumulate(ref, values, first):
    @pl.when(first)
    def _():
        ref[...] = values

    @pl.when(jnp.logical_not(first))
    def _():
        ref[...] = ref[...] + values


def align_of(durations_row, pairs):
    length = durations_row.shape[1]
    upper = jnp.where(iota((length, length), 0) <= iota((length, length), 1), 1.0, 0.0).astype(F32)
    high = (durations_row >> 5).astype(F32)
    low = (durations_row & 31).astype(F32)
    both = jnp.where(iota((8, length), 0) == 0, high, low).astype(BF16)
    sums = dot_nn(both, upper.astype(BF16))
    ends = (32.0 * sums[0:1] + sums[1:2]).astype(jnp.int32)
    starts = ends - durations_row
    frame = 2 * rows_of(pairs)
    even = (frame >= starts) & (frame < ends)
    odd = (frame + 1 >= starts) & (frame + 1 < ends)
    both = jnp.concatenate([jnp.where(even, 1.0, 0.0), jnp.where(odd, 1.0, 0.0)], axis=1)
    return both.astype(BF16)


def encoder_back_body(
    tok_ref,
    dur_ref,
    flow_ref,
    enc_ref,
    summed_ref,
    filt_ref,
    activ_ref,
    normed_low_ref,
    mixed_ref,
    attend_ref,
    att_ref,
    banded_ref,
    proj_ref,
    emb_low_ref,
    wide_ref,
    ff1_ref,
    ff2_ref,
    gain_two_ref,
    prior_ref,
    qkv_ref,
    relk_ref,
    relv_ref,
    out_ref,
    gain_ref,
    place_ref,
    kept_ref,
    sent_ref,
    one_acc,
    two_acc,
    rest_acc,
    table_acc,
    qkv_acc,
    out_acc,
    relk_acc,
    relv_acc,
    prior_acc,
    norm_acc,
    sems,
):
    group, length, _ = emb_low_ref.shape
    step = pl.program_id(0)
    first = step == 0
    last = step == pl.num_programs(0) - 1
    durations, inside = text_blocks(dur_ref, group)
    mine = place_ref[0] & 1
    deals = []
    begin = 0
    for source in (one_acc, two_acc, rest_acc):
        half = source.shape[0] // 2
        for side, target in ((mine, kept_ref), (1 - mine, sent_ref)):
            deals.append(
                pltpu.make_async_copy(
                    source.at[pl.ds(pl.multiple_of(side * half, 8), half), :],
                    target.at[pl.ds(begin, half), :],
                    sems.at[len(deals)],
                )
            )
        begin += half
    everything = (one_acc, two_acc, table_acc, qkv_acc, out_acc, relk_acc, relv_acc, prior_acc, norm_acc)

    @pl.when(first)
    def _():
        for ref in everything:
            ref[...] = jnp.zeros_like(ref)

    def rows(item):
        return slice(item * length, (item + 1) * length)

    def whole(ref):
        return jnp.concatenate([ref[i] for i in range(group)], axis=0)

    def norm_sums(at, gain_grad, shift_grad):
        norm_acc[at : at + 1, :] = norm_acc[at : at + 1, :] + gain_grad
        norm_acc[at + 1 : at + 2, :] = norm_acc[at + 1 : at + 2, :] + shift_grad

    half = wide_ref.shape[1] // 2
    gathered = []
    for item in range(group):
        align = align_of(durations[item], flow_ref.shape[1])
        spread = dot_tn(align, flow_ref[item])
        pieces = []
        for side in range(2):
            pieces += halves(spread[side * length : (side + 1) * length])
        gathered.append(jnp.concatenate(pieces, axis=1))
    chosen = jnp.concatenate(
        [wide_ref[:, side * half : (side + 1) * half] for side in (0, 0, 1, 1)], axis=1
    )
    grad = dot_nt(jnp.concatenate(gathered, axis=0), chosen)
    prior_low = jnp.where(inside, grad, 0.0).astype(BF16)
    prior_acc[...] = prior_acc[...] + dot_tn(prior_low, whole(enc_ref))
    enc_grad = jnp.where(inside, dot_nn(prior_low, prior_ref[...]), 0.0)
    summed_grad, gain_grad, shift_grad = norm_back(whole(summed_ref), gain_two_ref[...], enc_grad)
    norm_sums(2, gain_grad, shift_grad)
    second = jnp.where(inside, summed_grad, 0.0)
    taps = unfold_rows(second, KSIZE, length, reverse=True)
    sums = dot_tn(taps, whole(activ_ref))
    for tap in range(KSIZE):
        for part in range(2):
            begin = (2 * tap + part) * D
            two_acc[begin : begin + D, :] = (
                two_acc[begin : begin + D, :]
                + sums[tap * D : (tap + 1) * D, part * WIDE : (part + 1) * WIDE]
            )
    activ_grad = dot_nn(
        taps,
        jnp.concatenate(
            [ff2_ref[:, tap * FILTER : (tap + 1) * FILTER] for tap in range(KSIZE)], axis=0
        ),
    )
    filtered = whole(filt_ref).astype(F32)
    tanh = gelu_tanh(filtered)
    slope = 0.5 * (1.0 + tanh) + 0.5 * filtered * (1.0 - tanh * tanh) * GELU_A * (
        1.0 + 3.0 * GELU_B * filtered * filtered
    )
    first_grad = jnp.where(inside, activ_grad * slope, 0.0)
    taps = unfold_rows(first_grad, KSIZE, length, reverse=True)
    sums = dot_tn(whole(normed_low_ref), taps)
    for tap in range(KSIZE):
        for part in range(2):
            begin = part * KSIZE * D + tap * D
            column = tap * FILTER + part * WIDE
            one_acc[begin : begin + D, :] = (
                one_acc[begin : begin + D, :] + sums[:, column : column + WIDE]
            )
    back = dot_nt(
        taps,
        jnp.concatenate([ff1_ref[tap * D : (tap + 1) * D, :] for tap in range(KSIZE)], axis=1),
    )

    @pl.when(last)
    def _():
        for copy in deals[:4]:
            copy.start()

    normed_grad = summed_grad + jnp.where(inside, back, 0.0)
    mixed_grad, gain_grad, shift_grad = norm_back(whole(mixed_ref), gain_ref[...], normed_grad)
    norm_sums(0, gain_grad, shift_grad)
    out_low = mixed_grad.astype(BF16)
    out_acc[...] = out_acc[...] + dot_tn(whole(attend_ref), out_low)
    weight = dot_nt(out_low, out_ref[...]).astype(BF16)
    band = band_of(length)
    folding = folding_of(length)
    relk = one_turn(relk_ref[...])
    projected = []
    relk_sum = relk_acc[...]
    relv_sum = relv_acc[...]
    for item in range(group):
        queries, keys, values = [], [], []
        for head in range(HEADS):
            query, key, value = [
                proj_ref[item, :, part * LANES : (part + 1) * LANES]
                for part in (head, HEADS + head, 2 * HEADS + head)
            ]
            mine = weight[rows(item), head * LANES : (head + 1) * LANES]
            near = band_spread(dot_nt(mine, relv_ref[...]), band)
            grad = dot_nt(mine, value) + near
            low = att_ref[item, head]
            attention = low.astype(F32)
            values.append(dot_tn(low, mine))
            relv_sum = relv_sum + dot_tn(banded_ref[item, head], mine)
            score = attention * (grad - jnp.sum(attention * grad, axis=1, keepdims=True))
            score_low = (score * (1.0 / math.sqrt(HEAD))).astype(BF16)
            band_grad = band_gather(score_low, band, folding)
            queries.append(dot_nn(score_low, key) + dot_nn(band_grad, relk))
            keys.append(dot_tn(score_low, query))
            relk_sum = relk_sum + dot_tn(band_grad, query)
        projected.append(jnp.concatenate(queries + keys + values, axis=1))
    relk_acc[...] = relk_sum
    relv_acc[...] = relv_sum
    proj_low = jnp.concatenate(projected, axis=0).astype(BF16)
    qkv_acc[...] = qkv_acc[...] + dot_tn(whole(emb_low_ref), proj_low)
    embed_grad = jnp.where(inside, mixed_grad + dot_nt(proj_low, qkv_ref[...]), 0.0) * math.sqrt(D)
    hot = jnp.concatenate(
        [token_table(tok_ref, step * group + item) for item in range(group)], axis=1
    )
    high, low = halves(embed_grad)
    table_acc[...] = table_acc[...] + dot_nn(
        jnp.concatenate([hot, hot], axis=1), jnp.concatenate([high, low], axis=0)
    )

    @pl.when(last)
    def _():
        def beside(left, right):
            return jnp.concatenate([left, right], axis=1)

        rest_acc[...] = jnp.zeros_like(rest_acc)
        packed = [qkv_acc[:, part * LANES : part * LANES + HEAD] for part in range(3 * HEADS)]
        side = D // 2
        rest_acc[:D, :] = jnp.concatenate(packed[:4], axis=1)
        rest_acc[D : D + side, :] = jnp.concatenate(
            [packed[4][:side], packed[5][:side], packed[4][side:], packed[5][side:]], axis=1
        )
        rest_acc[D + side : 2 * D, :] = beside(out_acc[:HEAD, :], out_acc[LANES : LANES + HEAD, :])
        rest_acc[ROW_TABLE : ROW_TABLE + MEL, :D] = table_acc[:MEL, :]
        rest_acc[ROW_TABLE : ROW_TABLE + VOCAB - MEL, D:] = table_acc[MEL:, :]
        rest_acc[ROW_PRIOR : ROW_PRIOR + MEL, :] = beside(prior_acc[:MEL, :], prior_acc[MEL:, :])
        rest_acc[ROW_NORM : ROW_NORM + 1, :] = beside(norm_acc[0:1, :], norm_acc[1:2, :])
        rest_acc[ROW_NORM + 1 : ROW_NORM + 2, :] = beside(norm_acc[2:3, :], norm_acc[3:4, :])
        rest_acc[ROW_REL : ROW_REL + PERIOD, :LANES] = relk_acc[:PERIOD, :]
        rest_acc[ROW_REL : ROW_REL + PERIOD, LANES : 2 * LANES] = relv_acc[:PERIOD, :]
        for copy in deals[4:]:
            copy.start()
        for copy in deals:
            copy.wait()


def split_pairs(mel_ref, rows_ref):
    frames = mel_ref.shape[2]
    pairs = frames // 2
    rows_ref[:, :MEL] = mel_ref[0].T
    pad = jnp.zeros((pairs, LANES - MEL), F32)
    even = rows_ref[pl.ds(0, pairs, stride=2), :][:, :MEL]
    odd = rows_ref[pl.ds(1, pairs, stride=2), :][:, :MEL]
    return jnp.concatenate([even, pad, odd, pad], axis=1)


def gates_of(pre):
    return jnp.tanh(pre[:, :HID]), 1.0 / (1.0 + jnp.exp(-pre[:, HID:]))


def dot_three(values, table, back=False):
    high, low = halves(values)
    table_high, table_low = halves(table)
    left = jnp.concatenate([high, low, high], axis=1)
    if back:
        return dot_nt(left, jnp.concatenate([table_high, table_high, table_low], axis=1))
    return dot_nn(left, jnp.concatenate([table_high, table_high, table_low], axis=0))


STEP_POST = WLAYERS + 1
STEPS = 2 * WLAYERS + 2


def decoder_body(
    mel_ref,
    dur_ref,
    expand_ref,
    expand_low_ref,
    stats_ref,
    mixm_ref,
    start_ref,
    win_ref,
    wres_ref,
    wend_ref,
    place_ref,
    kept_ref,
    sent_ref,
    last_kept_ref,
    last_sent_ref,
    flow_ref,
    ngrad_ref,
    normal,
    passive_low,
    hidden_low,
    pre,
    hidden,
    skip,
    active,
    skip_low,
    passive_grad,
    gated,
    part,
    spread,
    wide,
    unit,
    rows,
    end_acc,
    start_acc,
    mix_acc,
    tail,
    high,
    low,
    flow,
    sums,
    sems,
):
    step = pl.program_id(0)
    items, _, frames = mel_ref.shape
    pairs = frames // 2
    conv = WKER * HID
    fetch = [
        pltpu.make_async_copy(expand_ref, high, sems.at[0]),
        pltpu.make_async_copy(expand_low_ref, low, sems.at[1]),
    ]
    write = pltpu.make_async_copy(flow, flow_ref, sems.at[2])
    ngrad_write = pltpu.make_async_copy(normal, ngrad_ref, sems.at[5 + 2 * WLAYERS])
    mine = place_ref[0] & 1

    def deal(source, rows_each, targets, begin, first_sem):
        return [
            pltpu.make_async_copy(
                source.at[pl.ds(pl.multiple_of(side * rows_each, 8), rows_each), :],
                target.at[pl.ds(begin, rows_each), :],
                sems.at[first_sem + i],
            )
            for i, (side, target) in enumerate(((mine, targets[0]), (1 - mine, targets[1])))
        ]

    half = UNIT // 2
    deals = [deal(unit.at[0], half, (last_kept_ref, last_sent_ref), 0, 3)]
    for above in range(1, WLAYERS):
        begin = (WLAYERS - 1 - above) * half
        deals.append(deal(unit.at[above & 1], half, (kept_ref, sent_ref), begin, 3 + 2 * above))
    last_deal = deal(
        tail, TAIL // 2, (kept_ref, sent_ref), (WLAYERS - 1) * half, 3 + 2 * WLAYERS
    )

    def inside_item(item):
        return rows_of(pairs) < pair_rows(dur_ref[pl.ds(item, 1), :])

    def span(item):
        return pl.ds(pl.multiple_of(item * pairs, pairs), pairs)

    def each(body, count=items):
        def one(item, carry):
            body(item)
            return carry

        lax.fori_loop(0, count, one, 0)

    both = 2 if items % 2 == 0 else 1
    blocks = items // both
    block_rows = both * pairs

    def block_span(block):
        return pl.ds(pl.multiple_of(block * block_rows, block_rows), block_rows)

    def inside_block(block):
        return jnp.concatenate([inside_item(block * both + i) for i in range(both)], axis=0)

    @pl.when(step == 0)
    def _():
        for copy in fetch:
            copy.start()
        _, center, _, _, scale = read_stats(stats_ref[...])

        def one(item):
            inside = inside_item(item)
            rows[:, :MEL] = mel_ref[item].T
            pad = jnp.zeros((pairs, LANES - MEL), F32)
            even = rows[pl.ds(0, pairs, stride=2), :][:, :MEL]
            odd = rows[pl.ds(1, pairs, stride=2), :][:, :MEL]
            values = jnp.concatenate([even, pad, odd, pad], axis=1)
            normalized = jnp.where(inside, (values - center) * scale, 0.0)
            normal[item] = normalized
            turned = dot_three(normalized, mixm_ref[...])
            passive = turned[:, :LANES]
            passive_grad[item] = passive
            active[item] = turned[:, LANES:]
            low_now = passive.astype(BF16)
            passive_low[item] = low_now
            hidden[span(item), :] = jnp.where(inside, dot_nn(low_now, start_ref[...]), 0.0)
            skip[span(item), :] = jnp.zeros((pairs, HID), F32)

        each(one)

    @pl.when((step >= 1) & (step <= WLAYERS))
    def _():
        layer = step - 1

        def one(block):
            here = block_span(block)
            state = hidden[here, :]
            hidden_low[layer, here, :] = state.astype(BF16)
            pre_gate = dot_nn(unfold_rows(state, WKER, pairs), win_ref[0])
            pre[layer, here, :] = pre_gate.astype(BF16)
            tanh, gate = gates_of(pre_gate)
            sums = dot_nn((tanh * gate).astype(BF16), wres_ref[layer])
            hidden[here, :] = jnp.where(inside_block(block), state + sums[:, :HID], 0.0)
            skip[here, :] = skip[here, :] + sums[:, HID:]

        each(one, blocks)

    @pl.when(step == STEP_POST)
    def _():
        for copy in fetch:
            copy.wait()
        total, _, _, _, _ = read_stats(stats_ref[...])
        unit_grad = 1.0 / (2 * MEL * total)
        end_acc[...] = jnp.zeros_like(end_acc)
        sums[...] = jnp.zeros_like(sums)

        def one(item):
            inside = inside_item(item)
            output_low = jnp.where(inside, skip[span(item), :], 0.0).astype(BF16)
            coupled = jnp.where(inside, dot_nn(output_low, wend_ref[...]), 0.0)
            shift_part = coupled[:, :LANES]
            log_part = coupled[:, LANES:]
            growth = jnp.exp(log_part)
            moving = active[item]
            moved = jnp.where(inside, shift_part + growth * moving, 0.0)
            align = align_of(dur_ref[pl.ds(item, 1), :], pairs)
            prior = dot_nn(align, high[item]) + dot_nn(align, low[item])
            latent = jnp.concatenate([passive_grad[item], moved], axis=1)
            gap = latent - prior[:, : 2 * LANES]
            log_scales = prior[:, 2 * LANES :]
            scaled = jnp.exp(-2.0 * log_scales) * gap
            square = scaled * gap
            terms = jnp.where(inside, log_scales + 0.5 * square, 0.0)
            term = jnp.sum(terms, axis=0, keepdims=True)
            nll = term[:, :LANES] + term[:, LANES:] - jnp.sum(log_part, axis=0, keepdims=True)
            sums[4:5, :] = sums[4:5, :] + nll
            latent_grad = jnp.where(inside, unit_grad * scaled, 0.0)
            scale_grad = jnp.where(inside, unit_grad * (1.0 - square), 0.0)
            flow[item] = jnp.concatenate([-latent_grad, scale_grad], axis=1).astype(BF16)
            passive_grad[item] = latent_grad[:, :LANES]
            moved_grad = latent_grad[:, LANES:]
            active_grad = moved_grad * growth
            log_grad = jnp.where(inside, active_grad * moving - unit_grad, 0.0)
            active[item] = active_grad
            coupled_low = jnp.concatenate([moved_grad, log_grad], axis=1).astype(BF16)
            end_acc[...] = end_acc[...] + dot_tn(coupled_low, output_low)
            skip_grad = jnp.where(inside, dot_nt(coupled_low, wend_ref[...]), 0.0)
            skip_low[span(item), :] = skip_grad.astype(BF16)
            hidden[span(item), :] = jnp.zeros((pairs, HID), F32)

        each(one)
        write.start()

    @pl.when(step > STEP_POST)
    def _():
        layer = STEPS - 1 - step
        for tap in range(WKER):
            wide[:, tap * 2 * HID : (tap + 1) * 2 * HID] = win_ref[
                0, tap * HID : (tap + 1) * HID, :
            ]

        def one(block):
            here = block_span(block)
            tanh, gate = gates_of(pre[layer, here, :].astype(F32))
            gated[here, :] = (tanh * gate).astype(BF16)
            kept = hidden[here, :]
            left = jnp.concatenate([kept, skip_low[here, :].astype(F32)], axis=1).astype(BF16)
            part[here, :] = left
            gated_grad = dot_nt(left, wres_ref[layer])
            tanh_grad = gated_grad * gate * (1.0 - tanh * tanh)
            gate_grad = gated_grad * tanh * gate * (1.0 - gate)
            pre_grad = jnp.concatenate([tanh_grad, gate_grad], axis=1)
            taps = unfold_rows(pre_grad, WKER, pairs, reverse=True)
            spread[here, :] = taps
            back = kept + dot_nt(taps, wide[...])
            hidden[here, :] = jnp.where(inside_block(block), back, 0.0)

        each(one, blocks)
        for later in range(WLAYERS - 2):

            @pl.when(layer == later)
            def _(later=later):
                for copy in deals[later + 2]:
                    copy.wait()

        parity = layer & 1
        found = dot_tn(hidden_low[layer], spread[...])
        for tap in range(WKER):
            unit[parity, tap * HID : (tap + 1) * HID, :] = found[
                :, tap * 2 * HID : (tap + 1) * 2 * HID
            ]
        unit[parity, conv:, :] = dot_tn(gated[...], part[...])

        @pl.when(layer == WLAYERS - 1)
        def _():
            side = (WLAYERS - 1) & 1
            unit[side, conv : conv + MEL, :HID] = end_acc[:MEL, :]
            unit[side, conv + MEL : conv + 2 * MEL, :HID] = end_acc[LANES : LANES + MEL, :]

        for now in range(WLAYERS):

            @pl.when(layer == now)
            def _(now=now):
                for copy in deals[now]:
                    copy.start()

    @pl.when(step == STEPS - 1)
    def _():
        start_acc[...] = jnp.zeros_like(start_acc)
        mix_acc[...] = jnp.zeros_like(mix_acc)

        def one(item):
            start_low = hidden[span(item), :].astype(BF16)
            start_acc[...] = start_acc[...] + dot_tn(passive_low[item], start_low)
            turned_passive = passive_grad[item] + dot_nt(start_low, start_ref[...])
            turned_grad = jnp.concatenate([turned_passive, active[item]], axis=1)
            normalized = normal[item]
            mix_acc[...] = mix_acc[...] + dot_tn(
                normalized.astype(BF16), turned_grad.astype(BF16)
            )
            normal_grad = dot_three(turned_grad, mixm_ref[...], back=True)
            normal_grad = jnp.where(inside_item(item), normal_grad, 0.0)
            normal[item] = normal_grad
            one_sum = jnp.sum(normal_grad, axis=0, keepdims=True)
            two_sum = jnp.sum(normal_grad * normalized, axis=0, keepdims=True)
            for at, found in ((0, one_sum), (2, two_sum)):
                sums[at : at + 1, :] = sums[at : at + 1, :] + found[:, :LANES]
                sums[at + 1 : at + 2, :] = sums[at + 1 : at + 2, :] + found[:, LANES:]

        each(one)
        ngrad_write.start()
        tail[...] = jnp.zeros_like(tail)
        cut = MEL // 2
        tail[:cut, :] = jnp.concatenate([start_acc[:cut, :], start_acc[cut:MEL, :]], axis=1)
        row_member, col_member, match = mix_places()
        kept = jnp.where(match, mix_acc[...], 0.0)
        ri = iota((8, LANES), 0)
        ci = iota((8, LANES), 1)
        mixed = jnp.zeros((8, LANES), F32)
        for i in range(4):
            column = jnp.sum(jnp.where(col_member == i, kept, 0.0), axis=1, keepdims=True)
            for j in range(4):
                entry = jnp.sum(jnp.where(row_member == j, column, 0.0), axis=0, keepdims=True)
                mixed = jnp.where((ri == i) & (ci == j), entry, mixed)
        tail[cut : cut + 8, :LANES] = mixed
        tail[cut : cut + 8, LANES : 2 * LANES] = sums[...]
        for copy in last_deal:
            copy.start()
        for copy in (*last_deal, *deals[0], *deals[1], write, ngrad_write):
            copy.wait()


def frames_body(
    mel_ref, dur_ref, ngrad_ref, stats_ref, sums_ref, small_ref, out_ref, loss_ref, rows_ref
):
    pairs = mel_ref.shape[2] // 2
    inside = rows_of(pairs) < pair_rows(text_rows(dur_ref))
    total, center, variance, log_act, scale = read_stats(stats_ref[...])
    unit = 1.0 / (2 * MEL * total)
    sums = sums_ref[...]
    spot = iota((1, 2 * LANES), 1) & (LANES - 1)
    log_sum = jnp.sum(jnp.where(spot < MEL, log_act, 0.0), axis=1, keepdims=True)
    nll = jnp.sum(sums[4:5], axis=1, keepdims=True)
    log_det = jnp.log(small_ref[4:5, 0:1])
    loss = (nll - total * log_sum - total * (MEL // 2) * log_det) * unit
    loss_ref[...] = loss + 0.5 * math.log(2.0 * math.pi)
    one = jnp.concatenate([sums[0:1], sums[1:2]], axis=1)
    two = jnp.concatenate([sums[2:3], sums[3:4]], axis=1)
    log_grad = two - unit * total
    var_grad = -0.5 * log_grad / (variance + 1e-06)
    center_grad = -scale * one - 2.0 * center * var_grad
    values = split_pairs(mel_ref, rows_ref)
    grads = ngrad_ref[0] * scale + (2.0 * values * var_grad + center_grad) / total
    grads = jnp.where(inside, grads, 0.0) * (2 * MEL * total)
    rows_ref[pl.ds(0, pairs, stride=2), :] = grads[:, :LANES]
    rows_ref[pl.ds(1, pairs, stride=2), :] = grads[:, LANES:]
    out_ref[0] = rows_ref[...].T[:MEL, :]


def swap(values, bit, devices):
    return lax.ppermute(values, "dp", [(i, i ^ bit) for i in range(devices)])


def swap_half(unit, devices):
    kept, sent = unit
    return kept, swap(sent, 1, devices)


def digits(devices, shift=1):
    found = []
    while (1 << shift) < devices:
        radix = 4 if (1 << (shift + 2)) <= devices else 2
        found.append((shift, radix))
        shift += 2 if radix == 4 else 1
    return found


def whole_vmem(count):
    return [pl.BlockSpec(memory_space=pltpu.VMEM)] * count


def call_whole(body, place, ins, outs, scratch, after, micros, name):
    count, given = len(ins), len(outs)

    def wrapped(place_ref, *refs):
        sources, targets = refs[:count], refs[count : count + given]
        held, sems = refs[count + given : 2 * count + given], refs[-1]
        copies = [
            pltpu.make_async_copy(source, target, sems.at[i])
            for i, (source, target) in enumerate(zip(sources, held))
        ]
        for copy in copies:
            copy.start()
        for copy in copies:
            copy.wait()
        body(place_ref, *held, *targets, *refs[2 * count + given : -1])

    return run(
        wrapped,
        (),
        [place, *ins],
        [pl.BlockSpec(memory_space=pltpu.SMEM)] + [pl.BlockSpec(memory_space=pl.ANY)] * count,
        outs,
        whole_vmem(given),
        [pltpu.VMEM(array.shape, array.dtype) for array in ins]
        + list(scratch)
        + [pltpu.SemaphoreType.DMA((count,))],
        micros=micros,
        after=after,
        name=name,
        vmem=VMEM_WHOLE,
    )


def call_parts(plan, place, ins, outs, after, name):
    count, given = len(ins), len(outs)
    layers = 1 + max(
        layer for _, pieces in plan(None) for layer in (piece[4] for piece in pieces)
    )
    pieces_all = sum(len(pieces) for _, pieces in plan(None))

    def body(place_ref, *refs):
        sources, targets = refs[:count], refs[count : count + given]
        held = refs[count + given : count + 2 * given]
        in_sems, out_sems = refs[-2:]
        todo = []
        at = 0
        for out, pieces in plan(place_ref):
            copies = []
            for source, begin, rows, spot, layer in pieces:
                copies.append(
                    pltpu.make_async_copy(
                        sources[source].at[pl.ds(pl.multiple_of(begin, 8), rows), :],
                        held[out].at[(layer, *spot[:-1], pl.ds(spot[-1], rows))],
                        in_sems.at[at],
                    )
                )
                copies[-1].start()
                at += 1
            todo.append((out, copies))
        writes = []
        for out, copies in todo:
            for copy in copies:
                copy.wait()
            value = held[out][0]
            for layer in range(1, layers):
                value = value + held[out][layer]
            held[out][0] = value
            writes.append(pltpu.make_async_copy(held[out].at[0], targets[out], out_sems.at[out]))
            writes[-1].start()
        for write in writes:
            write.wait()

    anywhere = pl.BlockSpec(memory_space=pl.ANY)
    return run(
        body,
        (),
        [place, *ins],
        [pl.BlockSpec(memory_space=pltpu.SMEM)] + [anywhere] * count,
        outs,
        [anywhere] * given,
        [pltpu.VMEM((layers, *out.shape), F32) for out in outs]
        + [pltpu.SemaphoreType.DMA((pieces_all,)), pltpu.SemaphoreType.DMA((given,))],
        micros=25,
        after=after,
        name=name,
        vmem=VMEM_WHOLE,
    )


def hop_out(jobs, place, after=()):
    units, shift, radix = jobs[0]
    row = units[0][0].shape[0] // radix
    if len(jobs) == 1 and len(units) == 1 and row % 8 == 0:
        arrays = units[0]

        def by_parts(place_ref):
            digit = 0 if place_ref is None else (place_ref[0] >> shift) & (radix - 1)
            return [
                (step, [(k, (digit ^ step) * row, row, (0,), k) for k in range(len(arrays))])
                for step in (*range(1, radix), 0)
            ]

        return [call_parts(by_parts, place, arrays, [shape_of((row, WIDE))] * radix, after, "hop_out")]
    ins = []
    outs = []
    scratch = []
    plans = []
    for units, shift, radix in jobs:
        plan = []
        begin = 0
        for unit in units:
            row = unit[0].shape[0] // radix
            plan.append((len(ins), len(unit), row, begin))
            ins += unit
            begin += row
        plans.append((plan, len(outs), shift, radix))
        outs += [shape_of((begin, WIDE))] * radix
        aligned = all(row % 8 == 0 for _, _, row, _ in plan)
        scratch.append(pltpu.VMEM((1, 8, LANES) if aligned else (radix, begin, WIDE), F32))
    n_in, n_out = len(ins), len(outs)

    def body(place_ref, *refs):
        out_refs = refs[n_in : n_in + n_out]
        tables = refs[n_in + n_out :]
        for (plan, at, shift, radix), table in zip(plans, tables):
            digit = (place_ref[0] >> shift) & (radix - 1)
            if all(row % 8 == 0 for _, _, row, _ in plan):
                for step in range(radix):
                    for first, count, row, begin in plan:
                        span = pl.ds(pl.multiple_of((digit ^ step) * row, 8), row)
                        value = refs[first][span, :]
                        for extra in range(1, count):
                            value = value + refs[first + extra][span, :]
                        out_refs[at + step][begin : begin + row, :] = value
                continue
            for first, count, row, begin in plan:
                for part in range(radix):
                    span = slice(part * row, (part + 1) * row)
                    value = refs[first][span, :]
                    for extra in range(1, count):
                        value = value + refs[first + extra][span, :]
                    table[part, begin : begin + row, :] = value
            for step in range(radix):
                out_refs[at + step][...] = table[digit ^ step]

    found = call_whole(body, place, ins, outs, scratch, after, 25, "hop_out")
    return [found[at : at + radix] for _, at, _, radix in plans]


def hop_in(jobs, place, after=()):
    ins = []
    outs = []
    plans = []
    for parts, shift in jobs:
        plans.append((len(ins), len(parts), shift))
        ins += parts
        outs.append(shape_of((len(parts), *parts[0].shape)))
    n_in = len(ins)

    def body(place_ref, *refs):
        for (first, radix, shift), out in zip(plans, refs[n_in:]):
            digit = (place_ref[0] >> shift) & (radix - 1)
            for step in range(radix):
                out[digit ^ step] = refs[first + step][...]

    return call_whole(body, place, ins, outs, (), after, 25, "hop_in")


def add_parts(jobs, place, after=()):
    ins = [part for parts in jobs for part in parts]
    outs = [shape_of(parts[0].shape) for parts in jobs]
    n_in = len(ins)

    def body(place_ref, *refs):
        at = 0
        for parts, out in zip(jobs, refs[n_in:]):
            value = refs[at][...]
            for extra in range(at + 1, at + len(parts)):
                value = value + refs[extra][...]
            out[...] = value
            at += len(parts)

    return call_whole(body, place, ins, outs, (), after, 25, "add_parts")


def send_parts(parts, shift, devices):
    return [parts[0]] + [
        swap(part, step << shift, devices) for step, part in enumerate(parts) if step > 0
    ]


def spread_level(units, level, place, devices, after=()):
    shift, radix = digits(devices)[level]
    parts = hop_out([(units, shift, radix)], place, after)[0]
    return send_parts(parts, shift, devices)


def gather_level(part, level, place, devices, after=()):
    shift, radix = digits(devices)[level]
    return hop_in([(send_parts([part] * radix, shift, devices), shift)], place, after)[0]


def first_bits(place_ref):
    return (place_ref[0] >> 1) & 1, (place_ref[0] >> 2) & 1


def pair_send(pair, first_bit, second_bit, devices):
    (kept, sent), (other_kept, other_sent) = pair
    return [kept, swap(sent, first_bit, devices)], [other_kept, swap(other_sent, second_bit, devices)]


def pair_out(units, place, devices, after=()):
    ins = [array for unit in units for array in unit]
    rows = [unit[0].shape[0] // 8 for unit in units]
    total = sum(rows)

    def by_parts(place_ref):
        low, high = (0, 0) if place_ref is None else first_bits(place_ref)
        found = []
        for out, half, mine in ((1, 0, 1 - low), (3, 1, 1 - high), (0, 0, low), (2, 1, high)):
            pieces = []
            for other in range(2):
                digit = mine + 2 * other if half == 0 else other + 2 * mine
                at = 0
                begin = 0
                for unit, row in zip(units, rows):
                    for layer in range(len(unit)):
                        pieces.append(
                            (at + layer, (2 * digit + half) * row, row, (other, begin), layer)
                        )
                    at += len(unit)
                    begin += row
            found.append((out, pieces))
        return found

    outs = [shape_of((2, total, WIDE))] * 4
    found = call_parts(by_parts, place, ins, outs, after, "pair_out")
    return pair_send((found[:2], found[2:]), 2, 4, devices)


def pair_next(pair, place, devices, after=()):
    ins = [*pair[0], *pair[1]]

    def body(place_ref, one, one_more, two, two_more, *outs):
        low, high = first_bits(place_ref)
        for first, more, mine, kept, sent in (
            (one, one_more, high, outs[0], outs[1]),
            (two, two_more, low, outs[2], outs[3]),
        ):
            kept[...] = first[mine] + more[mine]
            sent[...] = first[1 - mine] + more[1 - mine]

    outs = [shape_of(ins[0].shape[1:])] * 4
    found = call_whole(body, place, ins, outs, (), after, 25, "pair_next")
    return pair_send((found[:2], found[2:]), 4, 2, devices)


def pair_level(pair, level, place, devices, after=()):
    shift, radix = digits(devices)[level]
    ins = [*pair[0], *pair[1]]
    rows = ins[0].shape[0]
    part = 2 * rows // radix

    def body(place_ref, one, one_more, two, two_more, *refs):
        table = refs[-1]
        digit = (place_ref[0] >> shift) & (radix - 1)
        for half, (first, more) in enumerate(((one, one_more), (two, two_more))):
            value = first[...] + more[...]
            for i in range(radix // 2):
                table[half * (radix // 2) + i] = value[i * part : (i + 1) * part, :]
        for step in range(radix):
            refs[step][...] = table[digit ^ step]

    outs = [shape_of((part, WIDE))] * radix
    scratch = [pltpu.VMEM((radix, part, WIDE), F32)]
    parts = call_whole(body, place, ins, outs, scratch, after, 25, "pair_level")
    return send_parts(parts, shift, devices)


def gather_pair(part, level, place, devices, after=()):
    shift, radix = digits(devices)[level]
    parts = send_parts([part.reshape(-1, WIDE)] * radix, shift, devices)
    rows = parts[0].shape[0]

    def body(place_ref, *refs):
        table = refs[-1]
        digit = (place_ref[0] >> shift) & (radix - 1)
        for step in range(radix):
            table[digit ^ step] = refs[step][...]
        for half in range(2):
            for i in range(radix // 2):
                refs[radix + half][i * rows : (i + 1) * rows, :] = table[half * (radix // 2) + i]

    outs = [shape_of((rows * radix // 2, WIDE))] * 2
    scratch = [pltpu.VMEM((radix, rows, WIDE), F32)]
    return call_whole(body, place, parts, outs, scratch, after, 25, "gather_pair")


def pair_join(one, two, place, devices, after=()):
    one_more = swap(one, 4, devices)
    two_more = swap(two, 2, devices)

    def body(place_ref, one_ref, one_more_ref, two_ref, two_more_ref, *outs):
        low, high = first_bits(place_ref)
        for first, more, mine, out in (
            (one_ref, one_more_ref, high, outs[0]),
            (two_ref, two_more_ref, low, outs[1]),
        ):
            out[mine] = first[...]
            out[1 - mine] = more[...]

    outs = [shape_of((2, *one.shape))] * 2
    ins = [one, one_more, two, two_more]
    one, two = call_whole(body, place, ins, outs, (), after, 25, "pair_join")
    return [one, swap(one, 2, devices), two, swap(two, 4, devices)]


def table_parts(place_ref, mine_refs, other_refs, table, sems):
    low, high = first_bits(place_ref)
    core = place_ref[0] & 1
    copies = []
    for side, refs in ((core, mine_refs), (1 - core, other_refs)):
        for half, bit in ((0, low), (1, high)):
            for step in range(2):
                mine = bit ^ step
                for other in range(2):
                    digit = mine + 2 * other if half == 0 else other + 2 * mine
                    copies.append(
                        pltpu.make_async_copy(
                            refs[2 * half + step].at[other],
                            table.at[side, 2 * digit + half],
                            sems.at[len(copies)],
                        )
                    )
    for copy in copies:
        copy.start()
    for copy in copies:
        copy.wait()


def segments(begin, count, rows):
    found = []
    at = begin
    while at < begin + count:
        part, row = divmod(at, rows)
        size = min(rows - row, begin + count - at)
        found.append((part, row, size, at - begin))
        at += size
    return found


def unpack_upper_body(place_ref, small_ref, *refs):
    mine, other = refs[:4], refs[4:8]
    in_ref, res_ref, last_ref, end_ref, start_ref, mix_ref, sums_ref, table, tail, sems, first_sems = refs[8:]
    table_parts(place_ref, mine, other, table, first_sems)
    rows = table.shape[2]
    conv = WKER * HID
    half = UNIT // 2
    copies = []

    def move(core, begin, count, target, at):
        for part, row, size, place in segments(begin, count, rows):
            copies.append(
                pltpu.make_async_copy(
                    table.at[core, part, pl.ds(row, size), :],
                    target.at[pl.ds(at + place, size), :],
                    sems.at[len(copies)],
                )
            )

    for layer in range(1, WLAYERS):
        begin = (WLAYERS - 1 - layer) * half
        move(0, begin, half, in_ref.at[layer], 0)
        move(1, begin, conv - half, in_ref.at[layer], half)
        if layer < WLAYERS - 1:
            move(1, begin + conv - half, HID, res_ref.at[layer], 0)
    for copy in copies:
        copy.start()
    for part, row, size, at in segments(conv - half, HID, rows):
        values = table[1, part, row : row + size, :]
        last_ref[at : at + size, :] = values[:, HID:]
        end_ref[at : at + size, :] = values[:, :HID]
    for core in range(2):
        for part, row, size, at in segments((WLAYERS - 1) * half, TAIL // 2, rows):
            begin = core * (TAIL // 2) + at
            tail[begin : begin + size, :] = table[core, part, row : row + size, :]
    cut = MEL // 2
    start_ref[:cut, :] = tail[:cut, :HID]
    start_ref[cut:, :] = tail[:cut, HID:]
    mix_ref[...] = tail[cut : cut + 8, :LANES] - small_ref[...] / 4.0
    sums_ref[...] = tail[cut : cut + 8, LANES : 2 * LANES]
    for copy in copies:
        copy.wait()


def unpack_upper(parts, other, place, small, after):
    vmem = pl.BlockSpec(memory_space=pltpu.VMEM)
    anywhere = pl.BlockSpec(memory_space=pl.ANY)
    outs = [
        shape_of((WLAYERS, WKER * HID, 2 * HID)),
        shape_of((WLAYERS - 1, HID, 2 * HID)),
        shape_of((HID, HID)),
        shape_of((HID, HID)),
        shape_of((MEL, HID)),
        shape_of((8, LANES)),
        shape_of((8, LANES)),
    ]
    return run(
        unpack_upper_body,
        (),
        [place, small, *parts, *other],
        [pl.BlockSpec(memory_space=pltpu.SMEM), vmem] + [anywhere] * 8,
        outs,
        [anywhere] * 2 + [vmem] * 5,
        [
            pltpu.VMEM((2, 8, *parts[0].shape[1:]), F32),
            pltpu.VMEM((TAIL, WIDE), F32),
            pltpu.SemaphoreType.DMA((64,)),
            pltpu.SemaphoreType.DMA((16,)),
        ],
        micros=5,
        after=after,
        name="unpack_upper",
        vmem=VMEM_WHOLE,
    )


def unpack_lower_body(place_ref, in_given, res_given, *refs):
    mine, other = refs[:4], refs[4:8]
    (
        in_ref,
        res_ref,
        one_ref,
        two_ref,
        table_ref,
        qkv_ref,
        out_ref,
        relk_ref,
        relv_ref,
        prior_ref,
        *norm_refs,
        table,
        rest,
        sems,
        first_sems,
    ) = refs[8:]
    table_parts(place_ref, mine, other, table, first_sems)
    conv = WKER * HID
    half = UNIT // 2
    eighth = half // 8
    copies = []
    for core in range(2):
        for block in range(8):
            at = core * half + block * eighth
            pieces = [(0, max(0, min(eighth, conv - at)), in_ref, at)]
            pieces.append((pieces[0][1], eighth - pieces[0][1], res_ref, at + pieces[0][1] - conv))
            for row, size, target, to in pieces:
                if size:
                    copies.append(
                        pltpu.make_async_copy(
                            table.at[core, block, pl.ds(row, size), :],
                            target.at[0, pl.ds(to, size), :],
                            sems.at[len(copies)],
                        )
                    )
    for copy in copies:
        copy.start()
    rows = table.shape[2] - eighth

    def read(core, begin, count):
        return [
            (table[core, part, eighth + row : eighth + row + size, :], at)
            for part, row, size, at in segments(begin, count, rows)
        ]

    for core in range(2):
        for values, at in read(core, 0, half):
            one_ref[at : at + values.shape[0], core * WIDE : (core + 1) * WIDE] = values
        for third in range(KSIZE):
            block = core * KSIZE + third
            for values, at in read(core, half + third * D, D):
                two_ref[at : at + values.shape[0], block * WIDE : (block + 1) * WIDE] = values
        for values, at in read(core, 2 * half, REST // 2):
            begin = core * (REST // 2) + at
            rest[begin : begin + values.shape[0], :] = values
    side = D // 2
    qkv_ref[:, :WIDE] = rest[:D, :]
    qkv_ref[:side, WIDE:] = rest[D : D + side, :D]
    qkv_ref[side:, WIDE:] = rest[D : D + side, D:]
    out_ref[:side, :] = rest[D + side : 2 * D, :D]
    out_ref[side:, :] = rest[D + side : 2 * D, D:]
    table_ref[:MEL, :] = rest[ROW_TABLE : ROW_TABLE + MEL, :D]
    table_ref[MEL:, :] = rest[ROW_TABLE : ROW_TABLE + VOCAB - MEL, D:]
    prior_ref[:MEL, :] = rest[ROW_PRIOR : ROW_PRIOR + MEL, :D]
    prior_ref[MEL:, :] = rest[ROW_PRIOR : ROW_PRIOR + MEL, D:]
    relk_ref[...] = rest[ROW_REL : ROW_REL + 2 * WINDOW + 1, :HEAD]
    relv_ref[...] = rest[ROW_REL : ROW_REL + 2 * WINDOW + 1, LANES : LANES + HEAD]
    for i, ref in enumerate(norm_refs):
        row = rest[ROW_NORM + (i >> 1) : ROW_NORM + (i >> 1) + 1, :]
        ref[...] = row[:, (i & 1) * D : (i & 1) * D + D].reshape(D)
    for copy in copies:
        copy.wait()


def unpack_lower(parts, other, place, in_grad, res_grad):
    vmem = pl.BlockSpec(memory_space=pltpu.VMEM)
    anywhere = pl.BlockSpec(memory_space=pl.ANY)
    reach = 2 * WINDOW + 1
    outs = [
        shape_of(in_grad.shape),
        shape_of(res_grad.shape),
        shape_of((KSIZE * D, FILTER)),
        shape_of((D, KSIZE * FILTER)),
        shape_of((VOCAB, D)),
        shape_of((D, 3 * D)),
        shape_of((D, D)),
        shape_of((reach, HEAD)),
        shape_of((reach, HEAD)),
        shape_of((2 * MEL, D)),
        *[shape_of((D,))] * 4,
    ]
    return run(
        unpack_lower_body,
        (),
        [place, in_grad, res_grad, *parts, *other],
        [pl.BlockSpec(memory_space=pltpu.SMEM)] + [anywhere] * 10,
        outs,
        [anywhere] * 2 + [vmem] * (len(outs) - 2),
        [
            pltpu.VMEM((2, 8, *parts[0].shape[1:]), F32),
            pltpu.VMEM((REST, WIDE), F32),
            pltpu.SemaphoreType.DMA((32,)),
            pltpu.SemaphoreType.DMA((16,)),
        ],
        micros=5,
        aliases={1: 0, 2: 1},
        name="unpack_lower",
        vmem=VMEM_WHOLE,
    )


def on_device(
    devices,
    token_ids,
    durations,
    mel_frames,
    embedding,
    w_qkv,
    rel_key,
    rel_value,
    w_out,
    attn_gain,
    attn_shift,
    w_ff1,
    w_ff2,
    ffn_gain,
    ffn_shift,
    w_prior,
    w_mix,
    w_start,
    w_in,
    w_res,
    w_skip_last,
    w_end,
):
    items, length = token_ids.shape
    frames = mel_frames.shape[1]
    mel_frames = mel_frames.transpose(0, 2, 1)
    ff2_t = w_ff2.T
    prior_t = w_prior.T
    end_t = w_end.T
    pairs = frames // 2
    grid = (items,)
    place = lax.axis_index("dp").reshape(1).astype(jnp.int32)

    def halves_of(rows):
        return [shape_of((rows // 2, WIDE))] * 2

    vmem = pl.BlockSpec(memory_space=pltpu.VMEM)
    smem = pl.BlockSpec(memory_space=pltpu.SMEM)
    gain_one = attn_gain.reshape(1, D)
    shift_one = attn_shift.reshape(1, D)
    gain_two = ffn_gain.reshape(1, D)
    shift_two = ffn_shift.reshape(1, D)

    stats = run(
        stats_body, (), [mel_frames, durations], [vmem] * 2, shape_of((8, LANES)), vmem, name="stats"
    )
    stats_steps = digits(devices, 0)
    shift, radix = stats_steps[0]
    local_stats = stats
    stats = sum(send_parts([stats] * radix, shift, devices))

    prepared = [
        shape_of((2 * LANES, 2 * LANES)),
        shape_of((8, LANES)),
        shape_of((D, 6 * LANES), BF16),
        shape_of((LANES, LANES), BF16),
        shape_of((LANES, LANES), BF16),
        shape_of((2 * LANES, D), BF16),
        shape_of((2 * MEL, 8 * LANES), BF16),
        shape_of((D, 8 * LANES), BF16),
        shape_of((LANES, HID), BF16),
        shape_of((HID, 2 * LANES), BF16),
        shape_of((WLAYERS, HID, 2 * HID), BF16),
    ]
    (
        mixm,
        small,
        qkv_pad,
        relk_pad,
        relv_pad,
        out_pad,
        wide,
        prior_pad,
        start_pad,
        end_pad,
        res_four,
    ) = run(
        weights_body,
        (),
        [w_mix, w_qkv, rel_key, rel_value, w_out, prior_t, w_start, end_t, w_res, w_skip_last],
        [smem] + [vmem] * 9,
        prepared,
        [vmem] * len(prepared),
        after=(local_stats,),
        name="weights",
    )

    group = 2 if items % 2 == 0 else 1

    def group_spec(array):
        rank = len(array.shape)
        return pl.BlockSpec((group,) + array.shape[1:], lambda b: (b,) + (0,) * (rank - 1))

    ins = [
        token_ids,
        durations,
        embedding,
        qkv_pad,
        relk_pad,
        relv_pad,
        out_pad,
        gain_one,
        shift_one,
        w_ff1,
        ff2_t,
        gain_two,
        shift_two,
        prior_pad,
    ]
    outs = [
        shape_of((items, length, D), BF16),
        shape_of((items, length, 6 * LANES), BF16),
        shape_of((items, HEADS, length, length), BF16),
        shape_of((items, HEADS, length, LANES), BF16),
        shape_of((items, length, 2 * LANES), BF16),
        shape_of((items, length, D)),
        shape_of((items, length, D), BF16),
        shape_of((items, length, FILTER), BF16),
        shape_of((items, length, FILTER), BF16),
        shape_of((items, length, D)),
        shape_of((items, length, D), BF16),
        shape_of((items, 2 * length, 4 * LANES), BF16),
        shape_of((items, 2 * length, 4 * LANES), BF16),
    ]
    (
        emb_low,
        proj,
        attention,
        banded,
        attend,
        mixed,
        normed_low,
        filtered,
        activ,
        summed,
        encoded,
        expand,
        expand_low,
    ) = run(
        encoder_body,
        (items // group,),
        ins,
        [full_spec(a) for a in ins],
        outs,
        [group_spec(a) for a in outs],
        micros=20,
        after=(stats,),
        name="encoder",
    )
    for shift, radix in stats_steps[1:]:
        stats = sum(send_parts([stats] * radix, shift, devices))

    ins = [mel_frames, durations, expand, expand_low, stats, mixm, start_pad, w_in, res_four, end_pad, place]
    kinds = [full_spec] * 10
    in_specs = [kind(a) for kind, a in zip(kinds, ins)] + [smem]
    in_specs[2] = in_specs[3] = pl.BlockSpec(memory_space=pl.ANY)
    in_specs[7] = pl.BlockSpec(
        (1,) + w_in.shape[1:],
        lambda s: (jnp.where(s <= STEP_POST, jnp.clip(s - 1, 0, WLAYERS - 1), STEPS - 1 - s), 0, 0),
    )
    dealt = ((WLAYERS - 1) * UNIT + TAIL) // 2
    outs = [
        *[shape_of((dealt, WIDE))] * 2,
        *halves_of(UNIT),
        shape_of((items, pairs, 4 * LANES), BF16),
        shape_of((items, pairs, 2 * LANES)),
    ]
    out_specs = [pl.BlockSpec(memory_space=pl.ANY)] * 6
    count = items * pairs
    kept, sent, last_kept, last_sent, flow, normal_grad = run(
        decoder_body,
        (STEPS,),
        ins,
        in_specs,
        outs,
        out_specs,
        [
            pltpu.VMEM((items, pairs, 2 * LANES), F32),
            pltpu.VMEM((items, pairs, LANES), BF16),
            pltpu.VMEM((WLAYERS, count, HID), BF16),
            pltpu.VMEM((WLAYERS, count, 2 * HID), BF16),
            pltpu.VMEM((count, HID), F32),
            pltpu.VMEM((count, HID), F32),
            pltpu.VMEM((items, pairs, LANES), F32),
            pltpu.VMEM((count, HID), BF16),
            pltpu.VMEM((items, pairs, LANES), F32),
            pltpu.VMEM((count, HID), BF16),
            pltpu.VMEM((count, 2 * HID), BF16),
            pltpu.VMEM((count, WKER * 2 * HID), BF16),
            pltpu.VMEM((HID, WKER * 2 * HID), BF16),
            pltpu.VMEM((2, UNIT, WIDE), F32),
            pltpu.VMEM((frames, LANES), F32),
            pltpu.VMEM((2 * LANES, HID), F32),
            pltpu.VMEM((LANES, HID), F32),
            pltpu.VMEM((2 * LANES, 2 * LANES), F32),
            pltpu.VMEM((TAIL, WIDE), F32),
            pltpu.VMEM(expand.shape, BF16),
            pltpu.VMEM(expand.shape, BF16),
            pltpu.VMEM((items, pairs, 4 * LANES), BF16),
            pltpu.VMEM((8, LANES), F32),
            pltpu.SemaphoreType.DMA((6 + 2 * WLAYERS,)),
        ],
        micros=80,
        name="decoder",
    )
    recv = swap(sent, 1, devices)
    upper = spread_level([[kept, recv]], 0, place, devices)
    last_recv = swap(last_sent, 1, devices)

    ins = [
        token_ids,
        durations,
        flow,
        encoded,
        summed,
        filtered,
        activ,
        normed_low,
        mixed,
        attend,
        attention,
        banded,
        proj,
        emb_low,
        wide,
        w_ff1,
        ff2_t,
        gain_two,
        prior_t,
        qkv_pad,
        relk_pad,
        relv_pad,
        out_pad,
        gain_one,
        place,
    ]
    kinds = [full_spec] * 2 + [group_spec] * 12 + [full_spec] * 10
    outs = halves_of(2 * UNIT + REST)
    fed_kept, fed_sent = run(
        encoder_back_body,
        (items // group,),
        ins,
        [kind(a) for kind, a in zip(kinds, ins)] + [smem],
        outs,
        [pl.BlockSpec(memory_space=pl.ANY)] * 2,
        [
            pltpu.VMEM((UNIT, WIDE), F32),
            pltpu.VMEM((UNIT, WIDE), F32),
            pltpu.VMEM((REST, WIDE), F32),
            pltpu.VMEM((VOCAB, D), F32),
            pltpu.VMEM((D, 6 * LANES), F32),
            pltpu.VMEM((2 * LANES, D), F32),
            pltpu.VMEM((LANES, LANES), F32),
            pltpu.VMEM((LANES, LANES), F32),
            pltpu.VMEM((2 * MEL, D), F32),
            pltpu.VMEM((8, D), F32),
            pltpu.SemaphoreType.DMA((6,)),
        ],
        after=(upper[0],),
        micros=30,
        name="encoder_back",
    )
    levels = len(digits(devices))
    upper, fed_sent, fed_kept = lax.optimization_barrier((upper, fed_sent, fed_kept))
    fed_recv = swap(fed_sent, 1, devices)
    for level in range(1, levels):
        upper = spread_level([upper], level, place, devices, (fed_kept,))
    units = [[last_kept, last_recv], [fed_kept, fed_recv]]
    lower = pair_out(units, place, devices, (upper[0],))
    upper = add_parts([upper], place, (lower[0][0],))[0]
    for level in reversed(range(2, levels)):
        upper = gather_level(upper, level, place, devices)
    lower = pair_next(lower, place, devices)
    upper = gather_pair(upper, 1, place, devices, (lower[0][0],))
    lower = pair_level(lower, 1, place, devices, (upper[0],))
    upper_parts = pair_join(*upper, place, devices, (lower[0],))
    for level in range(2, levels):
        lower = spread_level([lower], level, place, devices)
    lower = add_parts([lower], place, (upper_parts[0],))[0]
    for level in reversed(range(2, levels)):
        lower = gather_level(lower, level, place, devices)
    lower = gather_pair(lower, 1, place, devices)
    upper_parts, lower = lax.optimization_barrier((upper_parts, lower))
    upper_other = [swap(part, 1, devices) for part in upper_parts]
    lower_parts = pair_join(*lower, place, devices, (upper_other[0], upper_other[3]))
    in_grad, res_grad, last_grad, end_grad, start_grad, mix_grad, sums = unpack_upper(
        upper_parts, upper_other, place, small, ()
    )
    ins = [mel_frames, durations, normal_grad, stats, sums, small]
    kinds = [item_spec, full_spec, item_spec, full_spec, full_spec, full_spec]
    mel_grad, loss = run(
        frames_body,
        grid,
        ins,
        [kind(a) for kind, a in zip(kinds, ins)],
        [shape_of(mel_frames.shape), shape_of((1, 1))],
        [item_spec(mel_frames), pl.BlockSpec((1, 1), lambda b: (0, 0))],
        [pltpu.VMEM((frames, LANES), F32)],
        name="frames",
    )

    lower_parts = [lax.optimization_barrier((part, mel_grad))[0] for part in lower_parts]
    lower_other = [swap(part, 1, devices) for part in lower_parts]
    (
        in_grad,
        res_grad,
        ff1_grad,
        ff2_grad,
        table_grad,
        qkv_grad,
        out_grad,
        relk_grad,
        relv_grad,
        prior_grad,
        *norm_grads,
    ) = unpack_lower(lower_parts, lower_other, place, in_grad, res_grad)

    return (
        loss.reshape(()),
        mel_grad.transpose(0, 2, 1),
        table_grad,
        qkv_grad,
        relk_grad,
        relv_grad,
        out_grad,
        norm_grads[0],
        norm_grads[1],
        ff1_grad,
        ff2_grad.T,
        norm_grads[2],
        norm_grads[3],
        prior_grad.T,
        mix_grad[:4, :4],
        start_grad,
        in_grad,
        res_grad,
        last_grad,
        end_grad[: 2 * MEL].T,
    )


def solution(mesh):
    devices = mesh.shape["dp"]
    placed = (P("dp", None), P("dp", None), P("dp", None, None)) + (P(),) * 18
    return jax.shard_map(
        functools.partial(on_device, devices),
        mesh=mesh,
        in_specs=placed,
        out_specs=(P(), P("dp", None, None)) + (P(),) * 18,
        check_vma=False,
    )
```

```python
import functools
import math

import jax
import jax.numpy as jnp
from jax import lax
from jax.experimental import pallas as pl
from jax.experimental.pallas import tpu as pltpu
from jax.sharding import PartitionSpec as P

D = 192
HEADS = 2
HEAD = 96
LANES = 128
FILTER = 768
MEL = 80
HID = 192
VOCAB = 148
KSIZE = 3
WKER = 5
WLAYERS = 4
WINDOW = 4
PERIOD = 16

F32 = jnp.float32
BF16 = jnp.bfloat16
HIGH = lax.Precision.HIGHEST
VMEM_BYTES = 58 * 1024 * 1024
VMEM_WHOLE = 64 * 1024 * 1024
WIDE = 384
UNIT = 1152
REST = 640
TAIL = 128
COST = 1.15e9
ROW_TABLE = 2 * D
ROW_PRIOR = ROW_TABLE + MEL
ROW_NORM = ROW_PRIOR + MEL
ROW_REL = ROW_NORM + 8


def contract(first_op, second_op, dims, precision=None):
    return lax.dot_general(
        first_op, second_op, (dims, ((), ())), preferred_element_type=F32, precision=precision
    )


def dot_nn(first_op, second_op, precision=None):
    return contract(first_op, second_op, ((1,), (0,)), precision)


def dot_nt(first_op, second_op, precision=None):
    return contract(first_op, second_op, ((1,), (1,)), precision)


def dot_tn(first_op, second_op, precision=None):
    return contract(first_op, second_op, ((0,), (0,)), precision)


def halves(values):
    high = values.astype(BF16)
    low = (values - high.astype(F32)).astype(BF16)
    return high, low


def iota(shape, axis):
    return lax.broadcasted_iota(jnp.int32, shape, axis)


def rows_of(length):
    return iota((length, 1), 0)


def full_spec(array):
    rank = len(array.shape)
    return pl.BlockSpec(array.shape, lambda *_: (0,) * rank)


def item_spec(array):
    rank = len(array.shape)
    return pl.BlockSpec((1,) + array.shape[1:], lambda b: (b,) + (0,) * (rank - 1))


def layer_spec(array, layer):
    rank = len(array.shape)
    return pl.BlockSpec((1, 1) + array.shape[2:], lambda b: (layer, b) + (0,) * (rank - 2))


def weight_spec(array, layer):
    rank = len(array.shape)
    return pl.BlockSpec((1,) + array.shape[1:], lambda b: (layer,) + (0,) * (rank - 1))


def shape_of(shape, dtype=F32):
    return jax.ShapeDtypeStruct(shape, dtype)


def run(body, grid, ins, in_specs, outs, out_specs, scratch=(), micros=5, after=(), aliases=None, name=None, vmem=VMEM_BYTES):
    count, extra = len(ins), len(after)

    def wrapped(*refs):
        body(*refs[:count], *refs[count + extra :])

    return pl.pallas_call(
        wrapped,
        grid=grid,
        in_specs=list(in_specs) + [pl.BlockSpec(memory_space=pl.ANY)] * extra,
        out_specs=out_specs,
        out_shape=outs,
        scratch_shapes=list(scratch),
        compiler_params=pltpu.CompilerParams(vmem_limit_bytes=vmem),
        cost_estimate=pl.CostEstimate(
            flops=int(micros * COST), bytes_accessed=1 << 20, transcendentals=0
        ),
        input_output_aliases=aliases or {},
        name=name,
    )(*ins, *after)


def pair_rows(durations_row):
    return jnp.sum(durations_row, axis=1, keepdims=True) >> 1


def stats_body(mel_ref, dur_ref, out_ref):
    items, _, frames = mel_ref.shape
    lane = iota((1, frames), 1)
    count = jnp.zeros((1, 1), F32)
    sums = jnp.zeros((MEL, LANES), F32)
    squares = jnp.zeros((MEL, LANES), F32)
    for item in range(items):
        pair_count = pair_rows(dur_ref[item : item + 1, :])
        count = count + pair_count.astype(F32)
        values = jnp.where(lane < 2 * pair_count, mel_ref[item], 0.0)
        for part in range(frames // LANES):
            piece = values[:, part * LANES : (part + 1) * LANES]
            sums = sums + piece
            squares = squares + piece * piece
    place = iota((MEL, LANES), 1)
    table = jnp.zeros((MEL, LANES), F32)
    for side in range(2):
        chosen = (place & 1) == side
        for spot, held in ((side, sums), (2 + side, squares)):
            column = jnp.sum(jnp.where(chosen, held, 0.0), axis=1, keepdims=True)
            table = jnp.where(place == spot, column, table)
    table = jnp.concatenate([table, jnp.zeros((LANES - MEL, LANES), F32)], axis=0)
    rows = table.T[0:8]
    out_ref[...] = jnp.where(iota((8, LANES), 0) == 4, count, rows)


def read_stats(stats):
    total = stats[4:5, 0:1]
    sums = jnp.concatenate([stats[0:1], stats[1:2]], axis=1)
    squares = jnp.concatenate([stats[2:3], stats[3:4]], axis=1)
    center = sums / total
    variance = squares / total - center * center
    log_act = -0.5 * jnp.log(variance + 1e-06)
    return total, center, variance, log_act, jnp.exp(log_act)


def mix_places():
    row = rows_of(2 * LANES)
    col = iota((1, 2 * LANES), 1)
    row_lane = row & (LANES - 1)
    col_lane = col & (LANES - 1)
    upper = (row_lane >= MEL // 2).astype(jnp.int32)
    row_group = row_lane - upper * (MEL // 2)
    row_member = 2 * upper + (row >> 7)
    col_group = col_lane >> 1
    col_member = 2 * (col >> 7) + (col_lane & 1)
    match = (row_group == col_group) & (row_lane < MEL) & (col_lane < MEL)
    return row_member, col_member, match


def weights_body(
    mix_ref,
    qkv_ref,
    relk_ref,
    relv_ref,
    out_ref,
    prior_ref,
    start_ref,
    end_ref,
    res_ref,
    last_ref,
    mixm_ref,
    small_ref,
    qkv_pad_ref,
    relk_pad_ref,
    relv_pad_ref,
    out_pad_ref,
    wide_ref,
    prior_pad_ref,
    start_pad_ref,
    end_pad_ref,
    res_four_ref,
):
    row_member, col_member, match = mix_places()
    table = jnp.zeros((2 * LANES, 2 * LANES), F32)
    for i in range(4):
        column = jnp.zeros((2 * LANES, 1), F32)
        for j in range(4):
            column = jnp.where(row_member == j, mix_ref[i, j], column)
        table = jnp.where(col_member == i, column, table)
    mixm_ref[...] = jnp.where(match, table, 0.0)
    res_four_ref[: WLAYERS - 1] = res_ref[...]
    res_four_ref[WLAYERS - 1] = jnp.concatenate(
        [jnp.zeros((HID, HID), F32), last_ref[...].astype(F32)], axis=1
    ).astype(BF16)

    ri = iota((8, LANES), 0)
    ci = iota((8, LANES), 1)
    joined = jnp.where((ci == ri + 4) & (ri < 4), 1.0, 0.0).astype(F32)
    for i in range(4):
        for j in range(4):
            joined = jnp.where((ri == i) & (ci == j), mix_ref[i, j], joined)
    determinant = jnp.ones((1, 1), F32)
    for column in range(4):
        pivot = joined[column : column + 1, column : column + 1]
        determinant = determinant * pivot
        row_now = joined[column : column + 1, :] / pivot
        joined = joined - joined[:, column : column + 1] * row_now
        joined = jnp.where(ri == column, row_now, joined)
    turned = jnp.zeros((8, LANES), F32)
    for i in range(4):
        for j in range(4):
            turned = jnp.where((ri == j) & (ci == i), joined[i : i + 1, 4 + j : 5 + j], turned)
    small_ref[...] = jnp.where(ri == 4, determinant, turned)

    def select(count, wanted):
        return jnp.where(rows_of(count) == wanted, 1.0, 0.0).astype(BF16)

    place = iota((1, 6 * LANES), 1)
    lane = place & (LANES - 1)
    wanted = jnp.where(lane < HEAD, (place >> 7) * HEAD + lane, -1)
    qkv_pad_ref[...] = dot_nn(qkv_ref[...], select(3 * D, wanted)).astype(BF16)

    place = iota((1, 2 * LANES), 1)
    lane = place & (LANES - 1)
    wanted = jnp.where(lane < HEAD, (place >> 7) * HEAD + lane, -1)
    out_pad_ref[...] = dot_tn(select(D, wanted), out_ref[...]).astype(BF16)

    wanted = iota((1, LANES), 1) & (PERIOD - 1)
    repeat = select(2 * WINDOW + 1, wanted)
    pad = jnp.zeros((LANES, LANES - HEAD), F32)
    relk_pad_ref[...] = jnp.concatenate([dot_tn(repeat, relk_ref[...]), pad], axis=1).astype(BF16)
    relv_pad_ref[...] = jnp.concatenate([dot_tn(repeat, relv_ref[...]), pad], axis=1).astype(BF16)

    place = iota((1, 8 * LANES), 1)
    lane = place & (LANES - 1)
    group = (place >> 7) & 3
    fits = (lane < MEL) & ((lane & 1) == (place >> 9))
    wanted = jnp.where(fits, (group >> 1) * MEL + (group & 1) * (MEL // 2) + (lane >> 1), -1)
    wide = select(2 * MEL, wanted)
    wide_ref[...] = wide
    prior_pad_ref[...] = dot_tn(prior_ref[...], wide).astype(BF16)

    wanted = iota((1, LANES), 1)
    start_pad_ref[...] = dot_tn(select(MEL, wanted), start_ref[...]).astype(BF16)
    place = iota((1, 2 * LANES), 1)
    lane = place & (LANES - 1)
    wanted = jnp.where(lane < MEL, (place >> 7) * MEL + lane, -1)
    end_pad_ref[...] = dot_tn(end_ref[...], select(2 * MEL, wanted)).astype(BF16)


def text_rows(dur_ref):
    item = pl.program_id(0)
    return dur_ref[pl.ds(item, 1), :]


def text_inside(durations_row, length):
    tokens = jnp.sum((durations_row > 0).astype(jnp.int32), axis=1, keepdims=True)
    return rows_of(length) < tokens


def norm_parts(inputs):
    centered = inputs - jnp.mean(inputs, axis=1, keepdims=True)
    spread = jnp.mean(centered * centered, axis=1, keepdims=True)
    inverse = lax.rsqrt(spread + 1e-05)
    return centered * inverse, inverse


def norm_back(inputs, gain, gradient):
    unit, inverse = norm_parts(inputs)
    gain_grad = jnp.sum(gradient * unit, axis=0, keepdims=True)
    shift_grad = jnp.sum(gradient, axis=0, keepdims=True)
    scaled = gradient * gain
    mean_one = jnp.mean(scaled, axis=1, keepdims=True)
    mean_two = jnp.mean(scaled * unit, axis=1, keepdims=True)
    return inverse * (scaled - mean_one - unit * mean_two), gain_grad, shift_grad


def band_of(length):
    offset = iota((length, length), 1) - iota((length, length), 0)
    return (offset <= WINDOW) & (offset >= -WINDOW)


def turn_rows(values, left):
    pieces = []
    for block in range(values.shape[0] // 8):
        if left:
            first, stride = (WINDOW + 8 * (block & 1), PERIOD - 1)
        else:
            first, stride = (PERIOD - WINDOW + 8 * (block & 1), 1)
        piece = values[block * 8 : (block + 1) * 8]
        pieces.append(pltpu.roll(piece, first, 1, stride=stride, stride_axis=0))
    return jnp.concatenate(pieces, axis=0)


def band_gather(weights_low, band, folding):
    kept = jnp.where(band, weights_low, jnp.zeros_like(weights_low))
    return turn_rows(dot_nn(kept, folding), True).astype(BF16)


def band_spread(near, band):
    turned = turn_rows(near, False)
    count = band.shape[1] // LANES
    return jnp.where(band, jnp.concatenate([turned] * count, axis=1), 0.0)


def folding_of(length):
    same = (iota((length, LANES), 0) & (PERIOD - 1)) == (iota((length, LANES), 1) & (PERIOD - 1))
    return jnp.where(same, 1.0, 0.0).astype(BF16)


def one_turn(rel_pad):
    return jnp.where(rows_of(LANES) < PERIOD, rel_pad, jnp.zeros_like(rel_pad))


def shifted_rows(values, offset, period):
    if offset == 0:
        return values
    length = values.shape[0]
    moved = pltpu.roll(values, (-offset) % length, 0)
    place = rows_of(length) & (period - 1)
    keep = (place < period - offset) if offset > 0 else (place >= -offset)
    return jnp.where(keep, moved, 0.0)


def unfold_rows(values, kernel, period, reverse=False):
    half = kernel // 2
    steps = [step - half for step in range(kernel)]
    if reverse:
        steps = [-step for step in steps]
    return jnp.concatenate(
        [shifted_rows(values, step, period).astype(BF16) for step in steps], axis=1
    )


GELU_A = math.sqrt(2.0 / math.pi)
GELU_B = 0.044715


def gelu_tanh(values):
    return jnp.tanh(GELU_A * (values + GELU_B * values * values * values))


def text_blocks(dur_ref, items):
    item = pl.program_id(0) * items
    rows = [dur_ref[pl.ds(item + i, 1), :] for i in range(items)]
    inside = [text_inside(row, row.shape[1]) for row in rows]
    return rows, jnp.concatenate(inside, axis=0)


def token_table(tok_ref, item):
    tokens = tok_ref[pl.ds(item, 1), :]
    return jnp.where(iota((VOCAB, tokens.shape[1]), 0) == tokens, 1.0, 0.0).astype(BF16)


def encoder_body(
    tok_ref,
    dur_ref,
    emb_ref,
    qkv_ref,
    relk_ref,
    relv_ref,
    out_ref,
    gain_ref,
    shift_ref,
    ff1_ref,
    ff2_ref,
    gain_two_ref,
    shift_two_ref,
    prior_ref,
    emb_low_ref,
    proj_ref,
    att_ref,
    banded_ref,
    attend_ref,
    mixed_ref,
    normed_low_ref,
    filt_ref,
    activ_ref,
    summed_ref,
    enc_ref,
    expand_ref,
    expand_low_ref,
):
    group, length, _ = emb_low_ref.shape
    first = pl.program_id(0) * group
    durations, inside = text_blocks(dur_ref, group)

    def rows(item):
        return slice(item * length, (item + 1) * length)

    def keep(ref, values):
        for item in range(group):
            ref[item] = values[rows(item)]

    looked = [dot_tn(token_table(tok_ref, first + i), emb_ref[...]) for i in range(group)]
    embedded = jnp.where(inside, jnp.concatenate(looked, axis=0) * math.sqrt(D), 0.0)
    emb_low = embedded.astype(BF16)
    keep(emb_low_ref, emb_low)
    proj = dot_nn(emb_low, qkv_ref[...]).astype(BF16)
    keep(proj_ref, proj)
    band = band_of(length)
    folding = folding_of(length)
    relv = one_turn(relv_ref[...])
    attended = []
    for item in range(group):
        key_bias = jnp.where(durations[item] > 0, 0.0, -10000.0)
        parts = []
        for head in range(HEADS):
            query, key, value = [
                proj[rows(item), part * LANES : (part + 1) * LANES]
                for part in (head, HEADS + head, 2 * HEADS + head)
            ]
            near = band_spread(dot_nt(query, relk_ref[...]), band)
            scores = (dot_nt(query, key) + near) * (1.0 / math.sqrt(HEAD)) + key_bias
            raised = jnp.exp(scores - jnp.max(scores, axis=1, keepdims=True))
            attention = raised * (1.0 / jnp.sum(raised, axis=1, keepdims=True))
            low = attention.astype(BF16)
            att_ref[item, head] = low
            banded = band_gather(low, band, folding)
            banded_ref[item, head] = banded
            parts.append(dot_nn(low, value) + dot_nn(banded, relv))
        attended.append(jnp.concatenate(parts, axis=1))
    attend = jnp.concatenate(attended, axis=0).astype(BF16)
    keep(attend_ref, attend)
    mixed = embedded + dot_nn(attend, out_ref[...])
    keep(mixed_ref, mixed)
    unit, _ = norm_parts(mixed)
    normed = unit * gain_ref[...] + shift_ref[...]
    masked = jnp.where(inside, normed, 0.0)
    keep(normed_low_ref, masked.astype(BF16))
    filtered = dot_nn(unfold_rows(masked, KSIZE, length), ff1_ref[...])
    keep(filt_ref, filtered.astype(BF16))
    activ = jnp.where(inside, 0.5 * filtered * (1.0 + gelu_tanh(filtered)), 0.0)
    keep(activ_ref, activ.astype(BF16))
    second = dot_nt(unfold_rows(activ, KSIZE, length), ff2_ref[...])
    summed = normed + jnp.where(inside, second, 0.0)
    keep(summed_ref, summed)
    unit, _ = norm_parts(summed)
    encoded = jnp.where(inside, unit * gain_two_ref[...] + shift_two_ref[...], 0.0).astype(BF16)
    keep(enc_ref, encoded)
    prior = dot_nn(encoded, prior_ref[...])
    high, low = halves(prior)
    wide = prior.shape[1] // 2
    for item in range(group):
        for side in range(2):
            spot = slice(side * length, (side + 1) * length)
            columns = slice(side * wide, (side + 1) * wide)
            expand_ref[item, spot] = high[rows(item), columns]
            expand_low_ref[item, spot] = low[rows(item), columns]


def accumulate(ref, values, first):
    @pl.when(first)
    def _():
        ref[...] = values

    @pl.when(jnp.logical_not(first))
    def _():
        ref[...] = ref[...] + values


def align_of(durations_row, pairs):
    length = durations_row.shape[1]
    upper = jnp.where(iota((length, length), 0) <= iota((length, length), 1), 1.0, 0.0).astype(F32)
    high = (durations_row >> 5).astype(F32)
    low = (durations_row & 31).astype(F32)
    both = jnp.where(iota((8, length), 0) == 0, high, low).astype(BF16)
    sums = dot_nn(both, upper.astype(BF16))
    ends = (32.0 * sums[0:1] + sums[1:2]).astype(jnp.int32)
    starts = ends - durations_row
    frame = 2 * rows_of(pairs)
    even = (frame >= starts) & (frame < ends)
    odd = (frame + 1 >= starts) & (frame + 1 < ends)
    both = jnp.concatenate([jnp.where(even, 1.0, 0.0), jnp.where(odd, 1.0, 0.0)], axis=1)
    return both.astype(BF16)


def encoder_back_body(
    tok_ref,
    dur_ref,
    flow_ref,
    enc_ref,
    summed_ref,
    filt_ref,
    activ_ref,
    normed_low_ref,
    mixed_ref,
    attend_ref,
    att_ref,
    banded_ref,
    proj_ref,
    emb_low_ref,
    wide_ref,
    ff1_ref,
    ff2_ref,
    gain_two_ref,
    prior_ref,
    qkv_ref,
    relk_ref,
    relv_ref,
    out_ref,
    gain_ref,
    place_ref,
    kept_ref,
    sent_ref,
    one_acc,
    two_acc,
    rest_acc,
    table_acc,
    qkv_acc,
    out_acc,
    relk_acc,
    relv_acc,
    prior_acc,
    norm_acc,
    sems,
):
    group, length, _ = emb_low_ref.shape
    step = pl.program_id(0)
    first = step == 0
    last = step == pl.num_programs(0) - 1
    durations, inside = text_blocks(dur_ref, group)
    mine = place_ref[0] & 1
    deals = []
    begin = 0
    for source in (one_acc, two_acc, rest_acc):
        half = source.shape[0] // 2
        for side, target in ((mine, kept_ref), (1 - mine, sent_ref)):
            deals.append(
                pltpu.make_async_copy(
                    source.at[pl.ds(pl.multiple_of(side * half, 8), half), :],
                    target.at[pl.ds(begin, half), :],
                    sems.at[len(deals)],
                )
            )
        begin += half
    everything = (one_acc, two_acc, table_acc, qkv_acc, out_acc, relk_acc, relv_acc, prior_acc, norm_acc)

    @pl.when(first)
    def _():
        for ref in everything:
            ref[...] = jnp.zeros_like(ref)

    def rows(item):
        return slice(item * length, (item + 1) * length)

    def whole(ref):
        return jnp.concatenate([ref[i] for i in range(group)], axis=0)

    def norm_sums(at, gain_grad, shift_grad):
        norm_acc[at : at + 1, :] = norm_acc[at : at + 1, :] + gain_grad
        norm_acc[at + 1 : at + 2, :] = norm_acc[at + 1 : at + 2, :] + shift_grad

    half = wide_ref.shape[1] // 2
    gathered = []
    for item in range(group):
        align = align_of(durations[item], flow_ref.shape[1])
        spread = dot_tn(align, flow_ref[item])
        pieces = []
        for side in range(2):
            pieces += halves(spread[side * length : (side + 1) * length])
        gathered.append(jnp.concatenate(pieces, axis=1))
    chosen = jnp.concatenate(
        [wide_ref[:, side * half : (side + 1) * half] for side in (0, 0, 1, 1)], axis=1
    )
    grad = dot_nt(jnp.concatenate(gathered, axis=0), chosen)
    prior_low = jnp.where(inside, grad, 0.0).astype(BF16)
    prior_acc[...] = prior_acc[...] + dot_tn(prior_low, whole(enc_ref))
    enc_grad = jnp.where(inside, dot_nn(prior_low, prior_ref[...]), 0.0)
    summed_grad, gain_grad, shift_grad = norm_back(whole(summed_ref), gain_two_ref[...], enc_grad)
    norm_sums(2, gain_grad, shift_grad)
    second = jnp.where(inside, summed_grad, 0.0)
    taps = unfold_rows(second, KSIZE, length, reverse=True)
    sums = dot_tn(taps, whole(activ_ref))
    for tap in range(KSIZE):
        for part in range(2):
            begin = (2 * tap + part) * D
            two_acc[begin : begin + D, :] = (
                two_acc[begin : begin + D, :]
                + sums[tap * D : (tap + 1) * D, part * WIDE : (part + 1) * WIDE]
            )
    activ_grad = dot_nn(
        taps,
        jnp.concatenate(
            [ff2_ref[:, tap * FILTER : (tap + 1) * FILTER] for tap in range(KSIZE)], axis=0
        ),
    )
    filtered = whole(filt_ref).astype(F32)
    tanh = gelu_tanh(filtered)
    slope = 0.5 * (1.0 + tanh) + 0.5 * filtered * (1.0 - tanh * tanh) * GELU_A * (
        1.0 + 3.0 * GELU_B * filtered * filtered
    )
    first_grad = jnp.where(inside, activ_grad * slope, 0.0)
    taps = unfold_rows(first_grad, KSIZE, length, reverse=True)
    sums = dot_tn(whole(normed_low_ref), taps)
    for tap in range(KSIZE):
        for part in range(2):
            begin = part * KSIZE * D + tap * D
            column = tap * FILTER + part * WIDE
            one_acc[begin : begin + D, :] = (
                one_acc[begin : begin + D, :] + sums[:, column : column + WIDE]
            )
    back = dot_nt(
        taps,
        jnp.concatenate([ff1_ref[tap * D : (tap + 1) * D, :] for tap in range(KSIZE)], axis=1),
    )

    @pl.when(last)
    def _():
        for copy in deals[:4]:
            copy.start()

    normed_grad = summed_grad + jnp.where(inside, back, 0.0)
    mixed_grad, gain_grad, shift_grad = norm_back(whole(mixed_ref), gain_ref[...], normed_grad)
    norm_sums(0, gain_grad, shift_grad)
    out_low = mixed_grad.astype(BF16)
    out_acc[...] = out_acc[...] + dot_tn(whole(attend_ref), out_low)
    weight = dot_nt(out_low, out_ref[...]).astype(BF16)
    band = band_of(length)
    folding = folding_of(length)
    relk = one_turn(relk_ref[...])
    projected = []
    relk_sum = relk_acc[...]
    relv_sum = relv_acc[...]
    for item in range(group):
        queries, keys, values = [], [], []
        for head in range(HEADS):
            query, key, value = [
                proj_ref[item, :, part * LANES : (part + 1) * LANES]
                for part in (head, HEADS + head, 2 * HEADS + head)
            ]
            mine = weight[rows(item), head * LANES : (head + 1) * LANES]
            near = band_spread(dot_nt(mine, relv_ref[...]), band)
            grad = dot_nt(mine, value) + near
            low = att_ref[item, head]
            attention = low.astype(F32)
            values.append(dot_tn(low, mine))
            relv_sum = relv_sum + dot_tn(banded_ref[item, head], mine)
            score = attention * (grad - jnp.sum(attention * grad, axis=1, keepdims=True))
            score_low = (score * (1.0 / math.sqrt(HEAD))).astype(BF16)
            band_grad = band_gather(score_low, band, folding)
            queries.append(dot_nn(score_low, key) + dot_nn(band_grad, relk))
            keys.append(dot_tn(score_low, query))
            relk_sum = relk_sum + dot_tn(band_grad, query)
        projected.append(jnp.concatenate(queries + keys + values, axis=1))
    relk_acc[...] = relk_sum
    relv_acc[...] = relv_sum
    proj_low = jnp.concatenate(projected, axis=0).astype(BF16)
    qkv_acc[...] = qkv_acc[...] + dot_tn(whole(emb_low_ref), proj_low)
    embed_grad = jnp.where(inside, mixed_grad + dot_nt(proj_low, qkv_ref[...]), 0.0) * math.sqrt(D)
    hot = jnp.concatenate(
        [token_table(tok_ref, step * group + item) for item in range(group)], axis=1
    )
    high, low = halves(embed_grad)
    table_acc[...] = table_acc[...] + dot_nn(
        jnp.concatenate([hot, hot], axis=1), jnp.concatenate([high, low], axis=0)
    )

    @pl.when(last)
    def _():
        def beside(left, right):
            return jnp.concatenate([left, right], axis=1)

        rest_acc[...] = jnp.zeros_like(rest_acc)
        packed = [qkv_acc[:, part * LANES : part * LANES + HEAD] for part in range(3 * HEADS)]
        side = D // 2
        rest_acc[:D, :] = jnp.concatenate(packed[:4], axis=1)
        rest_acc[D : D + side, :] = jnp.concatenate(
            [packed[4][:side], packed[5][:side], packed[4][side:], packed[5][side:]], axis=1
        )
        rest_acc[D + side : 2 * D, :] = beside(out_acc[:HEAD, :], out_acc[LANES : LANES + HEAD, :])
        rest_acc[ROW_TABLE : ROW_TABLE + MEL, :D] = table_acc[:MEL, :]
        rest_acc[ROW_TABLE : ROW_TABLE + VOCAB - MEL, D:] = table_acc[MEL:, :]
        rest_acc[ROW_PRIOR : ROW_PRIOR + MEL, :] = beside(prior_acc[:MEL, :], prior_acc[MEL:, :])
        rest_acc[ROW_NORM : ROW_NORM + 1, :] = beside(norm_acc[0:1, :], norm_acc[1:2, :])
        rest_acc[ROW_NORM + 1 : ROW_NORM + 2, :] = beside(norm_acc[2:3, :], norm_acc[3:4, :])
        rest_acc[ROW_REL : ROW_REL + PERIOD, :LANES] = relk_acc[:PERIOD, :]
        rest_acc[ROW_REL : ROW_REL + PERIOD, LANES : 2 * LANES] = relv_acc[:PERIOD, :]
        for copy in deals[4:]:
            copy.start()
        for copy in deals:
            copy.wait()


def split_pairs(mel_ref, rows_ref):
    frames = mel_ref.shape[2]
    pairs = frames // 2
    rows_ref[:, :MEL] = mel_ref[0].T
    pad = jnp.zeros((pairs, LANES - MEL), F32)
    even = rows_ref[pl.ds(0, pairs, stride=2), :][:, :MEL]
    odd = rows_ref[pl.ds(1, pairs, stride=2), :][:, :MEL]
    return jnp.concatenate([even, pad, odd, pad], axis=1)


def gates_of(pre):
    return jnp.tanh(pre[:, :HID]), 0.5 + 0.5 * jnp.tanh(0.5 * pre[:, HID:])


def dot_three(values, table, back=False):
    high, low = halves(values)
    table_high, table_low = halves(table)
    left = jnp.concatenate([high, low, high], axis=1)
    if back:
        return dot_nt(left, jnp.concatenate([table_high, table_high, table_low], axis=1))
    return dot_nn(left, jnp.concatenate([table_high, table_high, table_low], axis=0))


STEP_POST = WLAYERS + 1
STEPS = 2 * WLAYERS + 2


def decoder_body(
    mel_ref,
    dur_ref,
    expand_ref,
    expand_low_ref,
    stats_ref,
    mixm_ref,
    start_ref,
    win_ref,
    wres_ref,
    wend_ref,
    place_ref,
    kept_ref,
    sent_ref,
    last_kept_ref,
    last_sent_ref,
    flow_ref,
    ngrad_ref,
    normal,
    passive_low,
    hidden_low,
    pre,
    hidden,
    skip,
    active,
    skip_low,
    passive_grad,
    gated,
    part,
    spread,
    wide,
    unit,
    rows,
    end_acc,
    start_acc,
    mix_acc,
    tail,
    high,
    low,
    flow,
    sums,
    sems,
):
    step = pl.program_id(0)
    items, _, frames = mel_ref.shape
    pairs = frames // 2
    conv = WKER * HID
    fetch = [
        pltpu.make_async_copy(expand_ref, high, sems.at[0]),
        pltpu.make_async_copy(expand_low_ref, low, sems.at[1]),
    ]
    write = pltpu.make_async_copy(flow, flow_ref, sems.at[2])
    ngrad_write = pltpu.make_async_copy(normal, ngrad_ref, sems.at[5 + 2 * WLAYERS])
    mine = place_ref[0] & 1

    def deal(source, rows_each, targets, begin, first_sem):
        return [
            pltpu.make_async_copy(
                source.at[pl.ds(pl.multiple_of(side * rows_each, 8), rows_each), :],
                target.at[pl.ds(begin, rows_each), :],
                sems.at[first_sem + i],
            )
            for i, (side, target) in enumerate(((mine, targets[0]), (1 - mine, targets[1])))
        ]

    half = UNIT // 2
    deals = [deal(unit.at[0], half, (last_kept_ref, last_sent_ref), 0, 3)]
    for above in range(1, WLAYERS):
        begin = (WLAYERS - 1 - above) * half
        deals.append(deal(unit.at[above & 1], half, (kept_ref, sent_ref), begin, 3 + 2 * above))
    last_deal = deal(
        tail, TAIL // 2, (kept_ref, sent_ref), (WLAYERS - 1) * half, 3 + 2 * WLAYERS
    )

    def inside_item(item):
        return rows_of(pairs) < pair_rows(dur_ref[pl.ds(item, 1), :])

    def span(item):
        return pl.ds(pl.multiple_of(item * pairs, pairs), pairs)

    def each(body, count=items):
        def one(item, carry):
            body(item)
            return carry

        lax.fori_loop(0, count, one, 0, unroll=2 if count % 2 == 0 else 1)

    both = 2 if items % 2 == 0 else 1
    blocks = items // both
    block_rows = both * pairs

    def block_span(block):
        return pl.ds(pl.multiple_of(block * block_rows, block_rows), block_rows)

    def inside_block(block):
        return jnp.concatenate([inside_item(block * both + i) for i in range(both)], axis=0)

    @pl.when(step == 0)
    def _():
        for copy in fetch:
            copy.start()
        _, center, _, _, scale = read_stats(stats_ref[...])

        def one(item):
            inside = inside_item(item)
            rows[:, :MEL] = mel_ref[item].T
            pad = jnp.zeros((pairs, LANES - MEL), F32)
            even = rows[pl.ds(0, pairs, stride=2), :][:, :MEL]
            odd = rows[pl.ds(1, pairs, stride=2), :][:, :MEL]
            values = jnp.concatenate([even, pad, odd, pad], axis=1)
            normalized = jnp.where(inside, (values - center) * scale, 0.0)
            normal[item] = normalized
            turned = dot_three(normalized, mixm_ref[...])
            passive = turned[:, :LANES]
            passive_grad[item] = passive
            active[item] = turned[:, LANES:]
            low_now = passive.astype(BF16)
            passive_low[item] = low_now
            hidden[span(item), :] = jnp.where(inside, dot_nn(low_now, start_ref[...]), 0.0)
            skip[span(item), :] = jnp.zeros((pairs, HID), F32)

        each(one)

    @pl.when((step >= 1) & (step <= WLAYERS))
    def _():
        layer = step - 1

        def one(block):
            here = block_span(block)
            state = hidden[here, :]
            hidden_low[layer, here, :] = state.astype(BF16)
            pre_gate = dot_nn(unfold_rows(state, WKER, pairs), win_ref[0])
            pre[layer, here, :] = pre_gate.astype(BF16)
            tanh, gate = gates_of(pre_gate)
            sums = dot_nn((tanh * gate).astype(BF16), wres_ref[layer])
            hidden[here, :] = jnp.where(inside_block(block), state + sums[:, :HID], 0.0)
            skip[here, :] = skip[here, :] + sums[:, HID:]

        each(one, blocks)

    @pl.when(step == STEP_POST)
    def _():
        for copy in fetch:
            copy.wait()
        total, _, _, _, _ = read_stats(stats_ref[...])
        unit_grad = 1.0 / (2 * MEL * total)
        end_acc[...] = jnp.zeros_like(end_acc)
        sums[...] = jnp.zeros_like(sums)

        def one(item):
            inside = inside_item(item)
            output_low = jnp.where(inside, skip[span(item), :], 0.0).astype(BF16)
            coupled = jnp.where(inside, dot_nn(output_low, wend_ref[...]), 0.0)
            shift_part = coupled[:, :LANES]
            log_part = coupled[:, LANES:]
            growth = jnp.exp(log_part)
            moving = active[item]
            moved = jnp.where(inside, shift_part + growth * moving, 0.0)
            align = align_of(dur_ref[pl.ds(item, 1), :], pairs)
            prior = dot_nn(align, high[item]) + dot_nn(align, low[item])
            latent = jnp.concatenate([passive_grad[item], moved], axis=1)
            gap = latent - prior[:, : 2 * LANES]
            log_scales = prior[:, 2 * LANES :]
            scaled = jnp.exp(-2.0 * log_scales) * gap
            square = scaled * gap
            terms = jnp.where(inside, log_scales + 0.5 * square, 0.0)
            term = jnp.sum(terms, axis=0, keepdims=True)
            nll = term[:, :LANES] + term[:, LANES:] - jnp.sum(log_part, axis=0, keepdims=True)
            sums[4:5, :] = sums[4:5, :] + nll
            latent_grad = jnp.where(inside, unit_grad * scaled, 0.0)
            scale_grad = jnp.where(inside, unit_grad * (1.0 - square), 0.0)
            flow[item] = jnp.concatenate([-latent_grad, scale_grad], axis=1).astype(BF16)
            passive_grad[item] = latent_grad[:, :LANES]
            moved_grad = latent_grad[:, LANES:]
            active_grad = moved_grad * growth
            log_grad = jnp.where(inside, active_grad * moving - unit_grad, 0.0)
            active[item] = active_grad
            coupled_low = jnp.concatenate([moved_grad, log_grad], axis=1).astype(BF16)
            end_acc[...] = end_acc[...] + dot_tn(coupled_low, output_low)
            skip_grad = jnp.where(inside, dot_nt(coupled_low, wend_ref[...]), 0.0)
            skip_low[span(item), :] = skip_grad.astype(BF16)
            hidden[span(item), :] = jnp.zeros((pairs, HID), F32)

        each(one)
        write.start()

    @pl.when(step > STEP_POST)
    def _():
        layer = STEPS - 1 - step
        for tap in range(WKER):
            wide[:, tap * 2 * HID : (tap + 1) * 2 * HID] = win_ref[
                0, tap * HID : (tap + 1) * HID, :
            ]

        def one(block):
            here = block_span(block)
            tanh, gate = gates_of(pre[layer, here, :].astype(F32))
            gated[here, :] = (tanh * gate).astype(BF16)
            kept = hidden[here, :]
            left = jnp.concatenate([kept, skip_low[here, :].astype(F32)], axis=1).astype(BF16)
            part[here, :] = left
            gated_grad = dot_nt(left, wres_ref[layer])
            tanh_grad = gated_grad * gate * (1.0 - tanh * tanh)
            gate_grad = gated_grad * tanh * gate * (1.0 - gate)
            pre_grad = jnp.concatenate([tanh_grad, gate_grad], axis=1)
            taps = unfold_rows(pre_grad, WKER, pairs, reverse=True)
            spread[here, :] = taps
            back = kept + dot_nt(taps, wide[...])
            hidden[here, :] = jnp.where(inside_block(block), back, 0.0)

        each(one, blocks)
        for later in range(WLAYERS - 2):

            @pl.when(layer == later)
            def _(later=later):
                for copy in deals[later + 2]:
                    copy.wait()

        parity = layer & 1
        found = dot_tn(hidden_low[layer], spread[...])
        for tap in range(WKER):
            unit[parity, tap * HID : (tap + 1) * HID, :] = found[
                :, tap * 2 * HID : (tap + 1) * 2 * HID
            ]
        unit[parity, conv:, :] = dot_tn(gated[...], part[...])

        @pl.when(layer == WLAYERS - 1)
        def _():
            side = (WLAYERS - 1) & 1
            unit[side, conv : conv + MEL, :HID] = end_acc[:MEL, :]
            unit[side, conv + MEL : conv + 2 * MEL, :HID] = end_acc[LANES : LANES + MEL, :]

        for now in range(WLAYERS):

            @pl.when(layer == now)
            def _(now=now):
                for copy in deals[now]:
                    copy.start()

    @pl.when(step == STEPS - 1)
    def _():
        start_acc[...] = jnp.zeros_like(start_acc)
        mix_acc[...] = jnp.zeros_like(mix_acc)

        def one(item):
            start_low = hidden[span(item), :].astype(BF16)
            start_acc[...] = start_acc[...] + dot_tn(passive_low[item], start_low)
            turned_passive = passive_grad[item] + dot_nt(start_low, start_ref[...])
            turned_grad = jnp.concatenate([turned_passive, active[item]], axis=1)
            normalized = normal[item]
            mix_acc[...] = mix_acc[...] + dot_tn(
                normalized.astype(BF16), turned_grad.astype(BF16)
            )
            normal_grad = dot_three(turned_grad, mixm_ref[...], back=True)
            normal_grad = jnp.where(inside_item(item), normal_grad, 0.0)
            normal[item] = normal_grad
            one_sum = jnp.sum(normal_grad, axis=0, keepdims=True)
            two_sum = jnp.sum(normal_grad * normalized, axis=0, keepdims=True)
            for at, found in ((0, one_sum), (2, two_sum)):
                sums[at : at + 1, :] = sums[at : at + 1, :] + found[:, :LANES]
                sums[at + 1 : at + 2, :] = sums[at + 1 : at + 2, :] + found[:, LANES:]

        each(one)
        ngrad_write.start()
        tail[...] = jnp.zeros_like(tail)
        cut = MEL // 2
        tail[:cut, :] = jnp.concatenate([start_acc[:cut, :], start_acc[cut:MEL, :]], axis=1)
        row_member, col_member, match = mix_places()
        kept = jnp.where(match, mix_acc[...], 0.0)
        ri = iota((8, LANES), 0)
        ci = iota((8, LANES), 1)
        mixed = jnp.zeros((8, LANES), F32)
        for i in range(4):
            column = jnp.sum(jnp.where(col_member == i, kept, 0.0), axis=1, keepdims=True)
            for j in range(4):
                entry = jnp.sum(jnp.where(row_member == j, column, 0.0), axis=0, keepdims=True)
                mixed = jnp.where((ri == i) & (ci == j), entry, mixed)
        tail[cut : cut + 8, :LANES] = mixed
        tail[cut : cut + 8, LANES : 2 * LANES] = sums[...]
        for copy in last_deal:
            copy.start()
        for copy in (*last_deal, *deals[0], *deals[1], write, ngrad_write):
            copy.wait()


def frames_body(
    mel_ref, dur_ref, ngrad_ref, stats_ref, sums_ref, small_ref, out_ref, loss_ref, rows_ref
):
    pairs = mel_ref.shape[2] // 2
    inside = rows_of(pairs) < pair_rows(text_rows(dur_ref))
    total, center, variance, log_act, scale = read_stats(stats_ref[...])
    unit = 1.0 / (2 * MEL * total)
    sums = sums_ref[...]
    spot = iota((1, 2 * LANES), 1) & (LANES - 1)
    log_sum = jnp.sum(jnp.where(spot < MEL, log_act, 0.0), axis=1, keepdims=True)
    nll = jnp.sum(sums[4:5], axis=1, keepdims=True)
    log_det = jnp.log(small_ref[4:5, 0:1])
    loss = (nll - total * log_sum - total * (MEL // 2) * log_det) * unit
    loss_ref[...] = loss + 0.5 * math.log(2.0 * math.pi)
    one = jnp.concatenate([sums[0:1], sums[1:2]], axis=1)
    two = jnp.concatenate([sums[2:3], sums[3:4]], axis=1)
    log_grad = two - unit * total
    var_grad = -0.5 * log_grad / (variance + 1e-06)
    center_grad = -scale * one - 2.0 * center * var_grad
    values = split_pairs(mel_ref, rows_ref)
    grads = ngrad_ref[0] * scale + (2.0 * values * var_grad + center_grad) / total
    grads = jnp.where(inside, grads, 0.0) * (2 * MEL * total)
    rows_ref[pl.ds(0, pairs, stride=2), :] = grads[:, :LANES]
    rows_ref[pl.ds(1, pairs, stride=2), :] = grads[:, LANES:]
    out_ref[0] = rows_ref[...].T[:MEL, :]


def swap(values, bit, devices):
    return lax.ppermute(values, "dp", [(i, i ^ bit) for i in range(devices)])


def swap_half(unit, devices):
    kept, sent = unit
    return kept, swap(sent, 1, devices)


def digits(devices, shift=1):
    found = []
    while (1 << shift) < devices:
        radix = 4 if (1 << (shift + 2)) <= devices else 2
        found.append((shift, radix))
        shift += 2 if radix == 4 else 1
    return found


def whole_vmem(count):
    return [pl.BlockSpec(memory_space=pltpu.VMEM)] * count


def call_whole(body, place, ins, outs, scratch, after, micros, name):
    count, given = len(ins), len(outs)

    def wrapped(place_ref, *refs):
        sources, targets = refs[:count], refs[count : count + given]
        held, sems = refs[count + given : 2 * count + given], refs[-1]
        copies = [
            pltpu.make_async_copy(source, target, sems.at[i])
            for i, (source, target) in enumerate(zip(sources, held))
        ]
        for copy in copies:
            copy.start()
        for copy in copies:
            copy.wait()
        body(place_ref, *held, *targets, *refs[2 * count + given : -1])

    return run(
        wrapped,
        (),
        [place, *ins],
        [pl.BlockSpec(memory_space=pltpu.SMEM)] + [pl.BlockSpec(memory_space=pl.ANY)] * count,
        outs,
        whole_vmem(given),
        [pltpu.VMEM(array.shape, array.dtype) for array in ins]
        + list(scratch)
        + [pltpu.SemaphoreType.DMA((count,))],
        micros=micros,
        after=after,
        name=name,
        vmem=VMEM_WHOLE,
    )


def call_parts(plan, place, ins, outs, after, name):
    count, given = len(ins), len(outs)
    layers = 1 + max(
        layer for _, pieces in plan(None) for layer in (piece[4] for piece in pieces)
    )
    pieces_all = sum(len(pieces) for _, pieces in plan(None))

    def body(place_ref, *refs):
        sources, targets = refs[:count], refs[count : count + given]
        held = refs[count + given : count + 2 * given]
        in_sems, out_sems = refs[-2:]
        todo = []
        at = 0
        for out, pieces in plan(place_ref):
            copies = []
            for source, begin, rows, spot, layer in pieces:
                copies.append(
                    pltpu.make_async_copy(
                        sources[source].at[pl.ds(pl.multiple_of(begin, 8), rows), :],
                        held[out].at[(layer, *spot[:-1], pl.ds(spot[-1], rows))],
                        in_sems.at[at],
                    )
                )
                copies[-1].start()
                at += 1
            todo.append((out, copies))
        writes = []
        for out, copies in todo:
            for copy in copies:
                copy.wait()
            value = held[out][0]
            for layer in range(1, layers):
                value = value + held[out][layer]
            held[out][0] = value
            writes.append(pltpu.make_async_copy(held[out].at[0], targets[out], out_sems.at[out]))
            writes[-1].start()
        for write in writes:
            write.wait()

    anywhere = pl.BlockSpec(memory_space=pl.ANY)
    return run(
        body,
        (),
        [place, *ins],
        [pl.BlockSpec(memory_space=pltpu.SMEM)] + [anywhere] * count,
        outs,
        [anywhere] * given,
        [pltpu.VMEM((layers, *out.shape), F32) for out in outs]
        + [pltpu.SemaphoreType.DMA((pieces_all,)), pltpu.SemaphoreType.DMA((given,))],
        micros=25,
        after=after,
        name=name,
        vmem=VMEM_WHOLE,
    )


def hop_out(jobs, place, after=()):
    units, shift, radix = jobs[0]
    row = units[0][0].shape[0] // radix
    if len(jobs) == 1 and len(units) == 1 and row % 8 == 0:
        arrays = units[0]

        def by_parts(place_ref):
            digit = 0 if place_ref is None else (place_ref[0] >> shift) & (radix - 1)
            return [
                (step, [(k, (digit ^ step) * row, row, (0,), k) for k in range(len(arrays))])
                for step in (*range(1, radix), 0)
            ]

        return [call_parts(by_parts, place, arrays, [shape_of((row, WIDE))] * radix, after, "hop_out")]
    ins = []
    outs = []
    scratch = []
    plans = []
    for units, shift, radix in jobs:
        plan = []
        begin = 0
        for unit in units:
            row = unit[0].shape[0] // radix
            plan.append((len(ins), len(unit), row, begin))
            ins += unit
            begin += row
        plans.append((plan, len(outs), shift, radix))
        outs += [shape_of((begin, WIDE))] * radix
        aligned = all(row % 8 == 0 for _, _, row, _ in plan)
        scratch.append(pltpu.VMEM((1, 8, LANES) if aligned else (radix, begin, WIDE), F32))
    n_in, n_out = len(ins), len(outs)

    def body(place_ref, *refs):
        out_refs = refs[n_in : n_in + n_out]
        tables = refs[n_in + n_out :]
        for (plan, at, shift, radix), table in zip(plans, tables):
            digit = (place_ref[0] >> shift) & (radix - 1)
            if all(row % 8 == 0 for _, _, row, _ in plan):
                for step in range(radix):
                    for first, count, row, begin in plan:
                        span = pl.ds(pl.multiple_of((digit ^ step) * row, 8), row)
                        value = refs[first][span, :]
                        for extra in range(1, count):
                            value = value + refs[first + extra][span, :]
                        out_refs[at + step][begin : begin + row, :] = value
                continue
            for first, count, row, begin in plan:
                for part in range(radix):
                    span = slice(part * row, (part + 1) * row)
                    value = refs[first][span, :]
                    for extra in range(1, count):
                        value = value + refs[first + extra][span, :]
                    table[part, begin : begin + row, :] = value
            for step in range(radix):
                out_refs[at + step][...] = table[digit ^ step]

    found = call_whole(body, place, ins, outs, scratch, after, 25, "hop_out")
    return [found[at : at + radix] for _, at, _, radix in plans]


def hop_in(jobs, place, after=()):
    ins = []
    outs = []
    plans = []
    for parts, shift in jobs:
        plans.append((len(ins), len(parts), shift))
        ins += parts
        outs.append(shape_of((len(parts), *parts[0].shape)))
    n_in = len(ins)

    def body(place_ref, *refs):
        for (first, radix, shift), out in zip(plans, refs[n_in:]):
            digit = (place_ref[0] >> shift) & (radix - 1)
            for step in range(radix):
                out[digit ^ step] = refs[first + step][...]

    return call_whole(body, place, ins, outs, (), after, 25, "hop_in")


def add_parts(jobs, place, after=()):
    ins = [part for parts in jobs for part in parts]
    outs = [shape_of(parts[0].shape) for parts in jobs]
    n_in = len(ins)

    def body(place_ref, *refs):
        at = 0
        for parts, out in zip(jobs, refs[n_in:]):
            value = refs[at][...]
            for extra in range(at + 1, at + len(parts)):
                value = value + refs[extra][...]
            out[...] = value
            at += len(parts)

    return call_whole(body, place, ins, outs, (), after, 25, "add_parts")


def send_parts(parts, shift, devices):
    return [parts[0]] + [
        swap(part, step << shift, devices) for step, part in enumerate(parts) if step > 0
    ]


def spread_level(units, level, place, devices, after=()):
    shift, radix = digits(devices)[level]
    parts = hop_out([(units, shift, radix)], place, after)[0]
    return send_parts(parts, shift, devices)


def gather_level(part, level, place, devices, after=()):
    shift, radix = digits(devices)[level]
    return hop_in([(send_parts([part] * radix, shift, devices), shift)], place, after)[0]


def first_bits(place_ref):
    return (place_ref[0] >> 1) & 1, (place_ref[0] >> 2) & 1


def pair_send(pair, first_bit, second_bit, devices):
    (kept, sent), (other_kept, other_sent) = pair
    return [kept, swap(sent, first_bit, devices)], [other_kept, swap(other_sent, second_bit, devices)]


def pair_out(units, place, devices, after=()):
    ins = [array for unit in units for array in unit]
    rows = [unit[0].shape[0] // 8 for unit in units]
    total = sum(rows)

    def by_parts(place_ref):
        low, high = (0, 0) if place_ref is None else first_bits(place_ref)
        found = []
        for out, half, mine in ((1, 0, 1 - low), (3, 1, 1 - high), (0, 0, low), (2, 1, high)):
            pieces = []
            for other in range(2):
                digit = mine + 2 * other if half == 0 else other + 2 * mine
                at = 0
                begin = 0
                for unit, row in zip(units, rows):
                    for layer in range(len(unit)):
                        pieces.append(
                            (at + layer, (2 * digit + half) * row, row, (other, begin), layer)
                        )
                    at += len(unit)
                    begin += row
            found.append((out, pieces))
        return found

    outs = [shape_of((2, total, WIDE))] * 4
    found = call_parts(by_parts, place, ins, outs, after, "pair_out")
    return pair_send((found[:2], found[2:]), 2, 4, devices)


def pair_next(pair, place, devices, after=()):
    ins = [*pair[0], *pair[1]]

    def body(place_ref, one, one_more, two, two_more, *outs):
        low, high = first_bits(place_ref)
        for first, more, mine, kept, sent in (
            (one, one_more, high, outs[0], outs[1]),
            (two, two_more, low, outs[2], outs[3]),
        ):
            kept[...] = first[mine] + more[mine]
            sent[...] = first[1 - mine] + more[1 - mine]

    outs = [shape_of(ins[0].shape[1:])] * 4
    found = call_whole(body, place, ins, outs, (), after, 25, "pair_next")
    return pair_send((found[:2], found[2:]), 4, 2, devices)


def pair_level(pair, level, place, devices, after=()):
    shift, radix = digits(devices)[level]
    ins = [*pair[0], *pair[1]]
    rows = ins[0].shape[0]
    part = 2 * rows // radix

    def body(place_ref, one, one_more, two, two_more, *refs):
        table = refs[-1]
        digit = (place_ref[0] >> shift) & (radix - 1)
        for half, (first, more) in enumerate(((one, one_more), (two, two_more))):
            value = first[...] + more[...]
            for i in range(radix // 2):
                table[half * (radix // 2) + i] = value[i * part : (i + 1) * part, :]
        for step in range(radix):
            refs[step][...] = table[digit ^ step]

    outs = [shape_of((part, WIDE))] * radix
    scratch = [pltpu.VMEM((radix, part, WIDE), F32)]
    parts = call_whole(body, place, ins, outs, scratch, after, 25, "pair_level")
    return send_parts(parts, shift, devices)


def gather_pair(part, level, place, devices, after=()):
    shift, radix = digits(devices)[level]
    parts = send_parts([part.reshape(-1, WIDE)] * radix, shift, devices)
    rows = parts[0].shape[0]

    def body(place_ref, *refs):
        table = refs[-1]
        digit = (place_ref[0] >> shift) & (radix - 1)
        for step in range(radix):
            table[digit ^ step] = refs[step][...]
        for half in range(2):
            for i in range(radix // 2):
                refs[radix + half][i * rows : (i + 1) * rows, :] = table[half * (radix // 2) + i]

    outs = [shape_of((rows * radix // 2, WIDE))] * 2
    scratch = [pltpu.VMEM((radix, rows, WIDE), F32)]
    return call_whole(body, place, parts, outs, scratch, after, 25, "gather_pair")


def pair_join(one, two, place, devices, after=()):
    one_more = swap(one, 4, devices)
    two_more = swap(two, 2, devices)

    def body(place_ref, one_ref, one_more_ref, two_ref, two_more_ref, *outs):
        low, high = first_bits(place_ref)
        for first, more, mine, out in (
            (one_ref, one_more_ref, high, outs[0]),
            (two_ref, two_more_ref, low, outs[1]),
        ):
            out[mine] = first[...]
            out[1 - mine] = more[...]

    outs = [shape_of((2, *one.shape))] * 2
    ins = [one, one_more, two, two_more]
    one, two = call_whole(body, place, ins, outs, (), after, 25, "pair_join")
    return [one, swap(one, 2, devices), two, swap(two, 4, devices)]


def table_parts(place_ref, mine_refs, other_refs, table, sems):
    low, high = first_bits(place_ref)
    core = place_ref[0] & 1
    copies = []
    for side, refs in ((core, mine_refs), (1 - core, other_refs)):
        for half, bit in ((0, low), (1, high)):
            for step in range(2):
                mine = bit ^ step
                for other in range(2):
                    digit = mine + 2 * other if half == 0 else other + 2 * mine
                    copies.append(
                        pltpu.make_async_copy(
                            refs[2 * half + step].at[other],
                            table.at[side, 2 * digit + half],
                            sems.at[len(copies)],
                        )
                    )
    for copy in copies:
        copy.start()
    for copy in copies:
        copy.wait()


def segments(begin, count, rows):
    found = []
    at = begin
    while at < begin + count:
        part, row = divmod(at, rows)
        size = min(rows - row, begin + count - at)
        found.append((part, row, size, at - begin))
        at += size
    return found


def unpack_upper_body(place_ref, small_ref, *refs):
    mine, other = refs[:4], refs[4:8]
    in_ref, res_ref, last_ref, end_ref, start_ref, mix_ref, sums_ref, table, tail, sems, first_sems = refs[8:]
    table_parts(place_ref, mine, other, table, first_sems)
    rows = table.shape[2]
    conv = WKER * HID
    half = UNIT // 2
    copies = []

    def move(core, begin, count, target, at):
        for part, row, size, place in segments(begin, count, rows):
            copies.append(
                pltpu.make_async_copy(
                    table.at[core, part, pl.ds(row, size), :],
                    target.at[pl.ds(at + place, size), :],
                    sems.at[len(copies)],
                )
            )

    for layer in range(1, WLAYERS):
        begin = (WLAYERS - 1 - layer) * half
        move(0, begin, half, in_ref.at[layer], 0)
        move(1, begin, conv - half, in_ref.at[layer], half)
        if layer < WLAYERS - 1:
            move(1, begin + conv - half, HID, res_ref.at[layer], 0)
    for copy in copies:
        copy.start()
    for part, row, size, at in segments(conv - half, HID, rows):
        values = table[1, part, row : row + size, :]
        last_ref[at : at + size, :] = values[:, HID:]
        end_ref[at : at + size, :] = values[:, :HID]
    for core in range(2):
        for part, row, size, at in segments((WLAYERS - 1) * half, TAIL // 2, rows):
            begin = core * (TAIL // 2) + at
            tail[begin : begin + size, :] = table[core, part, row : row + size, :]
    cut = MEL // 2
    start_ref[:cut, :] = tail[:cut, :HID]
    start_ref[cut:, :] = tail[:cut, HID:]
    mix_ref[...] = tail[cut : cut + 8, :LANES] - small_ref[...] / 4.0
    sums_ref[...] = tail[cut : cut + 8, LANES : 2 * LANES]
    for copy in copies:
        copy.wait()


def unpack_upper(parts, other, place, small, after):
    vmem = pl.BlockSpec(memory_space=pltpu.VMEM)
    anywhere = pl.BlockSpec(memory_space=pl.ANY)
    outs = [
        shape_of((WLAYERS, WKER * HID, 2 * HID)),
        shape_of((WLAYERS - 1, HID, 2 * HID)),
        shape_of((HID, HID)),
        shape_of((HID, HID)),
        shape_of((MEL, HID)),
        shape_of((8, LANES)),
        shape_of((8, LANES)),
    ]
    return run(
        unpack_upper_body,
        (),
        [place, small, *parts, *other],
        [pl.BlockSpec(memory_space=pltpu.SMEM), vmem] + [anywhere] * 8,
        outs,
        [anywhere] * 2 + [vmem] * 5,
        [
            pltpu.VMEM((2, 8, *parts[0].shape[1:]), F32),
            pltpu.VMEM((TAIL, WIDE), F32),
            pltpu.SemaphoreType.DMA((64,)),
            pltpu.SemaphoreType.DMA((16,)),
        ],
        micros=5,
        after=after,
        name="unpack_upper",
        vmem=VMEM_WHOLE,
    )


def unpack_lower_body(place_ref, in_given, res_given, *refs):
    mine, other = refs[:4], refs[4:8]
    (
        in_ref,
        res_ref,
        one_ref,
        two_ref,
        table_ref,
        qkv_ref,
        out_ref,
        relk_ref,
        relv_ref,
        prior_ref,
        *norm_refs,
        table,
        rest,
        sems,
        first_sems,
    ) = refs[8:]
    table_parts(place_ref, mine, other, table, first_sems)
    conv = WKER * HID
    half = UNIT // 2
    eighth = half // 8
    copies = []
    for core in range(2):
        for block in range(8):
            at = core * half + block * eighth
            pieces = [(0, max(0, min(eighth, conv - at)), in_ref, at)]
            pieces.append((pieces[0][1], eighth - pieces[0][1], res_ref, at + pieces[0][1] - conv))
            for row, size, target, to in pieces:
                if size:
                    copies.append(
                        pltpu.make_async_copy(
                            table.at[core, block, pl.ds(row, size), :],
                            target.at[0, pl.ds(to, size), :],
                            sems.at[len(copies)],
                        )
                    )
    for copy in copies:
        copy.start()
    rows = table.shape[2] - eighth

    def read(core, begin, count):
        return [
            (table[core, part, eighth + row : eighth + row + size, :], at)
            for part, row, size, at in segments(begin, count, rows)
        ]

    for core in range(2):
        for values, at in read(core, 0, half):
            one_ref[at : at + values.shape[0], core * WIDE : (core + 1) * WIDE] = values
        for third in range(KSIZE):
            block = core * KSIZE + third
            for values, at in read(core, half + third * D, D):
                two_ref[at : at + values.shape[0], block * WIDE : (block + 1) * WIDE] = values
        for values, at in read(core, 2 * half, REST // 2):
            begin = core * (REST // 2) + at
            rest[begin : begin + values.shape[0], :] = values
    side = D // 2
    qkv_ref[:, :WIDE] = rest[:D, :]
    qkv_ref[:side, WIDE:] = rest[D : D + side, :D]
    qkv_ref[side:, WIDE:] = rest[D : D + side, D:]
    out_ref[:side, :] = rest[D + side : 2 * D, :D]
    out_ref[side:, :] = rest[D + side : 2 * D, D:]
    table_ref[:MEL, :] = rest[ROW_TABLE : ROW_TABLE + MEL, :D]
    table_ref[MEL:, :] = rest[ROW_TABLE : ROW_TABLE + VOCAB - MEL, D:]
    prior_ref[:MEL, :] = rest[ROW_PRIOR : ROW_PRIOR + MEL, :D]
    prior_ref[MEL:, :] = rest[ROW_PRIOR : ROW_PRIOR + MEL, D:]
    relk_ref[...] = rest[ROW_REL : ROW_REL + 2 * WINDOW + 1, :HEAD]
    relv_ref[...] = rest[ROW_REL : ROW_REL + 2 * WINDOW + 1, LANES : LANES + HEAD]
    for i, ref in enumerate(norm_refs):
        row = rest[ROW_NORM + (i >> 1) : ROW_NORM + (i >> 1) + 1, :]
        ref[...] = row[:, (i & 1) * D : (i & 1) * D + D].reshape(D)
    for copy in copies:
        copy.wait()


def unpack_lower(parts, other, place, in_grad, res_grad):
    vmem = pl.BlockSpec(memory_space=pltpu.VMEM)
    anywhere = pl.BlockSpec(memory_space=pl.ANY)
    reach = 2 * WINDOW + 1
    outs = [
        shape_of(in_grad.shape),
        shape_of(res_grad.shape),
        shape_of((KSIZE * D, FILTER)),
        shape_of((D, KSIZE * FILTER)),
        shape_of((VOCAB, D)),
        shape_of((D, 3 * D)),
        shape_of((D, D)),
        shape_of((reach, HEAD)),
        shape_of((reach, HEAD)),
        shape_of((2 * MEL, D)),
        *[shape_of((D,))] * 4,
    ]
    return run(
        unpack_lower_body,
        (),
        [place, in_grad, res_grad, *parts, *other],
        [pl.BlockSpec(memory_space=pltpu.SMEM)] + [anywhere] * 10,
        outs,
        [anywhere] * 2 + [vmem] * (len(outs) - 2),
        [
            pltpu.VMEM((2, 8, *parts[0].shape[1:]), F32),
            pltpu.VMEM((REST, WIDE), F32),
            pltpu.SemaphoreType.DMA((32,)),
            pltpu.SemaphoreType.DMA((16,)),
        ],
        micros=5,
        aliases={1: 0, 2: 1},
        name="unpack_lower",
        vmem=VMEM_WHOLE,
    )


def on_device(
    devices,
    token_ids,
    durations,
    mel_frames,
    embedding,
    w_qkv,
    rel_key,
    rel_value,
    w_out,
    attn_gain,
    attn_shift,
    w_ff1,
    w_ff2,
    ffn_gain,
    ffn_shift,
    w_prior,
    w_mix,
    w_start,
    w_in,
    w_res,
    w_skip_last,
    w_end,
):
    items, length = token_ids.shape
    frames = mel_frames.shape[1]
    mel_frames = mel_frames.transpose(0, 2, 1)
    ff2_t = w_ff2.T
    prior_t = w_prior.T
    end_t = w_end.T
    pairs = frames // 2
    grid = (items,)
    place = lax.axis_index("dp").reshape(1).astype(jnp.int32)

    def halves_of(rows):
        return [shape_of((rows // 2, WIDE))] * 2

    vmem = pl.BlockSpec(memory_space=pltpu.VMEM)
    smem = pl.BlockSpec(memory_space=pltpu.SMEM)
    gain_one = attn_gain.reshape(1, D)
    shift_one = attn_shift.reshape(1, D)
    gain_two = ffn_gain.reshape(1, D)
    shift_two = ffn_shift.reshape(1, D)

    stats = run(
        stats_body, (), [mel_frames, durations], [vmem] * 2, shape_of((8, LANES)), vmem, name="stats"
    )
    stats_steps = digits(devices, 0)
    shift, radix = stats_steps[0]
    local_stats = stats
    stats = sum(send_parts([stats] * radix, shift, devices))

    prepared = [
        shape_of((2 * LANES, 2 * LANES)),
        shape_of((8, LANES)),
        shape_of((D, 6 * LANES), BF16),
        shape_of((LANES, LANES), BF16),
        shape_of((LANES, LANES), BF16),
        shape_of((2 * LANES, D), BF16),
        shape_of((2 * MEL, 8 * LANES), BF16),
        shape_of((D, 8 * LANES), BF16),
        shape_of((LANES, HID), BF16),
        shape_of((HID, 2 * LANES), BF16),
        shape_of((WLAYERS, HID, 2 * HID), BF16),
    ]
    (
        mixm,
        small,
        qkv_pad,
        relk_pad,
        relv_pad,
        out_pad,
        wide,
        prior_pad,
        start_pad,
        end_pad,
        res_four,
    ) = run(
        weights_body,
        (),
        [w_mix, w_qkv, rel_key, rel_value, w_out, prior_t, w_start, end_t, w_res, w_skip_last],
        [smem] + [vmem] * 9,
        prepared,
        [vmem] * len(prepared),
        after=(local_stats,),
        name="weights",
    )

    group = 2 if items % 2 == 0 else 1

    def group_spec(array):
        rank = len(array.shape)
        return pl.BlockSpec((group,) + array.shape[1:], lambda b: (b,) + (0,) * (rank - 1))

    ins = [
        token_ids,
        durations,
        embedding,
        qkv_pad,
        relk_pad,
        relv_pad,
        out_pad,
        gain_one,
        shift_one,
        w_ff1,
        ff2_t,
        gain_two,
        shift_two,
        prior_pad,
    ]
    outs = [
        shape_of((items, length, D), BF16),
        shape_of((items, length, 6 * LANES), BF16),
        shape_of((items, HEADS, length, length), BF16),
        shape_of((items, HEADS, length, LANES), BF16),
        shape_of((items, length, 2 * LANES), BF16),
        shape_of((items, length, D)),
        shape_of((items, length, D), BF16),
        shape_of((items, length, FILTER), BF16),
        shape_of((items, length, FILTER), BF16),
        shape_of((items, length, D)),
        shape_of((items, length, D), BF16),
        shape_of((items, 2 * length, 4 * LANES), BF16),
        shape_of((items, 2 * length, 4 * LANES), BF16),
    ]
    (
        emb_low,
        proj,
        attention,
        banded,
        attend,
        mixed,
        normed_low,
        filtered,
        activ,
        summed,
        encoded,
        expand,
        expand_low,
    ) = run(
        encoder_body,
        (items // group,),
        ins,
        [full_spec(a) for a in ins],
        outs,
        [group_spec(a) for a in outs],
        micros=20,
        after=(stats,),
        name="encoder",
    )
    for shift, radix in stats_steps[1:]:
        stats = sum(send_parts([stats] * radix, shift, devices))

    ins = [mel_frames, durations, expand, expand_low, stats, mixm, start_pad, w_in, res_four, end_pad, place]
    kinds = [full_spec] * 10
    in_specs = [kind(a) for kind, a in zip(kinds, ins)] + [smem]
    in_specs[2] = in_specs[3] = pl.BlockSpec(memory_space=pl.ANY)
    in_specs[7] = pl.BlockSpec(
        (1,) + w_in.shape[1:],
        lambda s: (jnp.where(s <= STEP_POST, jnp.clip(s - 1, 0, WLAYERS - 1), STEPS - 1 - s), 0, 0),
    )
    dealt = ((WLAYERS - 1) * UNIT + TAIL) // 2
    outs = [
        *[shape_of((dealt, WIDE))] * 2,
        *halves_of(UNIT),
        shape_of((items, pairs, 4 * LANES), BF16),
        shape_of((items, pairs, 2 * LANES)),
    ]
    out_specs = [pl.BlockSpec(memory_space=pl.ANY)] * 6
    count = items * pairs
    kept, sent, last_kept, last_sent, flow, normal_grad = run(
        decoder_body,
        (STEPS,),
        ins,
        in_specs,
        outs,
        out_specs,
        [
            pltpu.VMEM((items, pairs, 2 * LANES), F32),
            pltpu.VMEM((items, pairs, LANES), BF16),
            pltpu.VMEM((WLAYERS, count, HID), BF16),
            pltpu.VMEM((WLAYERS, count, 2 * HID), BF16),
            pltpu.VMEM((count, HID), F32),
            pltpu.VMEM((count, HID), F32),
            pltpu.VMEM((items, pairs, LANES), F32),
            pltpu.VMEM((count, HID), BF16),
            pltpu.VMEM((items, pairs, LANES), F32),
            pltpu.VMEM((count, HID), BF16),
            pltpu.VMEM((count, 2 * HID), BF16),
            pltpu.VMEM((count, WKER * 2 * HID), BF16),
            pltpu.VMEM((HID, WKER * 2 * HID), BF16),
            pltpu.VMEM((2, UNIT, WIDE), F32),
            pltpu.VMEM((frames, LANES), F32),
            pltpu.VMEM((2 * LANES, HID), F32),
            pltpu.VMEM((LANES, HID), F32),
            pltpu.VMEM((2 * LANES, 2 * LANES), F32),
            pltpu.VMEM((TAIL, WIDE), F32),
            pltpu.VMEM(expand.shape, BF16),
            pltpu.VMEM(expand.shape, BF16),
            pltpu.VMEM((items, pairs, 4 * LANES), BF16),
            pltpu.VMEM((8, LANES), F32),
            pltpu.SemaphoreType.DMA((6 + 2 * WLAYERS,)),
        ],
        micros=80,
        name="decoder",
    )
    recv = swap(sent, 1, devices)
    upper = spread_level([[kept, recv]], 0, place, devices)
    last_recv = swap(last_sent, 1, devices)

    ins = [
        token_ids,
        durations,
        flow,
        encoded,
        summed,
        filtered,
        activ,
        normed_low,
        mixed,
        attend,
        attention,
        banded,
        proj,
        emb_low,
        wide,
        w_ff1,
        ff2_t,
        gain_two,
        prior_t,
        qkv_pad,
        relk_pad,
        relv_pad,
        out_pad,
        gain_one,
        place,
    ]
    kinds = [full_spec] * 2 + [group_spec] * 12 + [full_spec] * 10
    outs = halves_of(2 * UNIT + REST)
    fed_kept, fed_sent = run(
        encoder_back_body,
        (items // group,),
        ins,
        [kind(a) for kind, a in zip(kinds, ins)] + [smem],
        outs,
        [pl.BlockSpec(memory_space=pl.ANY)] * 2,
        [
            pltpu.VMEM((UNIT, WIDE), F32),
            pltpu.VMEM((UNIT, WIDE), F32),
            pltpu.VMEM((REST, WIDE), F32),
            pltpu.VMEM((VOCAB, D), F32),
            pltpu.VMEM((D, 6 * LANES), F32),
            pltpu.VMEM((2 * LANES, D), F32),
            pltpu.VMEM((LANES, LANES), F32),
            pltpu.VMEM((LANES, LANES), F32),
            pltpu.VMEM((2 * MEL, D), F32),
            pltpu.VMEM((8, D), F32),
            pltpu.SemaphoreType.DMA((6,)),
        ],
        after=(upper[0],),
        micros=30,
        name="encoder_back",
    )
    levels = len(digits(devices))
    upper, fed_sent, fed_kept = lax.optimization_barrier((upper, fed_sent, fed_kept))
    fed_recv = swap(fed_sent, 1, devices)
    for level in range(1, levels):
        upper = spread_level([upper], level, place, devices, (fed_kept,))
    units = [[last_kept, last_recv], [fed_kept, fed_recv]]
    lower = pair_out(units, place, devices, (upper[0],))
    upper = add_parts([upper], place, (lower[0][0],))[0]
    for level in reversed(range(2, levels)):
        upper = gather_level(upper, level, place, devices)
    lower = pair_next(lower, place, devices)
    upper = gather_pair(upper, 1, place, devices, (lower[0][0],))
    lower = pair_level(lower, 1, place, devices, (upper[0],))
    upper_parts = pair_join(*upper, place, devices, (lower[0],))
    for level in range(2, levels):
        lower = spread_level([lower], level, place, devices)
    lower = add_parts([lower], place, (upper_parts[0],))[0]
    for level in reversed(range(2, levels)):
        lower = gather_level(lower, level, place, devices)
    lower = gather_pair(lower, 1, place, devices)
    upper_parts, lower = lax.optimization_barrier((upper_parts, lower))
    upper_other = [swap(part, 1, devices) for part in upper_parts]
    lower_parts = pair_join(*lower, place, devices, (upper_other[0], upper_other[3]))
    in_grad, res_grad, last_grad, end_grad, start_grad, mix_grad, sums = unpack_upper(
        upper_parts, upper_other, place, small, ()
    )
    ins = [mel_frames, durations, normal_grad, stats, sums, small]
    kinds = [item_spec, full_spec, item_spec, full_spec, full_spec, full_spec]
    mel_grad, loss = run(
        frames_body,
        grid,
        ins,
        [kind(a) for kind, a in zip(kinds, ins)],
        [shape_of(mel_frames.shape), shape_of((1, 1))],
        [item_spec(mel_frames), pl.BlockSpec((1, 1), lambda b: (0, 0))],
        [pltpu.VMEM((frames, LANES), F32)],
        name="frames",
    )

    lower_parts = [lax.optimization_barrier((part, mel_grad))[0] for part in lower_parts]
    lower_other = [swap(part, 1, devices) for part in lower_parts]
    (
        in_grad,
        res_grad,
        ff1_grad,
        ff2_grad,
        table_grad,
        qkv_grad,
        out_grad,
        relk_grad,
        relv_grad,
        prior_grad,
        *norm_grads,
    ) = unpack_lower(lower_parts, lower_other, place, in_grad, res_grad)

    return (
        loss.reshape(()),
        mel_grad.transpose(0, 2, 1),
        table_grad,
        qkv_grad,
        relk_grad,
        relv_grad,
        out_grad,
        norm_grads[0],
        norm_grads[1],
        ff1_grad,
        ff2_grad.T,
        norm_grads[2],
        norm_grads[3],
        prior_grad.T,
        mix_grad[:4, :4],
        start_grad,
        in_grad,
        res_grad,
        last_grad,
        end_grad[: 2 * MEL].T,
    )


def solution(mesh):
    devices = mesh.shape["dp"]
    placed = (P("dp", None), P("dp", None), P("dp", None, None)) + (P(),) * 18
    return jax.shard_map(
        functools.partial(on_device, devices),
        mesh=mesh,
        in_specs=placed,
        out_specs=(P(), P("dp", None, None)) + (P(),) * 18,
        check_vma=False,
    )
```
